32 devices in a mesh: seq: 8 (over y, x, core), tp: 4 (over z).
Axes of the slice: x: 2, y: 2, z: 4, core: 2. Of those that a mesh axis runs over, the one named last changes fastest.
Arguments:
- block_in: bfloat16 [8, 1024, 2048], P(None, 'seq'), may hold values from -6 to 6
- segment_ids: int32 [8, 1024], replicated, may hold values from 0 to 7, as said below
- first_gain: bfloat16 [2048], replicated, may hold values from 0.25 to 1.75
- first_bias: bfloat16 [2048], replicated, may hold values from -3 to 3
- w_query: bfloat16 [2048, 2048], P(None, 'tp'), may hold values from -0.125 to 0.125
- w_key: bfloat16 [2048, 2048], P(None, 'tp'), may hold values from -0.125 to 0.125
- w_value: bfloat16 [2048, 2048], P(None, 'tp'), may hold values from -0.125 to 0.125
- head_gain: bfloat16 [2048], P('tp'), may hold values from 0.25 to 1.75
- head_bias: bfloat16 [2048], P('tp'), may hold values from -3 to 3
- w_out: bfloat16 [2048, 2048], P(None, 'tp'), may hold values from -0.125 to 0.125
- second_gain: bfloat16 [2048], replicated, may hold values from 0.25 to 1.75
- second_bias: bfloat16 [2048], replicated, may hold values from -3 to 3
- w_up: bfloat16 [2048, 8192], P(None, 'tp'), may hold values from -0.125 to 0.125
- hidden_gain: bfloat16 [8192], P('tp'), may hold values from 0.25 to 1.75
- hidden_bias: bfloat16 [8192], P('tp'), may hold values from -3 to 3
- w_down: bfloat16 [2048, 8192], P(None, 'tp'), may hold values from -0.088388348 to 0.088388348
- out_cotangent: bfloat16 [8, 1024, 2048], P(None, 'seq'), may hold values from -6 to 6
Outputs:
- block_out: bfloat16 [8, 1024, 2048], P(None, 'seq')
- input_grad: bfloat16 [8, 1024, 2048], P(None, 'seq')
- first_gain_grad: float32 [2048], P('seq')
- first_bias_grad: float32 [2048], P('seq')
- w_query_grad: float32 [2048, 2048], P('seq', 'tp')
- w_key_grad: float32 [2048, 2048], P('seq', 'tp')
- w_value_grad: float32 [2048, 2048], P('seq', 'tp')
- head_gain_grad: float32 [2048], P('tp')
- head_bias_grad: float32 [2048], P('tp')
- w_out_grad: float32 [2048, 2048], P('seq', 'tp')
- second_gain_grad: float32 [2048], P('seq')
- second_bias_grad: float32 [2048], P('seq')
- w_up_grad: float32 [2048, 8192], P('seq', 'tp')
- hidden_gain_grad: float32 [8192], P('tp')
- hidden_bias_grad: float32 [8192], P('tp')
- w_down_grad: float32 [2048, 8192], P('seq', 'tp')
The draws below stay inside these ranges and needn't reach their ends.
Inputs may be any that keep to these rules, and one draw needn't show every extreme that they name: `segment_ids`: in each row the ids start at 0, never fall and rise by at most one from one place to the next; a row holds 1 to 8 documents; in every draw one row, drawn from the seed, is a single document and another holds exactly 8.
All inputs are finite; a program needn't handle non-finite values.
Results may differ from the reference program's by a relative error of at most 0.02.
Values may be sent and summed in bfloat16 or wider, within the bound.
A program may use at most 320 MiB of HBM per device.

```python
import jax
import jax.numpy as jnp
from jax import lax

D = 2048
HEADS = 32
HEAD = 64
FF = 8192
ROWS = 8
MAXSEG = 8
LENGTH = 1024


def draw_segment_ids(key, part):
    key = jax.random.fold_in(key, 7)
    count_key, choose_key, place_key = jax.random.split(key, 3)
    doc_counts = jax.random.randint(count_key, (ROWS,), 1, MAXSEG + 1)
    row_order = jax.random.permutation(choose_key, ROWS)
    doc_counts = jnp.where(row_order == 0, 1, doc_counts)
    doc_counts = jnp.where(row_order == 1, MAXSEG, doc_counts)
    rank_table = jax.vmap(lambda row_key: jax.random.permutation(row_key, LENGTH - 1))(jax.random.split(place_key, ROWS))
    boundary = (rank_table < doc_counts[:, None] - 1).astype(jnp.int32)
    doc_ids = jnp.concatenate([jnp.zeros((ROWS, 1), jnp.int32), jnp.cumsum(boundary, axis=1)], axis=1)
    return doc_ids.astype(jnp.int32)


def draw_w_down(key, part):
    key = jax.random.fold_in(key, 11)
    noise_key, offset_key = jax.random.split(key)
    noise = jax.random.truncated_normal(noise_key, -6.0, 6.0, (D, FF), jnp.float32)
    offset = jax.random.truncated_normal(offset_key, -3.0, 3.0, (D, 1), jnp.float32)
    return ((noise + 0.5 * offset) * (1.0 / FF ** 0.5)).astype(jnp.bfloat16)


def raised(array, rng, source, target, blocks, factor):
    owner, partner = [(jnp.arange(array.shape[dim]) // (array.shape[dim] // blocks)).reshape([-1 if axis == dim else 1 for axis in range(array.ndim)]) for dim in (source, target)]
    chosen = jax.random.permutation(rng, blocks)[partner]
    strong = (owner == chosen) | (owner == (partner + blocks // 2) % blocks)
    return jnp.where(strong, factor * array, array)


def shard_levels(key, dims, pieces, low, high):
    def one(position, blocks):
        draws = jax.random.uniform(jax.random.fold_in(jax.random.fold_in(key, 6), position), (blocks,), jnp.float32, low / len(pieces), high / len(pieces))
        return jnp.repeat(jnp.exp(draws), dims[position] // blocks).reshape((-1,) + (1,) * (len(dims) - position - 1))

    loudness = one(*pieces[0])
    for cut in pieces[1:]:
        loudness = loudness * one(*cut)
    return loudness


def centred(own_key, dims, width, most, cuts=(), kind=jnp.bfloat16):
    factor_of = shard_levels(own_key, dims, cuts, -0.22, 0.18) if cuts else 1.0
    entries = jax.random.normal(own_key, dims, jnp.float32) * width * factor_of
    return jnp.minimum(jnp.maximum(entries, -most), most).astype(kind)


def bell_draw_with(stream_key, dims, deviation, bound, shards, heavy, kind=jnp.bfloat16):
    entries = deviation * jax.random.normal(stream_key, dims, jnp.float32)
    if shards:
        entries = entries * shard_levels(stream_key, dims, shards, -0.22, 0.18)
    return jnp.clip(raised(entries, jax.random.fold_in(stream_key, 3), *heavy), -bound, bound).astype(kind)


def setup_inputs(seed: int = 0) -> dict:
    arg_keys = jax.random.split(jax.random.key(seed), 18)
    block_in = centred(arg_keys[0], (ROWS, LENGTH, D), 1.0, 6.0, ((1, 8),))
    segment_ids = draw_segment_ids(jax.random.fold_in(arg_keys[17], 71), 0)
    first_gain = jnp.clip(1.0 + 0.15 * jax.random.normal(arg_keys[2], (D,), jnp.float32), 0.25, 1.75).astype(jnp.bfloat16)
    first_bias = centred(arg_keys[3], (D,), 0.5, 3.0)
    w_query = centred(arg_keys[4], (D, D), D ** -0.5, 0.125, ((1, 4),))
    w_key = centred(arg_keys[5], (D, D), D ** -0.5, 0.125, ((1, 4),))
    w_value = centred(arg_keys[6], (D, D), D ** -0.5, 0.125, ((1, 4),))
    head_gain = jnp.clip(1.0 + 0.15 * jax.random.normal(arg_keys[7], (D,), jnp.float32), 0.25, 1.75).astype(jnp.bfloat16)
    head_bias = centred(arg_keys[8], (D,), 0.5, 3.0, ((0, 4),))
    w_out = centred(arg_keys[9], (D, D), D ** -0.5, 0.125, ((1, 4),))
    second_gain = jnp.clip(1.0 + 0.15 * jax.random.normal(arg_keys[10], (D,), jnp.float32), 0.25, 1.75).astype(jnp.bfloat16)
    second_bias = centred(arg_keys[11], (D,), 0.5, 3.0)
    w_up = centred(arg_keys[12], (D, FF), D ** -0.5, 0.125, ((1, 4),))
    hidden_gain = jnp.clip(1.0 + 0.15 * jax.random.normal(arg_keys[13], (FF,), jnp.float32), 0.25, 1.75).astype(jnp.bfloat16)
    hidden_bias = centred(arg_keys[14], (FF,), 0.5, 3.0, ((0, 4),))
    w_down = draw_w_down(jax.random.fold_in(arg_keys[17], 71), 0)
    out_cotangent = bell_draw_with(arg_keys[16], (ROWS, LENGTH, D), 1.0, 6.0, ((1, 8),), (1, 2, 8, 2.0))
    return {"block_in": block_in, "segment_ids": segment_ids, "first_gain": first_gain, "first_bias": first_bias, "w_query": w_query, "w_key": w_key, "w_value": w_value, "head_gain": head_gain, "head_bias": head_bias, "w_out": w_out, "second_gain": second_gain, "second_bias": second_bias, "w_up": w_up, "hidden_gain": hidden_gain, "hidden_bias": hidden_bias, "w_down": w_down, "out_cotangent": out_cotangent}


EPSILON = 1e-05
MASKED = -1e+30
HIGHEST_PRECISION = lax.Precision.HIGHEST

@jax.custom_vjp
def low(v):
    return lax.optimization_barrier(v.astype(jnp.bfloat16)).astype(jnp.float32)

@jax.custom_vjp
def low_back(v):
    return v

def low_keep(v):
    return (low(v), None)

def low_pass(kept, grad):
    return (grad,)

def back_keep(v):
    return (v, None)

def back_low(kept, grad):
    return (low(grad),)
low.defvjp(low_keep, low_pass)
low_back.defvjp(back_keep, back_low)

def layer_norm(values, gain_vec, bias_vec):
    center = lax.optimization_barrier(jnp.mean(values, axis=-1, keepdims=True))
    spread = lax.optimization_barrier(jnp.mean(jnp.square(values - center), axis=-1, keepdims=True))
    return (values - center) * lax.rsqrt(spread + EPSILON) * gain_vec + bias_vec

def rotation_tables(positions, head_size):
    half_size = head_size // 2
    index_pairs = jnp.arange(half_size, dtype=jnp.float32)
    theta_rate = jnp.exp(-2.0 * index_pairs / head_size * jnp.log(10000.0))
    zeta_base = (2.0 * index_pairs + 0.4 * head_size) / (1.4 * head_size)
    place_float = positions.astype(jnp.float32)[..., None]
    angles = place_float * theta_rate
    growth = jnp.exp(jnp.log(zeta_base) * place_float / 512.0)
    return (jnp.cos(angles), jnp.sin(angles), growth)

def rotate(values, cos_table, sin_table, factor):
    half_size = values.shape[-1] // 2
    first_half = values[..., :half_size]
    second_half = values[..., half_size:]
    cos_heads = cos_table[..., None, :]
    sin_heads = sin_table[..., None, :]
    factor_heads = factor[..., None, :]
    return jnp.concatenate([(first_half * cos_heads - second_half * sin_heads) * factor_heads, (second_half * cos_heads + first_half * sin_heads) * factor_heads], axis=-1)

def positions_and_mask(segments):
    index_row = jnp.arange(segments.shape[-1], dtype=jnp.int32)
    earlier = lax.optimization_barrier(jnp.sum((segments[:, None, :] < segments[:, :, None]).astype(jnp.int32), axis=-1))
    causal = index_row[None, :] <= index_row[:, None]
    same_doc = segments[:, :, None] == segments[:, None, :]
    return (index_row[None, :] - earlier, causal[None] & same_doc)

@jax.checkpoint
def attend_block(operands):
    query_block, key_block, value_block, mask_block = operands
    scores = jnp.einsum('qhd,khd->hqk', query_block, key_block, precision=HIGHEST_PRECISION)
    scores = low_back(scores * HEAD ** (-0.5))
    scores = jnp.where(mask_block[None], scores, MASKED)
    top_score = lax.optimization_barrier(jnp.max(scores, axis=-1, keepdims=True))
    expo = jnp.exp(scores - top_score)
    prob_rows = low(expo / lax.optimization_barrier(jnp.sum(expo, axis=-1, keepdims=True)))
    return jnp.einsum('hqk,khd->qhd', prob_rows, value_block, precision=HIGHEST_PRECISION)

def forward(weights, block_rows, segments):
    first_gain, first_bias, w_query, w_key, w_value, head_gain, head_bias, w_out, second_gain, second_bias, w_up, hidden_gain, hidden_bias, w_down = weights
    group_rows, row_len, feature_count = block_rows.shape
    positions, visible = positions_and_mask(segments)
    cos_table, sin_table, growth = rotation_tables(positions, HEAD)
    first_act = low(layer_norm(block_rows, first_gain, first_bias))
    query_pre = low_back(jnp.matmul(first_act, w_query, precision=HIGHEST_PRECISION)).reshape(group_rows, row_len, HEADS, HEAD)
    key_pre = low_back(jnp.matmul(first_act, w_key, precision=HIGHEST_PRECISION)).reshape(group_rows, row_len, HEADS, HEAD)
    value_pre = low_back(jnp.matmul(first_act, w_value, precision=HIGHEST_PRECISION)).reshape(group_rows, row_len, HEADS, HEAD)
    query_rot = low(rotate(query_pre, cos_table, sin_table, growth))
    key_rot = low(rotate(key_pre, cos_table, sin_table, 1.0 / growth))
    value_low = low(value_pre)
    block_count = HEADS // 8

    def by_blocks(values):
        shaped = values.reshape(group_rows, row_len, block_count, 8, HEAD).transpose(0, 2, 1, 3, 4)
        return shaped.reshape(group_rows * block_count, row_len, 8, HEAD)
    mask_blocks = jnp.repeat(visible, block_count, axis=0)
    mixed_out = lax.map(attend_block, (by_blocks(query_rot), by_blocks(key_rot), by_blocks(value_low), mask_blocks))
    mixed_out = mixed_out.reshape(group_rows, block_count, row_len, 8, HEAD).transpose(0, 2, 1, 3, 4)
    mixed_out = low_back(mixed_out.reshape(group_rows, row_len, feature_count))
    head_act = low(layer_norm(mixed_out, head_gain, head_bias))
    middle = block_rows + low_back(jnp.matmul(head_act, w_out.T, precision=HIGHEST_PRECISION))
    second_act = low(layer_norm(middle, second_gain, second_bias))
    up_pre = low_back(jnp.matmul(second_act, w_up, precision=HIGHEST_PRECISION))
    hidden_act = low(layer_norm(jax.nn.gelu(up_pre, approximate=False), hidden_gain, hidden_bias))
    return middle + low_back(jnp.matmul(hidden_act, w_down.T, precision=HIGHEST_PRECISION))

def reference(block_in, segment_ids, first_gain, first_bias, w_query, w_key, w_value, head_gain, head_bias, w_out, second_gain, second_bias, w_up, hidden_gain, hidden_bias, w_down, out_cotangent):
    weights = tuple((weight.astype(jnp.float32) for weight in (first_gain, first_bias, w_query, w_key, w_value, head_gain, head_bias, w_out, second_gain, second_bias, w_up, hidden_gain, hidden_bias, w_down)))
    groups = ROWS // 2
    blocks = block_in.astype(jnp.float32).reshape(groups, 2, LENGTH, D)
    seg_groups = segment_ids.reshape(groups, 2, LENGTH)
    cot_groups = out_cotangent.astype(jnp.float32).reshape(groups, 2, LENGTH, D)

    def scan_step(totals, step_items):
        block_rows, segments, cotangent = step_items
        result, pullback = jax.vjp(lambda params, inputs: forward(params, inputs, segments), weights, block_rows)
        grad_weights, grad_block = pullback(cotangent)
        totals = jax.tree.map(jnp.add, totals, grad_weights)
        return (totals, (result.astype(jnp.bfloat16), grad_block.astype(jnp.bfloat16)))
    zero_grads = tuple((jnp.zeros_like(weight) for weight in weights))
    totals, (out_rows, grad_rows) = lax.scan(scan_step, zero_grads, (blocks, seg_groups, cot_groups))
    block_out = out_rows.reshape(ROWS, LENGTH, D)
    input_grad = grad_rows.reshape(ROWS, LENGTH, D)
    return (block_out, input_grad, totals[0], totals[1], totals[2], totals[3], totals[4], totals[5], totals[6], totals[7], totals[8], totals[9], totals[10], totals[11], totals[12], totals[13])
```

```python
import functools
import math

import jax
import jax.numpy as jnp
from jax import lax
from jax.experimental import pallas as pl
from jax.experimental.pallas import tpu as pltpu
from jax.sharding import PartitionSpec as P

HEAD = 64
LANES = 128
BLOCK = 256
EPSILON = 1e-05
MASKED = -1e30
MESH = pl.DeviceIdType.MESH
F32 = jnp.float32
BF16 = jnp.bfloat16
VMEM_LIMIT = 58 * 1024 * 1024


def dot(left, right, left_dim, right_dim):
    return lax.dot_general(
        left, right, (((left_dim,), (right_dim,)), ((), ())), preferred_element_type=F32
    )


def seq_barrier(count):
    me = lax.axis_index("seq")
    barrier = pltpu.get_barrier_semaphore()
    for k in range(1, count):
        pl.semaphore_signal(
            barrier, inc=1, device_id={"seq": lax.rem(me + k, count)}, device_id_type=MESH
        )
    pl.semaphore_wait(barrier, count - 1)


def rows_out_kernel(count, groups, num, *refs):
    sources, targets = refs[:num], refs[num : 2 * num]
    send_sem, recv_sem, own_sem = refs[2 * num :]
    me = lax.axis_index("seq")
    span = sources[0].shape[1]
    width = targets[0].shape[1]
    seq_barrier(count)

    def piece(source, device):
        lane = pl.multiple_of(lax.rem(device, groups) * width, LANES)
        return source.at[device // groups, :, pl.ds(lane, width)]

    def place(target):
        return target.at[pl.ds(pl.multiple_of(me * span, LANES), span), :]

    copies = []
    for k in range(1, count):
        device = lax.rem(me + k, count)
        for i in range(num):
            copy = pltpu.make_async_remote_copy(
                src_ref=piece(sources[i], device),
                dst_ref=place(targets[i]),
                send_sem=send_sem.at[i, k],
                recv_sem=recv_sem.at[i, k],
                device_id={"seq": device},
                device_id_type=MESH,
            )
            copy.start()
            copies.append(copy)
    for i in range(num):
        copy = pltpu.make_async_copy(piece(sources[i], me), place(targets[i]), own_sem.at[i])
        copy.start()
        copies.append(copy)
    for copy in copies:
        copy.wait()


def rows_back_kernel(count, groups, num, *refs):
    sources, targets = refs[:num], refs[num : 2 * num]
    send_sem, recv_sem, own_sem = refs[2 * num :]
    me = lax.axis_index("seq")
    span = targets[0].shape[1]
    width = sources[0].shape[1]
    seq_barrier(count)

    def piece(source, device):
        return source.at[pl.ds(pl.multiple_of(device * span, LANES), span), :]

    def place(target):
        lane = pl.multiple_of(lax.rem(me, groups) * width, LANES)
        return target.at[me // groups, :, pl.ds(lane, width)]

    copies = []
    for k in range(1, count):
        device = lax.rem(me + k, count)
        for i in range(num):
            copy = pltpu.make_async_remote_copy(
                src_ref=piece(sources[i], device),
                dst_ref=place(targets[i]),
                send_sem=send_sem.at[i, k],
                recv_sem=recv_sem.at[i, k],
                device_id={"seq": device},
                device_id_type=MESH,
            )
            copy.start()
            copies.append(copy)
    for i in range(num):
        copy = pltpu.make_async_copy(piece(sources[i], me), place(targets[i]), own_sem.at[i])
        copy.start()
        copies.append(copy)
    for copy in copies:
        copy.wait()


def exchange(kernel, count, groups, arrays, shape, collective_id):
    num = len(arrays)
    outs = pl.pallas_call(
        functools.partial(kernel, count, groups, num),
        out_shape=[jax.ShapeDtypeStruct(shape, BF16)] * num,
        in_specs=[pl.BlockSpec(memory_space=pl.ANY)] * num,
        out_specs=[pl.BlockSpec(memory_space=pl.ANY)] * num,
        scratch_shapes=[
            pltpu.SemaphoreType.DMA((num, count)),
            pltpu.SemaphoreType.DMA((num, count)),
            pltpu.SemaphoreType.DMA((num,)),
        ],
        compiler_params=pltpu.CompilerParams(collective_id=collective_id, has_side_effects=True),
    )(*arrays)
    return outs


def swap_halves(values):
    lane = lax.broadcasted_iota(jnp.int32, values.shape, 1)
    return jnp.where(
        lane % HEAD < HEAD // 2,
        pltpu.roll(values, LANES - HEAD // 2, 1),
        pltpu.roll(values, HEAD // 2, 1),
    )


def head_masks(values):
    lane = lax.broadcasted_iota(jnp.int32, values.shape, 1)
    zero = jnp.zeros_like(values)
    return jnp.where(lane < HEAD, values, zero), jnp.where(lane < HEAD, zero, values)


def attend_kernel(length, q_ref, k_ref, v_ref, tab_ref, segc_ref, segr_ref, o_ref, lse_ref, bias, qs, ks):
    blocks = length // BLOCK

    @pl.when(pl.program_id(0) == 0)
    def _():
        for qb in range(blocks):
            rows = slice(qb * BLOCK, (qb + 1) * BLOCK)
            keys = (qb + 1) * BLOCK
            same = segc_ref[rows, :] == segr_ref[:, :keys]
            row = lax.broadcasted_iota(jnp.int32, (BLOCK, keys), 0) + qb * BLOCK
            col = lax.broadcasted_iota(jnp.int32, (BLOCK, keys), 1)
            bias[rows, :keys] = jnp.where(same & (col <= row), 0.0, MASKED)

    for qb in range(blocks):
        rows = slice(qb * BLOCK, (qb + 1) * BLOCK)
        q = q_ref[rows, :].astype(F32)
        q = (q * tab_ref[0, rows, :] + swap_halves(q) * tab_ref[1, rows, :]) * (HEAD**-0.5)
        q0, q1 = head_masks(q)
        qs[0, rows, :] = q0.astype(BF16)
        qs[1, rows, :] = q1.astype(BF16)
        k = k_ref[rows, :].astype(F32)
        k = k * tab_ref[2, rows, :] + swap_halves(k) * tab_ref[3, rows, :]
        ks[rows, :] = k.astype(BF16)
    for qb in range(blocks):
        rows = slice(qb * BLOCK, (qb + 1) * BLOCK)
        keys = (qb + 1) * BLOCK
        outs = []
        logs = []
        for h in range(2):
            scores = dot(qs[h, rows, :], ks[:keys, :], 1, 1) + bias[rows, :keys]
            top = jnp.max(scores, axis=1, keepdims=True)
            expo = jnp.exp(scores - top)
            total = jnp.sum(expo, axis=1, keepdims=True)
            outs.append(dot(expo.astype(BF16), v_ref[:keys, :], 1, 0) / total)
            logs.append(jnp.broadcast_to(top + jnp.log(total), (BLOCK, LANES)))
        lane = lax.broadcasted_iota(jnp.int32, (BLOCK, LANES), 1)
        o_ref[rows, :] = jnp.where(lane < HEAD, outs[0], outs[1]).astype(BF16)
        logs_t = jnp.transpose(jnp.where(lane < HEAD, logs[0], logs[1]))
        lse_ref[0, 0:1, rows] = logs_t[0:1]
        lse_ref[0, 1:2, rows] = logs_t[HEAD : HEAD + 1]


def attend(q, k, v, tables, seg_col, seg_row):
    length, width = q.shape
    pairs = width // LANES
    lane_block = pl.BlockSpec((length, LANES), lambda p: (0, p))
    return pl.pallas_call(
        functools.partial(attend_kernel, length),
        grid=(pairs,),
        out_shape=[
            jax.ShapeDtypeStruct((length, width), BF16),
            jax.ShapeDtypeStruct((pairs, 8, length), F32),
        ],
        in_specs=[
            lane_block,
            lane_block,
            lane_block,
            pl.BlockSpec((4, length, LANES), lambda p: (0, 0, 0)),
            pl.BlockSpec((length, 1), lambda p: (0, 0)),
            pl.BlockSpec((1, length), lambda p: (0, 0)),
        ],
        out_specs=[lane_block, pl.BlockSpec((1, 8, length), lambda p: (p, 0, 0))],
        scratch_shapes=[
            pltpu.VMEM((length, length), F32),
            pltpu.VMEM((2, length, LANES), BF16),
            pltpu.VMEM((length, LANES), BF16),
        ],
        compiler_params=pltpu.CompilerParams(vmem_limit_bytes=VMEM_LIMIT),
    )(q, k, v, tables, seg_col, seg_row)


def attend_back_kernel(
    length, q_ref, k_ref, v_ref, do_ref, o_ref, lse_ref, tab_ref, segc_ref, segr_ref,
    dq_ref, dk_ref, dv_ref, bias, qs, ks, kms, dos, delta, dq, dk, dv,
):
    blocks = length // BLOCK

    @pl.when(pl.program_id(0) == 0)
    def _():
        for kb in range(blocks):
            rows = slice(kb * BLOCK, (kb + 1) * BLOCK)
            first = kb * BLOCK
            shape = (BLOCK, length - first)
            same = segc_ref[rows, :] == segr_ref[:, first:]
            key = lax.broadcasted_iota(jnp.int32, shape, 0)
            query = lax.broadcasted_iota(jnp.int32, shape, 1)
            bias[rows, first:] = jnp.where(same & (key <= query), 0.0, MASKED)

    for qb in range(blocks):
        rows = slice(qb * BLOCK, (qb + 1) * BLOCK)
        q = q_ref[rows, :].astype(F32)
        q = (q * tab_ref[0, rows, :] + swap_halves(q) * tab_ref[1, rows, :]) * (HEAD**-0.5)
        q0, q1 = head_masks(q)
        qs[0, rows, :] = q0.astype(BF16)
        qs[1, rows, :] = q1.astype(BF16)
        k = k_ref[rows, :].astype(F32)
        k = k * tab_ref[2, rows, :] + swap_halves(k) * tab_ref[3, rows, :]
        ks[rows, :] = k.astype(BF16)
        k0, k1 = head_masks(k)
        kms[0, rows, :] = k0.astype(BF16)
        kms[1, rows, :] = k1.astype(BF16)
        grad = do_ref[rows, :].astype(F32)
        d0, d1 = head_masks(grad)
        dos[0, rows, :] = d0.astype(BF16)
        dos[1, rows, :] = d1.astype(BF16)
        prod = jnp.transpose(grad * o_ref[rows, :].astype(F32))
        delta[0:1, rows] = jnp.sum(prod[:HEAD], axis=0, keepdims=True)
        delta[1:2, rows] = jnp.sum(prod[HEAD:], axis=0, keepdims=True)
    dq[...] = jnp.zeros_like(dq)
    dk[...] = jnp.zeros_like(dk)
    dv[...] = jnp.zeros_like(dv)
    for qb in range(blocks):
        cols = slice(qb * BLOCK, (qb + 1) * BLOCK)
        for kb in range(qb + 1):
            rows = slice(kb * BLOCK, (kb + 1) * BLOCK)
            for h in range(2):
                scores = dot(ks[rows, :], qs[h, cols, :], 1, 1) + bias[rows, cols]
                probs = jnp.exp(scores - lse_ref[0, h : h + 1, cols])
                grads = dot(v_ref[rows, :], dos[h, cols, :], 1, 1)
                dscores = (probs * (grads - delta[h : h + 1, cols])).astype(BF16)
                dv[rows, :] += dot(probs.astype(BF16), dos[h, cols, :], 1, 0)
                dk[rows, :] += dot(dscores, qs[h, cols, :], 1, 0)
                dq[cols, :] += dot(dscores, kms[h, rows, :], 0, 0)
    for qb in range(blocks):
        rows = slice(qb * BLOCK, (qb + 1) * BLOCK)
        grad = dq[rows, :] * (HEAD**-0.5)
        dq_ref[rows, :] = (
            grad * tab_ref[0, rows, :] - swap_halves(grad) * tab_ref[1, rows, :]
        ).astype(BF16)
        grad = dk[rows, :]
        dk_ref[rows, :] = (
            grad * tab_ref[2, rows, :] - swap_halves(grad) * tab_ref[3, rows, :]
        ).astype(BF16)
        dv_ref[rows, :] = dv[rows, :].astype(BF16)


def attend_back(q, k, v, do, o, lse, tables, seg_col, seg_row):
    length, width = q.shape
    pairs = width // LANES
    lane_block = pl.BlockSpec((length, LANES), lambda p: (0, p))
    return pl.pallas_call(
        functools.partial(attend_back_kernel, length),
        grid=(pairs,),
        out_shape=[jax.ShapeDtypeStruct((length, width), BF16)] * 3,
        in_specs=[lane_block] * 5
        + [
            pl.BlockSpec((1, 8, length), lambda p: (p, 0, 0)),
            pl.BlockSpec((4, length, LANES), lambda p: (0, 0, 0)),
            pl.BlockSpec((length, 1), lambda p: (0, 0)),
            pl.BlockSpec((1, length), lambda p: (0, 0)),
        ],
        out_specs=[lane_block] * 3,
        scratch_shapes=[
            pltpu.VMEM((length, length), F32),
            pltpu.VMEM((2, length, LANES), BF16),
            pltpu.VMEM((length, LANES), BF16),
            pltpu.VMEM((2, length, LANES), BF16),
            pltpu.VMEM((2, length, LANES), BF16),
            pltpu.VMEM((8, length), F32),
            pltpu.VMEM((length, LANES), F32),
            pltpu.VMEM((length, LANES), F32),
            pltpu.VMEM((length, LANES), F32),
        ],
        compiler_params=pltpu.CompilerParams(vmem_limit_bytes=VMEM_LIMIT),
    )(q, k, v, do, o, lse, tables, seg_col, seg_row)


def norm_parts(values):
    center = jnp.mean(values, axis=-1, keepdims=True)
    shifted = values - center
    inverse = lax.rsqrt(jnp.mean(shifted * shifted, axis=-1, keepdims=True) + EPSILON)
    return shifted * inverse, inverse


def fold(values):
    rows, width = values.shape
    return jnp.sum(values.reshape(rows // 8, 8, width), axis=0)


def finish_middle(total, here, own, ins, outs):
    x_ref, gain_ref, bias_ref = ins
    middle = x_ref[here, :].astype(F32) + total
    outs[0][own, :] = middle
    normed, _ = norm_parts(middle)
    return normed * gain_ref[...] + bias_ref[...]


def finish_out(total, here, own, ins, outs):
    return ins[0][own, :] + total


def finish_back(total, here, own, ins, outs):
    base_ref, values_ref, gain_ref = ins[:3]
    flip = len(outs) == 1
    base = base_ref[own if flip else here, :].astype(F32)
    values = values_ref[here if flip else own, :].astype(F32)
    normed, inverse = norm_parts(values)
    scaled = total * gain_ref[...]
    grad = base + inverse * (
        scaled
        - jnp.mean(scaled, axis=-1, keepdims=True)
        - normed * jnp.mean(scaled * normed, axis=-1, keepdims=True)
    )
    outs[0][0] += fold(total * normed)
    outs[0][1] += fold(total)
    if not flip:
        outs[1][own, :] = grad
    return grad


def line_kernel(finish, count, chunks, num_in, num_out, clear, *refs):
    part_ref, ins = refs[0], refs[1 : 1 + num_in]
    out_ref, outs = refs[1 + num_in], refs[2 + num_in : 2 + num_in + num_out]
    in_a, in_b, send_a, send_b = refs[2 + num_in + num_out : 6 + num_in + num_out]
    (rsa_s, rsa_r, rsb_s, rsb_r, aga_s, aga_r, agb_s, agb_r) = refs[6 + num_in + num_out :]
    z = lax.axis_index("tp")
    half = part_ref.shape[0] // 2
    size = half // chunks
    lag = 2 * (count - 1)
    first, last = z == 0, z == count - 1
    up = jnp.minimum(z + 1, count - 1)
    down = jnp.maximum(z - 1, 0)

    barrier = pltpu.get_barrier_semaphore()

    @pl.when(jnp.logical_not(last))
    def _():
        pl.semaphore_signal(barrier, inc=1, device_id={"tp": up}, device_id_type=MESH)

    @pl.when(jnp.logical_not(first))
    def _():
        pl.semaphore_signal(barrier, inc=1, device_id={"tp": down}, device_id_type=MESH)

    @pl.when(first | last)
    def _():
        pl.semaphore_wait(barrier, 1)

    @pl.when(jnp.logical_not(first | last))
    def _():
        pl.semaphore_wait(barrier, 2)

    if clear:
        outs[0][...] = jnp.zeros_like(outs[0])

    def own_rows(c):
        return pl.ds(pl.multiple_of(c * size, size), size)

    def a_rows(c):
        return own_rows(c)

    def b_rows(c):
        return pl.ds(pl.multiple_of(half + c * size, size), size)

    def hop(source, target, send, recv, c, device):
        return pltpu.make_async_remote_copy(
            src_ref=source,
            dst_ref=target,
            send_sem=send.at[c],
            recv_sem=recv.at[c],
            device_id={"tp": device},
            device_id_type=MESH,
        )

    def gather_a(c):
        rows = out_ref.at[a_rows(c), :]
        return hop(rows, rows, aga_s, aga_r, c, up)

    def gather_b(c):
        rows = out_ref.at[b_rows(c), :]
        return hop(rows, rows, agb_s, agb_r, c, down)

    def reduce_a(c, source):
        return hop(source, in_a.at[own_rows(c), :], rsa_s, rsa_r, c, down)

    def reduce_b(c, source):
        return hop(source, in_b.at[own_rows(c), :], rsb_s, rsb_r, c, up)

    def reduce_step(c, rows, landed, staged, move, gather, starts, ends):
        here = rows(c)
        own = own_rows(c)

        @pl.when(starts)
        def _():
            move(c, part_ref.at[here, :]).start()

        @pl.when(jnp.logical_not(starts))
        def _():
            move(c, part_ref.at[here, :]).wait_recv()

        @pl.when(jnp.logical_not(starts | ends))
        def _():
            staged[own, :] = (
                landed[own, :].astype(F32) + part_ref[here, :].astype(F32)
            ).astype(BF16)
            move(c, staged.at[own, :]).start()

        @pl.when(ends)
        def _():
            total = landed[own, :].astype(F32) + part_ref[here, :].astype(F32)
            out_ref[here, :] = finish(total, here, own, ins, outs).astype(BF16)
            gather(c).start()

    def gather_step(c, gather, starts, ends):
        @pl.when(jnp.logical_not(starts))
        def _():
            gather(c).wait_recv()

        @pl.when(jnp.logical_not(starts | ends))
        def _():
            gather(c).start()

    def step(t, carry):
        @pl.when(t < chunks)
        def _():
            reduce_step(t, a_rows, in_a, send_a, reduce_a, gather_a, last, first)
            reduce_step(t, b_rows, in_b, send_b, reduce_b, gather_b, first, last)

        @pl.when(t >= lag)
        def _():
            gather_step(t - lag, gather_a, first, last)
            gather_step(t - lag, gather_b, last, first)

        return carry

    lax.fori_loop(0, chunks + lag, step, 0)

    def drain(c, carry):
        @pl.when(jnp.logical_not(first))
        def _():
            reduce_a(c, send_a.at[own_rows(c), :]).wait_send()
            gather_b(c).wait_send()

        @pl.when(jnp.logical_not(last))
        def _():
            reduce_b(c, send_b.at[own_rows(c), :]).wait_send()
            gather_a(c).wait_send()

        return carry

    lax.fori_loop(0, chunks, drain, 0)


def line_sum(finish, count, part, ins, out_shapes, clear, collective_id):
    tokens, width = part.shape
    half = tokens // 2
    chunks = 16
    whole = pl.BlockSpec(memory_space=pltpu.VMEM)
    return pl.pallas_call(
        functools.partial(
            line_kernel, finish, count, chunks, len(ins), len(out_shapes), clear
        ),
        out_shape=[jax.ShapeDtypeStruct((tokens, width), BF16)] + out_shapes,
        in_specs=[whole] * (1 + len(ins)),
        out_specs=[whole] * (1 + len(out_shapes)),
        scratch_shapes=[pltpu.VMEM((half, width), BF16)] * 4
        + [pltpu.SemaphoreType.DMA((chunks,))] * 8,
        compiler_params=pltpu.CompilerParams(
            collective_id=collective_id, has_side_effects=True, vmem_limit_bytes=VMEM_LIMIT
        ),
    )(part, *ins)


def matmul(left, right, left_dim, right_dim, kind=F32):
    return dot(left, right, left_dim, right_dim).astype(kind)


def rotation_tables(positions):
    half_size = HEAD // 2
    index_pairs = jnp.arange(half_size, dtype=F32)
    theta_rate = jnp.exp(-2.0 * index_pairs / HEAD * jnp.log(10000.0))
    zeta_base = (2.0 * index_pairs + 0.4 * HEAD) / (1.4 * HEAD)
    place_float = positions.astype(F32)[..., None]
    angles = place_float * theta_rate
    power = jnp.log(zeta_base) * place_float / 512.0
    cos_part, sin_part = jnp.cos(angles), jnp.sin(angles)
    grow, shrink = jnp.exp(power), jnp.exp(-power)
    cos_full = jnp.concatenate([cos_part] * 4, axis=-1)
    sin_full = jnp.concatenate([-sin_part, sin_part] * 2, axis=-1)
    grow = jnp.concatenate([grow] * 4, axis=-1)
    shrink = jnp.concatenate([shrink] * 4, axis=-1)
    return jnp.stack([cos_full * grow, sin_full * grow, cos_full * shrink, sin_full * shrink])


def body(
    seq_count,
    tp_count,
    block_in,
    segment_ids,
    first_gain,
    first_bias,
    w_query,
    w_key,
    w_value,
    head_gain,
    head_bias,
    w_out,
    second_gain,
    second_bias,
    w_up,
    hidden_gain,
    hidden_bias,
    w_down,
    out_cotangent,
):
    seq_index = lax.axis_index("seq")
    row_count, span, model_width = block_in.shape
    length = span * seq_count
    tokens = row_count * span
    head_width = w_query.shape[1]
    hidden_width = w_up.shape[1] * tp_count
    groups = seq_count // row_count
    width = head_width // groups

    first_gain_f = first_gain.astype(F32)[None]
    first_bias_f = first_bias.astype(F32)[None]
    second_gain_f = second_gain.astype(F32)[None]
    second_bias_f = second_bias.astype(F32)[None]
    head_gain_f = head_gain.astype(F32)[None]
    head_bias_f = head_bias.astype(F32)[None]
    hidden_gain_f = hidden_gain.astype(F32)[None]
    hidden_bias_f = hidden_bias.astype(F32)[None]

    seg_row = lax.dynamic_slice_in_dim(segment_ids, seq_index // groups, 1, 0)
    seg_col = seg_row.reshape(length, 1)
    earlier = jnp.sum((seg_row < seg_col).astype(jnp.int32), axis=-1)
    tables = rotation_tables(jnp.arange(length, dtype=jnp.int32) - earlier)

    block = block_in.reshape(tokens, model_width)
    cotangent = out_cotangent.reshape(tokens, model_width)

    normed_one, _ = norm_parts(block.astype(F32))
    first_act = (normed_one * first_gain_f + first_bias_f).astype(BF16)
    shape3 = (row_count, span, head_width)
    query = matmul(first_act, w_query, 1, 0, BF16).reshape(shape3)
    key = matmul(first_act, w_key, 1, 0, BF16).reshape(shape3)
    value = matmul(first_act, w_value, 1, 0, BF16).reshape(shape3)
    q_row, k_row, v_row = exchange(
        rows_out_kernel, seq_count, groups, (query, key, value), (length, width), 1
    )
    o_row, lse = attend(q_row, k_row, v_row, tables, seg_col, seg_row)
    (mixed,) = exchange(rows_back_kernel, seq_count, groups, (o_row,), shape3, 2)
    mixed = mixed.reshape(tokens, head_width).astype(F32)
    head_sums = lax.psum(jnp.stack([jnp.sum(mixed, axis=-1), jnp.sum(mixed * mixed, axis=-1)]), "tp")
    head_center = head_sums[0][:, None] / model_width
    head_inverse = lax.rsqrt(
        head_sums[1][:, None] / model_width - head_center * head_center + EPSILON
    )
    head_normed = (mixed - head_center) * head_inverse
    head_act = (head_normed * head_gain_f + head_bias_f).astype(BF16)
    out_part = matmul(head_act, w_out, 1, 1, BF16)
    own_shape = jax.ShapeDtypeStruct((tokens // 2, model_width), F32)
    sums_shape = jax.ShapeDtypeStruct((2, 8, model_width), F32)
    second_act, middle_own = line_sum(
        finish_middle, tp_count, out_part, (block, second_gain_f, second_bias_f), [own_shape], False, 3
    )

    up_pre = matmul(second_act, w_up, 1, 0)
    grad_hidden_act = matmul(cotangent, w_down, 1, 0)
    cdf = 0.5 * lax.erfc(up_pre * (-(0.5**0.5)))
    gelu_out = up_pre * cdf
    hidden_scaled = grad_hidden_act * hidden_gain_f
    stats = lax.psum(
        jnp.stack(
            [
                jnp.sum(gelu_out, axis=-1),
                jnp.sum(gelu_out * gelu_out, axis=-1),
                jnp.sum(hidden_scaled, axis=-1),
                jnp.sum(hidden_scaled * gelu_out, axis=-1),
            ]
        ),
        "tp",
    )
    stats = stats[:, :, None] / hidden_width
    hidden_center = stats[0]
    hidden_inverse = lax.rsqrt(stats[1] - hidden_center * hidden_center + EPSILON)
    hidden_normed = (gelu_out - hidden_center) * hidden_inverse
    hidden_act = (hidden_normed * hidden_gain_f + hidden_bias_f).astype(BF16)
    hidden_gain_grad = jnp.sum(grad_hidden_act * hidden_normed, axis=0)
    hidden_bias_grad = jnp.sum(grad_hidden_act, axis=0)
    hidden_cross = hidden_inverse * (stats[3] - hidden_center * stats[2])
    grad_gelu = hidden_inverse * (hidden_scaled - stats[2] - hidden_normed * hidden_cross)
    pdf = jnp.exp(-0.5 * up_pre * up_pre) * (1.0 / math.sqrt(2.0 * math.pi))
    grad_up = (grad_gelu * (cdf + up_pre * pdf)).astype(BF16)

    second_part = matmul(grad_up, w_up, 1, 1, BF16)
    grad_middle_low, second_sums, grad_middle_own = line_sum(
        finish_back,
        tp_count,
        second_part,
        (cotangent, middle_own, second_gain_f),
        [sums_shape, own_shape],
        True,
        4,
    )
    down_part = matmul(hidden_act, w_down, 1, 1, BF16)
    (block_out,) = line_sum(finish_out, tp_count, down_part, (middle_own,), [], False, 5)

    def scatter(grad):
        return lax.psum_scatter(grad, "seq", scatter_dimension=0, tiled=True).astype(F32)

    w_down_grad = scatter(matmul(cotangent, hidden_act, 0, 0, BF16))
    w_up_grad = scatter(matmul(second_act, grad_up, 0, 0, BF16))
    w_out_grad = scatter(matmul(grad_middle_low, head_act, 0, 0, BF16))

    grad_head_act = matmul(grad_middle_low, w_out, 1, 0)
    head_gain_grad = jnp.sum(grad_head_act * head_normed, axis=0)
    head_bias_grad = jnp.sum(grad_head_act, axis=0)
    head_scaled = grad_head_act * head_gain_f
    head_back = lax.psum(
        jnp.stack([jnp.sum(head_scaled, axis=-1), jnp.sum(head_scaled * head_normed, axis=-1)]), "tp"
    )
    head_back = head_back[:, :, None] / model_width
    grad_mixed = head_inverse * (head_scaled - head_back[0] - head_normed * head_back[1])
    (do_row,) = exchange(
        rows_out_kernel,
        seq_count,
        groups,
        (grad_mixed.astype(BF16).reshape(shape3),),
        (length, width),
        6,
    )
    grads_row = attend_back(q_row, k_row, v_row, do_row, o_row, lse, tables, seg_col, seg_row)
    grads = exchange(rows_back_kernel, seq_count, groups, grads_row, shape3, 7)
    grad_query, grad_key, grad_value = (g.reshape(tokens, head_width) for g in grads)
    first_part = (
        dot(grad_query, w_query, 1, 1) + dot(grad_key, w_key, 1, 1) + dot(grad_value, w_value, 1, 1)
    ).astype(BF16)
    w_query_grad = scatter(matmul(first_act, grad_query, 0, 0, BF16))
    w_key_grad = scatter(matmul(first_act, grad_key, 0, 0, BF16))
    w_value_grad = scatter(matmul(first_act, grad_value, 0, 0, BF16))
    input_grad, first_sums = line_sum(
        finish_back, tp_count, first_part, (grad_middle_own, block, first_gain_f), [sums_shape], True, 8
    )

    norm_sums = lax.psum(
        jnp.concatenate([jnp.sum(second_sums, axis=1), jnp.sum(first_sums, axis=1)]), ("seq", "tp")
    )
    own_width = model_width // seq_count
    norm_own = lax.dynamic_slice_in_dim(norm_sums, seq_index * own_width, own_width, 1)
    split_sums = lax.psum((head_gain_grad, head_bias_grad, hidden_gain_grad, hidden_bias_grad), "seq")
    return (
        block_out.reshape(block_in.shape),
        input_grad.reshape(block_in.shape),
        norm_own[2],
        norm_own[3],
        w_query_grad,
        w_key_grad,
        w_value_grad,
        split_sums[0],
        split_sums[1],
        w_out_grad,
        norm_own[0],
        norm_own[1],
        w_up_grad,
        split_sums[2],
        split_sums[3],
        w_down_grad,
    )


def solution(mesh):
    return jax.shard_map(
        functools.partial(body, mesh.shape["seq"], mesh.shape["tp"]),
        mesh=mesh,
        in_specs=(
            P(None, "seq", None),
            P(),
            P(),
            P(),
            P(None, "tp"),
            P(None, "tp"),
            P(None, "tp"),
            P("tp"),
            P("tp"),
            P(None, "tp"),
            P(),
            P(),
            P(None, "tp"),
            P("tp"),
            P("tp"),
            P(None, "tp"),
            P(None, "seq", None),
        ),
        out_specs=(
            P(None, "seq", None),
            P(None, "seq", None),
            P("seq"),
            P("seq"),
            P("seq", "tp"),
            P("seq", "tp"),
            P("seq", "tp"),
            P("tp"),
            P("tp"),
            P("seq", "tp"),
            P("seq"),
            P("seq"),
            P("seq", "tp"),
            P("tp"),
            P("tp"),
            P("seq", "tp"),
        ),
        check_vma=False,
    )
```

```python
import functools
import math

import jax
import jax.numpy as jnp
from jax import lax
from jax.experimental import pallas as pl
from jax.experimental.pallas import tpu as pltpu
from jax.sharding import PartitionSpec as P

HEAD = 64
LANES = 128
BLOCK = 256
EPSILON = 1e-05
MASKED = -1e30
MESH = pl.DeviceIdType.MESH
F32 = jnp.float32
BF16 = jnp.bfloat16
CHUNKS = 16
SLACK = 2
VMEM_LIMIT = 58 * 1024 * 1024


def cost(micros):
    return pl.CostEstimate(flops=int(micros * 1.1e9), bytes_accessed=0, transcendentals=0)


def dot(left, right, left_dim, right_dim):
    return lax.dot_general(
        left, right, (((left_dim,), (right_dim,)), ((), ())), preferred_element_type=F32
    )


def seq_barrier(count):
    me = lax.axis_index("seq")
    barrier = pltpu.get_barrier_semaphore()
    for k in range(1, count):
        pl.semaphore_signal(
            barrier, inc=1, device_id={"seq": lax.rem(me + k, count)}, device_id_type=MESH
        )
    pl.semaphore_wait(barrier, count - 1)


def rows_out_kernel(count, groups, num, *refs):
    sources, targets = refs[:num], refs[num : 2 * num]
    send_sem, recv_sem, own_sem = refs[2 * num :]
    me = lax.axis_index("seq")
    span = sources[0].shape[1]
    width = targets[0].shape[1]
    seq_barrier(count)

    def piece(source, device):
        lane = pl.multiple_of(lax.rem(device, groups) * width, LANES)
        return source.at[device // groups, :, pl.ds(lane, width)]

    def place(target):
        return target.at[pl.ds(pl.multiple_of(me * span, LANES), span), :]

    copies = []
    for k in range(1, count):
        device = lax.rem(me + k, count)
        for i in range(num):
            copy = pltpu.make_async_remote_copy(
                src_ref=piece(sources[i], device),
                dst_ref=place(targets[i]),
                send_sem=send_sem.at[i, k],
                recv_sem=recv_sem.at[i, k],
                device_id={"seq": device},
                device_id_type=MESH,
            )
            copy.start()
            copies.append(copy)
    for i in range(num):
        copy = pltpu.make_async_copy(piece(sources[i], me), place(targets[i]), own_sem.at[i])
        copy.start()
        copies.append(copy)
    for copy in copies:
        copy.wait()


def rows_back_kernel(count, groups, num, *refs):
    sources, targets = refs[:num], refs[num : 2 * num]
    send_sem, recv_sem, own_sem = refs[2 * num :]
    me = lax.axis_index("seq")
    span = targets[0].shape[1]
    width = sources[0].shape[1]
    seq_barrier(count)

    def piece(source, device):
        return source.at[pl.ds(pl.multiple_of(device * span, LANES), span), :]

    def place(target):
        lane = pl.multiple_of(lax.rem(me, groups) * width, LANES)
        return target.at[me // groups, :, pl.ds(lane, width)]

    copies = []
    for k in range(1, count):
        device = lax.rem(me + k, count)
        for i in range(num):
            copy = pltpu.make_async_remote_copy(
                src_ref=piece(sources[i], device),
                dst_ref=place(targets[i]),
                send_sem=send_sem.at[i, k],
                recv_sem=recv_sem.at[i, k],
                device_id={"seq": device},
                device_id_type=MESH,
            )
            copy.start()
            copies.append(copy)
    for i in range(num):
        copy = pltpu.make_async_copy(piece(sources[i], me), place(targets[i]), own_sem.at[i])
        copy.start()
        copies.append(copy)
    for copy in copies:
        copy.wait()


def exchange(kernel, count, groups, arrays, shape, collective_id):
    num = len(arrays)
    outs = pl.pallas_call(
        functools.partial(kernel, count, groups, num),
        out_shape=[jax.ShapeDtypeStruct(shape, BF16)] * num,
        in_specs=[pl.BlockSpec(memory_space=pl.ANY)] * num,
        out_specs=[pl.BlockSpec(memory_space=pl.ANY)] * num,
        scratch_shapes=[
            pltpu.SemaphoreType.DMA((num, count)),
            pltpu.SemaphoreType.DMA((num, count)),
            pltpu.SemaphoreType.DMA((num,)),
        ],
        compiler_params=pltpu.CompilerParams(collective_id=collective_id, has_side_effects=True),
        cost_estimate=cost(4 + 12 * num),
    )(*arrays)
    return outs


def swap_halves(values):
    lane = lax.broadcasted_iota(jnp.int32, values.shape, 1)
    return jnp.where(
        lane % HEAD < HEAD // 2,
        pltpu.roll(values, LANES - HEAD // 2, 1),
        pltpu.roll(values, HEAD // 2, 1),
    )


def head_masks(values):
    lane = lax.broadcasted_iota(jnp.int32, values.shape, 1)
    zero = jnp.zeros_like(values)
    return jnp.where(lane < HEAD, values, zero), jnp.where(lane < HEAD, zero, values)


def attend_kernel(length, q_ref, k_ref, v_ref, tab_ref, segc_ref, segr_ref, o_ref, lse_ref, bias, qs, ks):
    blocks = length // BLOCK

    @pl.when(pl.program_id(0) == 0)
    def _():
        for qb in range(blocks):
            rows = slice(qb * BLOCK, (qb + 1) * BLOCK)
            keys = (qb + 1) * BLOCK
            same = segc_ref[rows, :] == segr_ref[:, :keys]
            row = lax.broadcasted_iota(jnp.int32, (BLOCK, keys), 0) + qb * BLOCK
            col = lax.broadcasted_iota(jnp.int32, (BLOCK, keys), 1)
            bias[rows, :keys] = jnp.where(same & (col <= row), 0.0, MASKED)

    for qb in range(blocks):
        rows = slice(qb * BLOCK, (qb + 1) * BLOCK)
        q = q_ref[rows, :].astype(F32)
        q = (q * tab_ref[0, rows, :] + swap_halves(q) * tab_ref[1, rows, :]) * (HEAD**-0.5)
        q0, q1 = head_masks(q)
        qs[0, rows, :] = q0.astype(BF16)
        qs[1, rows, :] = q1.astype(BF16)
        k = k_ref[rows, :].astype(F32)
        k = k * tab_ref[2, rows, :] + swap_halves(k) * tab_ref[3, rows, :]
        ks[rows, :] = k.astype(BF16)
    for qb in range(blocks):
        rows = slice(qb * BLOCK, (qb + 1) * BLOCK)
        keys = (qb + 1) * BLOCK
        outs = []
        logs = []
        for h in range(2):
            scores = dot(qs[h, rows, :], ks[:keys, :], 1, 1) + bias[rows, :keys]
            top = jnp.max(scores, axis=1, keepdims=True)
            expo = jnp.exp(scores - top)
            total = jnp.sum(expo, axis=1, keepdims=True)
            outs.append(dot(expo.astype(BF16), v_ref[:keys, :], 1, 0) / total)
            logs.append(jnp.broadcast_to(top + jnp.log(total), (BLOCK, LANES)))
        lane = lax.broadcasted_iota(jnp.int32, (BLOCK, LANES), 1)
        o_ref[rows, :] = jnp.where(lane < HEAD, outs[0], outs[1]).astype(BF16)
        logs_t = jnp.transpose(jnp.where(lane < HEAD, logs[0], logs[1]))
        lse_ref[0, 0:1, rows] = logs_t[0:1]
        lse_ref[0, 1:2, rows] = logs_t[HEAD : HEAD + 1]


def attend(q, k, v, tables, seg_col, seg_row):
    length, width = q.shape
    pairs = width // LANES
    lane_block = pl.BlockSpec((length, LANES), lambda p: (0, p))
    return pl.pallas_call(
        functools.partial(attend_kernel, length),
        grid=(pairs,),
        out_shape=[
            jax.ShapeDtypeStruct((length, width), BF16),
            jax.ShapeDtypeStruct((pairs, 8, length), F32),
        ],
        in_specs=[
            lane_block,
            lane_block,
            lane_block,
            pl.BlockSpec((4, length, LANES), lambda p: (0, 0, 0)),
            pl.BlockSpec((length, 1), lambda p: (0, 0)),
            pl.BlockSpec((1, length), lambda p: (0, 0)),
        ],
        out_specs=[lane_block, pl.BlockSpec((1, 8, length), lambda p: (p, 0, 0))],
        scratch_shapes=[
            pltpu.VMEM((length, length), F32),
            pltpu.VMEM((2, length, LANES), BF16),
            pltpu.VMEM((length, LANES), BF16),
        ],
        compiler_params=pltpu.CompilerParams(vmem_limit_bytes=VMEM_LIMIT),
        cost_estimate=cost(17),
    )(q, k, v, tables, seg_col, seg_row)


def attend_back_kernel(
    length, q_ref, k_ref, v_ref, do_ref, o_ref, lse_ref, tab_ref, segc_ref, segr_ref,
    dq_ref, dk_ref, dv_ref, bias, qs, ks, kms, dos, delta, dq, dk, dv,
):
    blocks = length // BLOCK

    @pl.when(pl.program_id(0) == 0)
    def _():
        for kb in range(blocks):
            rows = slice(kb * BLOCK, (kb + 1) * BLOCK)
            first = kb * BLOCK
            shape = (BLOCK, length - first)
            same = segc_ref[rows, :] == segr_ref[:, first:]
            key = lax.broadcasted_iota(jnp.int32, shape, 0)
            query = lax.broadcasted_iota(jnp.int32, shape, 1)
            bias[rows, first:] = jnp.where(same & (key <= query), 0.0, MASKED)

    for qb in range(blocks):
        rows = slice(qb * BLOCK, (qb + 1) * BLOCK)
        q = q_ref[rows, :].astype(F32)
        q = (q * tab_ref[0, rows, :] + swap_halves(q) * tab_ref[1, rows, :]) * (HEAD**-0.5)
        q0, q1 = head_masks(q)
        qs[0, rows, :] = q0.astype(BF16)
        qs[1, rows, :] = q1.astype(BF16)
        k = k_ref[rows, :].astype(F32)
        k = k * tab_ref[2, rows, :] + swap_halves(k) * tab_ref[3, rows, :]
        ks[rows, :] = k.astype(BF16)
        k0, k1 = head_masks(k)
        kms[0, rows, :] = k0.astype(BF16)
        kms[1, rows, :] = k1.astype(BF16)
        grad = do_ref[rows, :].astype(F32)
        d0, d1 = head_masks(grad)
        dos[0, rows, :] = d0.astype(BF16)
        dos[1, rows, :] = d1.astype(BF16)
        prod = jnp.transpose(grad * o_ref[rows, :].astype(F32))
        delta[0:1, rows] = jnp.sum(prod[:HEAD], axis=0, keepdims=True)
        delta[1:2, rows] = jnp.sum(prod[HEAD:], axis=0, keepdims=True)
    dq[...] = jnp.zeros_like(dq)
    dk[...] = jnp.zeros_like(dk)
    dv[...] = jnp.zeros_like(dv)
    for qb in range(blocks):
        cols = slice(qb * BLOCK, (qb + 1) * BLOCK)
        for kb in range(qb + 1):
            rows = slice(kb * BLOCK, (kb + 1) * BLOCK)
            for h in range(2):
                scores = dot(ks[rows, :], qs[h, cols, :], 1, 1) + bias[rows, cols]
                probs = jnp.exp(scores - lse_ref[0, h : h + 1, cols])
                grads = dot(v_ref[rows, :], dos[h, cols, :], 1, 1)
                dscores = (probs * (grads - delta[h : h + 1, cols])).astype(BF16)
                dv[rows, :] += dot(probs.astype(BF16), dos[h, cols, :], 1, 0)
                dk[rows, :] += dot(dscores, qs[h, cols, :], 1, 0)
                dq[cols, :] += dot(dscores, kms[h, rows, :], 0, 0)
    for qb in range(blocks):
        rows = slice(qb * BLOCK, (qb + 1) * BLOCK)
        grad = dq[rows, :] * (HEAD**-0.5)
        dq_ref[rows, :] = (
            grad * tab_ref[0, rows, :] - swap_halves(grad) * tab_ref[1, rows, :]
        ).astype(BF16)
        grad = dk[rows, :]
        dk_ref[rows, :] = (
            grad * tab_ref[2, rows, :] - swap_halves(grad) * tab_ref[3, rows, :]
        ).astype(BF16)
        dv_ref[rows, :] = dv[rows, :].astype(BF16)


def attend_back(q, k, v, do, o, lse, tables, seg_col, seg_row):
    length, width = q.shape
    pairs = width // LANES
    lane_block = pl.BlockSpec((length, LANES), lambda p: (0, p))
    return pl.pallas_call(
        functools.partial(attend_back_kernel, length),
        grid=(pairs,),
        out_shape=[jax.ShapeDtypeStruct((length, width), BF16)] * 3,
        in_specs=[lane_block] * 5
        + [
            pl.BlockSpec((1, 8, length), lambda p: (p, 0, 0)),
            pl.BlockSpec((4, length, LANES), lambda p: (0, 0, 0)),
            pl.BlockSpec((length, 1), lambda p: (0, 0)),
            pl.BlockSpec((1, length), lambda p: (0, 0)),
        ],
        out_specs=[lane_block] * 3,
        scratch_shapes=[
            pltpu.VMEM((length, length), F32),
            pltpu.VMEM((2, length, LANES), BF16),
            pltpu.VMEM((length, LANES), BF16),
            pltpu.VMEM((2, length, LANES), BF16),
            pltpu.VMEM((2, length, LANES), BF16),
            pltpu.VMEM((8, length), F32),
            pltpu.VMEM((length, LANES), F32),
            pltpu.VMEM((length, LANES), F32),
            pltpu.VMEM((length, LANES), F32),
        ],
        compiler_params=pltpu.CompilerParams(vmem_limit_bytes=VMEM_LIMIT),
        cost_estimate=cost(30),
    )(q, k, v, do, o, lse, tables, seg_col, seg_row)


def norm_parts(values):
    center = jnp.mean(values, axis=-1, keepdims=True)
    shifted = values - center
    inverse = lax.rsqrt(jnp.mean(shifted * shifted, axis=-1, keepdims=True) + EPSILON)
    return shifted * inverse, inverse


def fold(values):
    rows, width = values.shape
    return jnp.sum(values.reshape(rows // 8, 8, width), axis=0)


def finish_middle(total, here, own, ins, outs):
    x_ref, gain_ref, bias_ref = ins
    middle = x_ref[here, :].astype(F32) + total
    outs[0][own, :] = middle
    normed, _ = norm_parts(middle)
    return normed * gain_ref[...] + bias_ref[...]


def finish_back(total, here, own, ins, outs):
    base_ref, values_ref, gain_ref = ins[:3]
    flip = len(outs) == 1
    base = base_ref[own if flip else here, :].astype(F32)
    values = values_ref[here if flip else own, :].astype(F32)
    normed, inverse = norm_parts(values)
    scaled = total * gain_ref[...]
    grad = base + inverse * (
        scaled
        - jnp.mean(scaled, axis=-1, keepdims=True)
        - normed * jnp.mean(scaled * normed, axis=-1, keepdims=True)
    )
    outs[0][0] += fold(total * normed)
    outs[0][1] += fold(total)
    if not flip:
        outs[1][own, :] = grad
    return grad


def line_kernel(finish, count, chunks, slack, num_in, num_out, clear, *refs):
    part_ref, ins = refs[0], refs[1 : 1 + num_in]
    out_ref, outs = refs[1 + num_in], refs[2 + num_in : 2 + num_in + num_out]
    in_a, in_b = refs[2 + num_in + num_out : 4 + num_in + num_out]
    (rsa_s, rsa_r, rsb_s, rsb_r, aga_s, aga_r, agb_s, agb_r) = refs[4 + num_in + num_out :]
    z = lax.axis_index("tp")
    half = part_ref.shape[0] // 2
    size = half // chunks
    ahead = slack * (count - 1)
    from_first, from_last = slack * z, slack * (count - 1 - z)
    first, last = z == 0, z == count - 1
    up = jnp.minimum(z + 1, count - 1)
    down = jnp.maximum(z - 1, 0)

    barrier = pltpu.get_barrier_semaphore()

    @pl.when(jnp.logical_not(last))
    def _():
        pl.semaphore_signal(barrier, inc=1, device_id={"tp": up}, device_id_type=MESH)

    @pl.when(jnp.logical_not(first))
    def _():
        pl.semaphore_signal(barrier, inc=1, device_id={"tp": down}, device_id_type=MESH)

    @pl.when(first | last)
    def _():
        pl.semaphore_wait(barrier, 1)

    @pl.when(jnp.logical_not(first | last))
    def _():
        pl.semaphore_wait(barrier, 2)

    if clear:
        outs[0][...] = jnp.zeros_like(outs[0])

    def own_rows(c):
        return pl.ds(pl.multiple_of(c * size, size), size)

    def a_rows(c):
        return own_rows(c)

    def b_rows(c):
        return pl.ds(pl.multiple_of(half + c * size, size), size)

    def hop(source, target, send, recv, c, device):
        return pltpu.make_async_remote_copy(
            src_ref=source,
            dst_ref=target,
            send_sem=send.at[c],
            recv_sem=recv.at[c],
            device_id={"tp": device},
            device_id_type=MESH,
        )

    def gather_a(c):
        rows = out_ref.at[a_rows(c), :]
        return hop(rows, rows, aga_s, aga_r, c, up)

    def gather_b(c):
        rows = out_ref.at[b_rows(c), :]
        return hop(rows, rows, agb_s, agb_r, c, down)

    def reduce_a(c, source):
        return hop(source, in_a.at[own_rows(c), :], rsa_s, rsa_r, c, down)

    def reduce_b(c, source):
        return hop(source, in_b.at[own_rows(c), :], rsb_s, rsb_r, c, up)

    def reduce_step(c, rows, landed, move, gather, starts, ends):
        here = rows(c)
        own = own_rows(c)

        @pl.when(starts)
        def _():
            move(c, part_ref.at[here, :]).start()

        @pl.when(jnp.logical_not(starts))
        def _():
            move(c, part_ref.at[here, :]).wait_recv()

        @pl.when(jnp.logical_not(starts | ends))
        def _():
            landed[own, :] = (
                landed[own, :].astype(F32) + part_ref[here, :].astype(F32)
            ).astype(BF16)
            move(c, landed.at[own, :]).start()

        @pl.when(ends)
        def _():
            total = landed[own, :].astype(F32) + part_ref[here, :].astype(F32)
            out_ref[here, :] = finish(total, here, own, ins, outs).astype(BF16)
            gather(c).start()

    def gather_step(c, gather, starts, ends):
        @pl.when(jnp.logical_not(starts))
        def _():
            gather(c).wait_recv()

        @pl.when(jnp.logical_not(starts | ends))
        def _():
            gather(c).start()

    def when_chunk(c, work):
        pl.when((c >= 0) & (c < chunks))(lambda: work(c))

    def step(t, carry):
        when_chunk(
            t - from_last,
            lambda c: reduce_step(c, a_rows, in_a, reduce_a, gather_a, last, first),
        )
        when_chunk(
            t - from_first,
            lambda c: reduce_step(c, b_rows, in_b, reduce_b, gather_b, first, last),
        )
        when_chunk(t - ahead - from_first, lambda c: gather_step(c, gather_a, first, last))
        when_chunk(t - ahead - from_last, lambda c: gather_step(c, gather_b, last, first))
        return carry

    lax.fori_loop(0, chunks + 2 * ahead, step, 0)

    def drain(c, carry):
        @pl.when(jnp.logical_not(first))
        def _():
            reduce_a(c, in_a.at[own_rows(c), :]).wait_send()
            gather_b(c).wait_send()

        @pl.when(jnp.logical_not(last))
        def _():
            reduce_b(c, in_b.at[own_rows(c), :]).wait_send()
            gather_a(c).wait_send()

        return carry

    lax.fori_loop(0, chunks, drain, 0)


def line_sum(finish, count, part, ins, out_shapes, clear, collective_id):
    tokens, width = part.shape
    half = tokens // 2
    chunks = CHUNKS
    whole = pl.BlockSpec(memory_space=pltpu.VMEM)
    return pl.pallas_call(
        functools.partial(
            line_kernel, finish, count, CHUNKS, SLACK, len(ins), len(out_shapes), clear
        ),
        out_shape=[jax.ShapeDtypeStruct((tokens, width), BF16)] + out_shapes,
        in_specs=[whole] * (1 + len(ins)),
        out_specs=[whole] * (1 + len(out_shapes)),
        scratch_shapes=[pltpu.VMEM((half, width), BF16)] * 2
        + [pltpu.SemaphoreType.DMA((chunks,))] * 8,
        compiler_params=pltpu.CompilerParams(
            collective_id=collective_id, has_side_effects=True, vmem_limit_bytes=VMEM_LIMIT
        ),
        cost_estimate=cost(120),
    )(part, *ins)


def axis_barrier(counts):
    barrier = pltpu.get_barrier_semaphore()
    for axis, count in counts:
        me = lax.axis_index(axis)
        for k in range(1, count):
            pl.semaphore_signal(
                barrier, inc=1, device_id={axis: lax.rem(me + k, count)}, device_id_type=MESH
            )
    pl.semaphore_wait(barrier, sum(count - 1 for _, count in counts))


def share(axis, count, pick, landed, send_sem, recv_sem):
    me = lax.axis_index(axis)
    copies = []
    for k in range(1, count):
        device = lax.rem(me + k, count)
        copy = pltpu.make_async_remote_copy(
            src_ref=pick(device),
            dst_ref=landed.at[me],
            send_sem=send_sem.at[k],
            recv_sem=recv_sem.at[k],
            device_id={axis: device},
            device_id_type=MESH,
        )
        copy.start()
        copies.append(copy)
    return copies


def total_of(landed, count):
    total = landed[0]
    for k in range(1, count):
        total = total + landed[k]
    return total


def tp_sum_kernel(count, x_ref, out_ref, landed, send_sem, recv_sem):
    axis_barrier([("tp", count)])
    copies = share("tp", count, lambda d: x_ref, landed, send_sem, recv_sem)
    landed[lax.axis_index("tp")] = x_ref[...]
    for copy in copies:
        copy.wait()
    out_ref[...] = total_of(landed, count)


def tp_sum(values, count, collective_id):
    whole = pl.BlockSpec(memory_space=pltpu.VMEM)
    return pl.pallas_call(
        functools.partial(tp_sum_kernel, count),
        out_shape=jax.ShapeDtypeStruct(values.shape, F32),
        in_specs=[whole],
        out_specs=whole,
        scratch_shapes=[
            pltpu.VMEM((count,) + values.shape, F32),
            pltpu.SemaphoreType.DMA((count,)),
            pltpu.SemaphoreType.DMA((count,)),
        ],
        compiler_params=pltpu.CompilerParams(collective_id=collective_id, has_side_effects=True),
        cost_estimate=cost(5),
    )(values)


def norm_sum_kernel(
    seq_count, tp_count, full_ref, split_ref, own_ref, sum_ref,
    tp_landed, summed, own_landed, split_landed, sem_a, sem_b, sem_c, sem_d, sem_e, sem_f,
):
    me = lax.axis_index("seq")
    axis_barrier([("seq", seq_count), ("tp", tp_count)])
    tp_copies = share("tp", tp_count, lambda d: full_ref, tp_landed, sem_a, sem_b)
    split_copies = share("seq", seq_count, lambda d: split_ref, split_landed, sem_c, sem_d)
    tp_landed[lax.axis_index("tp")] = full_ref[...]
    split_landed[me] = split_ref[...]
    for copy in tp_copies:
        copy.wait()
    summed[...] = total_of(tp_landed, tp_count)
    own_copies = share("seq", seq_count, lambda d: summed.at[d], own_landed, sem_e, sem_f)
    own_landed[me] = summed[me]
    for copy in split_copies:
        copy.wait()
    sum_ref[...] = total_of(split_landed, seq_count)
    for copy in own_copies:
        copy.wait()
    own_ref[...] = total_of(own_landed, seq_count)


def norm_sum(full, split, seq_count, tp_count, collective_id):
    whole = pl.BlockSpec(memory_space=pltpu.VMEM)
    piece = full.shape[1:]
    return pl.pallas_call(
        functools.partial(norm_sum_kernel, seq_count, tp_count),
        out_shape=[
            jax.ShapeDtypeStruct(piece, F32),
            jax.ShapeDtypeStruct(split.shape, F32),
        ],
        in_specs=[whole] * 2,
        out_specs=[whole] * 2,
        scratch_shapes=[
            pltpu.VMEM((tp_count,) + full.shape, F32),
            pltpu.VMEM(full.shape, F32),
            pltpu.VMEM((seq_count,) + piece, F32),
            pltpu.VMEM((seq_count,) + split.shape, F32),
            pltpu.SemaphoreType.DMA((tp_count,)),
            pltpu.SemaphoreType.DMA((tp_count,)),
        ]
        + [pltpu.SemaphoreType.DMA((seq_count,))] * 4,
        compiler_params=pltpu.CompilerParams(collective_id=collective_id, has_side_effects=True),
        cost_estimate=cost(10),
    )(full, split)


def matmul(left, right, left_dim, right_dim, kind=F32):
    return dot(left, right, left_dim, right_dim).astype(kind)


def rotation_tables(positions):
    half_size = HEAD // 2
    index_pairs = jnp.arange(half_size, dtype=F32)
    theta_rate = jnp.exp(-2.0 * index_pairs / HEAD * jnp.log(10000.0))
    zeta_base = (2.0 * index_pairs + 0.4 * HEAD) / (1.4 * HEAD)
    place_float = positions.astype(F32)[..., None]
    angles = place_float * theta_rate
    power = jnp.log(zeta_base) * place_float / 512.0
    cos_part, sin_part = jnp.cos(angles), jnp.sin(angles)
    grow, shrink = jnp.exp(power), jnp.exp(-power)
    cos_full = jnp.concatenate([cos_part] * 4, axis=-1)
    sin_full = jnp.concatenate([-sin_part, sin_part] * 2, axis=-1)
    grow = jnp.concatenate([grow] * 4, axis=-1)
    shrink = jnp.concatenate([shrink] * 4, axis=-1)
    return jnp.stack([cos_full * grow, sin_full * grow, cos_full * shrink, sin_full * shrink])


def body(
    seq_count,
    tp_count,
    block_in,
    segment_ids,
    first_gain,
    first_bias,
    w_query,
    w_key,
    w_value,
    head_gain,
    head_bias,
    w_out,
    second_gain,
    second_bias,
    w_up,
    hidden_gain,
    hidden_bias,
    w_down,
    out_cotangent,
):
    seq_index = lax.axis_index("seq")
    row_count, span, model_width = block_in.shape
    length = span * seq_count
    tokens = row_count * span
    head_width = w_query.shape[1]
    hidden_width = w_up.shape[1] * tp_count
    groups = seq_count // row_count
    width = head_width // groups

    first_gain_f = first_gain.astype(F32)[None]
    first_bias_f = first_bias.astype(F32)[None]
    second_gain_f = second_gain.astype(F32)[None]
    second_bias_f = second_bias.astype(F32)[None]
    head_gain_f = head_gain.astype(F32)[None]
    head_bias_f = head_bias.astype(F32)[None]
    hidden_gain_f = hidden_gain.astype(F32)[None]
    hidden_bias_f = hidden_bias.astype(F32)[None]

    seg_row = lax.dynamic_slice_in_dim(segment_ids, seq_index // groups, 1, 0)
    seg_col = seg_row.reshape(length, 1)
    earlier = jnp.sum((seg_row < seg_col).astype(jnp.int32), axis=-1)
    tables = rotation_tables(jnp.arange(length, dtype=jnp.int32) - earlier)

    block = block_in.reshape(tokens, model_width)
    cotangent = out_cotangent.reshape(tokens, model_width)

    normed_one, _ = norm_parts(block.astype(F32))
    first_act = (normed_one * first_gain_f + first_bias_f).astype(BF16)
    shape3 = (row_count, span, head_width)
    query = matmul(first_act, w_query, 1, 0, BF16).reshape(shape3)
    key = matmul(first_act, w_key, 1, 0, BF16).reshape(shape3)
    value = matmul(first_act, w_value, 1, 0, BF16).reshape(shape3)
    q_row, k_row, v_row = exchange(
        rows_out_kernel, seq_count, groups, (query, key, value), (length, width), 1
    )
    o_row, lse = attend(q_row, k_row, v_row, tables, seg_col, seg_row)
    (mixed,) = exchange(rows_back_kernel, seq_count, groups, (o_row,), shape3, 2)
    mixed = mixed.reshape(tokens, head_width).astype(F32)
    head_sums = tp_sum(
        jnp.stack([jnp.sum(mixed, axis=-1), jnp.sum(mixed * mixed, axis=-1)]), tp_count, 9
    )
    head_center = head_sums[0][:, None] / model_width
    head_inverse = lax.rsqrt(
        head_sums[1][:, None] / model_width - head_center * head_center + EPSILON
    )
    head_normed = (mixed - head_center) * head_inverse
    head_act = (head_normed * head_gain_f + head_bias_f).astype(BF16)
    out_part = matmul(head_act, w_out, 1, 1, BF16)
    own_shape = jax.ShapeDtypeStruct((tokens // 2, model_width), F32)
    sums_shape = jax.ShapeDtypeStruct((2, 8, model_width), F32)
    second_act, middle_own = line_sum(
        finish_middle, tp_count, out_part, (block, second_gain_f, second_bias_f), [own_shape], False, 3
    )

    up_pre = matmul(second_act, w_up, 1, 0)
    grad_hidden_act = matmul(cotangent, w_down, 1, 0)
    cdf = 0.5 * lax.erfc(up_pre * (-(0.5**0.5)))
    gelu_out = up_pre * cdf
    hidden_scaled = grad_hidden_act * hidden_gain_f
    stats = tp_sum(
        jnp.stack(
            [
                jnp.sum(gelu_out, axis=-1),
                jnp.sum(gelu_out * gelu_out, axis=-1),
                jnp.sum(hidden_scaled, axis=-1),
                jnp.sum(hidden_scaled * gelu_out, axis=-1),
            ]
        ),
        tp_count,
        10,
    )
    stats = stats[:, :, None] / hidden_width
    hidden_center = stats[0]
    hidden_inverse = lax.rsqrt(stats[1] - hidden_center * hidden_center + EPSILON)
    hidden_normed = (gelu_out - hidden_center) * hidden_inverse
    hidden_act = (hidden_normed * hidden_gain_f + hidden_bias_f).astype(BF16)
    hidden_gain_grad = jnp.sum(grad_hidden_act * hidden_normed, axis=0)
    hidden_bias_grad = jnp.sum(grad_hidden_act, axis=0)
    hidden_cross = hidden_inverse * (stats[3] - hidden_center * stats[2])
    grad_gelu = hidden_inverse * (hidden_scaled - stats[2] - hidden_normed * hidden_cross)
    pdf = jnp.exp(-0.5 * up_pre * up_pre) * (1.0 / math.sqrt(2.0 * math.pi))
    grad_up = (grad_gelu * (cdf + up_pre * pdf)).astype(BF16)

    w_down_terms = matmul(cotangent, hidden_act, 0, 0, BF16)
    w_up_terms = matmul(second_act, grad_up, 0, 0, BF16)
    second_part = matmul(grad_up, w_up, 1, 1, BF16)
    second_part, w_down_terms, w_up_terms = lax.optimization_barrier(
        (second_part, w_down_terms, w_up_terms)
    )
    grad_middle_low, second_sums, grad_middle_own = line_sum(
        finish_back,
        tp_count,
        second_part,
        (cotangent, middle_own, second_gain_f),
        [sums_shape, own_shape],
        True,
        4,
    )
    hidden_late, _ = lax.optimization_barrier((hidden_act, grad_middle_low))
    down_part = matmul(hidden_late, w_down, 1, 1)
    tp_index = lax.axis_index("tp")
    half = tokens // 2
    owner = jnp.where(tp_index == 0, 0, jnp.where(tp_index == tp_count - 1, 1, 2))
    mine = (jnp.arange(2, dtype=jnp.int32) == owner)[:, None, None]
    down_part = down_part.reshape(2, half, model_width) + jnp.where(mine, middle_own[None], 0.0)
    block_out = lax.psum(down_part.astype(BF16), "tp")

    def scatter(grad):
        return lax.psum_scatter(grad, "seq", scatter_dimension=0, tiled=True)

    w_down_grad = scatter(w_down_terms)
    w_up_grad = scatter(w_up_terms)

    grad_head_act = matmul(grad_middle_low, w_out, 1, 0)
    head_gain_grad = jnp.sum(grad_head_act * head_normed, axis=0)
    head_bias_grad = jnp.sum(grad_head_act, axis=0)
    head_scaled = grad_head_act * head_gain_f
    head_back = tp_sum(
        jnp.stack([jnp.sum(head_scaled, axis=-1), jnp.sum(head_scaled * head_normed, axis=-1)]),
        tp_count,
        11,
    )
    head_back = head_back[:, :, None] / model_width
    grad_mixed = head_inverse * (head_scaled - head_back[0] - head_normed * head_back[1])
    grad_mixed, w_down_grad, w_up_grad = lax.optimization_barrier(
        (grad_mixed.astype(BF16), w_down_grad, w_up_grad)
    )
    (do_row,) = exchange(
        rows_out_kernel,
        seq_count,
        groups,
        (grad_mixed.reshape(shape3),),
        (length, width),
        6,
    )
    grads_row = attend_back(q_row, k_row, v_row, do_row, o_row, lse, tables, seg_col, seg_row)
    grads = exchange(rows_back_kernel, seq_count, groups, grads_row, shape3, 7)
    grad_query, grad_key, grad_value = (g.reshape(tokens, head_width) for g in grads)
    first_part = (
        dot(grad_query, w_query, 1, 1) + dot(grad_key, w_key, 1, 1) + dot(grad_value, w_value, 1, 1)
    ).astype(BF16)
    first_part, block_out = lax.optimization_barrier((first_part, block_out))
    head_grads = scatter(
        jnp.concatenate(
            [
                matmul(first_act, grad_query, 0, 0, BF16),
                matmul(first_act, grad_key, 0, 0, BF16),
                matmul(first_act, grad_value, 0, 0, BF16),
                matmul(grad_middle_low, head_act, 0, 0, BF16),
            ],
            axis=1,
        )
    )
    w_query_grad, w_key_grad, w_value_grad, w_out_grad = jnp.split(
        head_grads.astype(F32), 4, axis=1
    )
    input_grad, first_sums = line_sum(
        finish_back, tp_count, first_part, (grad_middle_own, block, first_gain_f), [sums_shape], True, 8
    )

    own_width = model_width // seq_count
    full = jnp.concatenate([jnp.sum(second_sums, axis=1), jnp.sum(first_sums, axis=1)])
    full = full.reshape(4, seq_count, own_width).transpose(1, 0, 2)
    full = full.reshape(seq_count, 4 * own_width // LANES, LANES)
    split = jnp.concatenate([hidden_gain_grad, hidden_bias_grad, head_gain_grad, head_bias_grad])
    norm_own, split = norm_sum(
        full, split.reshape(split.shape[0] // LANES, LANES), seq_count, tp_count, 12
    )
    norm_own = norm_own.reshape(4, own_width)
    split = split.reshape(-1)
    hidden_size = hidden_gain.shape[0]
    split_sums = (
        split[2 * hidden_size : 2 * hidden_size + head_width],
        split[2 * hidden_size + head_width :],
        split[:hidden_size],
        split[hidden_size : 2 * hidden_size],
    )
    return (
        block_out.reshape(block_in.shape),
        input_grad.reshape(block_in.shape),
        norm_own[2],
        norm_own[3],
        w_query_grad,
        w_key_grad,
        w_value_grad,
        split_sums[0],
        split_sums[1],
        w_out_grad,
        norm_own[0],
        norm_own[1],
        w_up_grad.astype(F32),
        split_sums[2],
        split_sums[3],
        w_down_grad.astype(F32),
    )


def solution(mesh):
    return jax.shard_map(
        functools.partial(body, mesh.shape["seq"], mesh.shape["tp"]),
        mesh=mesh,
        in_specs=(
            P(None, "seq", None),
            P(),
            P(),
            P(),
            P(None, "tp"),
            P(None, "tp"),
            P(None, "tp"),
            P("tp"),
            P("tp"),
            P(None, "tp"),
            P(),
            P(),
            P(None, "tp"),
            P("tp"),
            P("tp"),
            P(None, "tp"),
            P(None, "seq", None),
        ),
        out_specs=(
            P(None, "seq", None),
            P(None, "seq", None),
            P("seq"),
            P("seq"),
            P("seq", "tp"),
            P("seq", "tp"),
            P("seq", "tp"),
            P("tp"),
            P("tp"),
            P("seq", "tp"),
            P("seq"),
            P("seq"),
            P("seq", "tp"),
            P("tp"),
            P("tp"),
            P("seq", "tp"),
        ),
        check_vma=False,
    )
```

```python
import functools
import math

import jax
import jax.numpy as jnp
from jax import lax
from jax.experimental import pallas as pl
from jax.experimental.pallas import tpu as pltpu
from jax.sharding import PartitionSpec as P

HEAD = 64
LANES = 128
BLOCK = 256
EPSILON = 1e-05
MASKED = -1e30
MESH = pl.DeviceIdType.MESH
F32 = jnp.float32
BF16 = jnp.bfloat16
CHUNKS = 16
SLACK = 2
GROUP = 4
ROWS = 256
TILE = 512
VMEM_LIMIT = 60 * 1024 * 1024


def cost(micros):
    return pl.CostEstimate(flops=int(micros * 1.1e9), bytes_accessed=0, transcendentals=0)


def dot(left, right, left_dim, right_dim):
    return lax.dot_general(
        left, right, (((left_dim,), (right_dim,)), ((), ())), preferred_element_type=F32
    )


def seq_barrier(count):
    me = lax.axis_index("seq")
    barrier = pltpu.get_barrier_semaphore()
    for k in range(1, count):
        pl.semaphore_signal(
            barrier, inc=1, device_id={"seq": lax.rem(me + k, count)}, device_id_type=MESH
        )
    pl.semaphore_wait(barrier, count - 1)


def rows_out_kernel(count, groups, num, *refs):
    sources, targets = refs[:num], refs[num : 2 * num]
    send_sem, recv_sem, own_sem = refs[2 * num :]
    me = lax.axis_index("seq")
    span = sources[0].shape[1]
    width = targets[0].shape[1]
    seq_barrier(count)

    def piece(source, device):
        lane = pl.multiple_of(lax.rem(device, groups) * width, LANES)
        return source.at[device // groups, :, pl.ds(lane, width)]

    def place(target):
        return target.at[pl.ds(pl.multiple_of(me * span, LANES), span), :]

    copies = []
    for k in range(1, count):
        device = lax.rem(me + k, count)
        for i in range(num):
            copy = pltpu.make_async_remote_copy(
                src_ref=piece(sources[i], device),
                dst_ref=place(targets[i]),
                send_sem=send_sem.at[i, k],
                recv_sem=recv_sem.at[i, k],
                device_id={"seq": device},
                device_id_type=MESH,
            )
            copy.start()
            copies.append(copy)
    for i in range(num):
        copy = pltpu.make_async_copy(piece(sources[i], me), place(targets[i]), own_sem.at[i])
        copy.start()
        copies.append(copy)
    for copy in copies:
        copy.wait()


def rows_back_kernel(count, groups, num, *refs):
    sources, targets = refs[:num], refs[num : 2 * num]
    send_sem, recv_sem, own_sem = refs[2 * num :]
    me = lax.axis_index("seq")
    span = targets[0].shape[1]
    width = sources[0].shape[1]
    seq_barrier(count)

    def piece(source, device):
        return source.at[pl.ds(pl.multiple_of(device * span, LANES), span), :]

    def place(target):
        lane = pl.multiple_of(lax.rem(me, groups) * width, LANES)
        return target.at[me // groups, :, pl.ds(lane, width)]

    copies = []
    for k in range(1, count):
        device = lax.rem(me + k, count)
        for i in range(num):
            copy = pltpu.make_async_remote_copy(
                src_ref=piece(sources[i], device),
                dst_ref=place(targets[i]),
                send_sem=send_sem.at[i, k],
                recv_sem=recv_sem.at[i, k],
                device_id={"seq": device},
                device_id_type=MESH,
            )
            copy.start()
            copies.append(copy)
    for i in range(num):
        copy = pltpu.make_async_copy(piece(sources[i], me), place(targets[i]), own_sem.at[i])
        copy.start()
        copies.append(copy)
    for copy in copies:
        copy.wait()


def exchange(kernel, count, groups, arrays, shape, collective_id):
    num = len(arrays)
    outs = pl.pallas_call(
        functools.partial(kernel, count, groups, num),
        out_shape=[jax.ShapeDtypeStruct(shape, BF16)] * num,
        in_specs=[pl.BlockSpec(memory_space=pl.ANY)] * num,
        out_specs=[pl.BlockSpec(memory_space=pl.ANY)] * num,
        scratch_shapes=[
            pltpu.SemaphoreType.DMA((num, count)),
            pltpu.SemaphoreType.DMA((num, count)),
            pltpu.SemaphoreType.DMA((num,)),
        ],
        compiler_params=pltpu.CompilerParams(collective_id=collective_id, has_side_effects=True),
        cost_estimate=cost(4 + 12 * num),
    )(*arrays)
    return outs


def swap_halves(values):
    lane = lax.broadcasted_iota(jnp.int32, values.shape, 1)
    return jnp.where(
        lane % HEAD < HEAD // 2,
        pltpu.roll(values, LANES - HEAD // 2, 1),
        pltpu.roll(values, HEAD // 2, 1),
    )


def head_masks(values):
    lane = lax.broadcasted_iota(jnp.int32, values.shape, 1)
    zero = jnp.zeros_like(values)
    return jnp.where(lane < HEAD, values, zero), jnp.where(lane < HEAD, zero, values)


def attend_kernel(length, q_ref, k_ref, v_ref, tab_ref, segc_ref, segr_ref, o_ref, lse_ref, bias, qs, ks):
    blocks = length // BLOCK

    @pl.when(pl.program_id(0) == 0)
    def _():
        for qb in range(blocks):
            rows = slice(qb * BLOCK, (qb + 1) * BLOCK)
            keys = (qb + 1) * BLOCK
            same = segc_ref[rows, :] == segr_ref[:, :keys]
            row = lax.broadcasted_iota(jnp.int32, (BLOCK, keys), 0) + qb * BLOCK
            col = lax.broadcasted_iota(jnp.int32, (BLOCK, keys), 1)
            bias[rows, :keys] = jnp.where(same & (col <= row), 0.0, MASKED)

    for qb in range(blocks):
        rows = slice(qb * BLOCK, (qb + 1) * BLOCK)
        q = q_ref[rows, :].astype(F32)
        q = (q * tab_ref[0, rows, :] + swap_halves(q) * tab_ref[1, rows, :]) * (HEAD**-0.5)
        q0, q1 = head_masks(q)
        qs[0, rows, :] = q0.astype(BF16)
        qs[1, rows, :] = q1.astype(BF16)
        k = k_ref[rows, :].astype(F32)
        k = k * tab_ref[2, rows, :] + swap_halves(k) * tab_ref[3, rows, :]
        ks[rows, :] = k.astype(BF16)
    for qb in range(blocks):
        rows = slice(qb * BLOCK, (qb + 1) * BLOCK)
        keys = (qb + 1) * BLOCK
        outs = []
        logs = []
        for h in range(2):
            scores = dot(qs[h, rows, :], ks[:keys, :], 1, 1) + bias[rows, :keys]
            top = jnp.max(scores, axis=1, keepdims=True)
            expo = jnp.exp(scores - top)
            total = jnp.sum(expo, axis=1, keepdims=True)
            outs.append(dot(expo.astype(BF16), v_ref[:keys, :], 1, 0) / total)
            logs.append(jnp.broadcast_to(top + jnp.log(total), (BLOCK, LANES)))
        lane = lax.broadcasted_iota(jnp.int32, (BLOCK, LANES), 1)
        o_ref[rows, :] = jnp.where(lane < HEAD, outs[0], outs[1]).astype(BF16)
        logs_t = jnp.transpose(jnp.where(lane < HEAD, logs[0], logs[1]))
        lse_ref[0, 0:1, rows] = logs_t[0:1]
        lse_ref[0, 1:2, rows] = logs_t[HEAD : HEAD + 1]


def attend(q, k, v, tables, seg_col, seg_row):
    length, width = q.shape
    pairs = width // LANES
    lane_block = pl.BlockSpec((length, LANES), lambda p: (0, p))
    return pl.pallas_call(
        functools.partial(attend_kernel, length),
        grid=(pairs,),
        out_shape=[
            jax.ShapeDtypeStruct((length, width), BF16),
            jax.ShapeDtypeStruct((pairs, 8, length), F32),
        ],
        in_specs=[
            lane_block,
            lane_block,
            lane_block,
            pl.BlockSpec((4, length, LANES), lambda p: (0, 0, 0)),
            pl.BlockSpec((length, 1), lambda p: (0, 0)),
            pl.BlockSpec((1, length), lambda p: (0, 0)),
        ],
        out_specs=[lane_block, pl.BlockSpec((1, 8, length), lambda p: (p, 0, 0))],
        scratch_shapes=[
            pltpu.VMEM((length, length), F32),
            pltpu.VMEM((2, length, LANES), BF16),
            pltpu.VMEM((length, LANES), BF16),
        ],
        compiler_params=pltpu.CompilerParams(vmem_limit_bytes=VMEM_LIMIT),
        cost_estimate=cost(17),
    )(q, k, v, tables, seg_col, seg_row)


def attend_back_kernel(
    length, q_ref, k_ref, v_ref, do_ref, o_ref, lse_ref, tab_ref, segc_ref, segr_ref,
    dq_ref, dk_ref, dv_ref, bias, qs, ks, kms, dos, delta, dq, dk, dv,
):
    blocks = length // BLOCK

    @pl.when(pl.program_id(0) == 0)
    def _():
        for kb in range(blocks):
            rows = slice(kb * BLOCK, (kb + 1) * BLOCK)
            first = kb * BLOCK
            shape = (BLOCK, length - first)
            same = segc_ref[rows, :] == segr_ref[:, first:]
            key = lax.broadcasted_iota(jnp.int32, shape, 0)
            query = lax.broadcasted_iota(jnp.int32, shape, 1)
            bias[rows, first:] = jnp.where(same & (key <= query), 0.0, MASKED)

    for qb in range(blocks):
        rows = slice(qb * BLOCK, (qb + 1) * BLOCK)
        q = q_ref[rows, :].astype(F32)
        q = (q * tab_ref[0, rows, :] + swap_halves(q) * tab_ref[1, rows, :]) * (HEAD**-0.5)
        q0, q1 = head_masks(q)
        qs[0, rows, :] = q0.astype(BF16)
        qs[1, rows, :] = q1.astype(BF16)
        k = k_ref[rows, :].astype(F32)
        k = k * tab_ref[2, rows, :] + swap_halves(k) * tab_ref[3, rows, :]
        ks[rows, :] = k.astype(BF16)
        k0, k1 = head_masks(k)
        kms[0, rows, :] = k0.astype(BF16)
        kms[1, rows, :] = k1.astype(BF16)
        grad = do_ref[rows, :].astype(F32)
        d0, d1 = head_masks(grad)
        dos[0, rows, :] = d0.astype(BF16)
        dos[1, rows, :] = d1.astype(BF16)
        prod = jnp.transpose(grad * o_ref[rows, :].astype(F32))
        delta[0:1, rows] = jnp.sum(prod[:HEAD], axis=0, keepdims=True)
        delta[1:2, rows] = jnp.sum(prod[HEAD:], axis=0, keepdims=True)
    dq[...] = jnp.zeros_like(dq)
    dk[...] = jnp.zeros_like(dk)
    dv[...] = jnp.zeros_like(dv)
    for qb in range(blocks):
        cols = slice(qb * BLOCK, (qb + 1) * BLOCK)
        for kb in range(qb + 1):
            rows = slice(kb * BLOCK, (kb + 1) * BLOCK)
            for h in range(2):
                scores = dot(ks[rows, :], qs[h, cols, :], 1, 1) + bias[rows, cols]
                probs = jnp.exp(scores - lse_ref[0, h : h + 1, cols])
                grads = dot(v_ref[rows, :], dos[h, cols, :], 1, 1)
                dscores = (probs * (grads - delta[h : h + 1, cols])).astype(BF16)
                dv[rows, :] += dot(probs.astype(BF16), dos[h, cols, :], 1, 0)
                dk[rows, :] += dot(dscores, qs[h, cols, :], 1, 0)
                dq[cols, :] += dot(dscores, kms[h, rows, :], 0, 0)
    for qb in range(blocks):
        rows = slice(qb * BLOCK, (qb + 1) * BLOCK)
        grad = dq[rows, :] * (HEAD**-0.5)
        dq_ref[rows, :] = (
            grad * tab_ref[0, rows, :] - swap_halves(grad) * tab_ref[1, rows, :]
        ).astype(BF16)
        grad = dk[rows, :]
        dk_ref[rows, :] = (
            grad * tab_ref[2, rows, :] - swap_halves(grad) * tab_ref[3, rows, :]
        ).astype(BF16)
        dv_ref[rows, :] = dv[rows, :].astype(BF16)


def attend_back(q, k, v, do, o, lse, tables, seg_col, seg_row):
    length, width = q.shape
    pairs = width // LANES
    lane_block = pl.BlockSpec((length, LANES), lambda p: (0, p))
    return pl.pallas_call(
        functools.partial(attend_back_kernel, length),
        grid=(pairs,),
        out_shape=[jax.ShapeDtypeStruct((length, width), BF16)] * 3,
        in_specs=[lane_block] * 5
        + [
            pl.BlockSpec((1, 8, length), lambda p: (p, 0, 0)),
            pl.BlockSpec((4, length, LANES), lambda p: (0, 0, 0)),
            pl.BlockSpec((length, 1), lambda p: (0, 0)),
            pl.BlockSpec((1, length), lambda p: (0, 0)),
        ],
        out_specs=[lane_block] * 3,
        scratch_shapes=[
            pltpu.VMEM((length, length), F32),
            pltpu.VMEM((2, length, LANES), BF16),
            pltpu.VMEM((length, LANES), BF16),
            pltpu.VMEM((2, length, LANES), BF16),
            pltpu.VMEM((2, length, LANES), BF16),
            pltpu.VMEM((8, length), F32),
            pltpu.VMEM((length, LANES), F32),
            pltpu.VMEM((length, LANES), F32),
            pltpu.VMEM((length, LANES), F32),
        ],
        compiler_params=pltpu.CompilerParams(vmem_limit_bytes=VMEM_LIMIT),
        cost_estimate=cost(30),
    )(q, k, v, do, o, lse, tables, seg_col, seg_row)


def norm_parts(values):
    center = jnp.mean(values, axis=-1, keepdims=True)
    shifted = values - center
    inverse = lax.rsqrt(jnp.mean(shifted * shifted, axis=-1, keepdims=True) + EPSILON)
    return shifted * inverse, inverse


def fold(values):
    rows, width = values.shape
    return jnp.sum(values.reshape(rows // 8, 8, width), axis=0)


def finish_middle(total, here, own, held, vecs, outs):
    middle = held["block"][here, :].astype(F32) + total
    outs[0][own, :] = middle
    normed, _ = norm_parts(middle)
    return normed * vecs[0][...] + vecs[1][...]


def norm_back(base, values, total, vecs, sums):
    normed, inverse = norm_parts(values)
    scaled = total * vecs[0][...]
    grad = base + inverse * (
        scaled
        - jnp.mean(scaled, axis=-1, keepdims=True)
        - normed * jnp.mean(scaled * normed, axis=-1, keepdims=True)
    )
    sums[0] += fold(total * normed)
    sums[1] += fold(total)
    return grad


def finish_second(total, here, own, held, vecs, outs):
    base = held["cotangent"][here, :].astype(F32)
    grad = norm_back(base, held["middle"][own, :], total, vecs, outs[0])
    outs[1][own, :] = grad
    return grad


def finish_first(total, here, own, held, vecs, outs):
    values = held["block"][here, :].astype(F32)
    return norm_back(held["middle_grad"][own, :], values, total, vecs, outs[0])


def line_kernel(plan, count, chunks, slack, *refs):
    finish, clear = plan["finish"], plan["clear"]
    names, parts, tasks = plan["names"], plan["parts"], plan["tasks"]
    num_vec, num_own, num_task = plan["vecs"], plan["owns"], len(tasks)
    refs = list(refs)

    def take(number):
        taken = refs[:number]
        del refs[:number]
        return taken

    sources = take(len(names))
    vecs = take(num_vec)
    (out_ref,) = take(1)
    outs = take(num_own)
    task_outs = take(num_task)
    held = dict(zip(names, take(len(names))))
    in_a, in_b, part, turned, stage = take(5)
    load_sem, stage_sem = take(2)
    (rsa_s, rsa_r, rsb_s, rsb_r, aga_s, aga_r, agb_s, agb_r) = refs
    z = lax.axis_index("tp")
    tokens, width = out_ref.shape
    half = tokens // 2
    size = half // chunks
    ahead = slack * (count - 1)
    steps = chunks + 2 * ahead
    from_first, from_last = slack * z, slack * (count - 1 - z)
    first, last = z == 0, z == count - 1
    up = jnp.minimum(z + 1, count - 1)
    down = jnp.maximum(z - 1, 0)

    loads = {
        name: pltpu.make_async_copy(source, held[name], load_sem.at[i])
        for i, (name, source) in enumerate(zip(names, sources))
    }
    for name in names:
        loads[name].start()

    barrier = pltpu.get_barrier_semaphore()

    @pl.when(jnp.logical_not(last))
    def _():
        pl.semaphore_signal(barrier, inc=1, device_id={"tp": up}, device_id_type=MESH)

    @pl.when(jnp.logical_not(first))
    def _():
        pl.semaphore_signal(barrier, inc=1, device_id={"tp": down}, device_id_type=MESH)

    @pl.when(first | last)
    def _():
        pl.semaphore_wait(barrier, 1)

    @pl.when(jnp.logical_not(first | last))
    def _():
        pl.semaphore_wait(barrier, 2)

    if clear:
        outs[0][...] = jnp.zeros_like(outs[0])

    def own_rows(c):
        return pl.ds(pl.multiple_of(c * size, size), size)

    def a_rows(c):
        return own_rows(c)

    def b_rows(c):
        return pl.ds(pl.multiple_of(half + c * size, size), size)

    def hop(source, target, send, recv, c, device):
        return pltpu.make_async_remote_copy(
            src_ref=source,
            dst_ref=target,
            send_sem=send.at[c],
            recv_sem=recv.at[c],
            device_id={"tp": device},
            device_id_type=MESH,
        )

    def gather_a(c):
        rows = out_ref.at[a_rows(c), :]
        return hop(rows, rows, aga_s, aga_r, c, up)

    def gather_b(c):
        rows = out_ref.at[b_rows(c), :]
        return hop(rows, rows, agb_s, agb_r, c, down)

    def reduce_a(c):
        rows = in_a.at[own_rows(c), :]
        return hop(rows, rows, rsa_s, rsa_r, c, down)

    def reduce_b(c):
        rows = in_b.at[own_rows(c), :]
        return hop(rows, rows, rsb_s, rsb_r, c, up)

    def block_start(t, offset):
        return jnp.clip((t - lax.rem(t, GROUP) - offset) * size, 0, half - GROUP * size)

    def reduce_step(t, c, offset, place, rows, landed, move, gather, starts, ends):
        here = rows(c)
        own = own_rows(c)
        row = place * GROUP * size + c * size - block_start(t, offset)
        term_rows = pl.ds(pl.multiple_of(row, size), size)

        @pl.when(starts)
        def _():
            landed[own, :] = part[term_rows, :].astype(BF16)
            move(c).start()

        @pl.when(jnp.logical_not(starts))
        def _():
            move(c).wait_recv()

        @pl.when(jnp.logical_not(starts | ends))
        def _():
            landed[own, :] = (landed[own, :].astype(F32) + part[term_rows, :]).astype(BF16)
            move(c).start()

        @pl.when(ends)
        def _():
            total = landed[own, :].astype(F32) + part[term_rows, :]
            out_ref[here, :] = finish(total, here, own, held, vecs, outs).astype(BF16)
            gather(c).start()

    def gather_step(c, gather, starts, ends):
        @pl.when(jnp.logical_not(starts))
        def _():
            gather(c).wait_recv()

        @pl.when(jnp.logical_not(starts | ends))
        def _():
            gather(c).start()

    def when_chunk(c, work):
        pl.when((c >= 0) & (c < chunks))(lambda: work(c))

    def make_parts(t):
        top = pl.ds(pl.multiple_of(block_start(t, from_last), size), GROUP * size)
        low = pl.ds(pl.multiple_of(half + block_start(t, from_first), size), GROUP * size)

        def columns(n, carry):
            cols = pl.ds(pl.multiple_of(n * TILE, TILE), TILE)
            total = 0.0
            for left, right in parts:
                rows = jnp.concatenate([held[left][top, :], held[left][low, :]], axis=0)
                total = total + dot(rows, held[right][cols, :], 1, 1)
            part[:, cols] = total
            return carry

        lax.fori_loop(0, width // TILE, columns, 0)

    def run_task(index, tile, slot):
        kind, left, right = tasks[index]
        target = task_outs[index]
        wide = target.shape[1]
        rows = pl.ds(pl.multiple_of(tile * ROWS, ROWS), ROWS)
        if kind == "weight":
            depth = tokens
            turned[:, :depth] = jnp.transpose(held[left][:, rows])

        def columns(n, carry):
            cols = pl.ds(pl.multiple_of(n * TILE, TILE), TILE)
            if kind == "weight":
                value = dot(turned[:, :depth], held[right][:, cols], 1, 0)
            elif kind == "rows":
                value = dot(held[left][rows, :], held[right][:, cols], 1, 0)
            else:
                value = dot(held[left][rows, :], held[right][cols, :], 1, 1)
                top = tile * ROWS < half
                mine = (first & top) | (last & jnp.logical_not(top))
                own = pl.multiple_of(lax.rem(tile * ROWS, half), ROWS)
                base = held["middle"][pl.ds(own, ROWS), cols]
                value = value + jnp.where(mine, base, 0.0)
            stage[slot, :, cols] = value.astype(BF16)
            return carry

        lax.fori_loop(0, wide // TILE, columns, 0)
        stage_copy(index, tile, slot).start()

    def stage_copy(index, tile, slot):
        target = task_outs[index]
        rows = pl.ds(pl.multiple_of(tile * ROWS, ROWS), ROWS)
        return pltpu.make_async_copy(
            stage.at[slot, :, : target.shape[1]], target.at[rows, :], stage_sem.at[slot]
        )

    starts_at = [0]
    for index in range(num_task):
        starts_at.append(starts_at[-1] + task_outs[index].shape[0] // ROWS)
    task_total = starts_at[-1]
    per_group = GROUP - 1

    def step(t, carry):
        pl.when(lax.rem(t, GROUP) == 0)(lambda: make_parts(t))
        when_chunk(
            t - from_last,
            lambda c: reduce_step(t, c, from_last, 0, a_rows, in_a, reduce_a, gather_a, last, first),
        )
        when_chunk(
            t - from_first,
            lambda c: reduce_step(t, c, from_first, 1, b_rows, in_b, reduce_b, gather_b, first, last),
        )
        when_chunk(t - ahead - from_first, lambda c: gather_step(c, gather_a, first, last))
        when_chunk(t - ahead - from_last, lambda c: gather_step(c, gather_b, last, first))
        if num_task:
            turn = (t // GROUP) * per_group + lax.rem(t, GROUP) - 1
            free = lax.rem(t, GROUP) != 0
            slot = lax.rem(turn + per_group + 1, 2)

            @pl.when(t == 1)
            def _():
                for name in plan["late"]:
                    loads[name].wait()

            for index in range(num_task):
                low, high = starts_at[index] + 2, min(starts_at[index + 1] + 2, task_total)
                pl.when(free & (turn >= low) & (turn < high))(
                    lambda index=index, low=low: stage_copy(index, turn - low, slot).wait()
                )
            for index in range(num_task):
                low, high = starts_at[index], starts_at[index + 1]
                pl.when(free & (turn >= low) & (turn < high))(
                    lambda index=index, low=low: run_task(index, turn - low, slot)
                )
        return carry

    for name in names:
        if name not in plan["late"]:
            loads[name].wait()
    lax.fori_loop(0, steps, step, 0)
    if num_task:
        assert task_total >= 2 and (steps // GROUP) * per_group >= task_total
        for turn in (task_total - 2, task_total - 1):
            index = max(i for i in range(num_task) if starts_at[i] <= turn)
            stage_copy(index, turn - starts_at[index], turn % 2).wait()

    def drain(c, carry):
        @pl.when(jnp.logical_not(first))
        def _():
            reduce_a(c).wait_send()
            gather_b(c).wait_send()

        @pl.when(jnp.logical_not(last))
        def _():
            reduce_b(c).wait_send()
            gather_a(c).wait_send()

        return carry

    lax.fori_loop(0, chunks, drain, 0)


def line_sum(finish, count, held, vecs, parts, late, tasks, own_shapes, clear, collective_id):
    names = list(held)
    tokens = held[parts[0][0]].shape[0]
    width = held[parts[0][1]].shape[0]
    half = tokens // 2
    plan = dict(
        finish=finish,
        clear=clear,
        names=names,
        parts=parts,
        late=late,
        tasks=[task[:3] for task in tasks],
        vecs=len(vecs),
        owns=len(own_shapes),
    )
    whole = pl.BlockSpec(memory_space=pltpu.VMEM)
    any_space = pl.BlockSpec(memory_space=pl.ANY)
    depth = tokens if any(task[0] == "weight" for task in tasks) else LANES
    stage_width = max([task[3][1] for task in tasks] + [LANES])
    return pl.pallas_call(
        functools.partial(line_kernel, plan, count, CHUNKS, SLACK),
        out_shape=[jax.ShapeDtypeStruct((tokens, width), BF16)]
        + own_shapes
        + [jax.ShapeDtypeStruct(task[3], BF16) for task in tasks],
        in_specs=[any_space] * len(names) + [whole] * len(vecs),
        out_specs=[whole] * (1 + len(own_shapes)) + [any_space] * len(tasks),
        scratch_shapes=[pltpu.VMEM(array.shape, array.dtype) for array in held.values()]
        + [pltpu.VMEM((half, width), BF16)] * 2
        + [
            pltpu.VMEM((2 * GROUP * half // CHUNKS, width), F32),
            pltpu.VMEM((ROWS, depth), BF16),
            pltpu.VMEM((2, ROWS if tasks else 16, stage_width), BF16),
            pltpu.SemaphoreType.DMA((len(names),)),
            pltpu.SemaphoreType.DMA((2,)),
        ]
        + [pltpu.SemaphoreType.DMA((CHUNKS,))] * 8,
        compiler_params=pltpu.CompilerParams(
            collective_id=collective_id, has_side_effects=True, vmem_limit_bytes=VMEM_LIMIT
        ),
        cost_estimate=cost(110),
    )(*held.values(), *vecs)


def axis_barrier(counts):
    barrier = pltpu.get_barrier_semaphore()
    for axis, count in counts:
        me = lax.axis_index(axis)
        for k in range(1, count):
            pl.semaphore_signal(
                barrier, inc=1, device_id={axis: lax.rem(me + k, count)}, device_id_type=MESH
            )
    pl.semaphore_wait(barrier, sum(count - 1 for _, count in counts))


def share(axis, count, pick, landed, send_sem, recv_sem):
    me = lax.axis_index(axis)
    copies = []
    for k in range(1, count):
        device = lax.rem(me + k, count)
        copy = pltpu.make_async_remote_copy(
            src_ref=pick(device),
            dst_ref=landed.at[me],
            send_sem=send_sem.at[k],
            recv_sem=recv_sem.at[k],
            device_id={axis: device},
            device_id_type=MESH,
        )
        copy.start()
        copies.append(copy)
    return copies


def total_of(landed, count):
    total = landed[0]
    for k in range(1, count):
        total = total + landed[k]
    return total


def tp_sum_kernel(count, x_ref, out_ref, landed, send_sem, recv_sem):
    axis_barrier([("tp", count)])
    copies = share("tp", count, lambda d: x_ref, landed, send_sem, recv_sem)
    landed[lax.axis_index("tp")] = x_ref[...]
    for copy in copies:
        copy.wait()
    out_ref[...] = total_of(landed, count)


def tp_sum(values, count, collective_id):
    whole = pl.BlockSpec(memory_space=pltpu.VMEM)
    return pl.pallas_call(
        functools.partial(tp_sum_kernel, count),
        out_shape=jax.ShapeDtypeStruct(values.shape, F32),
        in_specs=[whole],
        out_specs=whole,
        scratch_shapes=[
            pltpu.VMEM((count,) + values.shape, F32),
            pltpu.SemaphoreType.DMA((count,)),
            pltpu.SemaphoreType.DMA((count,)),
        ],
        compiler_params=pltpu.CompilerParams(collective_id=collective_id, has_side_effects=True),
        cost_estimate=cost(5),
    )(values)


def norm_sum_kernel(
    seq_count, tp_count, full_ref, split_ref, own_ref, sum_ref,
    tp_landed, summed, own_landed, split_landed, sem_a, sem_b, sem_c, sem_d, sem_e, sem_f,
):
    me = lax.axis_index("seq")
    axis_barrier([("seq", seq_count), ("tp", tp_count)])
    tp_copies = share("tp", tp_count, lambda d: full_ref, tp_landed, sem_a, sem_b)
    split_copies = share("seq", seq_count, lambda d: split_ref, split_landed, sem_c, sem_d)
    tp_landed[lax.axis_index("tp")] = full_ref[...]
    split_landed[me] = split_ref[...]
    for copy in tp_copies:
        copy.wait()
    summed[...] = total_of(tp_landed, tp_count)
    own_copies = share("seq", seq_count, lambda d: summed.at[d], own_landed, sem_e, sem_f)
    own_landed[me] = summed[me]
    for copy in split_copies:
        copy.wait()
    sum_ref[...] = total_of(split_landed, seq_count)
    for copy in own_copies:
        copy.wait()
    own_ref[...] = total_of(own_landed, seq_count)


def norm_sum(full, split, seq_count, tp_count, collective_id):
    whole = pl.BlockSpec(memory_space=pltpu.VMEM)
    piece = full.shape[1:]
    return pl.pallas_call(
        functools.partial(norm_sum_kernel, seq_count, tp_count),
        out_shape=[
            jax.ShapeDtypeStruct(piece, F32),
            jax.ShapeDtypeStruct(split.shape, F32),
        ],
        in_specs=[whole] * 2,
        out_specs=[whole] * 2,
        scratch_shapes=[
            pltpu.VMEM((tp_count,) + full.shape, F32),
            pltpu.VMEM(full.shape, F32),
            pltpu.VMEM((seq_count,) + piece, F32),
            pltpu.VMEM((seq_count,) + split.shape, F32),
            pltpu.SemaphoreType.DMA((tp_count,)),
            pltpu.SemaphoreType.DMA((tp_count,)),
        ]
        + [pltpu.SemaphoreType.DMA((seq_count,))] * 4,
        compiler_params=pltpu.CompilerParams(collective_id=collective_id, has_side_effects=True),
        cost_estimate=cost(10),
    )(full, split)


def matmul(left, right, left_dim, right_dim, kind=F32):
    return dot(left, right, left_dim, right_dim).astype(kind)


def rotation_tables(positions):
    half_size = HEAD // 2
    index_pairs = jnp.arange(half_size, dtype=F32)
    theta_rate = jnp.exp(-2.0 * index_pairs / HEAD * jnp.log(10000.0))
    zeta_base = (2.0 * index_pairs + 0.4 * HEAD) / (1.4 * HEAD)
    place_float = positions.astype(F32)[..., None]
    angles = place_float * theta_rate
    power = jnp.log(zeta_base) * place_float / 512.0
    cos_part, sin_part = jnp.cos(angles), jnp.sin(angles)
    grow, shrink = jnp.exp(power), jnp.exp(-power)
    cos_full = jnp.concatenate([cos_part] * 4, axis=-1)
    sin_full = jnp.concatenate([-sin_part, sin_part] * 2, axis=-1)
    grow = jnp.concatenate([grow] * 4, axis=-1)
    shrink = jnp.concatenate([shrink] * 4, axis=-1)
    return jnp.stack([cos_full * grow, sin_full * grow, cos_full * shrink, sin_full * shrink])


def body(
    seq_count,
    tp_count,
    block_in,
    segment_ids,
    first_gain,
    first_bias,
    w_query,
    w_key,
    w_value,
    head_gain,
    head_bias,
    w_out,
    second_gain,
    second_bias,
    w_up,
    hidden_gain,
    hidden_bias,
    w_down,
    out_cotangent,
):
    seq_index = lax.axis_index("seq")
    row_count, span, model_width = block_in.shape
    length = span * seq_count
    tokens = row_count * span
    head_width = w_query.shape[1]
    hidden_width = w_up.shape[1] * tp_count
    groups = seq_count // row_count
    width = head_width // groups

    first_gain_f = first_gain.astype(F32)[None]
    first_bias_f = first_bias.astype(F32)[None]
    second_gain_f = second_gain.astype(F32)[None]
    second_bias_f = second_bias.astype(F32)[None]
    head_gain_f = head_gain.astype(F32)[None]
    head_bias_f = head_bias.astype(F32)[None]
    hidden_gain_f = hidden_gain.astype(F32)[None]
    hidden_bias_f = hidden_bias.astype(F32)[None]

    seg_row = lax.dynamic_slice_in_dim(segment_ids, seq_index // groups, 1, 0)
    seg_col = seg_row.reshape(length, 1)
    earlier = jnp.sum((seg_row < seg_col).astype(jnp.int32), axis=-1)
    tables = rotation_tables(jnp.arange(length, dtype=jnp.int32) - earlier)

    block = block_in.reshape(tokens, model_width)
    cotangent = out_cotangent.reshape(tokens, model_width)

    normed_one, _ = norm_parts(block.astype(F32))
    first_act = (normed_one * first_gain_f + first_bias_f).astype(BF16)
    shape3 = (row_count, span, head_width)
    query = matmul(first_act, w_query, 1, 0, BF16).reshape(shape3)
    key = matmul(first_act, w_key, 1, 0, BF16).reshape(shape3)
    value = matmul(first_act, w_value, 1, 0, BF16).reshape(shape3)
    q_row, k_row, v_row = exchange(
        rows_out_kernel, seq_count, groups, (query, key, value), (length, width), 1
    )
    o_row, lse = attend(q_row, k_row, v_row, tables, seg_col, seg_row)
    (mixed,) = exchange(rows_back_kernel, seq_count, groups, (o_row,), shape3, 2)
    mixed = mixed.reshape(tokens, head_width).astype(F32)
    head_sums = tp_sum(
        jnp.stack([jnp.sum(mixed, axis=-1), jnp.sum(mixed * mixed, axis=-1)]), tp_count, 9
    )
    head_center = head_sums[0][:, None] / model_width
    head_inverse = lax.rsqrt(
        head_sums[1][:, None] / model_width - head_center * head_center + EPSILON
    )
    head_normed = (mixed - head_center) * head_inverse
    head_act = (head_normed * head_gain_f + head_bias_f).astype(BF16)
    own_shape = jax.ShapeDtypeStruct((tokens // 2, model_width), F32)
    sums_shape = jax.ShapeDtypeStruct((2, 8, model_width), F32)
    hidden_size = hidden_gain.shape[0]
    second_act, middle_own, grad_hidden_act = line_sum(
        finish_middle,
        tp_count,
        dict(head_act=head_act, w_out=w_out, block=block, cotangent=cotangent, w_down=w_down),
        (second_gain_f, second_bias_f),
        [("head_act", "w_out")],
        ("cotangent", "w_down"),
        [("rows", "cotangent", "w_down", (tokens, hidden_size))],
        [own_shape],
        False,
        3,
    )
    grad_hidden_act = grad_hidden_act.astype(F32)

    up_pre = matmul(second_act, w_up, 1, 0)
    cdf = 0.5 * lax.erfc(up_pre * (-(0.5**0.5)))
    gelu_out = up_pre * cdf
    hidden_scaled = grad_hidden_act * hidden_gain_f
    stats = tp_sum(
        jnp.stack(
            [
                jnp.sum(gelu_out, axis=-1),
                jnp.sum(gelu_out * gelu_out, axis=-1),
                jnp.sum(hidden_scaled, axis=-1),
                jnp.sum(hidden_scaled * gelu_out, axis=-1),
            ]
        ),
        tp_count,
        10,
    )
    stats = stats[:, :, None] / hidden_width
    hidden_center = stats[0]
    hidden_inverse = lax.rsqrt(stats[1] - hidden_center * hidden_center + EPSILON)
    hidden_normed = (gelu_out - hidden_center) * hidden_inverse
    hidden_act = (hidden_normed * hidden_gain_f + hidden_bias_f).astype(BF16)
    hidden_gain_grad = jnp.sum(grad_hidden_act * hidden_normed, axis=0)
    hidden_bias_grad = jnp.sum(grad_hidden_act, axis=0)
    hidden_cross = hidden_inverse * (stats[3] - hidden_center * stats[2])
    grad_gelu = hidden_inverse * (hidden_scaled - stats[2] - hidden_normed * hidden_cross)
    pdf = jnp.exp(-0.5 * up_pre * up_pre) * (1.0 / math.sqrt(2.0 * math.pi))
    grad_up = (grad_gelu * (cdf + up_pre * pdf)).astype(BF16)

    weight_shape = (model_width, hidden_size)
    grad_middle_low, second_sums, grad_middle_own, down_part, w_down_terms, w_up_terms = line_sum(
        finish_second,
        tp_count,
        dict(
            grad_up=grad_up,
            w_up=w_up,
            cotangent=cotangent,
            middle=middle_own,
            hidden_act=hidden_act,
            w_down=w_down,
            second_act=second_act,
        ),
        (second_gain_f,),
        [("grad_up", "w_up")],
        ("hidden_act", "w_down", "second_act"),
        [
            ("down", "hidden_act", "w_down", (tokens, model_width)),
            ("weight", "cotangent", "hidden_act", weight_shape),
            ("weight", "second_act", "grad_up", weight_shape),
        ],
        [sums_shape, own_shape],
        True,
        4,
    )
    block_out = lax.psum(down_part, "tp")

    def scatter(grad):
        return lax.psum_scatter(grad, "seq", scatter_dimension=0, tiled=True)

    w_down_grad = scatter(w_down_terms)
    w_up_grad = scatter(w_up_terms)

    grad_head_act = matmul(grad_middle_low, w_out, 1, 0)
    head_gain_grad = jnp.sum(grad_head_act * head_normed, axis=0)
    head_bias_grad = jnp.sum(grad_head_act, axis=0)
    head_scaled = grad_head_act * head_gain_f
    head_back = tp_sum(
        jnp.stack([jnp.sum(head_scaled, axis=-1), jnp.sum(head_scaled * head_normed, axis=-1)]),
        tp_count,
        11,
    )
    head_back = head_back[:, :, None] / model_width
    grad_mixed = head_inverse * (head_scaled - head_back[0] - head_normed * head_back[1])
    (do_row,) = exchange(
        rows_out_kernel,
        seq_count,
        groups,
        (grad_mixed.astype(BF16).reshape(shape3),),
        (length, width),
        6,
    )
    grads_row = attend_back(q_row, k_row, v_row, do_row, o_row, lse, tables, seg_col, seg_row)
    grads = exchange(rows_back_kernel, seq_count, groups, grads_row, shape3, 7)
    grad_query, grad_key, grad_value = (g.reshape(tokens, head_width) for g in grads)
    head_terms = (
        jnp.concatenate(
            [
                matmul(first_act, grad_query, 0, 0, BF16),
                matmul(first_act, grad_key, 0, 0, BF16),
                matmul(first_act, grad_value, 0, 0, BF16),
                matmul(grad_middle_low, head_act, 0, 0, BF16),
            ],
            axis=1,
        )
    )
    grad_query, head_terms, w_down_grad, block_out = lax.optimization_barrier(
        (grad_query, head_terms, w_down_grad, block_out)
    )
    head_grads = scatter(head_terms)
    w_query_grad, w_key_grad, w_value_grad, w_out_grad = jnp.split(
        head_grads.astype(F32), 4, axis=1
    )
    input_grad, first_sums = line_sum(
        finish_first,
        tp_count,
        dict(
            grad_query=grad_query,
            w_query=w_query,
            grad_key=grad_key,
            w_key=w_key,
            grad_value=grad_value,
            w_value=w_value,
            block=block,
            middle_grad=grad_middle_own,
        ),
        (first_gain_f,),
        [("grad_query", "w_query"), ("grad_key", "w_key"), ("grad_value", "w_value")],
        (),
        [],
        [sums_shape],
        True,
        8,
    )

    own_width = model_width // seq_count
    full = jnp.concatenate([jnp.sum(second_sums, axis=1), jnp.sum(first_sums, axis=1)])
    full = full.reshape(4, seq_count, own_width).transpose(1, 0, 2)
    full = full.reshape(seq_count, 4 * own_width // LANES, LANES)
    split = jnp.concatenate([hidden_gain_grad, hidden_bias_grad, head_gain_grad, head_bias_grad])
    norm_own, split = norm_sum(
        full, split.reshape(split.shape[0] // LANES, LANES), seq_count, tp_count, 12
    )
    norm_own = norm_own.reshape(4, own_width)
    split = split.reshape(-1)
    split_sums = (
        split[2 * hidden_size : 2 * hidden_size + head_width],
        split[2 * hidden_size + head_width :],
        split[:hidden_size],
        split[hidden_size : 2 * hidden_size],
    )
    return (
        block_out.reshape(block_in.shape),
        input_grad.reshape(block_in.shape),
        norm_own[2],
        norm_own[3],
        w_query_grad,
        w_key_grad,
        w_value_grad,
        split_sums[0],
        split_sums[1],
        w_out_grad,
        norm_own[0],
        norm_own[1],
        w_up_grad.astype(F32),
        split_sums[2],
        split_sums[3],
        w_down_grad.astype(F32),
    )


def solution(mesh):
    return jax.shard_map(
        functools.partial(body, mesh.shape["seq"], mesh.shape["tp"]),
        mesh=mesh,
        in_specs=(
            P(None, "seq", None),
            P(),
            P(),
            P(),
            P(None, "tp"),
            P(None, "tp"),
            P(None, "tp"),
            P("tp"),
            P("tp"),
            P(None, "tp"),
            P(),
            P(),
            P(None, "tp"),
            P("tp"),
            P("tp"),
            P(None, "tp"),
            P(None, "seq", None),
        ),
        out_specs=(
            P(None, "seq", None),
            P(None, "seq", None),
            P("seq"),
            P("seq"),
            P("seq", "tp"),
            P("seq", "tp"),
            P("seq", "tp"),
            P("tp"),
            P("tp"),
            P("seq", "tp"),
            P("seq"),
            P("seq"),
            P("seq", "tp"),
            P("tp"),
            P("tp"),
            P("seq", "tp"),
        ),
        check_vma=False,
    )
```

```python
import functools
import math

import jax
import jax.numpy as jnp
from jax import lax
from jax.experimental import pallas as pl
from jax.experimental.pallas import tpu as pltpu
from jax.sharding import PartitionSpec as P

HEAD = 64
LANES = 128
BLOCK = 256
EPSILON = 1e-05
MASKED = -1e30
MESH = pl.DeviceIdType.MESH
F32 = jnp.float32
BF16 = jnp.bfloat16
CHUNKS = 16
SLACK = 2
GROUP = 4
ROWS = 256
TILE = 512
VMEM_LIMIT = 60 * 1024 * 1024


def cost(micros):
    return pl.CostEstimate(flops=int(micros * 1.1e9), bytes_accessed=0, transcendentals=0)


def dot(left, right, left_dim, right_dim):
    return lax.dot_general(
        left, right, (((left_dim,), (right_dim,)), ((), ())), preferred_element_type=F32
    )


def seq_signal(count):
    me = lax.axis_index("seq")
    barrier = pltpu.get_barrier_semaphore()
    for k in range(1, count):
        pl.semaphore_signal(
            barrier, inc=1, device_id={"seq": lax.rem(me + k, count)}, device_id_type=MESH
        )


def seq_wait(count):
    pl.semaphore_wait(pltpu.get_barrier_semaphore(), count - 1)


def send(source, target, send_sem, recv_sem, device):
    return pltpu.make_async_remote_copy(
        src_ref=source,
        dst_ref=target,
        send_sem=send_sem,
        recv_sem=recv_sem,
        device_id={"seq": device},
        device_id_type=MESH,
    )


def spans(index, span):
    return pl.ds(pl.multiple_of(index * span, LANES), span)


def swap_halves(values):
    lane = lax.broadcasted_iota(jnp.int32, values.shape, 1)
    return jnp.where(
        lane % HEAD < HEAD // 2,
        pltpu.roll(values, LANES - HEAD // 2, 1),
        pltpu.roll(values, HEAD // 2, 1),
    )


def head_masks(values):
    lane = lax.broadcasted_iota(jnp.int32, values.shape, 1)
    zero = jnp.zeros_like(values)
    return jnp.where(lane < HEAD, values, zero), jnp.where(lane < HEAD, zero, values)


def block_rows(index):
    return slice(index * BLOCK, (index + 1) * BLOCK)


def rotated(values, tables, first, rows):
    values = values.astype(F32)
    return values * tables[first, rows, :] + swap_halves(values) * tables[first + 1, rows, :]


def rotated_back(values, tables, first, rows):
    return values * tables[first, rows, :] - swap_halves(values) * tables[first + 1, rows, :]


def norm_parts(values):
    center = jnp.mean(values, axis=-1, keepdims=True)
    shifted = values - center
    inverse = lax.rsqrt(jnp.mean(shifted * shifted, axis=-1, keepdims=True) + EPSILON)
    return shifted * inverse, inverse


def front_kernel(
    count, groups, x_ref, wq_ref, wk_ref, wv_ref, gain_ref, bias_ref, tab_ref, segc_ref, segr_ref,
    act_ref, qkv_ref, o_ref, lse_ref, mixed_ref,
    weights, staged, bias, qs, ks, load_sem, send_sem, recv_sem, back_send_sem, back_recv_sem,
):
    me = lax.axis_index("seq")
    pairs, length = qkv_ref.shape[:2]
    tokens = x_ref.shape[0]
    span = length // count
    blocks = length // BLOCK
    mine, row = lax.rem(me, groups), me // groups
    seq_signal(count)
    loads = []
    for j in range(pairs * groups):
        for i, source in enumerate((wq_ref, wk_ref, wv_ref)):
            copy = pltpu.make_async_copy(
                source.at[:, j * LANES : (j + 1) * LANES],
                weights.at[j, :, i * LANES : (i + 1) * LANES],
                load_sem.at[3 * j + i],
            )
            copy.start()
            loads.append(copy)

    def norm_step(r, carry):
        rows = pl.ds(pl.multiple_of(r * LANES, LANES), LANES)
        normed, _ = norm_parts(x_ref[rows, :].astype(F32))
        act_ref[rows, :] = (normed * gain_ref[...] + bias_ref[...]).astype(BF16)
        return carry

    lax.fori_loop(0, tokens // LANES, norm_step, 0)
    for copy in loads:
        copy.wait()

    def there(p, k):
        device = lax.rem(me + k, count)
        return send(
            staged.at[lax.rem(device, groups) * pairs + p, spans(device // groups, span), :],
            qkv_ref.at[p, spans(me, span), :],
            send_sem.at[p, k],
            recv_sem.at[p, k],
            device,
        )

    def back(p, k):
        device = lax.rem(me + k, count)
        return send(
            o_ref.at[p, spans(device, span), :],
            mixed_ref.at[spans(row, span), spans(mine * pairs + p, LANES)],
            back_send_sem.at[p, k],
            back_recv_sem.at[p, k],
            device,
        )

    def project(p, carry):
        for group in range(groups):

            def rows_step(r, inner):
                rows = pl.ds(pl.multiple_of(r * BLOCK, BLOCK), BLOCK)
                j = group * pairs + p
                staged[j, rows, :] = dot(act_ref[rows, :], weights[j], 1, 0).astype(BF16)
                return inner

            lax.fori_loop(0, tokens // BLOCK, rows_step, 0)

        @pl.when(p == 0)
        def _():
            seq_wait(count)

        for k in range(1, count):
            there(p, k).start()
        qkv_ref[p, spans(me, span), :] = staged[mine * pairs + p, spans(row, span), :]
        return carry

    lax.fori_loop(0, pairs, project, 0)
    for qb in range(blocks):
        rows = block_rows(qb)
        keys = (qb + 1) * BLOCK
        same = segc_ref[rows, :] == segr_ref[:, :keys]
        query = lax.broadcasted_iota(jnp.int32, (BLOCK, keys), 0) + qb * BLOCK
        key = lax.broadcasted_iota(jnp.int32, (BLOCK, keys), 1)
        bias[rows, :keys] = jnp.where(same & (key <= query), 0.0, MASKED)

    def attend(p, carry):
        for k in range(1, count):
            there(p, k).wait_recv()
        for qb in range(blocks):
            rows = block_rows(qb)
            q = rotated(qkv_ref[p, rows, :LANES], tab_ref, 0, rows) * (HEAD**-0.5)
            q0, q1 = head_masks(q)
            qs[0, rows, :] = q0.astype(BF16)
            qs[1, rows, :] = q1.astype(BF16)
            k = rotated(qkv_ref[p, rows, LANES : 2 * LANES], tab_ref, 2, rows)
            ks[rows, :] = k.astype(BF16)
        for qb in range(blocks):
            rows = block_rows(qb)
            keys = (qb + 1) * BLOCK
            outs = []
            logs = []
            for h in range(2):
                scores = dot(qs[h, rows, :], ks[:keys, :], 1, 1) + bias[rows, :keys]
                top = jnp.max(scores, axis=1, keepdims=True)
                expo = jnp.exp(scores - top)
                total = jnp.sum(expo, axis=1, keepdims=True)
                outs.append(dot(expo.astype(BF16), qkv_ref[p, :keys, 2 * LANES :], 1, 0) / total)
                logs.append(jnp.broadcast_to(top + jnp.log(total), (BLOCK, LANES)))
            lane = lax.broadcasted_iota(jnp.int32, (BLOCK, LANES), 1)
            o_ref[p, rows, :] = jnp.where(lane < HEAD, outs[0], outs[1]).astype(BF16)
            logs_t = jnp.transpose(jnp.where(lane < HEAD, logs[0], logs[1]))
            lse_ref[p, 0:1, rows] = logs_t[0:1]
            lse_ref[p, 1:2, rows] = logs_t[HEAD : HEAD + 1]
        for k in range(1, count):
            back(p, k).start()
        mixed_ref[spans(row, span), spans(mine * pairs + p, LANES)] = o_ref[p, spans(me, span), :]
        return carry

    lax.fori_loop(0, pairs, attend, 0)

    def drain(p, carry):
        for k in range(1, count):
            there(p, k).wait_send()
            back(p, k).wait()
        return carry

    lax.fori_loop(0, pairs, drain, 0)


def front(x, w_query, w_key, w_value, gain, bias, tables, seg_col, seg_row, count, groups, collective_id):
    tokens, model_width = x.shape
    head_width = w_query.shape[1]
    length = seg_col.shape[0]
    pairs = head_width // groups // LANES
    whole = pl.BlockSpec(memory_space=pltpu.VMEM)
    any_space = pl.BlockSpec(memory_space=pl.ANY)
    return pl.pallas_call(
        functools.partial(front_kernel, count, groups),
        out_shape=[
            jax.ShapeDtypeStruct((tokens, model_width), BF16),
            jax.ShapeDtypeStruct((pairs, length, 3 * LANES), BF16),
            jax.ShapeDtypeStruct((pairs, length, LANES), BF16),
            jax.ShapeDtypeStruct((pairs, 8, length), F32),
            jax.ShapeDtypeStruct((tokens, head_width), BF16),
        ],
        in_specs=[whole] + [any_space] * 3 + [whole] * 5,
        out_specs=[whole] * 5,
        scratch_shapes=[
            pltpu.VMEM((pairs * groups, model_width, 3 * LANES), BF16),
            pltpu.VMEM((pairs * groups, tokens, 3 * LANES), BF16),
            pltpu.VMEM((length, length), F32),
            pltpu.VMEM((2, length, LANES), BF16),
            pltpu.VMEM((length, LANES), BF16),
            pltpu.SemaphoreType.DMA((3 * pairs * groups,)),
        ]
        + [pltpu.SemaphoreType.DMA((pairs, count))] * 4,
        compiler_params=pltpu.CompilerParams(
            collective_id=collective_id, has_side_effects=True, vmem_limit_bytes=VMEM_LIMIT
        ),
        cost_estimate=cost(60),
    )(x, w_query, w_key, w_value, gain, bias, tables, seg_col, seg_row)


def back_kernel(
    count, groups, do_ref, qkv_ref, o_ref, lse_ref, tab_ref, segc_ref, segr_ref, grads_ref,
    do_row, made, bias, qs, ks, kms, dos, delta, dq, dk, dv,
    send_sem, recv_sem, back_send_sem, back_recv_sem,
):
    me = lax.axis_index("seq")
    pairs, length = qkv_ref.shape[:2]
    span = length // count
    blocks = length // BLOCK
    mine, row = lax.rem(me, groups), me // groups
    seq_signal(count)

    def there(p, k):
        device = lax.rem(me + k, count)
        return send(
            do_ref.at[spans(device // groups, span), spans(lax.rem(device, groups) * pairs + p, LANES)],
            do_row.at[p, spans(me, span), :],
            send_sem.at[p, k],
            recv_sem.at[p, k],
            device,
        )

    def back(p, k):
        device = lax.rem(me + k, count)
        return send(
            made.at[p, :, spans(device, span), :],
            grads_ref.at[:, spans(row, span), spans(mine * pairs + p, LANES)],
            back_send_sem.at[p, k],
            back_recv_sem.at[p, k],
            device,
        )

    seq_wait(count)

    def share_out(p, carry):
        for k in range(1, count):
            there(p, k).start()
        do_row[p, spans(me, span), :] = do_ref[spans(row, span), spans(mine * pairs + p, LANES)]
        return carry

    lax.fori_loop(0, pairs, share_out, 0)
    for kb in range(blocks):
        rows = block_rows(kb)
        start = kb * BLOCK
        shape = (BLOCK, length - start)
        same = segc_ref[rows, :] == segr_ref[:, start:]
        key = lax.broadcasted_iota(jnp.int32, shape, 0)
        query = lax.broadcasted_iota(jnp.int32, shape, 1)
        bias[rows, start:] = jnp.where(same & (key <= query), 0.0, MASKED)

    def attend(p, carry):
        for qb in range(blocks):
            rows = block_rows(qb)
            q = rotated(qkv_ref[p, rows, :LANES], tab_ref, 0, rows) * (HEAD**-0.5)
            q0, q1 = head_masks(q)
            qs[0, rows, :] = q0.astype(BF16)
            qs[1, rows, :] = q1.astype(BF16)
            k = rotated(qkv_ref[p, rows, LANES : 2 * LANES], tab_ref, 2, rows)
            ks[rows, :] = k.astype(BF16)
            k0, k1 = head_masks(k)
            kms[0, rows, :] = k0.astype(BF16)
            kms[1, rows, :] = k1.astype(BF16)
        dq[...] = jnp.zeros_like(dq)
        dk[...] = jnp.zeros_like(dk)
        dv[...] = jnp.zeros_like(dv)
        for k in range(1, count):
            there(p, k).wait_recv()
        for qb in range(blocks):
            rows = block_rows(qb)
            grad = do_row[p, rows, :].astype(F32)
            d0, d1 = head_masks(grad)
            dos[0, rows, :] = d0.astype(BF16)
            dos[1, rows, :] = d1.astype(BF16)
            prod = jnp.transpose(grad * o_ref[p, rows, :].astype(F32))
            delta[0:1, rows] = jnp.sum(prod[:HEAD], axis=0, keepdims=True)
            delta[1:2, rows] = jnp.sum(prod[HEAD:], axis=0, keepdims=True)
        for qb in range(blocks):
            cols = block_rows(qb)
            for kb in range(qb + 1):
                rows = block_rows(kb)
                value = qkv_ref[p, rows, 2 * LANES :]
                for h in range(2):
                    scores = dot(ks[rows, :], qs[h, cols, :], 1, 1) + bias[rows, cols]
                    probs = jnp.exp(scores - lse_ref[p, h : h + 1, cols])
                    grads = dot(value, dos[h, cols, :], 1, 1)
                    dscores = (probs * (grads - delta[h : h + 1, cols])).astype(BF16)
                    dv[rows, :] += dot(probs.astype(BF16), dos[h, cols, :], 1, 0)
                    dk[rows, :] += dot(dscores, qs[h, cols, :], 1, 0)
                    dq[cols, :] += dot(dscores, kms[h, rows, :], 0, 0)
        for qb in range(blocks):
            rows = block_rows(qb)
            grad = dq[rows, :] * (HEAD**-0.5)
            made[p, 0, rows, :] = rotated_back(grad, tab_ref, 0, rows).astype(BF16)
            made[p, 1, rows, :] = rotated_back(dk[rows, :], tab_ref, 2, rows).astype(BF16)
            made[p, 2, rows, :] = dv[rows, :].astype(BF16)
        for k in range(1, count):
            back(p, k).start()
        for i in range(3):
            grads_ref[i, spans(row, span), spans(mine * pairs + p, LANES)] = made[
                p, i, spans(me, span), :
            ]
        return carry

    lax.fori_loop(0, pairs, attend, 0)

    def drain(p, carry):
        for k in range(1, count):
            there(p, k).wait_send()
            back(p, k).wait()
        return carry

    lax.fori_loop(0, pairs, drain, 0)


def attend_back(do, qkv, o, lse, tables, seg_col, seg_row, count, groups, collective_id):
    tokens, head_width = do.shape
    pairs, length = qkv.shape[:2]
    whole = pl.BlockSpec(memory_space=pltpu.VMEM)
    return pl.pallas_call(
        functools.partial(back_kernel, count, groups),
        out_shape=jax.ShapeDtypeStruct((3, tokens, head_width), BF16),
        in_specs=[whole] * 7,
        out_specs=whole,
        scratch_shapes=[
            pltpu.VMEM((pairs, length, LANES), BF16),
            pltpu.VMEM((pairs, 3, length, LANES), BF16),
            pltpu.VMEM((length, length), F32),
            pltpu.VMEM((2, length, LANES), BF16),
            pltpu.VMEM((length, LANES), BF16),
            pltpu.VMEM((2, length, LANES), BF16),
            pltpu.VMEM((2, length, LANES), BF16),
            pltpu.VMEM((8, length), F32),
            pltpu.VMEM((length, LANES), F32),
            pltpu.VMEM((length, LANES), F32),
            pltpu.VMEM((length, LANES), F32),
        ]
        + [pltpu.SemaphoreType.DMA((pairs, count))] * 4,
        compiler_params=pltpu.CompilerParams(
            collective_id=collective_id, has_side_effects=True, vmem_limit_bytes=VMEM_LIMIT
        ),
        cost_estimate=cost(60),
    )(do, qkv, o, lse, tables, seg_col, seg_row)


def fold(values):
    rows, width = values.shape
    return jnp.sum(values.reshape(rows // 8, 8, width), axis=0)


def finish_middle(total, here, own, held, vecs, outs):
    middle = held["block"][here, :].astype(F32) + total
    outs[0][own, :] = middle
    normed, _ = norm_parts(middle)
    return normed * vecs[0][...] + vecs[1][...]


def norm_back(base, values, total, vecs, sums):
    normed, inverse = norm_parts(values)
    scaled = total * vecs[0][...]
    grad = base + inverse * (
        scaled
        - jnp.mean(scaled, axis=-1, keepdims=True)
        - normed * jnp.mean(scaled * normed, axis=-1, keepdims=True)
    )
    sums[0] += fold(total * normed)
    sums[1] += fold(total)
    return grad


def finish_second(total, here, own, held, vecs, outs):
    base = held["cotangent"][here, :].astype(F32)
    grad = norm_back(base, held["middle"][own, :], total, vecs, outs[0])
    outs[1][own, :] = grad
    return grad


def finish_first(total, here, own, held, vecs, outs):
    values = held["block"][here, :].astype(F32)
    return norm_back(held["middle_grad"][own, :], values, total, vecs, outs[0])


def line_kernel(plan, count, chunks, slack, *refs):
    finish, clear = plan["finish"], plan["clear"]
    names, parts, tasks = plan["names"], plan["parts"], plan["tasks"]
    num_vec, num_own, num_task = plan["vecs"], plan["owns"], len(tasks)
    refs = list(refs)

    def take(number):
        taken = refs[:number]
        del refs[:number]
        return taken

    sources = take(len(names))
    vecs = take(num_vec)
    (out_ref,) = take(1)
    outs = take(num_own)
    task_outs = take(num_task)
    held = dict(zip(names, take(len(names))))
    in_a, in_b, part, turned, stage = take(5)
    load_sem, stage_sem = take(2)
    (rsa_s, rsa_r, rsb_s, rsb_r, aga_s, aga_r, agb_s, agb_r) = refs
    z = lax.axis_index("tp")
    tokens, width = out_ref.shape
    half = tokens // 2
    size = half // chunks
    ahead = slack * (count - 1)
    steps = chunks + 2 * ahead
    from_first, from_last = slack * z, slack * (count - 1 - z)
    first, last = z == 0, z == count - 1
    up = jnp.minimum(z + 1, count - 1)
    down = jnp.maximum(z - 1, 0)

    loads = {
        name: pltpu.make_async_copy(source, held[name], load_sem.at[i])
        for i, (name, source) in enumerate(zip(names, sources))
    }
    for name in names:
        loads[name].start()

    barrier = pltpu.get_barrier_semaphore()

    @pl.when(jnp.logical_not(last))
    def _():
        pl.semaphore_signal(barrier, inc=1, device_id={"tp": up}, device_id_type=MESH)

    @pl.when(jnp.logical_not(first))
    def _():
        pl.semaphore_signal(barrier, inc=1, device_id={"tp": down}, device_id_type=MESH)

    @pl.when(first | last)
    def _():
        pl.semaphore_wait(barrier, 1)

    @pl.when(jnp.logical_not(first | last))
    def _():
        pl.semaphore_wait(barrier, 2)

    if clear:
        outs[0][...] = jnp.zeros_like(outs[0])

    def own_rows(c):
        return pl.ds(pl.multiple_of(c * size, size), size)

    def a_rows(c):
        return own_rows(c)

    def b_rows(c):
        return pl.ds(pl.multiple_of(half + c * size, size), size)

    def hop(source, target, send, recv, c, device):
        return pltpu.make_async_remote_copy(
            src_ref=source,
            dst_ref=target,
            send_sem=send.at[c],
            recv_sem=recv.at[c],
            device_id={"tp": device},
            device_id_type=MESH,
        )

    def gather_a(c):
        rows = out_ref.at[a_rows(c), :]
        return hop(rows, rows, aga_s, aga_r, c, up)

    def gather_b(c):
        rows = out_ref.at[b_rows(c), :]
        return hop(rows, rows, agb_s, agb_r, c, down)

    def reduce_a(c):
        rows = in_a.at[own_rows(c), :]
        return hop(rows, rows, rsa_s, rsa_r, c, down)

    def reduce_b(c):
        rows = in_b.at[own_rows(c), :]
        return hop(rows, rows, rsb_s, rsb_r, c, up)

    def block_start(t, offset):
        return jnp.clip((t - lax.rem(t, GROUP) - offset) * size, 0, half - GROUP * size)

    def reduce_step(t, c, offset, place, rows, landed, move, gather, starts, ends):
        here = rows(c)
        own = own_rows(c)
        row = place * GROUP * size + c * size - block_start(t, offset)
        term_rows = pl.ds(pl.multiple_of(row, size), size)

        @pl.when(starts)
        def _():
            landed[own, :] = part[term_rows, :].astype(BF16)
            move(c).start()

        @pl.when(jnp.logical_not(starts))
        def _():
            move(c).wait_recv()

        @pl.when(jnp.logical_not(starts | ends))
        def _():
            landed[own, :] = (landed[own, :].astype(F32) + part[term_rows, :]).astype(BF16)
            move(c).start()

        @pl.when(ends)
        def _():
            total = landed[own, :].astype(F32) + part[term_rows, :]
            out_ref[here, :] = finish(total, here, own, held, vecs, outs).astype(BF16)
            gather(c).start()

    def gather_step(c, gather, starts, ends):
        @pl.when(jnp.logical_not(starts))
        def _():
            gather(c).wait_recv()

        @pl.when(jnp.logical_not(starts | ends))
        def _():
            gather(c).start()

    def when_chunk(c, work):
        pl.when((c >= 0) & (c < chunks))(lambda: work(c))

    def make_parts(t):
        top = pl.ds(pl.multiple_of(block_start(t, from_last), size), GROUP * size)
        low = pl.ds(pl.multiple_of(half + block_start(t, from_first), size), GROUP * size)

        def columns(n, carry):
            cols = pl.ds(pl.multiple_of(n * TILE, TILE), TILE)
            total = 0.0
            for left, right in parts:
                rows = jnp.concatenate([held[left][top, :], held[left][low, :]], axis=0)
                total = total + dot(rows, held[right][cols, :], 1, 1)
            part[:, cols] = total
            return carry

        lax.fori_loop(0, width // TILE, columns, 0)

    def run_task(index, tile, slot):
        kind, left, right = tasks[index]
        target = task_outs[index]
        wide = target.shape[1]
        rows = pl.ds(pl.multiple_of(tile * ROWS, ROWS), ROWS)
        if kind == "weight":
            depth = tokens
            turned[:, :depth] = jnp.transpose(held[left][:, rows])

        def columns(n, carry):
            cols = pl.ds(pl.multiple_of(n * TILE, TILE), TILE)
            if kind == "weight":
                value = dot(turned[:, :depth], held[right][:, cols], 1, 0)
            elif kind == "rows":
                value = dot(held[left][rows, :], held[right][:, cols], 1, 0)
            else:
                value = dot(held[left][rows, :], held[right][cols, :], 1, 1)
                top = tile * ROWS < half
                mine = (first & top) | (last & jnp.logical_not(top))
                own = pl.multiple_of(lax.rem(tile * ROWS, half), ROWS)
                base = held["middle"][pl.ds(own, ROWS), cols]
                value = value + jnp.where(mine, base, 0.0)
            stage[slot, :, cols] = value.astype(BF16)
            return carry

        lax.fori_loop(0, wide // TILE, columns, 0)
        stage_copy(index, tile, slot).start()

    def stage_copy(index, tile, slot):
        target = task_outs[index]
        rows = pl.ds(pl.multiple_of(tile * ROWS, ROWS), ROWS)
        return pltpu.make_async_copy(
            stage.at[slot, :, : target.shape[1]], target.at[rows, :], stage_sem.at[slot]
        )

    starts_at = [0]
    for index in range(num_task):
        starts_at.append(starts_at[-1] + task_outs[index].shape[0] // ROWS)
    task_total = starts_at[-1]
    per_group = GROUP - 1

    def step(t, carry):
        pl.when(lax.rem(t, GROUP) == 0)(lambda: make_parts(t))
        when_chunk(
            t - from_last,
            lambda c: reduce_step(t, c, from_last, 0, a_rows, in_a, reduce_a, gather_a, last, first),
        )
        when_chunk(
            t - from_first,
            lambda c: reduce_step(t, c, from_first, 1, b_rows, in_b, reduce_b, gather_b, first, last),
        )
        when_chunk(t - ahead - from_first, lambda c: gather_step(c, gather_a, first, last))
        when_chunk(t - ahead - from_last, lambda c: gather_step(c, gather_b, last, first))
        if num_task:
            turn = (t // GROUP) * per_group + lax.rem(t, GROUP) - 1
            free = lax.rem(t, GROUP) != 0
            slot = lax.rem(turn + per_group + 1, 2)

            @pl.when(t == 1)
            def _():
                for name in plan["late"]:
                    loads[name].wait()

            for index in range(num_task):
                low, high = starts_at[index] + 2, min(starts_at[index + 1] + 2, task_total)
                pl.when(free & (turn >= low) & (turn < high))(
                    lambda index=index, low=low: stage_copy(index, turn - low, slot).wait()
                )
            for index in range(num_task):
                low, high = starts_at[index], starts_at[index + 1]
                pl.when(free & (turn >= low) & (turn < high))(
                    lambda index=index, low=low: run_task(index, turn - low, slot)
                )
        return carry

    for name in names:
        if name not in plan["late"]:
            loads[name].wait()
    lax.fori_loop(0, steps, step, 0)
    if num_task:
        assert task_total >= 2 and (steps // GROUP) * per_group >= task_total
        for turn in (task_total - 2, task_total - 1):
            index = max(i for i in range(num_task) if starts_at[i] <= turn)
            stage_copy(index, turn - starts_at[index], turn % 2).wait()

    def drain(c, carry):
        @pl.when(jnp.logical_not(first))
        def _():
            reduce_a(c).wait_send()
            gather_b(c).wait_send()

        @pl.when(jnp.logical_not(last))
        def _():
            reduce_b(c).wait_send()
            gather_a(c).wait_send()

        return carry

    lax.fori_loop(0, chunks, drain, 0)


def line_sum(finish, count, held, vecs, parts, late, tasks, own_shapes, clear, collective_id):
    names = list(held)
    tokens = held[parts[0][0]].shape[0]
    width = held[parts[0][1]].shape[0]
    half = tokens // 2
    plan = dict(
        finish=finish,
        clear=clear,
        names=names,
        parts=parts,
        late=late,
        tasks=[task[:3] for task in tasks],
        vecs=len(vecs),
        owns=len(own_shapes),
    )
    whole = pl.BlockSpec(memory_space=pltpu.VMEM)
    any_space = pl.BlockSpec(memory_space=pl.ANY)
    depth = tokens if any(task[0] == "weight" for task in tasks) else LANES
    stage_width = max([task[3][1] for task in tasks] + [LANES])
    return pl.pallas_call(
        functools.partial(line_kernel, plan, count, CHUNKS, SLACK),
        out_shape=[jax.ShapeDtypeStruct((tokens, width), BF16)]
        + own_shapes
        + [jax.ShapeDtypeStruct(task[3], BF16) for task in tasks],
        in_specs=[any_space] * len(names) + [whole] * len(vecs),
        out_specs=[whole] * (1 + len(own_shapes)) + [any_space] * len(tasks),
        scratch_shapes=[pltpu.VMEM(array.shape, array.dtype) for array in held.values()]
        + [pltpu.VMEM((half, width), BF16)] * 2
        + [
            pltpu.VMEM((2 * GROUP * half // CHUNKS, width), F32),
            pltpu.VMEM((ROWS, depth), BF16),
            pltpu.VMEM((2, ROWS if tasks else 16, stage_width), BF16),
            pltpu.SemaphoreType.DMA((len(names),)),
            pltpu.SemaphoreType.DMA((2,)),
        ]
        + [pltpu.SemaphoreType.DMA((CHUNKS,))] * 8,
        compiler_params=pltpu.CompilerParams(
            collective_id=collective_id, has_side_effects=True, vmem_limit_bytes=VMEM_LIMIT
        ),
        cost_estimate=cost(110),
    )(*held.values(), *vecs)


def axis_barrier(counts):
    barrier = pltpu.get_barrier_semaphore()
    for axis, count in counts:
        me = lax.axis_index(axis)
        for k in range(1, count):
            pl.semaphore_signal(
                barrier, inc=1, device_id={axis: lax.rem(me + k, count)}, device_id_type=MESH
            )
    pl.semaphore_wait(barrier, sum(count - 1 for _, count in counts))


def share(axis, count, pick, landed, send_sem, recv_sem):
    me = lax.axis_index(axis)
    copies = []
    for k in range(1, count):
        device = lax.rem(me + k, count)
        copy = pltpu.make_async_remote_copy(
            src_ref=pick(device),
            dst_ref=landed.at[me],
            send_sem=send_sem.at[k],
            recv_sem=recv_sem.at[k],
            device_id={axis: device},
            device_id_type=MESH,
        )
        copy.start()
        copies.append(copy)
    return copies


def total_of(landed, count):
    total = landed[0]
    for k in range(1, count):
        total = total + landed[k]
    return total


def tp_sum_kernel(count, x_ref, out_ref, landed, send_sem, recv_sem):
    axis_barrier([("tp", count)])
    copies = share("tp", count, lambda d: x_ref, landed, send_sem, recv_sem)
    landed[lax.axis_index("tp")] = x_ref[...]
    for copy in copies:
        copy.wait()
    out_ref[...] = total_of(landed, count)


def tp_sum(values, count, collective_id):
    whole = pl.BlockSpec(memory_space=pltpu.VMEM)
    return pl.pallas_call(
        functools.partial(tp_sum_kernel, count),
        out_shape=jax.ShapeDtypeStruct(values.shape, F32),
        in_specs=[whole],
        out_specs=whole,
        scratch_shapes=[
            pltpu.VMEM((count,) + values.shape, F32),
            pltpu.SemaphoreType.DMA((count,)),
            pltpu.SemaphoreType.DMA((count,)),
        ],
        compiler_params=pltpu.CompilerParams(collective_id=collective_id, has_side_effects=True),
        cost_estimate=cost(5),
    )(values)


def norm_sum_kernel(
    seq_count, tp_count, full_ref, split_ref, own_ref, sum_ref,
    tp_landed, summed, own_landed, split_landed, sem_a, sem_b, sem_c, sem_d, sem_e, sem_f,
):
    me = lax.axis_index("seq")
    axis_barrier([("seq", seq_count), ("tp", tp_count)])
    tp_copies = share("tp", tp_count, lambda d: full_ref, tp_landed, sem_a, sem_b)
    split_copies = share("seq", seq_count, lambda d: split_ref, split_landed, sem_c, sem_d)
    tp_landed[lax.axis_index("tp")] = full_ref[...]
    split_landed[me] = split_ref[...]
    for copy in tp_copies:
        copy.wait()
    summed[...] = total_of(tp_landed, tp_count)
    own_copies = share("seq", seq_count, lambda d: summed.at[d], own_landed, sem_e, sem_f)
    own_landed[me] = summed[me]
    for copy in split_copies:
        copy.wait()
    sum_ref[...] = total_of(split_landed, seq_count)
    for copy in own_copies:
        copy.wait()
    own_ref[...] = total_of(own_landed, seq_count)


def norm_sum(full, split, seq_count, tp_count, collective_id):
    whole = pl.BlockSpec(memory_space=pltpu.VMEM)
    piece = full.shape[1:]
    return pl.pallas_call(
        functools.partial(norm_sum_kernel, seq_count, tp_count),
        out_shape=[
            jax.ShapeDtypeStruct(piece, F32),
            jax.ShapeDtypeStruct(split.shape, F32),
        ],
        in_specs=[whole] * 2,
        out_specs=[whole] * 2,
        scratch_shapes=[
            pltpu.VMEM((tp_count,) + full.shape, F32),
            pltpu.VMEM(full.shape, F32),
            pltpu.VMEM((seq_count,) + piece, F32),
            pltpu.VMEM((seq_count,) + split.shape, F32),
            pltpu.SemaphoreType.DMA((tp_count,)),
            pltpu.SemaphoreType.DMA((tp_count,)),
        ]
        + [pltpu.SemaphoreType.DMA((seq_count,))] * 4,
        compiler_params=pltpu.CompilerParams(collective_id=collective_id, has_side_effects=True),
        cost_estimate=cost(10),
    )(full, split)


def matmul(left, right, left_dim, right_dim, kind=F32):
    return dot(left, right, left_dim, right_dim).astype(kind)


def rotation_tables(positions):
    half_size = HEAD // 2
    index_pairs = jnp.arange(half_size, dtype=F32)
    theta_rate = jnp.exp(-2.0 * index_pairs / HEAD * jnp.log(10000.0))
    zeta_base = (2.0 * index_pairs + 0.4 * HEAD) / (1.4 * HEAD)
    place_float = positions.astype(F32)[..., None]
    angles = place_float * theta_rate
    power = jnp.log(zeta_base) * place_float / 512.0
    cos_part, sin_part = jnp.cos(angles), jnp.sin(angles)
    grow, shrink = jnp.exp(power), jnp.exp(-power)
    cos_full = jnp.concatenate([cos_part] * 4, axis=-1)
    sin_full = jnp.concatenate([-sin_part, sin_part] * 2, axis=-1)
    grow = jnp.concatenate([grow] * 4, axis=-1)
    shrink = jnp.concatenate([shrink] * 4, axis=-1)
    return jnp.stack([cos_full * grow, sin_full * grow, cos_full * shrink, sin_full * shrink])


def body(
    seq_count,
    tp_count,
    block_in,
    segment_ids,
    first_gain,
    first_bias,
    w_query,
    w_key,
    w_value,
    head_gain,
    head_bias,
    w_out,
    second_gain,
    second_bias,
    w_up,
    hidden_gain,
    hidden_bias,
    w_down,
    out_cotangent,
):
    seq_index = lax.axis_index("seq")
    row_count, span, model_width = block_in.shape
    length = span * seq_count
    tokens = row_count * span
    head_width = w_query.shape[1]
    hidden_width = w_up.shape[1] * tp_count
    groups = seq_count // row_count

    first_gain_f = first_gain.astype(F32)[None]
    first_bias_f = first_bias.astype(F32)[None]
    second_gain_f = second_gain.astype(F32)[None]
    second_bias_f = second_bias.astype(F32)[None]
    head_gain_f = head_gain.astype(F32)[None]
    head_bias_f = head_bias.astype(F32)[None]
    hidden_gain_f = hidden_gain.astype(F32)[None]
    hidden_bias_f = hidden_bias.astype(F32)[None]

    seg_row = lax.dynamic_slice_in_dim(segment_ids, seq_index // groups, 1, 0)
    seg_col = seg_row.reshape(length, 1)
    earlier = jnp.sum((seg_row < seg_col).astype(jnp.int32), axis=-1)
    tables = rotation_tables(jnp.arange(length, dtype=jnp.int32) - earlier)

    block = block_in.reshape(tokens, model_width)
    cotangent = out_cotangent.reshape(tokens, model_width)

    first_act, qkv_row, o_row, lse, mixed = front(
        block,
        w_query,
        w_key,
        w_value,
        first_gain_f,
        first_bias_f,
        tables,
        seg_col,
        seg_row,
        seq_count,
        groups,
        1,
    )
    mixed = mixed.astype(F32)
    head_sums = tp_sum(
        jnp.stack([jnp.sum(mixed, axis=-1), jnp.sum(mixed * mixed, axis=-1)]), tp_count, 9
    )
    head_center = head_sums[0][:, None] / model_width
    head_inverse = lax.rsqrt(
        head_sums[1][:, None] / model_width - head_center * head_center + EPSILON
    )
    head_normed = (mixed - head_center) * head_inverse
    head_act = (head_normed * head_gain_f + head_bias_f).astype(BF16)
    own_shape = jax.ShapeDtypeStruct((tokens // 2, model_width), F32)
    sums_shape = jax.ShapeDtypeStruct((2, 8, model_width), F32)
    hidden_size = hidden_gain.shape[0]
    second_act, middle_own, grad_hidden_act = line_sum(
        finish_middle,
        tp_count,
        dict(head_act=head_act, w_out=w_out, block=block, cotangent=cotangent, w_down=w_down),
        (second_gain_f, second_bias_f),
        [("head_act", "w_out")],
        ("cotangent", "w_down"),
        [("rows", "cotangent", "w_down", (tokens, hidden_size))],
        [own_shape],
        False,
        3,
    )
    grad_hidden_act = grad_hidden_act.astype(F32)

    up_pre = matmul(second_act, w_up, 1, 0)
    cdf = 0.5 * lax.erfc(up_pre * (-(0.5**0.5)))
    gelu_out = up_pre * cdf
    hidden_scaled = grad_hidden_act * hidden_gain_f
    stats = tp_sum(
        jnp.stack(
            [
                jnp.sum(gelu_out, axis=-1),
                jnp.sum(gelu_out * gelu_out, axis=-1),
                jnp.sum(hidden_scaled, axis=-1),
                jnp.sum(hidden_scaled * gelu_out, axis=-1),
            ]
        ),
        tp_count,
        10,
    )
    stats = stats[:, :, None] / hidden_width
    hidden_center = stats[0]
    hidden_inverse = lax.rsqrt(stats[1] - hidden_center * hidden_center + EPSILON)
    hidden_normed = (gelu_out - hidden_center) * hidden_inverse
    hidden_act = (hidden_normed * hidden_gain_f + hidden_bias_f).astype(BF16)
    hidden_gain_grad = jnp.sum(grad_hidden_act * hidden_normed, axis=0)
    hidden_bias_grad = jnp.sum(grad_hidden_act, axis=0)
    hidden_cross = hidden_inverse * (stats[3] - hidden_center * stats[2])
    grad_gelu = hidden_inverse * (hidden_scaled - stats[2] - hidden_normed * hidden_cross)
    pdf = jnp.exp(-0.5 * up_pre * up_pre) * (1.0 / math.sqrt(2.0 * math.pi))
    grad_up = (grad_gelu * (cdf + up_pre * pdf)).astype(BF16)

    weight_shape = (model_width, hidden_size)
    grad_middle_low, second_sums, grad_middle_own, down_part, w_down_terms, w_up_terms = line_sum(
        finish_second,
        tp_count,
        dict(
            grad_up=grad_up,
            w_up=w_up,
            cotangent=cotangent,
            middle=middle_own,
            hidden_act=hidden_act,
            w_down=w_down,
            second_act=second_act,
        ),
        (second_gain_f,),
        [("grad_up", "w_up")],
        ("hidden_act", "w_down", "second_act"),
        [
            ("down", "hidden_act", "w_down", (tokens, model_width)),
            ("weight", "cotangent", "hidden_act", weight_shape),
            ("weight", "second_act", "grad_up", weight_shape),
        ],
        [sums_shape, own_shape],
        True,
        4,
    )
    block_out = lax.psum(down_part, "tp")

    def scatter(grad):
        return lax.psum_scatter(grad, "seq", scatter_dimension=0, tiled=True)

    w_down_grad = scatter(w_down_terms)
    w_up_grad = scatter(w_up_terms)

    grad_head_act = matmul(grad_middle_low, w_out, 1, 0)
    head_gain_grad = jnp.sum(grad_head_act * head_normed, axis=0)
    head_bias_grad = jnp.sum(grad_head_act, axis=0)
    head_scaled = grad_head_act * head_gain_f
    head_back = tp_sum(
        jnp.stack([jnp.sum(head_scaled, axis=-1), jnp.sum(head_scaled * head_normed, axis=-1)]),
        tp_count,
        11,
    )
    head_back = head_back[:, :, None] / model_width
    grad_mixed = head_inverse * (head_scaled - head_back[0] - head_normed * head_back[1])
    grads = attend_back(
        grad_mixed.astype(BF16), qkv_row, o_row, lse, tables, seg_col, seg_row, seq_count, groups, 6
    )
    grad_query, grad_key, grad_value = grads[0], grads[1], grads[2]
    head_terms = (
        jnp.concatenate(
            [
                matmul(first_act, grad_query, 0, 0, BF16),
                matmul(first_act, grad_key, 0, 0, BF16),
                matmul(first_act, grad_value, 0, 0, BF16),
                matmul(grad_middle_low, head_act, 0, 0, BF16),
            ],
            axis=1,
        )
    )
    grad_query, head_terms, w_down_grad = lax.optimization_barrier(
        (grad_query, head_terms, w_down_grad)
    )
    head_grads = scatter(head_terms)
    w_query_grad, w_key_grad, w_value_grad, w_out_grad = jnp.split(
        head_grads.astype(F32), 4, axis=1
    )
    input_grad, first_sums = line_sum(
        finish_first,
        tp_count,
        dict(
            grad_query=grad_query,
            w_query=w_query,
            grad_key=grad_key,
            w_key=w_key,
            grad_value=grad_value,
            w_value=w_value,
            block=block,
            middle_grad=grad_middle_own,
        ),
        (first_gain_f,),
        [("grad_query", "w_query"), ("grad_key", "w_key"), ("grad_value", "w_value")],
        (),
        [],
        [sums_shape],
        True,
        8,
    )

    own_width = model_width // seq_count
    full = jnp.concatenate([jnp.sum(second_sums, axis=1), jnp.sum(first_sums, axis=1)])
    full = full.reshape(4, seq_count, own_width).transpose(1, 0, 2)
    full = full.reshape(seq_count, 4 * own_width // LANES, LANES)
    split = jnp.concatenate([hidden_gain_grad, hidden_bias_grad, head_gain_grad, head_bias_grad])
    norm_own, split = norm_sum(
        full, split.reshape(split.shape[0] // LANES, LANES), seq_count, tp_count, 12
    )
    norm_own = norm_own.reshape(4, own_width)
    split = split.reshape(-1)
    split_sums = (
        split[2 * hidden_size : 2 * hidden_size + head_width],
        split[2 * hidden_size + head_width :],
        split[:hidden_size],
        split[hidden_size : 2 * hidden_size],
    )
    return (
        block_out.reshape(block_in.shape),
        input_grad.reshape(block_in.shape),
        norm_own[2],
        norm_own[3],
        w_query_grad,
        w_key_grad,
        w_value_grad,
        split_sums[0],
        split_sums[1],
        w_out_grad,
        norm_own[0],
        norm_own[1],
        w_up_grad.astype(F32),
        split_sums[2],
        split_sums[3],
        w_down_grad.astype(F32),
    )


def solution(mesh):
    return jax.shard_map(
        functools.partial(body, mesh.shape["seq"], mesh.shape["tp"]),
        mesh=mesh,
        in_specs=(
            P(None, "seq", None),
            P(),
            P(),
            P(),
            P(None, "tp"),
            P(None, "tp"),
            P(None, "tp"),
            P("tp"),
            P("tp"),
            P(None, "tp"),
            P(),
            P(),
            P(None, "tp"),
            P("tp"),
            P("tp"),
            P(None, "tp"),
            P(None, "seq", None),
        ),
        out_specs=(
            P(None, "seq", None),
            P(None, "seq", None),
            P("seq"),
            P("seq"),
            P("seq", "tp"),
            P("seq", "tp"),
            P("seq", "tp"),
            P("tp"),
            P("tp"),
            P("seq", "tp"),
            P("seq"),
            P("seq"),
            P("seq", "tp"),
            P("tp"),
            P("tp"),
            P("seq", "tp"),
        ),
        check_vma=False,
    )
```

```python
import functools
import math

import jax
import jax.numpy as jnp
from jax import lax
from jax.experimental import pallas as pl
from jax.experimental.pallas import tpu as pltpu
from jax.sharding import PartitionSpec as P

HEAD = 64
LANES = 128
BLOCK = 256
EPSILON = 1e-05
MASKED = -1e30
MESH = pl.DeviceIdType.MESH
F32 = jnp.float32
BF16 = jnp.bfloat16
CHUNKS = 16
SLACK = 2
GROUP = 4
ROWS = 256
TILE = 512
VMEM_LIMIT = 60 * 1024 * 1024


def cost(micros):
    return pl.CostEstimate(flops=int(micros * 1.1e9), bytes_accessed=0, transcendentals=0)


def dot(left, right, left_dim, right_dim):
    return lax.dot_general(
        left, right, (((left_dim,), (right_dim,)), ((), ())), preferred_element_type=F32
    )


def seq_signal(count):
    me = lax.axis_index("seq")
    barrier = pltpu.get_barrier_semaphore()
    for k in range(1, count):
        pl.semaphore_signal(
            barrier, inc=1, device_id={"seq": lax.rem(me + k, count)}, device_id_type=MESH
        )


def seq_wait(count):
    pl.semaphore_wait(pltpu.get_barrier_semaphore(), count - 1)


def send(source, target, send_sem, recv_sem, device):
    return pltpu.make_async_remote_copy(
        src_ref=source,
        dst_ref=target,
        send_sem=send_sem,
        recv_sem=recv_sem,
        device_id={"seq": device},
        device_id_type=MESH,
    )


def spans(index, span):
    return pl.ds(pl.multiple_of(index * span, LANES), span)


def swap_halves(values):
    lane = lax.broadcasted_iota(jnp.int32, values.shape, 1)
    return jnp.where(
        lane % HEAD < HEAD // 2,
        pltpu.roll(values, LANES - HEAD // 2, 1),
        pltpu.roll(values, HEAD // 2, 1),
    )


def head_masks(values):
    lane = lax.broadcasted_iota(jnp.int32, values.shape, 1)
    zero = jnp.zeros_like(values)
    return jnp.where(lane < HEAD, values, zero), jnp.where(lane < HEAD, zero, values)


def block_rows(index):
    return slice(index * BLOCK, (index + 1) * BLOCK)


def rotated(values, tables, first, rows):
    values = values.astype(F32)
    return values * tables[first, rows, :] + swap_halves(values) * tables[first + 1, rows, :]


def rotated_back(values, tables, first, rows):
    return values * tables[first, rows, :] - swap_halves(values) * tables[first + 1, rows, :]


def norm_parts(values):
    center = jnp.mean(values, axis=-1, keepdims=True)
    shifted = values - center
    inverse = lax.rsqrt(jnp.mean(shifted * shifted, axis=-1, keepdims=True) + EPSILON)
    return shifted * inverse, inverse


def front_kernel(
    count, groups, x_ref, wq_ref, wk_ref, wv_ref, gains_ref, tab_ref, segc_ref, segr_ref,
    act_ref, qkv_ref, o_ref, lse_ref, mixed_ref,
    weights, staged, bias, qs, ks, load_sem, send_sem, recv_sem, back_send_sem, back_recv_sem,
):
    me = lax.axis_index("seq")
    pairs, length = qkv_ref.shape[:2]
    tokens = x_ref.shape[0]
    span = length // count
    blocks = length // BLOCK
    mine, row = lax.rem(me, groups), me // groups
    seq_signal(count)
    loads = []
    for j in range(pairs * groups):
        for i, source in enumerate((wq_ref, wk_ref, wv_ref)):
            copy = pltpu.make_async_copy(
                source.at[:, j * LANES : (j + 1) * LANES],
                weights.at[j, :, i * LANES : (i + 1) * LANES],
                load_sem.at[3 * j + i],
            )
            copy.start()
            loads.append(copy)

    def norm_step(r, carry):
        rows = pl.ds(pl.multiple_of(r * LANES, LANES), LANES)
        normed, _ = norm_parts(x_ref[rows, :].astype(F32))
        act_ref[rows, :] = (normed * gains_ref[0:1] + gains_ref[1:2]).astype(BF16)
        return carry

    lax.fori_loop(0, tokens // LANES, norm_step, 0)
    for copy in loads:
        copy.wait()

    def there(p, k):
        device = lax.rem(me + k, count)
        return send(
            staged.at[lax.rem(device, groups) * pairs + p, spans(device // groups, span), :],
            qkv_ref.at[p, spans(me, span), :],
            send_sem.at[p, k],
            recv_sem.at[p, k],
            device,
        )

    def back(p, k):
        device = lax.rem(me + k, count)
        return send(
            o_ref.at[p, spans(device, span), :],
            mixed_ref.at[spans(row, span), spans(mine * pairs + p, LANES)],
            back_send_sem.at[p, k],
            back_recv_sem.at[p, k],
            device,
        )

    def project(p, carry):
        for group in range(groups):

            def rows_step(r, inner):
                rows = pl.ds(pl.multiple_of(r * BLOCK, BLOCK), BLOCK)
                j = group * pairs + p
                staged[j, rows, :] = dot(act_ref[rows, :], weights[j], 1, 0).astype(BF16)
                return inner

            lax.fori_loop(0, tokens // BLOCK, rows_step, 0)

        @pl.when(p == 0)
        def _():
            seq_wait(count)

        for k in range(1, count):
            there(p, k).start()
        qkv_ref[p, spans(me, span), :] = staged[mine * pairs + p, spans(row, span), :]
        return carry

    lax.fori_loop(0, pairs, project, 0)
    for qb in range(blocks):
        rows = block_rows(qb)
        keys = (qb + 1) * BLOCK
        same = segc_ref[rows, :] == segr_ref[:, :keys]
        query = lax.broadcasted_iota(jnp.int32, (BLOCK, keys), 0) + qb * BLOCK
        key = lax.broadcasted_iota(jnp.int32, (BLOCK, keys), 1)
        bias[rows, :keys] = jnp.where(same & (key <= query), 0.0, MASKED)

    def attend(p, carry):
        for k in range(1, count):
            there(p, k).wait_recv()
        for qb in range(blocks):
            rows = block_rows(qb)
            q = rotated(qkv_ref[p, rows, :LANES], tab_ref, 0, rows) * (HEAD**-0.5)
            q0, q1 = head_masks(q)
            qs[0, rows, :] = q0.astype(BF16)
            qs[1, rows, :] = q1.astype(BF16)
            k = rotated(qkv_ref[p, rows, LANES : 2 * LANES], tab_ref, 2, rows)
            ks[rows, :] = k.astype(BF16)
        for qb in range(blocks):
            rows = block_rows(qb)
            keys = (qb + 1) * BLOCK
            outs = []
            logs = []
            for h in range(2):
                scores = dot(qs[h, rows, :], ks[:keys, :], 1, 1) + bias[rows, :keys]
                top = jnp.max(scores, axis=1, keepdims=True)
                expo = jnp.exp(scores - top)
                total = jnp.sum(expo, axis=1, keepdims=True)
                outs.append(dot(expo.astype(BF16), qkv_ref[p, :keys, 2 * LANES :], 1, 0) / total)
                logs.append(jnp.broadcast_to(top + jnp.log(total), (BLOCK, LANES)))
            lane = lax.broadcasted_iota(jnp.int32, (BLOCK, LANES), 1)
            o_ref[p, rows, :] = jnp.where(lane < HEAD, outs[0], outs[1]).astype(BF16)
            logs_t = jnp.transpose(jnp.where(lane < HEAD, logs[0], logs[1]))
            lse_ref[p, 0:1, rows] = logs_t[0:1]
            lse_ref[p, 1:2, rows] = logs_t[HEAD : HEAD + 1]
        for k in range(1, count):
            back(p, k).start()
        mixed_ref[spans(row, span), spans(mine * pairs + p, LANES)] = o_ref[p, spans(me, span), :]
        return carry

    lax.fori_loop(0, pairs, attend, 0)

    def drain(p, carry):
        for k in range(1, count):
            there(p, k).wait_send()
            back(p, k).wait()
        return carry

    lax.fori_loop(0, pairs, drain, 0)


def front(x, w_query, w_key, w_value, gains, tables, seg_col, seg_row, count, groups, collective_id):
    tokens, model_width = x.shape
    head_width = w_query.shape[1]
    length = seg_col.shape[0]
    pairs = head_width // groups // LANES
    whole = pl.BlockSpec(memory_space=pltpu.VMEM)
    any_space = pl.BlockSpec(memory_space=pl.ANY)
    return pl.pallas_call(
        functools.partial(front_kernel, count, groups),
        out_shape=[
            jax.ShapeDtypeStruct((tokens, model_width), BF16),
            jax.ShapeDtypeStruct((pairs, length, 3 * LANES), BF16),
            jax.ShapeDtypeStruct((pairs, length, LANES), BF16),
            jax.ShapeDtypeStruct((pairs, 8, length), F32),
            jax.ShapeDtypeStruct((tokens, head_width), BF16),
        ],
        in_specs=[whole] + [any_space] * 3 + [whole] * 4,
        out_specs=[whole] * 5,
        scratch_shapes=[
            pltpu.VMEM((pairs * groups, model_width, 3 * LANES), BF16),
            pltpu.VMEM((pairs * groups, tokens, 3 * LANES), BF16),
            pltpu.VMEM((length, length), F32),
            pltpu.VMEM((2, length, LANES), BF16),
            pltpu.VMEM((length, LANES), BF16),
            pltpu.SemaphoreType.DMA((3 * pairs * groups,)),
        ]
        + [pltpu.SemaphoreType.DMA((pairs, count))] * 4,
        compiler_params=pltpu.CompilerParams(
            collective_id=collective_id, has_side_effects=True, vmem_limit_bytes=VMEM_LIMIT
        ),
        cost_estimate=cost(60),
    )(x, w_query, w_key, w_value, gains, tables, seg_col, seg_row)


def back_kernel(
    count, groups, do_ref, qkv_ref, o_ref, lse_ref, tab_ref, segc_ref, segr_ref, grads_ref,
    do_row, made, bias, qs, ks, kms, dos, delta, dq, dk, dv,
    send_sem, recv_sem, back_send_sem, back_recv_sem,
):
    me = lax.axis_index("seq")
    pairs, length = qkv_ref.shape[:2]
    span = length // count
    blocks = length // BLOCK
    mine, row = lax.rem(me, groups), me // groups
    seq_signal(count)

    def there(p, k):
        device = lax.rem(me + k, count)
        return send(
            do_ref.at[spans(device // groups, span), spans(lax.rem(device, groups) * pairs + p, LANES)],
            do_row.at[p, spans(me, span), :],
            send_sem.at[p, k],
            recv_sem.at[p, k],
            device,
        )

    def back(p, k):
        device = lax.rem(me + k, count)
        return send(
            made.at[p, :, spans(device, span), :],
            grads_ref.at[:, spans(row, span), spans(mine * pairs + p, LANES)],
            back_send_sem.at[p, k],
            back_recv_sem.at[p, k],
            device,
        )

    seq_wait(count)

    def share_out(p, carry):
        for k in range(1, count):
            there(p, k).start()
        do_row[p, spans(me, span), :] = do_ref[spans(row, span), spans(mine * pairs + p, LANES)]
        return carry

    lax.fori_loop(0, pairs, share_out, 0)
    for kb in range(blocks):
        rows = block_rows(kb)
        start = kb * BLOCK
        shape = (BLOCK, length - start)
        same = segc_ref[rows, :] == segr_ref[:, start:]
        key = lax.broadcasted_iota(jnp.int32, shape, 0)
        query = lax.broadcasted_iota(jnp.int32, shape, 1)
        bias[rows, start:] = jnp.where(same & (key <= query), 0.0, MASKED)

    def attend(p, carry):
        for qb in range(blocks):
            rows = block_rows(qb)
            q = rotated(qkv_ref[p, rows, :LANES], tab_ref, 0, rows) * (HEAD**-0.5)
            q0, q1 = head_masks(q)
            qs[0, rows, :] = q0.astype(BF16)
            qs[1, rows, :] = q1.astype(BF16)
            k = rotated(qkv_ref[p, rows, LANES : 2 * LANES], tab_ref, 2, rows)
            ks[rows, :] = k.astype(BF16)
            k0, k1 = head_masks(k)
            kms[0, rows, :] = k0.astype(BF16)
            kms[1, rows, :] = k1.astype(BF16)
        dq[...] = jnp.zeros_like(dq)
        dk[...] = jnp.zeros_like(dk)
        dv[...] = jnp.zeros_like(dv)
        for k in range(1, count):
            there(p, k).wait_recv()
        for qb in range(blocks):
            rows = block_rows(qb)
            grad = do_row[p, rows, :].astype(F32)
            d0, d1 = head_masks(grad)
            dos[0, rows, :] = d0.astype(BF16)
            dos[1, rows, :] = d1.astype(BF16)
            prod = jnp.transpose(grad * o_ref[p, rows, :].astype(F32))
            delta[0:1, rows] = jnp.sum(prod[:HEAD], axis=0, keepdims=True)
            delta[1:2, rows] = jnp.sum(prod[HEAD:], axis=0, keepdims=True)
        for qb in range(blocks):
            cols = block_rows(qb)
            for kb in range(qb + 1):
                rows = block_rows(kb)
                value = qkv_ref[p, rows, 2 * LANES :]
                for h in range(2):
                    scores = dot(ks[rows, :], qs[h, cols, :], 1, 1) + bias[rows, cols]
                    probs = jnp.exp(scores - lse_ref[p, h : h + 1, cols])
                    grads = dot(value, dos[h, cols, :], 1, 1)
                    dscores = (probs * (grads - delta[h : h + 1, cols])).astype(BF16)
                    dv[rows, :] += dot(probs.astype(BF16), dos[h, cols, :], 1, 0)
                    dk[rows, :] += dot(dscores, qs[h, cols, :], 1, 0)
                    dq[cols, :] += dot(dscores, kms[h, rows, :], 0, 0)
        for qb in range(blocks):
            rows = block_rows(qb)
            grad = dq[rows, :] * (HEAD**-0.5)
            made[p, 0, rows, :] = rotated_back(grad, tab_ref, 0, rows).astype(BF16)
            made[p, 1, rows, :] = rotated_back(dk[rows, :], tab_ref, 2, rows).astype(BF16)
            made[p, 2, rows, :] = dv[rows, :].astype(BF16)
        for k in range(1, count):
            back(p, k).start()
        for i in range(3):
            grads_ref[i, spans(row, span), spans(mine * pairs + p, LANES)] = made[
                p, i, spans(me, span), :
            ]
        return carry

    lax.fori_loop(0, pairs, attend, 0)

    def drain(p, carry):
        for k in range(1, count):
            there(p, k).wait_send()
            back(p, k).wait()
        return carry

    lax.fori_loop(0, pairs, drain, 0)


def attend_back(do, qkv, o, lse, tables, seg_col, seg_row, count, groups, collective_id):
    tokens, head_width = do.shape
    pairs, length = qkv.shape[:2]
    whole = pl.BlockSpec(memory_space=pltpu.VMEM)
    return pl.pallas_call(
        functools.partial(back_kernel, count, groups),
        out_shape=jax.ShapeDtypeStruct((3, tokens, head_width), BF16),
        in_specs=[whole] * 7,
        out_specs=whole,
        scratch_shapes=[
            pltpu.VMEM((pairs, length, LANES), BF16),
            pltpu.VMEM((pairs, 3, length, LANES), BF16),
            pltpu.VMEM((length, length), F32),
            pltpu.VMEM((2, length, LANES), BF16),
            pltpu.VMEM((length, LANES), BF16),
            pltpu.VMEM((2, length, LANES), BF16),
            pltpu.VMEM((2, length, LANES), BF16),
            pltpu.VMEM((8, length), F32),
            pltpu.VMEM((length, LANES), F32),
            pltpu.VMEM((length, LANES), F32),
            pltpu.VMEM((length, LANES), F32),
        ]
        + [pltpu.SemaphoreType.DMA((pairs, count))] * 4,
        compiler_params=pltpu.CompilerParams(
            collective_id=collective_id, has_side_effects=True, vmem_limit_bytes=VMEM_LIMIT
        ),
        cost_estimate=cost(60),
    )(do, qkv, o, lse, tables, seg_col, seg_row)


def fold(values):
    rows, width = values.shape
    return jnp.sum(values.reshape(rows // 8, 8, width), axis=0)


def finish_middle(total, here, own, env):
    middle = env["block"][here, :].astype(F32) + total
    env["middle"][own, :] = middle
    normed, _ = norm_parts(middle)
    return normed * env["gains"][2:3] + env["gains"][3:4]


def norm_back(base, values, total, gain, sums):
    normed, inverse = norm_parts(values)
    scaled = total * gain
    grad = base + inverse * (
        scaled
        - jnp.mean(scaled, axis=-1, keepdims=True)
        - normed * jnp.mean(scaled * normed, axis=-1, keepdims=True)
    )
    sums[0] += fold(total * normed)
    sums[1] += fold(total)
    return grad


def finish_second(total, here, own, env):
    base = env["cotangent"][here, :].astype(F32)
    grad = norm_back(base, env["middle"][own, :], total, env["gains"][2:3], env["sums"])
    env["middle_grad"][own, :] = grad
    return grad


def finish_first(total, here, own, env):
    values = env["block"][here, :].astype(F32)
    return norm_back(env["middle_grad"][own, :], values, total, env["gains"][0:1], env["sums"])


def to_row(columns):
    lane = lax.broadcasted_iota(jnp.int32, (LANES, LANES), 1)
    packed = jnp.zeros((LANES, LANES), F32)
    for i, column in enumerate(columns):
        packed = jnp.where(lane == i, column, packed)
    return jnp.transpose(packed)[:8]


def to_columns(rows, number):
    packed = jnp.transpose(jnp.concatenate([rows] * (LANES // 8), axis=0))
    return [packed[:, i : i + 1] for i in range(number)]


def row_block(r):
    return pl.ds(pl.multiple_of(r * LANES, LANES), LANES)


def tp_total(part, landed, send_sem, recv_sem, count):
    copies = share("tp", count, lambda d: part, landed, send_sem, recv_sem)
    landed[lax.axis_index("tp")] = part[...]
    for copy in copies:
        copy.wait()
    part[...] = total_of(landed, count)


def norm_heads(env, count, features):
    mixed, act, part = env["mixed"], env["head_act"], env["head_sums"]
    blocks = mixed.shape[0] // LANES

    def sums(r, carry):
        values = mixed[row_block(r), :].astype(F32)
        part[:, row_block(r)] = to_row(
            [
                jnp.sum(values, axis=-1, keepdims=True),
                jnp.sum(values * values, axis=-1, keepdims=True),
            ]
        )
        return carry

    lax.fori_loop(0, blocks, sums, 0)
    tp_total(part, env["head_landed"], env["head_send"], env["head_recv"], count)

    def apply(r, carry):
        first, second = to_columns(part[:, row_block(r)], 2)
        center = first / features
        inverse = lax.rsqrt(second / features - center * center + EPSILON)
        values = (mixed[row_block(r), :].astype(F32) - center) * inverse
        act[row_block(r), :] = (values * env["head_vecs"][0:1] + env["head_vecs"][1:2]).astype(BF16)
        return carry

    lax.fori_loop(0, blocks, apply, 0)


def normal_parts(values):
    size = jnp.abs(values) * (0.5**0.5)
    bell = jnp.exp(-0.5 * values * values)
    t = 1.0 / (1.0 + 0.3275911 * size)
    poly = 1.061405429
    for factor in (-1.453152027, 1.421413741, -0.284496736, 0.254829592):
        poly = poly * t + factor
    tail = 0.5 * poly * t * bell
    return jnp.where(values < 0.0, tail, 1.0 - tail), bell * (1.0 / math.sqrt(2.0 * math.pi))


def hidden_rows(env, rows, row):
    width = env["w_up"].shape[1]
    sums = [jnp.zeros((LANES, 1), F32)] * 4
    for n in range(width // TILE):
        cols = slice(n * TILE, (n + 1) * TILE)
        values = dot(env["out"][rows, :], env["w_up"][:, cols], 1, 0)
        below, density = normal_parts(values)
        active = values * below
        env["hidden_act"][rows, cols] = active.astype(BF16)
        env["grad_up"][rows, cols] = (below + values * density).astype(BF16)
        scaled = env["hidden_grad"][rows, cols].astype(F32) * env["hidden_vecs"][0:1, cols]
        for i, term in enumerate((active, active * active, scaled, scaled * active)):
            sums[i] = sums[i] + jnp.sum(term, axis=-1, keepdims=True)
    env["hidden_sums"][:, row] = to_row(sums)


def norm_hidden(env, count, features):
    act, slope, part = env["hidden_act"], env["grad_up"], env["hidden_sums"]
    tokens, width = act.shape
    tp_total(part, env["hidden_landed"], env["hidden_send"], env["hidden_recv"], count)
    env["hidden_vec_grads"][...] = jnp.zeros_like(env["hidden_vec_grads"])

    def apply(r, carry):
        rows = row_block(r)
        sums = [column / features for column in to_columns(part[:, rows], 4)]
        center = sums[0]
        inverse = lax.rsqrt(sums[1] - center * center + EPSILON)
        cross = inverse * (sums[3] - center * sums[2])
        for n in range(width // TILE):
            cols = slice(n * TILE, (n + 1) * TILE)
            gain = env["hidden_vecs"][0:1, cols]
            normed = (act[rows, cols].astype(F32) - center) * inverse
            grad = env["hidden_grad"][rows, cols].astype(F32)
            back = inverse * (grad * gain - sums[2] - normed * cross)
            slope[rows, cols] = (back * slope[rows, cols].astype(F32)).astype(BF16)
            act[rows, cols] = (normed * gain + env["hidden_vecs"][1:2, cols]).astype(BF16)
            env["hidden_vec_grads"][0, :, cols] += fold(grad * normed)
            env["hidden_vec_grads"][1, :, cols] += fold(grad)
        return carry

    lax.fori_loop(0, tokens // LANES, apply, 0)


def line_kernel(plan, count, chunks, slack, *refs):
    env = dict(zip(plan["order"], refs, strict=True))
    finish, parts, tasks = plan["finish"], plan["parts"], plan["tasks"]
    num_task = len(tasks)
    out_ref, part = env["out"], env["part"]
    in_a, in_b = env["in_a"], env["in_b"]
    rsa_s, rsa_r, rsb_s, rsb_r = (env[name] for name in ("rsa_s", "rsa_r", "rsb_s", "rsb_r"))
    aga_s, aga_r, agb_s, agb_r = (env[name] for name in ("aga_s", "aga_r", "agb_s", "agb_r"))
    z = lax.axis_index("tp")
    tokens, width = out_ref.shape
    half = tokens // 2
    size = half // chunks
    ahead = slack * (count - 1)
    steps = chunks + 2 * ahead
    from_first, from_last = slack * z, slack * (count - 1 - z)
    first, last = z == 0, z == count - 1
    up = jnp.minimum(z + 1, count - 1)
    down = jnp.maximum(z - 1, 0)

    loads = {
        name: pltpu.make_async_copy(env["source " + name], env[name], env["load_sem"].at[i])
        for i, name in enumerate(plan["held"])
    }
    for name in plan["held"]:
        loads[name].start()
    axis_barrier([("tp", count)])
    if "sums" in env:
        env["sums"][...] = jnp.zeros_like(env["sums"])

    def own_rows(c):
        return pl.ds(pl.multiple_of(c * size, size), size)

    def a_rows(c):
        return own_rows(c)

    def b_rows(c):
        return pl.ds(pl.multiple_of(half + c * size, size), size)

    def hop(source, target, send, recv, c, device):
        return pltpu.make_async_remote_copy(
            src_ref=source,
            dst_ref=target,
            send_sem=send.at[c],
            recv_sem=recv.at[c],
            device_id={"tp": device},
            device_id_type=MESH,
        )

    def gather_a(c):
        rows = out_ref.at[a_rows(c), :]
        return hop(rows, rows, aga_s, aga_r, c, up)

    def gather_b(c):
        rows = out_ref.at[b_rows(c), :]
        return hop(rows, rows, agb_s, agb_r, c, down)

    def reduce_a(c):
        rows = in_a.at[own_rows(c), :]
        return hop(rows, rows, rsa_s, rsa_r, c, down)

    def reduce_b(c):
        rows = in_b.at[own_rows(c), :]
        return hop(rows, rows, rsb_s, rsb_r, c, up)

    def block_start(t, offset):
        return jnp.clip((t - lax.rem(t, GROUP) - offset) * size, 0, half - GROUP * size)

    def reduce_step(t, c, offset, place, rows, landed, move, gather, starts, ends):
        here = rows(c)
        own = own_rows(c)
        row = place * GROUP * size + c * size - block_start(t, offset)
        term_rows = pl.ds(pl.multiple_of(row, size), size)

        @pl.when(starts)
        def _():
            landed[own, :] = part[term_rows, :].astype(BF16)
            move(c).start()

        @pl.when(jnp.logical_not(starts))
        def _():
            move(c).wait_recv()

        @pl.when(jnp.logical_not(starts | ends))
        def _():
            landed[own, :] = (landed[own, :].astype(F32) + part[term_rows, :]).astype(BF16)
            move(c).start()

        @pl.when(ends)
        def _():
            total = landed[own, :].astype(F32) + part[term_rows, :]
            out_ref[here, :] = finish(total, here, own, env).astype(BF16)
            gather(c).start()

    def gather_step(c, gather, starts, ends):
        @pl.when(jnp.logical_not(starts))
        def _():
            gather(c).wait_recv()

        @pl.when(jnp.logical_not(starts | ends))
        def _():
            gather(c).start()

    def when_chunk(c, work):
        pl.when((c >= 0) & (c < chunks))(lambda: work(c))

    def make_parts(t):
        top = pl.ds(pl.multiple_of(block_start(t, from_last), size), GROUP * size)
        low = pl.ds(pl.multiple_of(half + block_start(t, from_first), size), GROUP * size)

        def columns(n, carry):
            cols = pl.ds(pl.multiple_of(n * TILE, TILE), TILE)
            total = 0.0
            for left, right in parts:
                rows = jnp.concatenate([env[left][top, :], env[left][low, :]], axis=0)
                total = total + dot(rows, env[right][cols, :], 1, 1)
            part[:, cols] = total
            return carry

        lax.fori_loop(0, width // TILE, columns, 0)

    def run_task(index, tile, slot):
        kind, left, right, name = tasks[index]
        target = env[name]
        rows = pl.ds(pl.multiple_of(tile * ROWS, ROWS), ROWS)
        if kind == "weight":
            env["turned"][...] = jnp.transpose(env[left][:, rows])

        def columns(n, carry):
            cols = pl.ds(pl.multiple_of(n * TILE, TILE), TILE)
            if kind == "weight":
                value = dot(env["turned"][...], env[right][:, cols], 1, 0)
            elif kind == "keep":
                value = dot(env[left][rows, :], env[right][:, cols], 1, 0)
            else:
                value = dot(env[left][rows, :], env[right][cols, :], 1, 1)
                top = tile * ROWS < half
                mine = (first & top) | (last & jnp.logical_not(top))
                own = pl.multiple_of(lax.rem(tile * ROWS, half), ROWS)
                base = env["middle"][pl.ds(own, ROWS), cols]
                value = value + jnp.where(mine, base, 0.0)
            if kind == "keep":
                target[rows, cols] = value.astype(BF16)
            else:
                env["stage"][slot, :, cols] = value.astype(BF16)
            return carry

        lax.fori_loop(0, target.shape[1] // TILE, columns, 0)
        if kind != "keep":
            stage_copy(index, tile, slot).start()

    def stage_copy(index, tile, slot):
        target = env[tasks[index][3]]
        rows = pl.ds(pl.multiple_of(tile * ROWS, ROWS), ROWS)
        return pltpu.make_async_copy(
            env["stage"].at[slot, :, : target.shape[1]], target.at[rows, :], env["stage_sem"].at[slot]
        )

    starts_at = [0]
    for task in tasks:
        starts_at.append(starts_at[-1] + env[task[3]].shape[0] // ROWS)
    task_total = starts_at[-1]
    per_group = GROUP - 1
    staged = any(task[0] != "keep" for task in tasks)

    def step(t, carry):
        pl.when(lax.rem(t, GROUP) == 0)(lambda: make_parts(t))
        when_chunk(
            t - from_last,
            lambda c: reduce_step(t, c, from_last, 0, a_rows, in_a, reduce_a, gather_a, last, first),
        )
        when_chunk(
            t - from_first,
            lambda c: reduce_step(t, c, from_first, 1, b_rows, in_b, reduce_b, gather_b, first, last),
        )
        when_chunk(t - ahead - from_first, lambda c: gather_step(c, gather_a, first, last))
        when_chunk(t - ahead - from_last, lambda c: gather_step(c, gather_b, last, first))
        if num_task:
            turn = (t // GROUP) * per_group + lax.rem(t, GROUP) - 1
            free = lax.rem(t, GROUP) != 0
            slot = lax.rem(turn + per_group + 1, 2)

            @pl.when(t == 1)
            def _():
                for name in plan["late"]:
                    loads[name].wait()

            for index in range(num_task if staged else 0):
                low, high = starts_at[index] + 2, min(starts_at[index + 1] + 2, task_total)
                pl.when(free & (turn >= low) & (turn < high))(
                    lambda index=index, low=low: stage_copy(index, turn - low, slot).wait()
                )
            for index in range(num_task):
                low, high = starts_at[index], starts_at[index + 1]
                pl.when(free & (turn >= low) & (turn < high))(
                    lambda index=index, low=low: run_task(index, turn - low, slot)
                )
        if plan["rows_done"]:
            done_a = t - ahead - from_first - (GROUP - 1)
            done_b = t - ahead - from_last - (GROUP - 1)
            has_a = (done_a >= 0) & (done_a < chunks) & (lax.rem(done_a + 64, GROUP) == 0)
            has_b = (done_b >= 0) & (done_b < chunks) & (lax.rem(done_b + 64, GROUP) == 0)

            @pl.when(has_a | has_b)
            def _():
                start = jnp.where(has_a, done_a * size, half + done_b * size)
                rows = pl.ds(pl.multiple_of(start, LANES), LANES)
                plan["rows_done"](env, rows, rows)

        return carry

    for name in plan["held"]:
        if name not in plan["late"]:
            loads[name].wait()
    if plan["before"]:
        plan["before"](env)
    lax.fori_loop(0, steps, step, 0)
    if num_task:
        assert (steps // GROUP) * per_group >= task_total
    if staged:
        assert task_total >= 2
        for turn in (task_total - 2, task_total - 1):
            index = max(i for i in range(num_task) if starts_at[i] <= turn)
            stage_copy(index, turn - starts_at[index], turn % 2).wait()
    if plan["after"]:
        plan["after"](env)

    def drain(c, carry):
        @pl.when(jnp.logical_not(first))
        def _():
            reduce_a(c).wait_send()
            gather_b(c).wait_send()

        @pl.when(jnp.logical_not(last))
        def _():
            reduce_b(c).wait_send()
            gather_a(c).wait_send()

        return carry

    lax.fori_loop(0, chunks, drain, 0)


def line_sum(
    finish, count, held, vecs, parts, collective_id, *, tokens, late=(), tasks=(), owns=(), sent=(),
    scratch=(), before=None, rows_done=None, after=None, micros=110,
):
    width = held[parts[0][1]].shape[0]
    half = tokens // 2
    depth = tokens if any(task[0] == "weight" for task in tasks) else LANES
    stage_width = max([shape.shape[1] for _, shape in sent] + [LANES])
    fixed = [
        ("in_a", pltpu.VMEM((half, width), BF16)),
        ("in_b", pltpu.VMEM((half, width), BF16)),
        ("part", pltpu.VMEM((2 * GROUP * half // CHUNKS, width), F32)),
        ("turned", pltpu.VMEM((ROWS, depth), BF16)),
        ("stage", pltpu.VMEM((2, ROWS if sent else 16, stage_width), BF16)),
        ("load_sem", pltpu.SemaphoreType.DMA((len(held),))),
        ("stage_sem", pltpu.SemaphoreType.DMA((2,))),
    ] + [
        (name, pltpu.SemaphoreType.DMA((CHUNKS,)))
        for name in ("rsa_s", "rsa_r", "rsb_s", "rsb_r", "aga_s", "aga_r", "agb_s", "agb_r")
    ]
    scratch = list(scratch) + fixed
    order = (
        ["source " + name for name in held]
        + list(vecs)
        + ["out"]
        + [name for name, _ in owns]
        + [name for name, _ in sent]
        + list(held)
        + [name for name, _ in scratch]
    )
    plan = dict(
        finish=finish,
        order=order,
        held=list(held),
        parts=parts,
        late=late,
        tasks=tasks,
        before=before,
        rows_done=rows_done,
        after=after,
    )
    whole = pl.BlockSpec(memory_space=pltpu.VMEM)
    any_space = pl.BlockSpec(memory_space=pl.ANY)
    return pl.pallas_call(
        functools.partial(line_kernel, plan, count, CHUNKS, SLACK),
        out_shape=[jax.ShapeDtypeStruct((tokens, width), BF16)]
        + [shape for _, shape in owns]
        + [shape for _, shape in sent],
        in_specs=[any_space] * len(held) + [whole] * len(vecs),
        out_specs=[whole] * (1 + len(owns)) + [any_space] * len(sent),
        scratch_shapes=[pltpu.VMEM(array.shape, array.dtype) for array in held.values()]
        + [shape for _, shape in scratch],
        compiler_params=pltpu.CompilerParams(
            collective_id=collective_id, has_side_effects=True, vmem_limit_bytes=VMEM_LIMIT
        ),
        cost_estimate=cost(micros),
    )(*held.values(), *vecs.values())


def axis_barrier(counts):
    barrier = pltpu.get_barrier_semaphore()
    for axis, count in counts:
        me = lax.axis_index(axis)
        for k in range(1, count):
            pl.semaphore_signal(
                barrier, inc=1, device_id={axis: lax.rem(me + k, count)}, device_id_type=MESH
            )
    pl.semaphore_wait(barrier, sum(count - 1 for _, count in counts))


def share(axis, count, pick, landed, send_sem, recv_sem):
    me = lax.axis_index(axis)
    copies = []
    for k in range(1, count):
        device = lax.rem(me + k, count)
        copy = pltpu.make_async_remote_copy(
            src_ref=pick(device),
            dst_ref=landed.at[me],
            send_sem=send_sem.at[k],
            recv_sem=recv_sem.at[k],
            device_id={axis: device},
            device_id_type=MESH,
        )
        copy.start()
        copies.append(copy)
    return copies


def total_of(landed, count):
    total = landed[0]
    for k in range(1, count):
        total = total + landed[k]
    return total


def tp_sum_kernel(count, x_ref, out_ref, landed, send_sem, recv_sem):
    axis_barrier([("tp", count)])
    copies = share("tp", count, lambda d: x_ref, landed, send_sem, recv_sem)
    landed[lax.axis_index("tp")] = x_ref[...]
    for copy in copies:
        copy.wait()
    out_ref[...] = total_of(landed, count)


def tp_sum(values, count, collective_id):
    whole = pl.BlockSpec(memory_space=pltpu.VMEM)
    return pl.pallas_call(
        functools.partial(tp_sum_kernel, count),
        out_shape=jax.ShapeDtypeStruct(values.shape, F32),
        in_specs=[whole],
        out_specs=whole,
        scratch_shapes=[
            pltpu.VMEM((count,) + values.shape, F32),
            pltpu.SemaphoreType.DMA((count,)),
            pltpu.SemaphoreType.DMA((count,)),
        ],
        compiler_params=pltpu.CompilerParams(collective_id=collective_id, has_side_effects=True),
        cost_estimate=cost(5),
    )(values)


def norm_sum_kernel(
    seq_count, tp_count, full_ref, split_ref, own_ref, sum_ref,
    tp_landed, summed, own_landed, split_landed, sem_a, sem_b, sem_c, sem_d, sem_e, sem_f,
):
    me = lax.axis_index("seq")
    axis_barrier([("seq", seq_count), ("tp", tp_count)])
    tp_copies = share("tp", tp_count, lambda d: full_ref, tp_landed, sem_a, sem_b)
    split_copies = share("seq", seq_count, lambda d: split_ref, split_landed, sem_c, sem_d)
    tp_landed[lax.axis_index("tp")] = full_ref[...]
    split_landed[me] = split_ref[...]
    for copy in tp_copies:
        copy.wait()
    summed[...] = total_of(tp_landed, tp_count)
    own_copies = share("seq", seq_count, lambda d: summed.at[d], own_landed, sem_e, sem_f)
    own_landed[me] = summed[me]
    for copy in split_copies:
        copy.wait()
    sum_ref[...] = total_of(split_landed, seq_count)
    for copy in own_copies:
        copy.wait()
    own_ref[...] = total_of(own_landed, seq_count)


def norm_sum(full, split, seq_count, tp_count, collective_id):
    whole = pl.BlockSpec(memory_space=pltpu.VMEM)
    piece = full.shape[1:]
    return pl.pallas_call(
        functools.partial(norm_sum_kernel, seq_count, tp_count),
        out_shape=[
            jax.ShapeDtypeStruct(piece, F32),
            jax.ShapeDtypeStruct(split.shape, F32),
        ],
        in_specs=[whole] * 2,
        out_specs=[whole] * 2,
        scratch_shapes=[
            pltpu.VMEM((tp_count,) + full.shape, F32),
            pltpu.VMEM(full.shape, F32),
            pltpu.VMEM((seq_count,) + piece, F32),
            pltpu.VMEM((seq_count,) + split.shape, F32),
            pltpu.SemaphoreType.DMA((tp_count,)),
            pltpu.SemaphoreType.DMA((tp_count,)),
        ]
        + [pltpu.SemaphoreType.DMA((seq_count,))] * 4,
        compiler_params=pltpu.CompilerParams(collective_id=collective_id, has_side_effects=True),
        cost_estimate=cost(10),
    )(full, split)


def matmul(left, right, left_dim, right_dim, kind=F32):
    return dot(left, right, left_dim, right_dim).astype(kind)


def rotation_tables(positions):
    half_size = HEAD // 2
    index_pairs = jnp.arange(half_size, dtype=F32)
    theta_rate = jnp.exp(-2.0 * index_pairs / HEAD * jnp.log(10000.0))
    zeta_base = (2.0 * index_pairs + 0.4 * HEAD) / (1.4 * HEAD)
    place_float = positions.astype(F32)[..., None]
    angles = place_float * theta_rate
    power = jnp.log(zeta_base) * place_float / 512.0
    cos_part, sin_part = jnp.cos(angles), jnp.sin(angles)
    grow, shrink = jnp.exp(power), jnp.exp(-power)
    cos_full = jnp.concatenate([cos_part] * 4, axis=-1)
    sin_full = jnp.concatenate([-sin_part, sin_part] * 2, axis=-1)
    grow = jnp.concatenate([grow] * 4, axis=-1)
    shrink = jnp.concatenate([shrink] * 4, axis=-1)
    return jnp.stack([cos_full * grow, sin_full * grow, cos_full * shrink, sin_full * shrink])


def body(
    seq_count,
    tp_count,
    block_in,
    segment_ids,
    first_gain,
    first_bias,
    w_query,
    w_key,
    w_value,
    head_gain,
    head_bias,
    w_out,
    second_gain,
    second_bias,
    w_up,
    hidden_gain,
    hidden_bias,
    w_down,
    out_cotangent,
):
    seq_index = lax.axis_index("seq")
    row_count, span, model_width = block_in.shape
    length = span * seq_count
    tokens = row_count * span
    head_width = w_query.shape[1]
    hidden_width = w_up.shape[1] * tp_count
    groups = seq_count // row_count

    gains = jnp.stack([first_gain, first_bias, second_gain, second_bias]).astype(F32)
    head_vecs = jnp.stack([head_gain, head_bias]).astype(F32)
    hidden_vecs = jnp.stack([hidden_gain, hidden_bias]).astype(F32)

    seg_row = lax.dynamic_slice_in_dim(segment_ids, seq_index // groups, 1, 0)
    seg_col = seg_row.reshape(length, 1)
    earlier = jnp.sum((seg_row < seg_col).astype(jnp.int32), axis=-1)
    tables = rotation_tables(jnp.arange(length, dtype=jnp.int32) - earlier)

    block = block_in.reshape(tokens, model_width)
    cotangent = out_cotangent.reshape(tokens, model_width)

    first_act, qkv_row, o_row, lse, mixed = front(
        block,
        w_query,
        w_key,
        w_value,
        gains,
        tables,
        seg_col,
        seg_row,
        seq_count,
        groups,
        1,
    )
    def shape_of(dims, kind=F32):
        return jax.ShapeDtypeStruct(dims, kind)

    hidden_size = hidden_gain.shape[0]
    own_shape = shape_of((tokens // 2, model_width))
    sums_shape = shape_of((2, 8, model_width))
    landed = pltpu.VMEM((tp_count, 8, tokens), F32)
    pair_sem = pltpu.SemaphoreType.DMA((tp_count,))
    (
        second_act, middle_own, head_act, head_sums, hidden_act, grad_up, hidden_vec_grads
    ) = line_sum(
        finish_middle,
        tp_count,
        dict(mixed=mixed, w_out=w_out, block=block, cotangent=cotangent, w_down=w_down, w_up=w_up),
        dict(gains=gains, head_vecs=head_vecs, hidden_vecs=hidden_vecs),
        (("head_act", "w_out"),),
        3,
        tokens=tokens,
        late=("cotangent", "w_down", "w_up"),
        tasks=(("keep", "cotangent", "w_down", "hidden_grad"),),
        owns=(
            ("middle", own_shape),
            ("head_act", shape_of((tokens, head_width), BF16)),
            ("head_sums", shape_of((8, tokens))),
            ("hidden_act", shape_of((tokens, hidden_size), BF16)),
            ("grad_up", shape_of((tokens, hidden_size), BF16)),
            ("hidden_vec_grads", shape_of((2, 8, hidden_size))),
        ),
        scratch=(
            ("hidden_grad", pltpu.VMEM((tokens, hidden_size), BF16)),
            ("hidden_sums", pltpu.VMEM((8, tokens), F32)),
            ("head_landed", landed),
            ("hidden_landed", landed),
            ("head_send", pair_sem),
            ("head_recv", pair_sem),
            ("hidden_send", pair_sem),
            ("hidden_recv", pair_sem),
        ),
        before=lambda env: norm_heads(env, tp_count, model_width),
        rows_done=hidden_rows,
        after=lambda env: norm_hidden(env, tp_count, hidden_width),
        micros=140,
    )

    weight_shape = shape_of((model_width, hidden_size), BF16)
    grad_middle_low, second_sums, grad_middle_own, down_part, w_down_terms, w_up_terms = line_sum(
        finish_second,
        tp_count,
        dict(
            grad_up=grad_up,
            w_up=w_up,
            cotangent=cotangent,
            middle=middle_own,
            hidden_act=hidden_act,
            w_down=w_down,
            second_act=second_act,
        ),
        dict(gains=gains),
        (("grad_up", "w_up"),),
        4,
        tokens=tokens,
        late=("hidden_act", "w_down", "second_act"),
        tasks=(
            ("down", "hidden_act", "w_down", "down_part"),
            ("weight", "cotangent", "hidden_act", "w_down_terms"),
            ("weight", "second_act", "grad_up", "w_up_terms"),
        ),
        owns=(("sums", sums_shape), ("middle_grad", own_shape)),
        sent=(
            ("down_part", shape_of((tokens, model_width), BF16)),
            ("w_down_terms", weight_shape),
            ("w_up_terms", weight_shape),
        ),
    )
    block_out = lax.psum(down_part, "tp")

    head_center = head_sums[0][:, None] / model_width
    head_inverse = lax.rsqrt(
        head_sums[1][:, None] / model_width - head_center * head_center + EPSILON
    )
    head_normed = (mixed.astype(F32) - head_center) * head_inverse

    def scatter(grad):
        return lax.psum_scatter(grad, "seq", scatter_dimension=0, tiled=True)

    w_down_grad = scatter(w_down_terms)
    w_up_grad = scatter(w_up_terms)

    grad_head_act = matmul(grad_middle_low, w_out, 1, 0)
    head_gain_grad = jnp.sum(grad_head_act * head_normed, axis=0)
    head_bias_grad = jnp.sum(grad_head_act, axis=0)
    head_scaled = grad_head_act * head_vecs[0:1]
    head_back = tp_sum(
        jnp.stack([jnp.sum(head_scaled, axis=-1), jnp.sum(head_scaled * head_normed, axis=-1)]),
        tp_count,
        11,
    )
    head_back = head_back[:, :, None] / model_width
    grad_mixed = head_inverse * (head_scaled - head_back[0] - head_normed * head_back[1])
    grads = attend_back(
        grad_mixed.astype(BF16), qkv_row, o_row, lse, tables, seg_col, seg_row, seq_count, groups, 6
    )
    grad_query, grad_key, grad_value = grads[0], grads[1], grads[2]
    head_terms = (
        jnp.concatenate(
            [
                matmul(first_act, grad_query, 0, 0, BF16),
                matmul(first_act, grad_key, 0, 0, BF16),
                matmul(first_act, grad_value, 0, 0, BF16),
                matmul(grad_middle_low, head_act, 0, 0, BF16),
            ],
            axis=1,
        )
    )
    grad_query, head_terms, w_down_grad = lax.optimization_barrier(
        (grad_query, head_terms, w_down_grad)
    )
    head_grads = scatter(head_terms)
    w_query_grad, w_key_grad, w_value_grad, w_out_grad = jnp.split(
        head_grads.astype(F32), 4, axis=1
    )
    input_grad, first_sums = line_sum(
        finish_first,
        tp_count,
        dict(
            grad_query=grad_query,
            w_query=w_query,
            grad_key=grad_key,
            w_key=w_key,
            grad_value=grad_value,
            w_value=w_value,
            block=block,
            middle_grad=grad_middle_own,
        ),
        dict(gains=gains),
        (("grad_query", "w_query"), ("grad_key", "w_key"), ("grad_value", "w_value")),
        8,
        tokens=tokens,
        owns=(("sums", sums_shape),),
    )

    own_width = model_width // seq_count
    full = jnp.concatenate([jnp.sum(second_sums, axis=1), jnp.sum(first_sums, axis=1)])
    full = full.reshape(4, seq_count, own_width).transpose(1, 0, 2)
    full = full.reshape(seq_count, 4 * own_width // LANES, LANES)
    hidden_vec_grads = jnp.sum(hidden_vec_grads, axis=1).reshape(-1)
    split = jnp.concatenate([hidden_vec_grads, head_gain_grad, head_bias_grad])
    norm_own, split = norm_sum(
        full, split.reshape(split.shape[0] // LANES, LANES), seq_count, tp_count, 12
    )
    norm_own = norm_own.reshape(4, own_width)
    split = split.reshape(-1)
    split_sums = (
        split[2 * hidden_size : 2 * hidden_size + head_width],
        split[2 * hidden_size + head_width :],
        split[:hidden_size],
        split[hidden_size : 2 * hidden_size],
    )
    return (
        block_out.reshape(block_in.shape),
        input_grad.reshape(block_in.shape),
        norm_own[2],
        norm_own[3],
        w_query_grad,
        w_key_grad,
        w_value_grad,
        split_sums[0],
        split_sums[1],
        w_out_grad,
        norm_own[0],
        norm_own[1],
        w_up_grad.astype(F32),
        split_sums[2],
        split_sums[3],
        w_down_grad.astype(F32),
    )


def solution(mesh):
    return jax.shard_map(
        functools.partial(body, mesh.shape["seq"], mesh.shape["tp"]),
        mesh=mesh,
        in_specs=(
            P(None, "seq", None),
            P(),
            P(),
            P(),
            P(None, "tp"),
            P(None, "tp"),
            P(None, "tp"),
            P("tp"),
            P("tp"),
            P(None, "tp"),
            P(),
            P(),
            P(None, "tp"),
            P("tp"),
            P("tp"),
            P(None, "tp"),
            P(None, "seq", None),
        ),
        out_specs=(
            P(None, "seq", None),
            P(None, "seq", None),
            P("seq"),
            P("seq"),
            P("seq", "tp"),
            P("seq", "tp"),
            P("seq", "tp"),
            P("tp"),
            P("tp"),
            P("seq", "tp"),
            P("seq"),
            P("seq"),
            P("seq", "tp"),
            P("tp"),
            P("tp"),
            P("seq", "tp"),
        ),
        check_vma=False,
    )
```

```python
import functools
import math

import jax
import jax.numpy as jnp
from jax import lax
from jax.experimental import pallas as pl
from jax.experimental.pallas import tpu as pltpu
from jax.sharding import PartitionSpec as P

HEAD = 64
LANES = 128
BLOCK = 256
EPSILON = 1e-05
MASKED = -1e30
MESH = pl.DeviceIdType.MESH
F32 = jnp.float32
BF16 = jnp.bfloat16
CHUNKS = 16
SLACK = 2
GROUP = 4
ROWS = 256
TILE = 512
VMEM_LIMIT = 60 * 1024 * 1024


def cost(micros):
    return pl.CostEstimate(flops=int(micros * 1.1e9), bytes_accessed=0, transcendentals=0)


def dot(left, right, left_dim, right_dim):
    return lax.dot_general(
        left, right, (((left_dim,), (right_dim,)), ((), ())), preferred_element_type=F32
    )


def seq_signal(count):
    me = lax.axis_index("seq")
    barrier = pltpu.get_barrier_semaphore()
    for k in range(1, count):
        pl.semaphore_signal(
            barrier, inc=1, device_id={"seq": lax.rem(me + k, count)}, device_id_type=MESH
        )


def seq_wait(count):
    pl.semaphore_wait(pltpu.get_barrier_semaphore(), count - 1)


def send(source, target, send_sem, recv_sem, device):
    return pltpu.make_async_remote_copy(
        src_ref=source,
        dst_ref=target,
        send_sem=send_sem,
        recv_sem=recv_sem,
        device_id={"seq": device},
        device_id_type=MESH,
    )


def spans(index, span):
    return pl.ds(pl.multiple_of(index * span, LANES), span)


def swap_halves(values):
    lane = lax.broadcasted_iota(jnp.int32, values.shape, 1)
    return jnp.where(
        lane % HEAD < HEAD // 2,
        pltpu.roll(values, LANES - HEAD // 2, 1),
        pltpu.roll(values, HEAD // 2, 1),
    )


def head_masks(values):
    lane = lax.broadcasted_iota(jnp.int32, values.shape, 1)
    zero = jnp.zeros_like(values)
    return jnp.where(lane < HEAD, values, zero), jnp.where(lane < HEAD, zero, values)


def block_rows(index):
    return slice(index * BLOCK, (index + 1) * BLOCK)


def rotated(values, tables, first, rows):
    values = values.astype(F32)
    return values * tables[first, rows, :] + swap_halves(values) * tables[first + 1, rows, :]


def rotated_back(values, tables, first, rows):
    return values * tables[first, rows, :] - swap_halves(values) * tables[first + 1, rows, :]


def norm_parts(values):
    center = jnp.mean(values, axis=-1, keepdims=True)
    shifted = values - center
    inverse = lax.rsqrt(jnp.mean(shifted * shifted, axis=-1, keepdims=True) + EPSILON)
    return shifted * inverse, inverse


def expand_tables(packed, tables):
    quarter = HEAD // 2
    for block in range(packed.shape[0] // BLOCK):
        rows = block_rows(block)
        lane = lax.broadcasted_iota(jnp.int32, (BLOCK, LANES), 1)
        group = lane // quarter
        turns = [packed[rows, :]]
        for k in range(1, 4):
            turns.append(pltpu.roll(turns[0], k * quarter, 1))

        def spread(index):
            values = turns[(0 - index) % 4]
            for g in range(1, 4):
                values = jnp.where(group == g, turns[(g - index) % 4], values)
            return values

        cos_part = spread(0)
        sin_part = spread(1)
        sin_part = jnp.where(lane % HEAD < quarter, -sin_part, sin_part)
        for k in range(2):
            factor = spread(2 + k)
            tables[2 * k, rows, :] = cos_part * factor
            tables[2 * k + 1, rows, :] = sin_part * factor


def front_kernel(
    count, groups, x_ref, wq_ref, wk_ref, wv_ref, vecs_ref, packed_ref, segc_ref, segr_ref,
    act_ref, qkv_ref, o_ref, lse_ref, mixed_ref,
    weights, staged, tab_ref, bias, qs, ks, load_sem, send_sem, recv_sem, back_send_sem, back_recv_sem,
):
    me = lax.axis_index("seq")
    pairs, length = qkv_ref.shape[:2]
    tokens, width = x_ref.shape
    span = length // count
    blocks = length // BLOCK
    mine, row = lax.rem(me, groups), me // groups
    seq_signal(count)
    loads = []
    for j in range(pairs * groups):
        for i, source in enumerate((wq_ref, wk_ref, wv_ref)):
            copy = pltpu.make_async_copy(
                source.at[:, j * LANES : (j + 1) * LANES],
                weights.at[j, :, i * LANES : (i + 1) * LANES],
                load_sem.at[3 * j + i],
            )
            copy.start()
            loads.append(copy)

    def norm_step(r, carry):
        rows = pl.ds(pl.multiple_of(r * LANES, LANES), LANES)
        normed, _ = norm_parts(x_ref[rows, :].astype(F32))
        act_ref[rows, :] = (normed * vecs_ref[:, :width] + vecs_ref[:, width : 2 * width]).astype(BF16)
        return carry

    lax.fori_loop(0, tokens // LANES, norm_step, 0)
    for copy in loads:
        copy.wait()

    def there(p, k):
        device = lax.rem(me + k, count)
        return send(
            staged.at[lax.rem(device, groups) * pairs + p, spans(device // groups, span), :],
            qkv_ref.at[p, spans(me, span), :],
            send_sem.at[p, k],
            recv_sem.at[p, k],
            device,
        )

    def back(p, k):
        device = lax.rem(me + k, count)
        return send(
            o_ref.at[p, spans(device, span), :],
            mixed_ref.at[spans(row, span), spans(mine * pairs + p, LANES)],
            back_send_sem.at[p, k],
            back_recv_sem.at[p, k],
            device,
        )

    def project(p, carry):
        for group in range(groups):

            def rows_step(r, inner):
                rows = pl.ds(pl.multiple_of(r * BLOCK, BLOCK), BLOCK)
                j = group * pairs + p
                staged[j, rows, :] = dot(act_ref[rows, :], weights[j], 1, 0).astype(BF16)
                return inner

            lax.fori_loop(0, tokens // BLOCK, rows_step, 0)

        @pl.when(p == 0)
        def _():
            seq_wait(count)

        for k in range(1, count):
            there(p, k).start()
        qkv_ref[p, spans(me, span), :] = staged[mine * pairs + p, spans(row, span), :]
        return carry

    lax.fori_loop(0, pairs, project, 0)
    expand_tables(packed_ref, tab_ref)
    for qb in range(blocks):
        rows = block_rows(qb)
        keys = (qb + 1) * BLOCK
        same = segc_ref[rows, :] == segr_ref[:, :keys]
        query = lax.broadcasted_iota(jnp.int32, (BLOCK, keys), 0) + qb * BLOCK
        key = lax.broadcasted_iota(jnp.int32, (BLOCK, keys), 1)
        bias[rows, :keys] = jnp.where(same & (key <= query), 0.0, MASKED)

    def attend(p, carry):
        for k in range(1, count):
            there(p, k).wait_recv()
        for qb in range(blocks):
            rows = block_rows(qb)
            q = rotated(qkv_ref[p, rows, :LANES], tab_ref, 0, rows) * (HEAD**-0.5)
            q0, q1 = head_masks(q)
            qs[0, rows, :] = q0.astype(BF16)
            qs[1, rows, :] = q1.astype(BF16)
            k = rotated(qkv_ref[p, rows, LANES : 2 * LANES], tab_ref, 2, rows)
            ks[rows, :] = k.astype(BF16)
        for qb in range(blocks):
            rows = block_rows(qb)
            keys = (qb + 1) * BLOCK
            outs = []
            logs = []
            for h in range(2):
                scores = dot(qs[h, rows, :], ks[:keys, :], 1, 1) + bias[rows, :keys]
                top = jnp.max(scores, axis=1, keepdims=True)
                expo = jnp.exp(scores - top)
                total = jnp.sum(expo, axis=1, keepdims=True)
                outs.append(dot(expo.astype(BF16), qkv_ref[p, :keys, 2 * LANES :], 1, 0) / total)
                logs.append(jnp.broadcast_to(top + jnp.log(total), (BLOCK, LANES)))
            lane = lax.broadcasted_iota(jnp.int32, (BLOCK, LANES), 1)
            o_ref[p, rows, :] = jnp.where(lane < HEAD, outs[0], outs[1]).astype(BF16)
            logs_t = jnp.transpose(jnp.where(lane < HEAD, logs[0], logs[1]))
            lse_ref[p, 0:1, rows] = logs_t[0:1]
            lse_ref[p, 1:2, rows] = logs_t[HEAD : HEAD + 1]
        for k in range(1, count):
            back(p, k).start()
        mixed_ref[spans(row, span), spans(mine * pairs + p, LANES)] = o_ref[p, spans(me, span), :]
        return carry

    lax.fori_loop(0, pairs, attend, 0)

    def drain(p, carry):
        for k in range(1, count):
            there(p, k).wait_send()
            back(p, k).wait()
        return carry

    lax.fori_loop(0, pairs, drain, 0)


def front(x, w_query, w_key, w_value, vecs, tables, seg_col, seg_row, count, groups, collective_id):
    tokens, model_width = x.shape
    head_width = w_query.shape[1]
    length = seg_col.shape[0]
    pairs = head_width // groups // LANES
    whole = pl.BlockSpec(memory_space=pltpu.VMEM)
    any_space = pl.BlockSpec(memory_space=pl.ANY)
    return pl.pallas_call(
        functools.partial(front_kernel, count, groups),
        out_shape=[
            jax.ShapeDtypeStruct((tokens, model_width), BF16),
            jax.ShapeDtypeStruct((pairs, length, 3 * LANES), BF16),
            jax.ShapeDtypeStruct((pairs, length, LANES), BF16),
            jax.ShapeDtypeStruct((pairs, 8, length), F32),
            jax.ShapeDtypeStruct((tokens, head_width), BF16),
        ],
        in_specs=[whole] + [any_space] * 3 + [whole] * 4,
        out_specs=[whole] * 5,
        scratch_shapes=[
            pltpu.VMEM((pairs * groups, model_width, 3 * LANES), BF16),
            pltpu.VMEM((pairs * groups, tokens, 3 * LANES), BF16),
            pltpu.VMEM((4, length, LANES), F32),
            pltpu.VMEM((length, length), F32),
            pltpu.VMEM((2, length, LANES), BF16),
            pltpu.VMEM((length, LANES), BF16),
            pltpu.SemaphoreType.DMA((3 * pairs * groups,)),
        ]
        + [pltpu.SemaphoreType.DMA((pairs, count))] * 4,
        compiler_params=pltpu.CompilerParams(
            collective_id=collective_id, has_side_effects=True, vmem_limit_bytes=VMEM_LIMIT
        ),
        cost_estimate=cost(60),
    )(x, w_query, w_key, w_value, vecs, tables, seg_col, seg_row)


def back_kernel(
    count, tp_count, groups, low_ref, wout_ref, mixed_ref, sums_ref, vecs_ref,
    qkv_ref, o_ref, lse_ref, packed_ref, segc_ref, segr_ref, grads_ref, vec_grads_ref,
    do_ref, scaled, part, landed, tab_ref,
    do_row, made, bias, qs, ks, kms, dos, delta, dq, dk, dv,
    tp_send, tp_recv, send_sem, recv_sem, back_send_sem, back_recv_sem,
):
    me = lax.axis_index("seq")
    pairs, length = qkv_ref.shape[:2]
    tokens, features = low_ref.shape
    head_width = mixed_ref.shape[1]
    span = length // count
    blocks = length // BLOCK
    mine, row = lax.rem(me, groups), me // groups
    axis_barrier([("seq", count), ("tp", tp_count)])
    gain = head_vec(vecs_ref, head_width, 0)
    vec_grads_ref[...] = jnp.zeros_like(vec_grads_ref)

    def normed_rows(rows):
        first, second = to_columns(sums_ref[:, rows], 2)
        center = first / features
        inverse = lax.rsqrt(second / features - center * center + EPSILON)
        return (mixed_ref[rows, :].astype(F32) - center) * inverse, inverse

    def head_terms(r, carry):
        wide = pl.ds(pl.multiple_of(r * BLOCK, BLOCK), BLOCK)
        scaled[wide, :] = dot(low_ref[wide, :], wout_ref[...], 1, 0)
        for k in range(BLOCK // LANES):
            rows = row_block(r * (BLOCK // LANES) + k)
            normed, _ = normed_rows(rows)
            grad = scaled[rows, :]
            vec_grads_ref[0] += fold(grad * normed)
            vec_grads_ref[1] += fold(grad)
            grad = grad * gain
            scaled[rows, :] = grad
            part[:, rows] = to_row(
                [
                    jnp.sum(grad, axis=-1, keepdims=True),
                    jnp.sum(grad * normed, axis=-1, keepdims=True),
                ]
            )
        return carry

    lax.fori_loop(0, tokens // BLOCK, head_terms, 0)
    tp_total(part, landed, tp_send, tp_recv, tp_count)

    def head_apply(r, carry):
        rows = row_block(r)
        normed, inverse = normed_rows(rows)
        first, second = to_columns(part[:, rows], 2)
        grad = scaled[rows, :] - first / features - normed * (second / features)
        do_ref[rows, :] = (inverse * grad).astype(BF16)
        return carry

    lax.fori_loop(0, tokens // LANES, head_apply, 0)

    def there(p, k):
        device = lax.rem(me + k, count)
        return send(
            do_ref.at[spans(device // groups, span), spans(lax.rem(device, groups) * pairs + p, LANES)],
            do_row.at[p, spans(me, span), :],
            send_sem.at[p, k],
            recv_sem.at[p, k],
            device,
        )

    def back(p, k):
        device = lax.rem(me + k, count)
        return send(
            made.at[p, spans(device, span), :],
            grads_ref.at[spans(row, span), spans(mine * pairs + p, 3 * LANES)],
            back_send_sem.at[p, k],
            back_recv_sem.at[p, k],
            device,
        )

    def share_out(p, carry):
        for k in range(1, count):
            there(p, k).start()
        do_row[p, spans(me, span), :] = do_ref[spans(row, span), spans(mine * pairs + p, LANES)]
        return carry

    lax.fori_loop(0, pairs, share_out, 0)
    expand_tables(packed_ref, tab_ref)
    for kb in range(blocks):
        rows = block_rows(kb)
        start = kb * BLOCK
        shape = (BLOCK, length - start)
        same = segc_ref[rows, :] == segr_ref[:, start:]
        key = lax.broadcasted_iota(jnp.int32, shape, 0)
        query = lax.broadcasted_iota(jnp.int32, shape, 1)
        bias[rows, start:] = jnp.where(same & (key <= query), 0.0, MASKED)

    def attend(p, carry):
        for qb in range(blocks):
            rows = block_rows(qb)
            q = rotated(qkv_ref[p, rows, :LANES], tab_ref, 0, rows) * (HEAD**-0.5)
            q0, q1 = head_masks(q)
            qs[0, rows, :] = q0.astype(BF16)
            qs[1, rows, :] = q1.astype(BF16)
            k = rotated(qkv_ref[p, rows, LANES : 2 * LANES], tab_ref, 2, rows)
            ks[rows, :] = k.astype(BF16)
            k0, k1 = head_masks(k)
            kms[0, rows, :] = k0.astype(BF16)
            kms[1, rows, :] = k1.astype(BF16)
        dq[...] = jnp.zeros_like(dq)
        dk[...] = jnp.zeros_like(dk)
        dv[...] = jnp.zeros_like(dv)
        for k in range(1, count):
            there(p, k).wait_recv()
        for qb in range(blocks):
            rows = block_rows(qb)
            grad = do_row[p, rows, :].astype(F32)
            d0, d1 = head_masks(grad)
            dos[0, rows, :] = d0.astype(BF16)
            dos[1, rows, :] = d1.astype(BF16)
            prod = jnp.transpose(grad * o_ref[p, rows, :].astype(F32))
            delta[0:1, rows] = jnp.sum(prod[:HEAD], axis=0, keepdims=True)
            delta[1:2, rows] = jnp.sum(prod[HEAD:], axis=0, keepdims=True)
        for qb in range(blocks):
            cols = block_rows(qb)
            for kb in range(qb + 1):
                rows = block_rows(kb)
                value = qkv_ref[p, rows, 2 * LANES :]
                for h in range(2):
                    scores = dot(ks[rows, :], qs[h, cols, :], 1, 1) + bias[rows, cols]
                    probs = jnp.exp(scores - lse_ref[p, h : h + 1, cols])
                    grads = dot(value, dos[h, cols, :], 1, 1)
                    dscores = (probs * (grads - delta[h : h + 1, cols])).astype(BF16)
                    dv[rows, :] += dot(probs.astype(BF16), dos[h, cols, :], 1, 0)
                    dk[rows, :] += dot(dscores, qs[h, cols, :], 1, 0)
                    dq[cols, :] += dot(dscores, kms[h, rows, :], 0, 0)
        for qb in range(blocks):
            rows = block_rows(qb)
            grad = dq[rows, :] * (HEAD**-0.5)
            made[p, rows, :LANES] = rotated_back(grad, tab_ref, 0, rows).astype(BF16)
            made[p, rows, LANES : 2 * LANES] = rotated_back(dk[rows, :], tab_ref, 2, rows).astype(BF16)
            made[p, rows, 2 * LANES :] = dv[rows, :].astype(BF16)
        for k in range(1, count):
            back(p, k).start()
        grads_ref[spans(row, span), spans(mine * pairs + p, 3 * LANES)] = made[p, spans(me, span), :]
        return carry

    lax.fori_loop(0, pairs, attend, 0)

    def drain(p, carry):
        for k in range(1, count):
            there(p, k).wait_send()
            back(p, k).wait()
        return carry

    lax.fori_loop(0, pairs, drain, 0)


def attend_back(
    low, w_out, mixed, head_sums, vecs, qkv, o, lse, tables, seg_col, seg_row, count, tp_count,
    groups, collective_id,
):
    tokens, head_width = mixed.shape
    pairs, length = qkv.shape[:2]
    whole = pl.BlockSpec(memory_space=pltpu.VMEM)
    return pl.pallas_call(
        functools.partial(back_kernel, count, tp_count, groups),
        out_shape=[
            jax.ShapeDtypeStruct((tokens, 3 * head_width), BF16),
            jax.ShapeDtypeStruct((2, 8, head_width), F32),
        ],
        in_specs=[whole] * 11,
        out_specs=[whole] * 2,
        scratch_shapes=[
            pltpu.VMEM((tokens, head_width), BF16),
            pltpu.VMEM((tokens, head_width), F32),
            pltpu.VMEM((8, tokens), F32),
            pltpu.VMEM((tp_count, 8, tokens), F32),
            pltpu.VMEM((4, length, LANES), F32),
            pltpu.VMEM((pairs, length, LANES), BF16),
            pltpu.VMEM((pairs, length, 3 * LANES), BF16),
            pltpu.VMEM((length, length), F32),
            pltpu.VMEM((2, length, LANES), BF16),
            pltpu.VMEM((length, LANES), BF16),
            pltpu.VMEM((2, length, LANES), BF16),
            pltpu.VMEM((2, length, LANES), BF16),
            pltpu.VMEM((8, length), F32),
            pltpu.VMEM((length, LANES), F32),
            pltpu.VMEM((length, LANES), F32),
            pltpu.VMEM((length, LANES), F32),
        ]
        + [pltpu.SemaphoreType.DMA((tp_count,))] * 2
        + [pltpu.SemaphoreType.DMA((pairs, count))] * 4,
        compiler_params=pltpu.CompilerParams(
            collective_id=collective_id, has_side_effects=True, vmem_limit_bytes=VMEM_LIMIT
        ),
        cost_estimate=cost(70),
    )(low, w_out, mixed, head_sums, vecs, qkv, o, lse, tables, seg_col, seg_row)


def weight_kernel(act_ref, grads_ref, low_ref, head_ref, out_ref):
    wide = grads_ref.shape[1]
    out_ref[:, :wide] = dot(jnp.transpose(act_ref[...]), grads_ref[...], 1, 0).astype(BF16)
    out_ref[:, wide:] = dot(jnp.transpose(low_ref[...]), head_ref[...], 1, 0).astype(BF16)


def head_weights(act, grads, low, head_act):
    tokens, model_width = act.shape
    wide, narrow = grads.shape[1], head_act.shape[1]
    tile = pl.BlockSpec((tokens, ROWS), lambda i: (0, i))
    return pl.pallas_call(
        weight_kernel,
        grid=(model_width // ROWS,),
        out_shape=jax.ShapeDtypeStruct((model_width, wide + narrow), BF16),
        in_specs=[
            tile,
            pl.BlockSpec((tokens, wide), lambda i: (0, 0)),
            tile,
            pl.BlockSpec((tokens, narrow), lambda i: (0, 0)),
        ],
        out_specs=pl.BlockSpec((ROWS, wide + narrow), lambda i: (i, 0)),
        compiler_params=pltpu.CompilerParams(vmem_limit_bytes=VMEM_LIMIT),
        cost_estimate=cost(10),
    )(act, grads, low, head_act)


def fold(values):
    rows, width = values.shape
    return jnp.sum(values.reshape(rows // 8, 8, width), axis=0)


def model_vec(env, index):
    width = env["out"].shape[1]
    return env["vecs"][:, index * width : (index + 1) * width]


def hidden_vec(env, index, cols=slice(None)):
    width = env["hidden_act"].shape[1]
    first = 4 * env["out"].shape[1] + index * width
    return env["vecs"][:, first : first + width][:, cols]


def head_vec(vecs_ref, width, index):
    total = vecs_ref.shape[1]
    first = total - (2 - index) * width
    return vecs_ref[:, first : first + width]


def finish_middle(total, here, own, env):
    middle = env["block"][here, :].astype(F32) + total
    env["middle"][own, :] = middle
    normed, _ = norm_parts(middle)
    return normed * model_vec(env, 2) + model_vec(env, 3)


def norm_back(base, values, total, gain, sums):
    normed, inverse = norm_parts(values)
    scaled = total * gain
    grad = base + inverse * (
        scaled
        - jnp.mean(scaled, axis=-1, keepdims=True)
        - normed * jnp.mean(scaled * normed, axis=-1, keepdims=True)
    )
    sums[0] += fold(total * normed)
    sums[1] += fold(total)
    return grad


def finish_second(total, here, own, env):
    base = env["cotangent"][here, :].astype(F32)
    grad = norm_back(base, env["middle"][own, :], total, model_vec(env, 2), env["sums"])
    env["middle_grad"][own, :] = grad
    return grad


def finish_first(total, here, own, env):
    values = env["block"][here, :].astype(F32)
    return norm_back(env["middle_grad"][own, :], values, total, model_vec(env, 0), env["sums"])


def to_row(columns):
    lane = lax.broadcasted_iota(jnp.int32, (LANES, LANES), 1)
    packed = jnp.zeros((LANES, LANES), F32)
    for i, column in enumerate(columns):
        packed = jnp.where(lane == i, column, packed)
    return jnp.transpose(packed)[:8]


def to_columns(rows, number):
    packed = jnp.transpose(jnp.concatenate([rows] * (LANES // 8), axis=0))
    return [packed[:, i : i + 1] for i in range(number)]


def row_block(r):
    return pl.ds(pl.multiple_of(r * LANES, LANES), LANES)


def tp_total(part, landed, send_sem, recv_sem, count):
    copies = share("tp", count, lambda d: part, landed, send_sem, recv_sem)
    landed[lax.axis_index("tp")] = part[...]
    for copy in copies:
        copy.wait()
    part[...] = total_of(landed, count)


def norm_heads(env, count, features):
    mixed, act, part = env["mixed"], env["head_act"], env["head_sums"]
    blocks = mixed.shape[0] // LANES

    def sums(r, carry):
        values = mixed[row_block(r), :].astype(F32)
        part[:, row_block(r)] = to_row(
            [
                jnp.sum(values, axis=-1, keepdims=True),
                jnp.sum(values * values, axis=-1, keepdims=True),
            ]
        )
        return carry

    lax.fori_loop(0, blocks, sums, 0)
    tp_total(part, env["head_landed"], env["head_send"], env["head_recv"], count)

    def apply(r, carry):
        first, second = to_columns(part[:, row_block(r)], 2)
        center = first / features
        inverse = lax.rsqrt(second / features - center * center + EPSILON)
        values = (mixed[row_block(r), :].astype(F32) - center) * inverse
        act[row_block(r), :] = (
            values * head_vec(env["vecs"], act.shape[1], 0) + head_vec(env["vecs"], act.shape[1], 1)
        ).astype(BF16)
        return carry

    lax.fori_loop(0, blocks, apply, 0)


def normal_parts(values):
    size = jnp.abs(values) * (0.5**0.5)
    bell = jnp.exp(-0.5 * values * values)
    t = 1.0 / (1.0 + 0.3275911 * size)
    poly = 1.061405429
    for factor in (-1.453152027, 1.421413741, -0.284496736, 0.254829592):
        poly = poly * t + factor
    tail = 0.5 * poly * t * bell
    return jnp.where(values < 0.0, tail, 1.0 - tail), bell * (1.0 / math.sqrt(2.0 * math.pi))


def hidden_rows(env, rows, row):
    width = env["w_up"].shape[1]
    sums = [jnp.zeros((LANES, 1), F32)] * 4
    for n in range(width // TILE):
        cols = slice(n * TILE, (n + 1) * TILE)
        values = dot(env["out"][rows, :], env["w_up"][:, cols], 1, 0)
        below, density = normal_parts(values)
        active = values * below
        env["hidden_act"][rows, cols] = active.astype(BF16)
        env["grad_up"][rows, cols] = (below + values * density).astype(BF16)
        scaled = env["hidden_grad"][rows, cols].astype(F32) * hidden_vec(env, 0, cols)
        for i, term in enumerate((active, active * active, scaled, scaled * active)):
            sums[i] = sums[i] + jnp.sum(term, axis=-1, keepdims=True)
    env["hidden_sums"][:, row] = to_row(sums)


def norm_hidden(env, count, features):
    act, slope, part = env["hidden_act"], env["grad_up"], env["hidden_sums"]
    tokens, width = act.shape
    tp_total(part, env["hidden_landed"], env["hidden_send"], env["hidden_recv"], count)
    env["hidden_vec_grads"][...] = jnp.zeros_like(env["hidden_vec_grads"])

    def apply(r, carry):
        rows = row_block(r)
        sums = [column / features for column in to_columns(part[:, rows], 4)]
        center = sums[0]
        inverse = lax.rsqrt(sums[1] - center * center + EPSILON)
        cross = inverse * (sums[3] - center * sums[2])
        for n in range(width // TILE):
            cols = slice(n * TILE, (n + 1) * TILE)
            gain = hidden_vec(env, 0, cols)
            normed = (act[rows, cols].astype(F32) - center) * inverse
            grad = env["hidden_grad"][rows, cols].astype(F32)
            back = inverse * (grad * gain - sums[2] - normed * cross)
            slope[rows, cols] = (back * slope[rows, cols].astype(F32)).astype(BF16)
            act[rows, cols] = (normed * gain + hidden_vec(env, 1, cols)).astype(BF16)
            env["hidden_vec_grads"][0, :, cols] += fold(grad * normed)
            env["hidden_vec_grads"][1, :, cols] += fold(grad)
        return carry

    lax.fori_loop(0, tokens // LANES, apply, 0)


def split_copies(env, seq_count):
    split = env["split"]
    return share("seq", seq_count, lambda d: split, env["split_landed"], *env_pair(env, "split"), False)


def env_pair(env, name):
    return env[name + "_send"], env[name + "_recv"]


def split_start(env, seq_count):
    hidden = env["hidden_vec_grads"].shape[2]
    split = env["split"]
    split[...] = jnp.zeros_like(split)
    for i in range(2):
        split[i : i + 1, :hidden] = jnp.sum(env["hidden_vec_grads"][i], axis=0, keepdims=True)
        split[i : i + 1, hidden:] = jnp.sum(env["head_vec_grads"][i], axis=0, keepdims=True)
    for copy in split_copies(env, seq_count):
        copy.start()
    env["split_landed"][lax.axis_index("seq")] = split[...]


def full_copies(env, count):
    full = env["full"]
    return share("tp", count, lambda d: full, env["full_landed"], *env_pair(env, "full"), False)


def full_start(env, count):
    full = env["full"]
    full[...] = jnp.zeros_like(full)
    for i in range(2):
        full[i : i + 1, :] = jnp.sum(env["second_sums"][i], axis=0, keepdims=True)
        full[2 + i : 3 + i, :] = jnp.sum(env["sums"][i], axis=0, keepdims=True)
    for copy in full_copies(env, count):
        copy.start()
    env["full_landed"][lax.axis_index("tp")] = full[...]


def norm_finish(env, seq_count, count):
    full, own = env["full"], env["norm_own"].shape[1]
    me = lax.axis_index("seq")
    for copy in full_copies(env, count):
        copy.wait()
    full[...] = total_of(env["full_landed"], count)

    def piece(device):
        return pl.ds(pl.multiple_of(device * own, LANES), own)

    copies = share(
        "seq", seq_count, lambda d: full.at[:, piece(d)], env["own_landed"], *env_pair(env, "own")
    )
    env["own_landed"][me] = full[:, piece(me)]
    for copy in split_copies(env, seq_count):
        copy.wait()
    env["norm_split"][...] = total_of(env["split_landed"], seq_count)
    for copy in copies:
        copy.wait()
    env["norm_own"][...] = total_of(env["own_landed"], seq_count)


def load_pairs(env):
    copies = []
    for i, name in enumerate(("w_query", "w_key", "w_value")):
        for j in range(env[name].shape[1] // LANES):
            copy = pltpu.make_async_copy(
                env[name].at[:, j * LANES : (j + 1) * LANES],
                env["w_pairs"].at[:, (3 * j + i) * LANES : (3 * j + i + 1) * LANES],
                env["pair_sem"].at[3 * j + i],
            )
            copy.start()
            copies.append(copy)
    return copies


def line_kernel(plan, count, chunks, slack, *refs):
    env = dict(zip(plan["order"], refs, strict=True))
    finish, parts, tasks = plan["finish"], plan["parts"], plan["tasks"]
    num_task = len(tasks)
    out_ref, part = env["out"], env["part"]
    in_a, in_b = env["in_a"], env["in_b"]
    rsa_s, rsa_r, rsb_s, rsb_r = (env[name] for name in ("rsa_s", "rsa_r", "rsb_s", "rsb_r"))
    aga_s, aga_r, agb_s, agb_r = (env[name] for name in ("aga_s", "aga_r", "agb_s", "agb_r"))
    z = lax.axis_index("tp")
    tokens, width = out_ref.shape
    half = tokens // 2
    size = half // chunks
    ahead = slack * (count - 1)
    steps = chunks + 2 * ahead
    from_first, from_last = slack * z, slack * (count - 1 - z)
    first, last = z == 0, z == count - 1
    up = jnp.minimum(z + 1, count - 1)
    down = jnp.maximum(z - 1, 0)

    loads = {
        name: pltpu.make_async_copy(env["source " + name], env[name], env["load_sem"].at[i])
        for i, name in enumerate(plan["held"])
    }
    for name in plan["held"]:
        loads[name].start()
    started = plan["start"](env) if plan["start"] else []
    seq_count = plan["seq_count"]
    axis_barrier([("tp", count)] + ([("seq", seq_count)] if seq_count else []))
    if "sums" in env:
        env["sums"][...] = jnp.zeros_like(env["sums"])
    if seq_count:
        split_start(env, seq_count)

    def own_rows(c):
        return pl.ds(pl.multiple_of(c * size, size), size)

    def a_rows(c):
        return own_rows(c)

    def b_rows(c):
        return pl.ds(pl.multiple_of(half + c * size, size), size)

    def hop(source, target, send, recv, c, device):
        return pltpu.make_async_remote_copy(
            src_ref=source,
            dst_ref=target,
            send_sem=send.at[c],
            recv_sem=recv.at[c],
            device_id={"tp": device},
            device_id_type=MESH,
        )

    def gather_a(c):
        rows = out_ref.at[a_rows(c), :]
        return hop(rows, rows, aga_s, aga_r, c, up)

    def gather_b(c):
        rows = out_ref.at[b_rows(c), :]
        return hop(rows, rows, agb_s, agb_r, c, down)

    def reduce_a(c):
        rows = in_a.at[own_rows(c), :]
        return hop(rows, rows, rsa_s, rsa_r, c, down)

    def reduce_b(c):
        rows = in_b.at[own_rows(c), :]
        return hop(rows, rows, rsb_s, rsb_r, c, up)

    def block_start(t, offset):
        return jnp.clip((t - lax.rem(t, GROUP) - offset) * size, 0, half - GROUP * size)

    def reduce_step(t, c, offset, place, rows, landed, move, gather, starts, ends):
        here = rows(c)
        own = own_rows(c)
        row = place * GROUP * size + c * size - block_start(t, offset)
        term_rows = pl.ds(pl.multiple_of(row, size), size)

        @pl.when(starts)
        def _():
            landed[own, :] = part[term_rows, :].astype(BF16)
            move(c).start()

        @pl.when(jnp.logical_not(starts))
        def _():
            move(c).wait_recv()

        @pl.when(jnp.logical_not(starts | ends))
        def _():
            landed[own, :] = (landed[own, :].astype(F32) + part[term_rows, :]).astype(BF16)
            move(c).start()

        @pl.when(ends)
        def _():
            total = landed[own, :].astype(F32) + part[term_rows, :]
            out_ref[here, :] = finish(total, here, own, env).astype(BF16)
            gather(c).start()

    def gather_step(c, gather, starts, ends):
        @pl.when(jnp.logical_not(starts))
        def _():
            gather(c).wait_recv()

        @pl.when(jnp.logical_not(starts | ends))
        def _():
            gather(c).start()

    def when_chunk(c, work):
        pl.when((c >= 0) & (c < chunks))(lambda: work(c))

    def make_parts(t):
        top = pl.ds(pl.multiple_of(block_start(t, from_last), size), GROUP * size)
        low = pl.ds(pl.multiple_of(half + block_start(t, from_first), size), GROUP * size)

        def columns(n, carry):
            cols = pl.ds(pl.multiple_of(n * TILE, TILE), TILE)
            total = 0.0
            for left, right in parts:
                rows = jnp.concatenate([env[left][top, :], env[left][low, :]], axis=0)
                total = total + dot(rows, env[right][cols, :], 1, 1)
            part[:, cols] = total
            return carry

        lax.fori_loop(0, width // TILE, columns, 0)

    def run_task(index, tile, slot):
        kind, left, right, name = tasks[index]
        target = env[name]
        rows = pl.ds(pl.multiple_of(tile * ROWS, ROWS), ROWS)
        if kind == "weight":
            env["turned"][...] = jnp.transpose(env[left][:, rows])

        def columns(n, carry):
            cols = pl.ds(pl.multiple_of(n * TILE, TILE), TILE)
            if kind == "weight":
                value = dot(env["turned"][...], env[right][:, cols], 1, 0)
            elif kind == "keep":
                value = dot(env[left][rows, :], env[right][:, cols], 1, 0)
            else:
                value = dot(env[left][rows, :], env[right][cols, :], 1, 1)
                top = tile * ROWS < half
                mine = (first & top) | (last & jnp.logical_not(top))
                own = pl.multiple_of(lax.rem(tile * ROWS, half), ROWS)
                base = env["middle"][pl.ds(own, ROWS), cols]
                value = value + jnp.where(mine, base, 0.0)
            if kind == "keep":
                target[rows, cols] = value.astype(BF16)
            else:
                env["stage"][slot, :, cols] = value.astype(BF16)
            return carry

        lax.fori_loop(0, target.shape[1] // TILE, columns, 0)
        if kind != "keep":
            stage_copy(index, tile, slot).start()

    def stage_copy(index, tile, slot):
        target = env[tasks[index][3]]
        rows = pl.ds(pl.multiple_of(tile * ROWS, ROWS), ROWS)
        return pltpu.make_async_copy(
            env["stage"].at[slot, :, : target.shape[1]], target.at[rows, :], env["stage_sem"].at[slot]
        )

    starts_at = [0]
    for task in tasks:
        starts_at.append(starts_at[-1] + env[task[3]].shape[0] // ROWS)
    task_total = starts_at[-1]
    per_group = GROUP - 1
    staged = any(task[0] != "keep" for task in tasks)

    def step(t, carry):
        pl.when(lax.rem(t, GROUP) == 0)(lambda: make_parts(t))
        when_chunk(
            t - from_last,
            lambda c: reduce_step(t, c, from_last, 0, a_rows, in_a, reduce_a, gather_a, last, first),
        )
        when_chunk(
            t - from_first,
            lambda c: reduce_step(t, c, from_first, 1, b_rows, in_b, reduce_b, gather_b, first, last),
        )
        when_chunk(t - ahead - from_first, lambda c: gather_step(c, gather_a, first, last))
        when_chunk(t - ahead - from_last, lambda c: gather_step(c, gather_b, last, first))
        if num_task:
            turn = (t // GROUP) * per_group + lax.rem(t, GROUP) - 1
            free = lax.rem(t, GROUP) != 0
            slot = lax.rem(turn + per_group + 1, 2)

            @pl.when(t == 1)
            def _():
                for name in plan["late"]:
                    loads[name].wait()

            for index in range(num_task if staged else 0):
                low, high = starts_at[index] + 2, min(starts_at[index + 1] + 2, task_total)
                pl.when(free & (turn >= low) & (turn < high))(
                    lambda index=index, low=low: stage_copy(index, turn - low, slot).wait()
                )
            for index in range(num_task):
                low, high = starts_at[index], starts_at[index + 1]
                pl.when(free & (turn >= low) & (turn < high))(
                    lambda index=index, low=low: run_task(index, turn - low, slot)
                )
        if seq_count:
            pl.when(t == chunks + ahead)(lambda: full_start(env, count))
        if plan["rows_done"]:
            done_a = t - ahead - from_first - (GROUP - 1)
            done_b = t - ahead - from_last - (GROUP - 1)
            has_a = (done_a >= 0) & (done_a < chunks) & (lax.rem(done_a + 64, GROUP) == 0)
            has_b = (done_b >= 0) & (done_b < chunks) & (lax.rem(done_b + 64, GROUP) == 0)

            @pl.when(has_a | has_b)
            def _():
                start = jnp.where(has_a, done_a * size, half + done_b * size)
                rows = pl.ds(pl.multiple_of(start, LANES), LANES)
                plan["rows_done"](env, rows, rows)

        return carry

    for name in plan["held"]:
        if name not in plan["late"]:
            loads[name].wait()
    for copy in started:
        copy.wait()
    if plan["before"]:
        plan["before"](env)
    lax.fori_loop(0, steps, step, 0)
    if num_task:
        assert (steps // GROUP) * per_group >= task_total
    if staged:
        assert task_total >= 2
        for turn in (task_total - 2, task_total - 1):
            index = max(i for i in range(num_task) if starts_at[i] <= turn)
            stage_copy(index, turn - starts_at[index], turn % 2).wait()
    if plan["after"]:
        plan["after"](env)
    if seq_count:
        norm_finish(env, seq_count, count)

    def drain(c, carry):
        @pl.when(jnp.logical_not(first))
        def _():
            reduce_a(c).wait_send()
            gather_b(c).wait_send()

        @pl.when(jnp.logical_not(last))
        def _():
            reduce_b(c).wait_send()
            gather_a(c).wait_send()

        return carry

    lax.fori_loop(0, chunks, drain, 0)


def line_sum(
    finish, count, held, vecs, parts, collective_id, *, tokens, late=(), tasks=(), owns=(), sent=(),
    scratch=(), loose=(), start=None, before=None, rows_done=None, after=None, seq_count=0, micros=110,
):
    names = dict(scratch)
    width = (held.get(parts[0][1]) if parts[0][1] in held else names[parts[0][1]]).shape[0]
    half = tokens // 2
    depth = tokens if any(task[0] == "weight" for task in tasks) else LANES
    stage_width = max([shape.shape[1] for _, shape in sent] + [LANES])
    fixed = [
        ("in_a", pltpu.VMEM((half, width), BF16)),
        ("in_b", pltpu.VMEM((half, width), BF16)),
        ("part", pltpu.VMEM((2 * GROUP * half // CHUNKS, width), F32)),
        ("turned", pltpu.VMEM((ROWS, depth), BF16)),
        ("stage", pltpu.VMEM((2, ROWS if sent else 16, stage_width), BF16)),
        ("load_sem", pltpu.SemaphoreType.DMA((len(held),))),
        ("stage_sem", pltpu.SemaphoreType.DMA((2,))),
    ] + [
        (name, pltpu.SemaphoreType.DMA((CHUNKS,)))
        for name in ("rsa_s", "rsa_r", "rsb_s", "rsb_r", "aga_s", "aga_r", "agb_s", "agb_r")
    ]
    scratch = list(scratch) + fixed
    loose = dict(loose)
    order = (
        ["source " + name for name in held]
        + list(loose)
        + list(vecs)
        + ["out"]
        + [name for name, _ in owns]
        + [name for name, _ in sent]
        + list(held)
        + [name for name, _ in scratch]
    )
    plan = dict(
        finish=finish,
        order=order,
        held=list(held),
        parts=parts,
        late=late,
        tasks=tasks,
        start=start,
        seq_count=seq_count,
        before=before,
        rows_done=rows_done,
        after=after,
    )
    whole = pl.BlockSpec(memory_space=pltpu.VMEM)
    any_space = pl.BlockSpec(memory_space=pl.ANY)
    return pl.pallas_call(
        functools.partial(line_kernel, plan, count, CHUNKS, SLACK),
        out_shape=[jax.ShapeDtypeStruct((tokens, width), BF16)]
        + [shape for _, shape in owns]
        + [shape for _, shape in sent],
        in_specs=[any_space] * (len(held) + len(loose)) + [whole] * len(vecs),
        out_specs=[whole] * (1 + len(owns)) + [any_space] * len(sent),
        scratch_shapes=[pltpu.VMEM(array.shape, array.dtype) for array in held.values()]
        + [shape for _, shape in scratch],
        compiler_params=pltpu.CompilerParams(
            collective_id=collective_id, has_side_effects=True, vmem_limit_bytes=VMEM_LIMIT
        ),
        cost_estimate=cost(micros),
    )(*held.values(), *loose.values(), *vecs.values())


def axis_barrier(counts):
    barrier = pltpu.get_barrier_semaphore()
    for axis, count in counts:
        me = lax.axis_index(axis)
        for k in range(1, count):
            pl.semaphore_signal(
                barrier, inc=1, device_id={axis: lax.rem(me + k, count)}, device_id_type=MESH
            )
    pl.semaphore_wait(barrier, sum(count - 1 for _, count in counts))


def share(axis, count, pick, landed, send_sem, recv_sem, start=True):
    me = lax.axis_index(axis)
    copies = []
    for k in range(1, count):
        device = lax.rem(me + k, count)
        copy = pltpu.make_async_remote_copy(
            src_ref=pick(device),
            dst_ref=landed.at[me],
            send_sem=send_sem.at[k],
            recv_sem=recv_sem.at[k],
            device_id={axis: device},
            device_id_type=MESH,
        )
        if start:
            copy.start()
        copies.append(copy)
    return copies


def total_of(landed, count):
    total = landed[0]
    for k in range(1, count):
        total = total + landed[k]
    return total


def matmul(left, right, left_dim, right_dim, kind=F32):
    return dot(left, right, left_dim, right_dim).astype(kind)


def rotation_tables(positions):
    half_size = HEAD // 2
    index_pairs = jnp.arange(half_size, dtype=F32)
    theta_rate = jnp.exp(-2.0 * index_pairs / HEAD * jnp.log(10000.0))
    zeta_base = (2.0 * index_pairs + 0.4 * HEAD) / (1.4 * HEAD)
    place_float = positions.astype(F32)[..., None]
    angles = place_float * theta_rate
    power = jnp.log(zeta_base) * place_float / 512.0
    return jnp.concatenate(
        [jnp.cos(angles), jnp.sin(angles), jnp.exp(power), jnp.exp(-power)], axis=-1
    )


def body(
    seq_count,
    tp_count,
    block_in,
    segment_ids,
    first_gain,
    first_bias,
    w_query,
    w_key,
    w_value,
    head_gain,
    head_bias,
    w_out,
    second_gain,
    second_bias,
    w_up,
    hidden_gain,
    hidden_bias,
    w_down,
    out_cotangent,
):
    seq_index = lax.axis_index("seq")
    row_count, span, model_width = block_in.shape
    length = span * seq_count
    tokens = row_count * span
    head_width = w_query.shape[1]
    hidden_width = w_up.shape[1] * tp_count
    groups = seq_count // row_count

    vecs = jnp.concatenate(
        [
            first_gain, first_bias, second_gain, second_bias,
            hidden_gain, hidden_bias, head_gain, head_bias,
        ]
    ).astype(F32)[None]

    seg_row = lax.dynamic_slice_in_dim(segment_ids, seq_index // groups, 1, 0)
    seg_col = seg_row.reshape(length, 1)
    earlier = jnp.sum((seg_row < seg_col).astype(jnp.int32), axis=-1)
    tables = rotation_tables(jnp.arange(length, dtype=jnp.int32) - earlier)

    block = block_in.reshape(tokens, model_width)
    cotangent = out_cotangent.reshape(tokens, model_width)

    first_act, qkv_row, o_row, lse, mixed = front(
        block,
        w_query,
        w_key,
        w_value,
        vecs,
        tables,
        seg_col,
        seg_row,
        seq_count,
        groups,
        1,
    )
    def shape_of(dims, kind=F32):
        return jax.ShapeDtypeStruct(dims, kind)

    hidden_size = hidden_gain.shape[0]
    own_shape = shape_of((tokens // 2, model_width))
    sums_shape = shape_of((2, 8, model_width))
    landed = pltpu.VMEM((tp_count, 8, tokens), F32)
    pair_sem = pltpu.SemaphoreType.DMA((tp_count,))
    (
        second_act, middle_own, head_act, head_sums, hidden_act, grad_up, hidden_vec_grads
    ) = line_sum(
        finish_middle,
        tp_count,
        dict(mixed=mixed, w_out=w_out, block=block, cotangent=cotangent, w_down=w_down, w_up=w_up),
        dict(vecs=vecs),
        (("head_act", "w_out"),),
        3,
        tokens=tokens,
        late=("cotangent", "w_down", "w_up"),
        tasks=(("keep", "cotangent", "w_down", "hidden_grad"),),
        owns=(
            ("middle", own_shape),
            ("head_act", shape_of((tokens, head_width), BF16)),
            ("head_sums", shape_of((8, tokens))),
            ("hidden_act", shape_of((tokens, hidden_size), BF16)),
            ("grad_up", shape_of((tokens, hidden_size), BF16)),
            ("hidden_vec_grads", shape_of((2, 8, hidden_size))),
        ),
        scratch=(
            ("hidden_grad", pltpu.VMEM((tokens, hidden_size), BF16)),
            ("hidden_sums", pltpu.VMEM((8, tokens), F32)),
            ("head_landed", landed),
            ("hidden_landed", landed),
            ("head_send", pair_sem),
            ("head_recv", pair_sem),
            ("hidden_send", pair_sem),
            ("hidden_recv", pair_sem),
        ),
        before=lambda env: norm_heads(env, tp_count, model_width),
        rows_done=hidden_rows,
        after=lambda env: norm_hidden(env, tp_count, hidden_width),
        micros=140,
    )

    weight_shape = shape_of((model_width, hidden_size), BF16)
    grad_middle_low, second_sums, grad_middle_own, down_part, w_down_terms, w_up_terms = line_sum(
        finish_second,
        tp_count,
        dict(
            grad_up=grad_up,
            w_up=w_up,
            cotangent=cotangent,
            middle=middle_own,
            hidden_act=hidden_act,
            w_down=w_down,
            second_act=second_act,
        ),
        dict(vecs=vecs),
        (("grad_up", "w_up"),),
        4,
        tokens=tokens,
        late=("hidden_act", "w_down", "second_act"),
        tasks=(
            ("down", "hidden_act", "w_down", "down_part"),
            ("weight", "cotangent", "hidden_act", "w_down_terms"),
            ("weight", "second_act", "grad_up", "w_up_terms"),
        ),
        owns=(("sums", sums_shape), ("middle_grad", own_shape)),
        sent=(
            ("down_part", shape_of((tokens, model_width), BF16)),
            ("w_down_terms", weight_shape),
            ("w_up_terms", weight_shape),
        ),
    )
    block_out = lax.psum(down_part, "tp")

    def scatter(grad):
        return lax.psum_scatter(grad, "seq", scatter_dimension=0, tiled=True)

    w_down_grad = scatter(w_down_terms)
    w_up_grad = scatter(w_up_terms)

    grads, head_vec_grads = attend_back(
        grad_middle_low,
        w_out,
        mixed,
        head_sums,
        vecs,
        qkv_row,
        o_row,
        lse,
        tables,
        seg_col,
        seg_row,
        seq_count,
        tp_count,
        groups,
        6,
    )
    head_terms = head_weights(first_act, grads, grad_middle_low, head_act)
    grads, head_terms, w_down_grad = lax.optimization_barrier((grads, head_terms, w_down_grad))
    head_grads = scatter(head_terms)
    own_width = model_width // seq_count
    split_width = hidden_size + head_width
    seq_sem = pltpu.SemaphoreType.DMA((seq_count,))
    input_grad, _, norm_own, norm_split = line_sum(
        finish_first,
        tp_count,
        dict(grads=grads, block=block, middle_grad=grad_middle_own),
        dict(
            vecs=vecs,
            second_sums=second_sums,
            hidden_vec_grads=hidden_vec_grads,
            head_vec_grads=head_vec_grads,
        ),
        (("grads", "w_pairs"),),
        8,
        tokens=tokens,
        loose=dict(w_query=w_query, w_key=w_key, w_value=w_value),
        owns=(
            ("sums", sums_shape),
            ("norm_own", shape_of((8, own_width))),
            ("norm_split", shape_of((8, split_width))),
        ),
        scratch=(
            ("w_pairs", pltpu.VMEM((model_width, 3 * head_width), BF16)),
            ("pair_sem", pltpu.SemaphoreType.DMA((3 * head_width // LANES,))),
            ("split", pltpu.VMEM((8, split_width), F32)),
            ("split_landed", pltpu.VMEM((seq_count, 8, split_width), F32)),
            ("full", pltpu.VMEM((8, model_width), F32)),
            ("full_landed", pltpu.VMEM((tp_count, 8, model_width), F32)),
            ("own_landed", pltpu.VMEM((seq_count, 8, own_width), F32)),
            ("split_send", seq_sem),
            ("split_recv", seq_sem),
            ("full_send", pair_sem),
            ("full_recv", pair_sem),
            ("own_send", seq_sem),
            ("own_recv", seq_sem),
        ),
        start=load_pairs,
        seq_count=seq_count,
    )
    block_out, input_grad = lax.optimization_barrier((block_out, input_grad))

    def head_grad(index):
        columns = [
            head_grads[:, (3 * j + index) * LANES : (3 * j + index + 1) * LANES]
            for j in range(head_width // LANES)
        ]
        return jnp.concatenate(columns, axis=1).astype(F32)

    return (
        block_out.reshape(block_in.shape),
        input_grad.reshape(block_in.shape),
        norm_own[2],
        norm_own[3],
        head_grad(0),
        head_grad(1),
        head_grad(2),
        norm_split[0, hidden_size:],
        norm_split[1, hidden_size:],
        head_grads[:, 3 * head_width :].astype(F32),
        norm_own[0],
        norm_own[1],
        w_up_grad.astype(F32),
        norm_split[0, :hidden_size],
        norm_split[1, :hidden_size],
        w_down_grad.astype(F32),
    )


def solution(mesh):
    return jax.shard_map(
        functools.partial(body, mesh.shape["seq"], mesh.shape["tp"]),
        mesh=mesh,
        in_specs=(
            P(None, "seq", None),
            P(),
            P(),
            P(),
            P(None, "tp"),
            P(None, "tp"),
            P(None, "tp"),
            P("tp"),
            P("tp"),
            P(None, "tp"),
            P(),
            P(),
            P(None, "tp"),
            P("tp"),
            P("tp"),
            P(None, "tp"),
            P(None, "seq", None),
        ),
        out_specs=(
            P(None, "seq", None),
            P(None, "seq", None),
            P("seq"),
            P("seq"),
            P("seq", "tp"),
            P("seq", "tp"),
            P("seq", "tp"),
            P("tp"),
            P("tp"),
            P("seq", "tp"),
            P("seq"),
            P("seq"),
            P("seq", "tp"),
            P("tp"),
            P("tp"),
            P("seq", "tp"),
        ),
        check_vma=False,
    )
```

```python
import functools
import math

import jax
import jax.numpy as jnp
from jax import lax
from jax.experimental import pallas as pl
from jax.experimental.pallas import tpu as pltpu
from jax.sharding import PartitionSpec as P

HEAD = 64
LANES = 128
BLOCK = 256
EPSILON = 1e-05
MASKED = -1e30
MESH = pl.DeviceIdType.MESH
F32 = jnp.float32
BF16 = jnp.bfloat16
CHUNKS = 16
SLACK = 2
GROUP = 4
ROWS = 256
TILE = 512
VMEM_LIMIT = 60 * 1024 * 1024


def cost(micros):
    return pl.CostEstimate(flops=int(micros * 1.1e9), bytes_accessed=0, transcendentals=0)


def dot(left, right, left_dim, right_dim):
    return lax.dot_general(
        left, right, (((left_dim,), (right_dim,)), ((), ())), preferred_element_type=F32
    )


def seq_signal(count):
    me = lax.axis_index("seq")
    barrier = pltpu.get_barrier_semaphore()
    for k in range(1, count):
        pl.semaphore_signal(
            barrier, inc=1, device_id={"seq": lax.rem(me + k, count)}, device_id_type=MESH
        )


def seq_wait(count):
    pl.semaphore_wait(pltpu.get_barrier_semaphore(), count - 1)


def send(source, target, send_sem, recv_sem, device):
    return pltpu.make_async_remote_copy(
        src_ref=source,
        dst_ref=target,
        send_sem=send_sem,
        recv_sem=recv_sem,
        device_id={"seq": device},
        device_id_type=MESH,
    )


def spans(index, span):
    return pl.ds(pl.multiple_of(index * span, LANES), span)


def swap_halves(values):
    lane = lax.broadcasted_iota(jnp.int32, values.shape, 1)
    return jnp.where(
        lane % HEAD < HEAD // 2,
        pltpu.roll(values, LANES - HEAD // 2, 1),
        pltpu.roll(values, HEAD // 2, 1),
    )


def head_masks(values):
    lane = lax.broadcasted_iota(jnp.int32, values.shape, 1)
    zero = jnp.zeros_like(values)
    return jnp.where(lane < HEAD, values, zero), jnp.where(lane < HEAD, zero, values)


def block_rows(index):
    return slice(index * BLOCK, (index + 1) * BLOCK)


def rotated(values, tables, first, rows):
    values = values.astype(F32)
    return values * tables[first, rows, :] + swap_halves(values) * tables[first + 1, rows, :]


def rotated_back(values, tables, first, rows):
    return values * tables[first, rows, :] - swap_halves(values) * tables[first + 1, rows, :]


def norm_parts(values):
    center = jnp.mean(values, axis=-1, keepdims=True)
    shifted = values - center
    inverse = lax.rsqrt(jnp.mean(shifted * shifted, axis=-1, keepdims=True) + EPSILON)
    return shifted * inverse, inverse


def expand_tables(packed, tables):
    quarter = HEAD // 2
    for block in range(packed.shape[0] // BLOCK):
        rows = block_rows(block)
        lane = lax.broadcasted_iota(jnp.int32, (BLOCK, LANES), 1)
        group = lane // quarter
        turns = [packed[rows, :]]
        for k in range(1, 4):
            turns.append(pltpu.roll(turns[0], k * quarter, 1))

        def spread(index):
            values = turns[(0 - index) % 4]
            for g in range(1, 4):
                values = jnp.where(group == g, turns[(g - index) % 4], values)
            return values

        cos_part = spread(0)
        sin_part = spread(1)
        sin_part = jnp.where(lane % HEAD < quarter, -sin_part, sin_part)
        for k in range(2):
            factor = spread(2 + k)
            tables[2 * k, rows, :] = cos_part * factor
            tables[2 * k + 1, rows, :] = sin_part * factor


def front_kernel(
    count, groups, x_ref, wq_ref, wk_ref, wv_ref, vecs_ref, packed_ref, segc_ref, segr_ref,
    act_ref, qkv_ref, o_ref, lse_ref, mixed_ref,
    weights, staged, tab_ref, bias, qs, ks, load_sem, send_sem, recv_sem, back_send_sem, back_recv_sem,
):
    me = lax.axis_index("seq")
    pairs, length = qkv_ref.shape[:2]
    tokens, width = x_ref.shape
    span = length // count
    blocks = length // BLOCK
    mine, row = lax.rem(me, groups), me // groups
    seq_signal(count)
    loads = []
    for j in range(pairs * groups):
        for i, source in enumerate((wq_ref, wk_ref, wv_ref)):
            copy = pltpu.make_async_copy(
                source.at[:, j * LANES : (j + 1) * LANES],
                weights.at[j, :, i * LANES : (i + 1) * LANES],
                load_sem.at[3 * j + i],
            )
            copy.start()
            loads.append(copy)

    def norm_step(r, carry):
        rows = pl.ds(pl.multiple_of(r * LANES, LANES), LANES)
        normed, _ = norm_parts(x_ref[rows, :].astype(F32))
        act_ref[rows, :] = (normed * vecs_ref[:, :width] + vecs_ref[:, width : 2 * width]).astype(BF16)
        return carry

    lax.fori_loop(0, tokens // LANES, norm_step, 0)
    for copy in loads:
        copy.wait()

    def there(p, k):
        device = lax.rem(me + k, count)
        return send(
            staged.at[lax.rem(device, groups) * pairs + p, spans(device // groups, span), :],
            qkv_ref.at[p, spans(me, span), :],
            send_sem.at[p, k],
            recv_sem.at[p, k],
            device,
        )

    def back(p, k):
        device = lax.rem(me + k, count)
        return send(
            o_ref.at[p, spans(device, span), :],
            mixed_ref.at[spans(row, span), spans(mine * pairs + p, LANES)],
            back_send_sem.at[p, k],
            back_recv_sem.at[p, k],
            device,
        )

    def project(p, carry):
        for group in range(groups):

            def rows_step(r, inner):
                rows = pl.ds(pl.multiple_of(r * BLOCK, BLOCK), BLOCK)
                j = group * pairs + p
                staged[j, rows, :] = dot(act_ref[rows, :], weights[j], 1, 0).astype(BF16)
                return inner

            lax.fori_loop(0, tokens // BLOCK, rows_step, 0)

        @pl.when(p == 0)
        def _():
            seq_wait(count)

        for k in range(1, count):
            there(p, k).start()
        qkv_ref[p, spans(me, span), :] = staged[mine * pairs + p, spans(row, span), :]
        return carry

    lax.fori_loop(0, pairs, project, 0)
    expand_tables(packed_ref, tab_ref)
    for qb in range(blocks):
        rows = block_rows(qb)
        keys = (qb + 1) * BLOCK
        same = segc_ref[rows, :] == segr_ref[:, :keys]
        query = lax.broadcasted_iota(jnp.int32, (BLOCK, keys), 0) + qb * BLOCK
        key = lax.broadcasted_iota(jnp.int32, (BLOCK, keys), 1)
        bias[rows, :keys] = jnp.where(same & (key <= query), 0.0, MASKED)

    def attend(p, carry):
        for k in range(1, count):
            there(p, k).wait_recv()
        for qb in range(blocks):
            rows = block_rows(qb)
            q = rotated(qkv_ref[p, rows, :LANES], tab_ref, 0, rows) * (HEAD**-0.5)
            q0, q1 = head_masks(q)
            qs[0, rows, :] = q0.astype(BF16)
            qs[1, rows, :] = q1.astype(BF16)
            k = rotated(qkv_ref[p, rows, LANES : 2 * LANES], tab_ref, 2, rows)
            ks[rows, :] = k.astype(BF16)
        for qb in range(blocks):
            rows = block_rows(qb)
            keys = (qb + 1) * BLOCK
            outs = []
            logs = []
            for h in range(2):
                scores = dot(qs[h, rows, :], ks[:keys, :], 1, 1) + bias[rows, :keys]
                top = jnp.max(scores, axis=1, keepdims=True)
                expo = jnp.exp(scores - top)
                total = jnp.sum(expo, axis=1, keepdims=True)
                outs.append(dot(expo.astype(BF16), qkv_ref[p, :keys, 2 * LANES :], 1, 0) / total)
                logs.append(jnp.broadcast_to(top + jnp.log(total), (BLOCK, LANES)))
            lane = lax.broadcasted_iota(jnp.int32, (BLOCK, LANES), 1)
            o_ref[p, rows, :] = jnp.where(lane < HEAD, outs[0], outs[1]).astype(BF16)
            logs_t = jnp.transpose(jnp.where(lane < HEAD, logs[0], logs[1]))
            lse_ref[p, 0:1, rows] = logs_t[0:1]
            lse_ref[p, 1:2, rows] = logs_t[HEAD : HEAD + 1]
        for k in range(1, count):
            back(p, k).start()
        mixed_ref[spans(row, span), spans(mine * pairs + p, LANES)] = o_ref[p, spans(me, span), :]
        return carry

    lax.fori_loop(0, pairs, attend, 0)

    def drain(p, carry):
        for k in range(1, count):
            there(p, k).wait_send()
            back(p, k).wait()
        return carry

    lax.fori_loop(0, pairs, drain, 0)


def front(x, w_query, w_key, w_value, vecs, tables, seg_col, seg_row, count, groups, collective_id):
    tokens, model_width = x.shape
    head_width = w_query.shape[1]
    length = seg_col.shape[0]
    pairs = head_width // groups // LANES
    whole = pl.BlockSpec(memory_space=pltpu.VMEM)
    any_space = pl.BlockSpec(memory_space=pl.ANY)
    return pl.pallas_call(
        functools.partial(front_kernel, count, groups),
        out_shape=[
            jax.ShapeDtypeStruct((tokens, model_width), BF16),
            jax.ShapeDtypeStruct((pairs, length, 3 * LANES), BF16),
            jax.ShapeDtypeStruct((pairs, length, LANES), BF16),
            jax.ShapeDtypeStruct((pairs, 8, length), F32),
            jax.ShapeDtypeStruct((tokens, head_width), BF16),
        ],
        in_specs=[whole] + [any_space] * 3 + [whole] * 4,
        out_specs=[whole] * 5,
        scratch_shapes=[
            pltpu.VMEM((pairs * groups, model_width, 3 * LANES), BF16),
            pltpu.VMEM((pairs * groups, tokens, 3 * LANES), BF16),
            pltpu.VMEM((4, length, LANES), F32),
            pltpu.VMEM((length, length), F32),
            pltpu.VMEM((2, length, LANES), BF16),
            pltpu.VMEM((length, LANES), BF16),
            pltpu.SemaphoreType.DMA((3 * pairs * groups,)),
        ]
        + [pltpu.SemaphoreType.DMA((pairs, count))] * 4,
        compiler_params=pltpu.CompilerParams(
            collective_id=collective_id, has_side_effects=True, vmem_limit_bytes=VMEM_LIMIT
        ),
        cost_estimate=cost(60),
    )(x, w_query, w_key, w_value, vecs, tables, seg_col, seg_row)


def back_work(env, count, tp_count, groups):
    low_ref, wout_ref, mixed_ref = env["low"], env["w_out"], env["mixed"]
    sums_ref, qkv_ref, o_ref, lse_ref = env["head_sums"], env["qkv"], env["o"], env["lse"]
    segc_ref, segr_ref, tab_ref, bias = env["seg_col"], env["seg_row"], env["tables"], env["bias"]
    grads_ref, vec_grads_ref = env["grads"], env["head_vec_grads"]
    do_ref, scaled, part = env["do"], env["scaled"], env["head_part"]
    do_row, made, delta = env["do_row"], env["made"], env["delta"]
    qs, ks, kms, dos, dq, dk, dv = (env[name] for name in ("qs", "ks", "kms", "dos", "dq", "dk", "dv"))
    me = lax.axis_index("seq")
    pairs, length = qkv_ref.shape[:2]
    tokens, features = low_ref.shape
    head_width = mixed_ref.shape[1]
    span = length // count
    blocks = length // BLOCK
    mine, row = lax.rem(me, groups), me // groups
    gain = head_vec(env["vecs"], head_width, 0)

    def normed_rows(rows):
        first, second = to_columns(sums_ref[:, rows], 2)
        center = first / features
        inverse = lax.rsqrt(second / features - center * center + EPSILON)
        return (mixed_ref[rows, :].astype(F32) - center) * inverse, inverse

    def head_terms(r):
        wide = pl.ds(pl.multiple_of(r * BLOCK, BLOCK), BLOCK)
        scaled[wide, :] = dot(low_ref[wide, :], wout_ref[...], 1, 0)
        for k in range(BLOCK // LANES):
            rows = row_block(r * (BLOCK // LANES) + k)
            normed, _ = normed_rows(rows)
            grad = scaled[rows, :]
            vec_grads_ref[0] += fold(grad * normed)
            vec_grads_ref[1] += fold(grad)
            grad = grad * gain
            scaled[rows, :] = grad
            part[:, rows] = to_row(
                [
                    jnp.sum(grad, axis=-1, keepdims=True),
                    jnp.sum(grad * normed, axis=-1, keepdims=True),
                ]
            )

    def part_copies(start):
        return share("tp", tp_count, lambda d: part, env["head_landed"], *env_pair(env, "head"), start)

    def head_apply(r, carry):
        rows = row_block(r)
        normed, inverse = normed_rows(rows)
        first, second = to_columns(part[:, rows], 2)
        grad = scaled[rows, :] - first / features - normed * (second / features)
        do_ref[rows, :] = (inverse * grad).astype(BF16)
        return carry

    def there(p, k):
        device = lax.rem(me + k, count)
        return send(
            do_ref.at[spans(device // groups, span), spans(lax.rem(device, groups) * pairs + p, LANES)],
            do_row.at[p, spans(me, span), :],
            env["there_send"].at[p, k],
            env["there_recv"].at[p, k],
            device,
        )

    def back(p, k):
        device = lax.rem(me + k, count)
        return send(
            made.at[p, spans(device, span), :],
            grads_ref.at[spans(row, span), spans(mine * pairs + p, 3 * LANES)],
            env["back_send"].at[p, k],
            env["back_recv"].at[p, k],
            device,
        )

    def share_out(p, carry):
        for k in range(1, count):
            there(p, k).start()
        do_row[p, spans(me, span), :] = do_ref[spans(row, span), spans(mine * pairs + p, LANES)]
        return carry

    def prepare():
        expand_tables(env["packed"], tab_ref)
        for kb in range(blocks):
            rows = block_rows(kb)
            start = kb * BLOCK
            shape = (BLOCK, length - start)
            same = segc_ref[rows, :] == segr_ref[:, start:]
            key = lax.broadcasted_iota(jnp.int32, shape, 0)
            query = lax.broadcasted_iota(jnp.int32, shape, 1)
            bias[rows, start:] = jnp.where(same & (key <= query), 0.0, MASKED)

    def pair_start(p):
        for qb in range(blocks):
            rows = block_rows(qb)
            q = rotated(qkv_ref[p, rows, :LANES], tab_ref, 0, rows) * (HEAD**-0.5)
            q0, q1 = head_masks(q)
            qs[0, rows, :] = q0.astype(BF16)
            qs[1, rows, :] = q1.astype(BF16)
            k = rotated(qkv_ref[p, rows, LANES : 2 * LANES], tab_ref, 2, rows)
            ks[rows, :] = k.astype(BF16)
            k0, k1 = head_masks(k)
            kms[0, rows, :] = k0.astype(BF16)
            kms[1, rows, :] = k1.astype(BF16)
        dq[...] = jnp.zeros_like(dq)
        dk[...] = jnp.zeros_like(dk)
        dv[...] = jnp.zeros_like(dv)
        for k in range(1, count):
            there(p, k).wait_recv()
        for qb in range(blocks):
            rows = block_rows(qb)
            grad = do_row[p, rows, :].astype(F32)
            d0, d1 = head_masks(grad)
            dos[0, rows, :] = d0.astype(BF16)
            dos[1, rows, :] = d1.astype(BF16)
            prod = jnp.transpose(grad * o_ref[p, rows, :].astype(F32))
            delta[0:1, rows] = jnp.sum(prod[:HEAD], axis=0, keepdims=True)
            delta[1:2, rows] = jnp.sum(prod[HEAD:], axis=0, keepdims=True)

    def pair_block(p, qb):
        cols = block_rows(qb)
        for kb in range(qb + 1):
            rows = block_rows(kb)
            value = qkv_ref[p, rows, 2 * LANES :]
            for h in range(2):
                scores = dot(ks[rows, :], qs[h, cols, :], 1, 1) + bias[rows, cols]
                probs = jnp.exp(scores - lse_ref[p, h : h + 1, cols])
                grads = dot(value, dos[h, cols, :], 1, 1)
                dscores = (probs * (grads - delta[h : h + 1, cols])).astype(BF16)
                dv[rows, :] += dot(probs.astype(BF16), dos[h, cols, :], 1, 0)
                dk[rows, :] += dot(dscores, qs[h, cols, :], 1, 0)
                dq[cols, :] += dot(dscores, kms[h, rows, :], 0, 0)

    def pair_end(p):
        for qb in range(blocks):
            rows = block_rows(qb)
            grad = dq[rows, :] * (HEAD**-0.5)
            made[p, rows, :LANES] = rotated_back(grad, tab_ref, 0, rows).astype(BF16)
            made[p, rows, LANES : 2 * LANES] = rotated_back(dk[rows, :], tab_ref, 2, rows).astype(BF16)
            made[p, rows, 2 * LANES :] = dv[rows, :].astype(BF16)
        for k in range(1, count):
            back(p, k).start()
        grads_ref[spans(row, span), spans(mine * pairs + p, 3 * LANES)] = made[p, spans(me, span), :]

    head_steps = tokens // BLOCK
    vec_grads_ref[...] = jnp.zeros_like(vec_grads_ref)

    def step(t):
        pl.when(t < head_steps)(lambda: head_terms(t))

        @pl.when(t == head_steps - 1)
        def _():
            part_copies(True)
            env["head_landed"][lax.axis_index("tp")] = part[...]

        pl.when(t == head_steps)(prepare)

        @pl.when(t == head_steps + 1)
        def _():
            for copy in part_copies(False):
                copy.wait()
            part[...] = total_of(env["head_landed"], tp_count)
            lax.fori_loop(0, tokens // LANES, head_apply, 0)
            lax.fori_loop(0, pairs, share_out, 0)

        turn = t - (head_steps + 3)
        p = turn // blocks
        for qb in range(blocks):

            @pl.when((turn >= 0) & (turn < pairs * blocks) & (lax.rem(turn + 8 * blocks, blocks) == qb))
            def _():
                if qb == 0:
                    pair_start(p)
                pair_block(p, qb)
                if qb == blocks - 1:
                    pair_end(p)

    def end():
        def drain(p, carry):
            for k in range(1, count):
                there(p, k).wait_send()
                back(p, k).wait()
            return carry

        lax.fori_loop(0, pairs, drain, 0)

    return step, end, head_steps + 3 + pairs * blocks


def weight_kernel(act_ref, grads_ref, low_ref, head_ref, out_ref):
    wide = grads_ref.shape[1]
    out_ref[:, :wide] = dot(jnp.transpose(act_ref[...]), grads_ref[...], 1, 0).astype(BF16)
    out_ref[:, wide:] = dot(jnp.transpose(low_ref[...]), head_ref[...], 1, 0).astype(BF16)


def head_weights(act, grads, low, head_act):
    tokens, model_width = act.shape
    wide, narrow = grads.shape[1], head_act.shape[1]
    tile = pl.BlockSpec((tokens, ROWS), lambda i: (0, i))
    return pl.pallas_call(
        weight_kernel,
        grid=(model_width // ROWS,),
        out_shape=jax.ShapeDtypeStruct((model_width, wide + narrow), BF16),
        in_specs=[
            tile,
            pl.BlockSpec((tokens, wide), lambda i: (0, 0)),
            tile,
            pl.BlockSpec((tokens, narrow), lambda i: (0, 0)),
        ],
        out_specs=pl.BlockSpec((ROWS, wide + narrow), lambda i: (i, 0)),
        compiler_params=pltpu.CompilerParams(vmem_limit_bytes=VMEM_LIMIT),
        cost_estimate=cost(10),
    )(act, grads, low, head_act)


def fold(values):
    rows, width = values.shape
    return jnp.sum(values.reshape(rows // 8, 8, width), axis=0)


def model_vec(env, index):
    width = env["out"].shape[1]
    return env["vecs"][:, index * width : (index + 1) * width]


def hidden_vec(env, index, cols=slice(None)):
    width = env["hidden_act"].shape[1]
    first = 4 * env["out"].shape[1] + index * width
    return env["vecs"][:, first : first + width][:, cols]


def head_vec(vecs_ref, width, index):
    total = vecs_ref.shape[1]
    first = total - (2 - index) * width
    return vecs_ref[:, first : first + width]


def finish_middle(total, here, own, env):
    middle = env["block"][here, :].astype(F32) + total
    env["middle"][own, :] = middle
    normed, _ = norm_parts(middle)
    return normed * model_vec(env, 2) + model_vec(env, 3)


def norm_back(base, values, total, gain, sums):
    normed, inverse = norm_parts(values)
    scaled = total * gain
    grad = base + inverse * (
        scaled
        - jnp.mean(scaled, axis=-1, keepdims=True)
        - normed * jnp.mean(scaled * normed, axis=-1, keepdims=True)
    )
    sums[0] += fold(total * normed)
    sums[1] += fold(total)
    return grad


def finish_second(total, here, own, env):
    base = env["cotangent"][here, :].astype(F32)
    grad = norm_back(base, env["middle"][own, :], total, model_vec(env, 2), env["sums"])
    env["middle_grad"][own, :] = grad
    return grad


def finish_first(total, here, own, env):
    values = env["block"][here, :].astype(F32)
    return norm_back(env["middle_grad"][own, :], values, total, model_vec(env, 0), env["sums"])


def to_row(columns):
    lane = lax.broadcasted_iota(jnp.int32, (LANES, LANES), 1)
    packed = jnp.zeros((LANES, LANES), F32)
    for i, column in enumerate(columns):
        packed = jnp.where(lane == i, column, packed)
    return jnp.transpose(packed)[:8]


def to_columns(rows, number):
    packed = jnp.transpose(jnp.concatenate([rows] * (LANES // 8), axis=0))
    return [packed[:, i : i + 1] for i in range(number)]


def row_block(r):
    return pl.ds(pl.multiple_of(r * LANES, LANES), LANES)


def tp_total(part, landed, send_sem, recv_sem, count):
    copies = share("tp", count, lambda d: part, landed, send_sem, recv_sem)
    landed[lax.axis_index("tp")] = part[...]
    for copy in copies:
        copy.wait()
    part[...] = total_of(landed, count)


def norm_heads(env, count, features):
    mixed, act, part = env["mixed"], env["head_act"], env["head_sums"]
    blocks = mixed.shape[0] // LANES

    def sums(r, carry):
        values = mixed[row_block(r), :].astype(F32)
        part[:, row_block(r)] = to_row(
            [
                jnp.sum(values, axis=-1, keepdims=True),
                jnp.sum(values * values, axis=-1, keepdims=True),
            ]
        )
        return carry

    lax.fori_loop(0, blocks, sums, 0)
    tp_total(part, env["head_landed"], env["head_send"], env["head_recv"], count)

    def apply(r, carry):
        first, second = to_columns(part[:, row_block(r)], 2)
        center = first / features
        inverse = lax.rsqrt(second / features - center * center + EPSILON)
        values = (mixed[row_block(r), :].astype(F32) - center) * inverse
        act[row_block(r), :] = (
            values * head_vec(env["vecs"], act.shape[1], 0) + head_vec(env["vecs"], act.shape[1], 1)
        ).astype(BF16)
        return carry

    lax.fori_loop(0, blocks, apply, 0)


def normal_parts(values):
    size = jnp.abs(values) * (0.5**0.5)
    bell = jnp.exp(-0.5 * values * values)
    t = 1.0 / (1.0 + 0.3275911 * size)
    poly = 1.061405429
    for factor in (-1.453152027, 1.421413741, -0.284496736, 0.254829592):
        poly = poly * t + factor
    tail = 0.5 * poly * t * bell
    return jnp.where(values < 0.0, tail, 1.0 - tail), bell * (1.0 / math.sqrt(2.0 * math.pi))


def hidden_rows(env, rows, row):
    width = env["w_up"].shape[1]
    sums = [jnp.zeros((LANES, 1), F32)] * 4
    for n in range(width // TILE):
        cols = slice(n * TILE, (n + 1) * TILE)
        values = dot(env["out"][rows, :], env["w_up"][:, cols], 1, 0)
        below, density = normal_parts(values)
        active = values * below
        env["hidden_act"][rows, cols] = active.astype(BF16)
        env["grad_up"][rows, cols] = (below + values * density).astype(BF16)
        scaled = env["hidden_grad"][rows, cols].astype(F32) * hidden_vec(env, 0, cols)
        for i, term in enumerate((active, active * active, scaled, scaled * active)):
            sums[i] = sums[i] + jnp.sum(term, axis=-1, keepdims=True)
    env["hidden_sums"][:, row] = to_row(sums)


def norm_hidden(env, count, features):
    act, slope, part = env["hidden_act"], env["grad_up"], env["hidden_sums"]
    tokens, width = act.shape
    tp_total(part, env["hidden_landed"], env["hidden_send"], env["hidden_recv"], count)
    env["hidden_vec_grads"][...] = jnp.zeros_like(env["hidden_vec_grads"])

    def apply(r, carry):
        rows = row_block(r)
        sums = [column / features for column in to_columns(part[:, rows], 4)]
        center = sums[0]
        inverse = lax.rsqrt(sums[1] - center * center + EPSILON)
        cross = inverse * (sums[3] - center * sums[2])
        for n in range(width // TILE):
            cols = slice(n * TILE, (n + 1) * TILE)
            gain = hidden_vec(env, 0, cols)
            normed = (act[rows, cols].astype(F32) - center) * inverse
            grad = env["hidden_grad"][rows, cols].astype(F32)
            back = inverse * (grad * gain - sums[2] - normed * cross)
            slope[rows, cols] = (back * slope[rows, cols].astype(F32)).astype(BF16)
            act[rows, cols] = (normed * gain + hidden_vec(env, 1, cols)).astype(BF16)
            env["hidden_vec_grads"][0, :, cols] += fold(grad * normed)
            env["hidden_vec_grads"][1, :, cols] += fold(grad)
        return carry

    lax.fori_loop(0, tokens // LANES, apply, 0)


def split_copies(env, seq_count):
    split = env["split"]
    return share("seq", seq_count, lambda d: split, env["split_landed"], *env_pair(env, "split"), False)


def env_pair(env, name):
    return env[name + "_send"], env[name + "_recv"]


def split_start(env, seq_count):
    hidden = env["hidden_vec_grads"].shape[2]
    split = env["split"]
    split[...] = jnp.zeros_like(split)
    for i in range(2):
        split[i : i + 1, :hidden] = jnp.sum(env["hidden_vec_grads"][i], axis=0, keepdims=True)
        split[i : i + 1, hidden:] = jnp.sum(env["head_vec_grads"][i], axis=0, keepdims=True)
    for copy in split_copies(env, seq_count):
        copy.start()
    env["split_landed"][lax.axis_index("seq")] = split[...]


def full_copies(env, count):
    full = env["full"]
    return share("tp", count, lambda d: full, env["full_landed"], *env_pair(env, "full"), False)


def full_start(env, count):
    full = env["full"]
    full[...] = jnp.zeros_like(full)
    for i in range(2):
        full[i : i + 1, :] = jnp.sum(env["second_sums"][i], axis=0, keepdims=True)
        full[2 + i : 3 + i, :] = jnp.sum(env["sums"][i], axis=0, keepdims=True)
    for copy in full_copies(env, count):
        copy.start()
    env["full_landed"][lax.axis_index("tp")] = full[...]


def norm_finish(env, seq_count, count):
    full, own = env["full"], env["norm_own"].shape[1]
    me = lax.axis_index("seq")
    for copy in full_copies(env, count):
        copy.wait()
    full[...] = total_of(env["full_landed"], count)

    def piece(device):
        return pl.ds(pl.multiple_of(device * own, LANES), own)

    copies = share(
        "seq", seq_count, lambda d: full.at[:, piece(d)], env["own_landed"], *env_pair(env, "own")
    )
    env["own_landed"][me] = full[:, piece(me)]
    for copy in split_copies(env, seq_count):
        copy.wait()
    env["norm_split"][...] = total_of(env["split_landed"], seq_count)
    for copy in copies:
        copy.wait()
    env["norm_own"][...] = total_of(env["own_landed"], seq_count)


def load_pairs(env):
    copies = []
    for i, name in enumerate(("w_query", "w_key", "w_value")):
        for j in range(env[name].shape[1] // LANES):
            copy = pltpu.make_async_copy(
                env[name].at[:, j * LANES : (j + 1) * LANES],
                env["w_pairs"].at[:, (3 * j + i) * LANES : (3 * j + i + 1) * LANES],
                env["pair_sem"].at[3 * j + i],
            )
            copy.start()
            copies.append(copy)
    return copies


def line_kernel(plan, count, chunks, slack, *refs):
    env = dict(zip(plan["order"], refs, strict=True))
    finish, parts, tasks = plan["finish"], plan["parts"], plan["tasks"]
    num_task = len(tasks)
    out_ref = env["out"]
    in_a, in_b = env["in_a"], env["in_b"]
    rsa_s, rsa_r, rsb_s, rsb_r = (env[name] for name in ("rsa_s", "rsa_r", "rsb_s", "rsb_r"))
    aga_s, aga_r, agb_s, agb_r = (env[name] for name in ("aga_s", "aga_r", "agb_s", "agb_r"))
    z = lax.axis_index("tp")
    tokens, width = out_ref.shape
    half = tokens // 2
    size = half // chunks
    ahead = slack * (count - 1)
    steps = chunks + 2 * ahead
    from_first, from_last = slack * z, slack * (count - 1 - z)
    first, last = z == 0, z == count - 1
    up = jnp.minimum(z + 1, count - 1)
    down = jnp.maximum(z - 1, 0)

    loads = {
        name: pltpu.make_async_copy(env["source " + name], env[name], env["load_sem"].at[i])
        for i, name in enumerate(plan["held"])
    }
    for name in plan["held"]:
        loads[name].start()
    started = plan["start"](env) if plan["start"] else []
    seq_count = plan["seq_count"]
    axis_barrier([("tp", count)] + ([("seq", plan["seq_barrier"])] if plan["seq_barrier"] else []))
    if "sums" in env:
        env["sums"][...] = jnp.zeros_like(env["sums"])
    if seq_count:
        split_start(env, seq_count)

    def own_rows(c):
        return pl.ds(pl.multiple_of(c * size, size), size)

    def a_rows(c):
        return own_rows(c)

    def b_rows(c):
        return pl.ds(pl.multiple_of(half + c * size, size), size)

    def hop(source, target, send, recv, c, device):
        return pltpu.make_async_remote_copy(
            src_ref=source,
            dst_ref=target,
            send_sem=send.at[c],
            recv_sem=recv.at[c],
            device_id={"tp": device},
            device_id_type=MESH,
        )

    def gather_a(c):
        rows = out_ref.at[a_rows(c), :]
        return hop(rows, rows, aga_s, aga_r, c, up)

    def gather_b(c):
        rows = out_ref.at[b_rows(c), :]
        return hop(rows, rows, agb_s, agb_r, c, down)

    def reduce_a(c):
        rows = in_a.at[own_rows(c), :]
        return hop(rows, rows, rsa_s, rsa_r, c, down)

    def reduce_b(c):
        rows = in_b.at[own_rows(c), :]
        return hop(rows, rows, rsb_s, rsb_r, c, up)

    def block_start(t, offset):
        return jnp.clip((t - lax.rem(t, GROUP) - offset) * size, 0, half - GROUP * size)

    def reduce_step(t, c, offset, place, rows, landed, move, gather, starts, ends):
        here = rows(c)
        own = own_rows(c)

        def term():
            if not parts:
                return env["ready"][here, :].astype(F32)
            row = place * GROUP * size + c * size - block_start(t, offset)
            return env["part"][pl.ds(pl.multiple_of(row, size), size), :]

        @pl.when(starts)
        def _():
            landed[own, :] = term().astype(BF16)
            move(c).start()

        @pl.when(jnp.logical_not(starts))
        def _():
            move(c).wait_recv()

        @pl.when(jnp.logical_not(starts | ends))
        def _():
            landed[own, :] = (landed[own, :].astype(F32) + term()).astype(BF16)
            move(c).start()

        @pl.when(ends)
        def _():
            total = landed[own, :].astype(F32) + term()
            out_ref[here, :] = finish(total, here, own, env).astype(BF16)
            gather(c).start()

    def gather_step(c, gather, starts, ends):
        @pl.when(jnp.logical_not(starts))
        def _():
            gather(c).wait_recv()

        @pl.when(jnp.logical_not(starts | ends))
        def _():
            gather(c).start()

    def when_chunk(c, work):
        pl.when((c >= 0) & (c < chunks))(lambda: work(c))

    def make_parts(t):
        top = pl.ds(pl.multiple_of(block_start(t, from_last), size), GROUP * size)
        low = pl.ds(pl.multiple_of(half + block_start(t, from_first), size), GROUP * size)

        def columns(n, carry):
            cols = pl.ds(pl.multiple_of(n * TILE, TILE), TILE)
            total = 0.0
            for left, right in parts:
                rows = jnp.concatenate([env[left][top, :], env[left][low, :]], axis=0)
                total = total + dot(rows, env[right][cols, :], 1, 1)
            env["part"][:, cols] = total
            return carry

        lax.fori_loop(0, width // TILE, columns, 0)

    def run_task(index, tile, slot):
        kind, left, right, name = tasks[index]
        target = env[name]
        rows = pl.ds(pl.multiple_of(tile * ROWS, ROWS), ROWS)
        if kind == "weight":
            env["turned"][...] = jnp.transpose(env[left][:, rows])

        def columns(n, carry):
            cols = pl.ds(pl.multiple_of(n * TILE, TILE), TILE)
            if kind == "weight":
                value = dot(env["turned"][...], env[right][:, cols], 1, 0)
            elif kind == "keep":
                value = dot(env[left][rows, :], env[right][:, cols], 1, 0)
            else:
                value = dot(env[left][rows, :], env[right][cols, :], 1, 1)
                top = tile * ROWS < half
                mine = (first & top) | (last & jnp.logical_not(top))
                own = pl.multiple_of(lax.rem(tile * ROWS, half), ROWS)
                base = env["middle"][pl.ds(own, ROWS), cols]
                value = value + jnp.where(mine, base, 0.0)
            if kind == "keep":
                target[rows, cols] = value.astype(BF16)
            else:
                env["stage"][slot, :, cols] = value.astype(BF16)
            return carry

        lax.fori_loop(0, target.shape[1] // TILE, columns, 0)
        if kind != "keep":
            stage_copy(index, tile, slot).start()

    def stage_copy(index, tile, slot):
        target = env[tasks[index][3]]
        rows = pl.ds(pl.multiple_of(tile * ROWS, ROWS), ROWS)
        return pltpu.make_async_copy(
            env["stage"].at[slot, :, : target.shape[1]], target.at[rows, :], env["stage_sem"].at[slot]
        )

    starts_at = [0]
    for task in tasks:
        starts_at.append(starts_at[-1] + env[task[3]].shape[0] // ROWS)
    task_total = starts_at[-1]
    per_group = GROUP - 1
    staged = any(task[0] != "keep" for task in tasks)

    def step(t, carry):
        if parts:
            pl.when(lax.rem(t, GROUP) == 0)(lambda: make_parts(t))
        when_chunk(
            t - from_last,
            lambda c: reduce_step(t, c, from_last, 0, a_rows, in_a, reduce_a, gather_a, last, first),
        )
        when_chunk(
            t - from_first,
            lambda c: reduce_step(t, c, from_first, 1, b_rows, in_b, reduce_b, gather_b, first, last),
        )
        when_chunk(t - ahead - from_first, lambda c: gather_step(c, gather_a, first, last))
        when_chunk(t - ahead - from_last, lambda c: gather_step(c, gather_b, last, first))
        if num_task:
            turn = (t // GROUP) * per_group + lax.rem(t, GROUP) - 1
            free = lax.rem(t, GROUP) != 0
            slot = lax.rem(turn + per_group + 1, 2)

            @pl.when(t == 1)
            def _():
                for name in plan["late"]:
                    loads[name].wait()

            for index in range(num_task if staged else 0):
                low, high = starts_at[index] + 2, min(starts_at[index + 1] + 2, task_total)
                pl.when(free & (turn >= low) & (turn < high))(
                    lambda index=index, low=low: stage_copy(index, turn - low, slot).wait()
                )
            for index in range(num_task):
                low, high = starts_at[index], starts_at[index + 1]
                pl.when(free & (turn >= low) & (turn < high))(
                    lambda index=index, low=low: run_task(index, turn - low, slot)
                )
        if work_step:
            work_step(t)
        if seq_count:
            pl.when(t == chunks + ahead)(lambda: full_start(env, count))
        if plan["rows_done"]:
            done_a = t - ahead - from_first - (GROUP - 1)
            done_b = t - ahead - from_last - (GROUP - 1)
            has_a = (done_a >= 0) & (done_a < chunks) & (lax.rem(done_a + 64, GROUP) == 0)
            has_b = (done_b >= 0) & (done_b < chunks) & (lax.rem(done_b + 64, GROUP) == 0)

            @pl.when(has_a | has_b)
            def _():
                start = jnp.where(has_a, done_a * size, half + done_b * size)
                rows = pl.ds(pl.multiple_of(start, LANES), LANES)
                plan["rows_done"](env, rows, rows)

        return carry

    for name in plan["held"]:
        if name not in plan["late"]:
            loads[name].wait()
    for copy in started:
        copy.wait()
    if plan["before"]:
        plan["before"](env)
    work_step = None
    if plan["work"]:
        work_step, work_end, work_steps = plan["work"](env)
        assert work_steps <= steps
    lax.fori_loop(0, steps, step, 0)
    if num_task:
        assert (steps // GROUP) * per_group >= task_total
    if staged:
        assert task_total >= 2
        for turn in (task_total - 2, task_total - 1):
            index = max(i for i in range(num_task) if starts_at[i] <= turn)
            stage_copy(index, turn - starts_at[index], turn % 2).wait()
    if plan["after"]:
        plan["after"](env)
    if work_step:
        work_end()
    if seq_count:
        norm_finish(env, seq_count, count)

    def drain(c, carry):
        @pl.when(jnp.logical_not(first))
        def _():
            reduce_a(c).wait_send()
            gather_b(c).wait_send()

        @pl.when(jnp.logical_not(last))
        def _():
            reduce_b(c).wait_send()
            gather_a(c).wait_send()

        return carry

    lax.fori_loop(0, chunks, drain, 0)


def line_sum(
    finish, count, held, vecs, parts, collective_id, *, tokens, late=(), tasks=(), owns=(), sent=(),
    scratch=(), loose=(), start=None, before=None, rows_done=None, after=None, work=None,
    seq_count=0, seq_barrier=0, micros=110,
):
    names = dict(scratch)
    if parts:
        width = (held.get(parts[0][1]) if parts[0][1] in held else names[parts[0][1]]).shape[0]
    else:
        width = held["ready"].shape[1]
    half = tokens // 2
    depth = tokens if any(task[0] == "weight" for task in tasks) else LANES
    stage_width = max([shape.shape[1] for _, shape in sent] + [LANES])
    fixed = [
        ("in_a", pltpu.VMEM((half, width), BF16)),
        ("in_b", pltpu.VMEM((half, width), BF16)),
        ("part", pltpu.VMEM((2 * GROUP * half // CHUNKS if parts else 8, width), F32)),
        ("turned", pltpu.VMEM((ROWS, depth), BF16)),
        ("stage", pltpu.VMEM((2, ROWS if sent else 16, stage_width), BF16)),
        ("load_sem", pltpu.SemaphoreType.DMA((len(held),))),
        ("stage_sem", pltpu.SemaphoreType.DMA((2,))),
    ] + [
        (name, pltpu.SemaphoreType.DMA((CHUNKS,)))
        for name in ("rsa_s", "rsa_r", "rsb_s", "rsb_r", "aga_s", "aga_r", "agb_s", "agb_r")
    ]
    scratch = list(scratch) + fixed
    loose = dict(loose)
    order = (
        ["source " + name for name in held]
        + list(loose)
        + list(vecs)
        + ["out"]
        + [name for name, _ in owns]
        + [name for name, _ in sent]
        + list(held)
        + [name for name, _ in scratch]
    )
    plan = dict(
        finish=finish,
        order=order,
        held=list(held),
        parts=parts,
        late=late,
        tasks=tasks,
        start=start,
        work=work,
        seq_count=seq_count,
        seq_barrier=seq_barrier or seq_count,
        before=before,
        rows_done=rows_done,
        after=after,
    )
    whole = pl.BlockSpec(memory_space=pltpu.VMEM)
    any_space = pl.BlockSpec(memory_space=pl.ANY)
    return pl.pallas_call(
        functools.partial(line_kernel, plan, count, CHUNKS, SLACK),
        out_shape=[jax.ShapeDtypeStruct((tokens, width), BF16)]
        + [shape for _, shape in owns]
        + [shape for _, shape in sent],
        in_specs=[any_space] * (len(held) + len(loose)) + [whole] * len(vecs),
        out_specs=[whole] * (1 + len(owns)) + [any_space] * len(sent),
        scratch_shapes=[pltpu.VMEM(array.shape, array.dtype) for array in held.values()]
        + [shape for _, shape in scratch],
        compiler_params=pltpu.CompilerParams(
            collective_id=collective_id, has_side_effects=True, vmem_limit_bytes=VMEM_LIMIT
        ),
        cost_estimate=cost(micros),
    )(*held.values(), *loose.values(), *vecs.values())


def axis_barrier(counts):
    barrier = pltpu.get_barrier_semaphore()
    for axis, count in counts:
        me = lax.axis_index(axis)
        for k in range(1, count):
            pl.semaphore_signal(
                barrier, inc=1, device_id={axis: lax.rem(me + k, count)}, device_id_type=MESH
            )
    pl.semaphore_wait(barrier, sum(count - 1 for _, count in counts))


def share(axis, count, pick, landed, send_sem, recv_sem, start=True):
    me = lax.axis_index(axis)
    copies = []
    for k in range(1, count):
        device = lax.rem(me + k, count)
        copy = pltpu.make_async_remote_copy(
            src_ref=pick(device),
            dst_ref=landed.at[me],
            send_sem=send_sem.at[k],
            recv_sem=recv_sem.at[k],
            device_id={axis: device},
            device_id_type=MESH,
        )
        if start:
            copy.start()
        copies.append(copy)
    return copies


def total_of(landed, count):
    total = landed[0]
    for k in range(1, count):
        total = total + landed[k]
    return total


def matmul(left, right, left_dim, right_dim, kind=F32):
    return dot(left, right, left_dim, right_dim).astype(kind)


def rotation_tables(positions):
    half_size = HEAD // 2
    index_pairs = jnp.arange(half_size, dtype=F32)
    theta_rate = jnp.exp(-2.0 * index_pairs / HEAD * jnp.log(10000.0))
    zeta_base = (2.0 * index_pairs + 0.4 * HEAD) / (1.4 * HEAD)
    place_float = positions.astype(F32)[..., None]
    angles = place_float * theta_rate
    power = jnp.log(zeta_base) * place_float / 512.0
    return jnp.concatenate(
        [jnp.cos(angles), jnp.sin(angles), jnp.exp(power), jnp.exp(-power)], axis=-1
    )


def body(
    seq_count,
    tp_count,
    block_in,
    segment_ids,
    first_gain,
    first_bias,
    w_query,
    w_key,
    w_value,
    head_gain,
    head_bias,
    w_out,
    second_gain,
    second_bias,
    w_up,
    hidden_gain,
    hidden_bias,
    w_down,
    out_cotangent,
):
    seq_index = lax.axis_index("seq")
    row_count, span, model_width = block_in.shape
    length = span * seq_count
    tokens = row_count * span
    head_width = w_query.shape[1]
    hidden_width = w_up.shape[1] * tp_count
    groups = seq_count // row_count

    vecs = jnp.concatenate(
        [
            first_gain, first_bias, second_gain, second_bias,
            hidden_gain, hidden_bias, head_gain, head_bias,
        ]
    ).astype(F32)[None]

    seg_row = lax.dynamic_slice_in_dim(segment_ids, seq_index // groups, 1, 0)
    seg_col = seg_row.reshape(length, 1)
    earlier = jnp.sum((seg_row < seg_col).astype(jnp.int32), axis=-1)
    tables = rotation_tables(jnp.arange(length, dtype=jnp.int32) - earlier)

    block = block_in.reshape(tokens, model_width)
    cotangent = out_cotangent.reshape(tokens, model_width)

    first_act, qkv_row, o_row, lse, mixed = front(
        block,
        w_query,
        w_key,
        w_value,
        vecs,
        tables,
        seg_col,
        seg_row,
        seq_count,
        groups,
        1,
    )
    def shape_of(dims, kind=F32):
        return jax.ShapeDtypeStruct(dims, kind)

    hidden_size = hidden_gain.shape[0]
    own_shape = shape_of((tokens // 2, model_width))
    sums_shape = shape_of((2, 8, model_width))
    landed = pltpu.VMEM((tp_count, 8, tokens), F32)
    pair_sem = pltpu.SemaphoreType.DMA((tp_count,))
    (
        second_act, middle_own, head_act, head_sums, hidden_act, grad_up, hidden_vec_grads
    ) = line_sum(
        finish_middle,
        tp_count,
        dict(mixed=mixed, w_out=w_out, block=block, cotangent=cotangent, w_down=w_down, w_up=w_up),
        dict(vecs=vecs),
        (("head_act", "w_out"),),
        3,
        tokens=tokens,
        late=("cotangent", "w_down", "w_up"),
        tasks=(("keep", "cotangent", "w_down", "hidden_grad"),),
        owns=(
            ("middle", own_shape),
            ("head_act", shape_of((tokens, head_width), BF16)),
            ("head_sums", shape_of((8, tokens))),
            ("hidden_act", shape_of((tokens, hidden_size), BF16)),
            ("grad_up", shape_of((tokens, hidden_size), BF16)),
            ("hidden_vec_grads", shape_of((2, 8, hidden_size))),
        ),
        scratch=(
            ("hidden_grad", pltpu.VMEM((tokens, hidden_size), BF16)),
            ("hidden_sums", pltpu.VMEM((8, tokens), F32)),
            ("head_landed", landed),
            ("hidden_landed", landed),
            ("head_send", pair_sem),
            ("head_recv", pair_sem),
            ("hidden_send", pair_sem),
            ("hidden_recv", pair_sem),
        ),
        before=lambda env: norm_heads(env, tp_count, model_width),
        rows_done=hidden_rows,
        after=lambda env: norm_hidden(env, tp_count, hidden_width),
        micros=140,
    )

    weight_shape = shape_of((model_width, hidden_size), BF16)
    grad_middle_low, second_sums, grad_middle_own, down_part, w_down_terms, w_up_terms = line_sum(
        finish_second,
        tp_count,
        dict(
            grad_up=grad_up,
            w_up=w_up,
            cotangent=cotangent,
            middle=middle_own,
            hidden_act=hidden_act,
            w_down=w_down,
            second_act=second_act,
        ),
        dict(vecs=vecs),
        (("grad_up", "w_up"),),
        4,
        tokens=tokens,
        late=("hidden_act", "w_down", "second_act"),
        tasks=(
            ("down", "hidden_act", "w_down", "down_part"),
            ("weight", "cotangent", "hidden_act", "w_down_terms"),
            ("weight", "second_act", "grad_up", "w_up_terms"),
        ),
        owns=(("sums", sums_shape), ("middle_grad", own_shape)),
        sent=(
            ("down_part", shape_of((tokens, model_width), BF16)),
            ("w_down_terms", weight_shape),
            ("w_up_terms", weight_shape),
        ),
    )
    def scatter(grad):
        return lax.psum_scatter(grad, "seq", scatter_dimension=0, tiled=True)

    w_down_grad = scatter(w_down_terms)
    w_up_grad = scatter(w_up_terms)

    pairs = head_width // groups // LANES
    many = pltpu.SemaphoreType.DMA((pairs, seq_count))
    pair_rows = pltpu.VMEM((length, LANES), BF16)
    pair_sums = pltpu.VMEM((length, LANES), F32)
    pair_heads = pltpu.VMEM((2, length, LANES), BF16)
    block_out, grads, head_vec_grads = line_sum(
        lambda total, here, own, env: total,
        tp_count,
        dict(
            ready=down_part,
            low=grad_middle_low,
            w_out=w_out,
            mixed=mixed,
            head_sums=head_sums,
            qkv=qkv_row,
            o=o_row,
            lse=lse,
            packed=tables,
        ),
        dict(vecs=vecs, seg_col=seg_col, seg_row=seg_row),
        (),
        5,
        tokens=tokens,
        owns=(
            ("grads", shape_of((tokens, 3 * head_width), BF16)),
            ("head_vec_grads", shape_of((2, 8, head_width))),
        ),
        scratch=(
            ("do", pltpu.VMEM((tokens, head_width), BF16)),
            ("scaled", pltpu.VMEM((tokens, head_width), F32)),
            ("head_part", pltpu.VMEM((8, tokens), F32)),
            ("head_landed", landed),
            ("tables", pltpu.VMEM((4, length, LANES), F32)),
            ("do_row", pltpu.VMEM((pairs, length, LANES), BF16)),
            ("made", pltpu.VMEM((pairs, length, 3 * LANES), BF16)),
            ("bias", pltpu.VMEM((length, length), F32)),
            ("qs", pair_heads),
            ("ks", pair_rows),
            ("kms", pair_heads),
            ("dos", pair_heads),
            ("delta", pltpu.VMEM((8, length), F32)),
            ("dq", pair_sums),
            ("dk", pair_sums),
            ("dv", pair_sums),
            ("head_send", pair_sem),
            ("head_recv", pair_sem),
            ("there_send", many),
            ("there_recv", many),
            ("back_send", many),
            ("back_recv", many),
        ),
        work=lambda env: back_work(env, seq_count, tp_count, groups),
        seq_barrier=seq_count,
    )
    head_terms = head_weights(first_act, grads, grad_middle_low, head_act)
    grads, head_terms, w_down_grad = lax.optimization_barrier((grads, head_terms, w_down_grad))
    head_grads = scatter(head_terms)
    own_width = model_width // seq_count
    split_width = hidden_size + head_width
    seq_sem = pltpu.SemaphoreType.DMA((seq_count,))
    input_grad, _, norm_own, norm_split = line_sum(
        finish_first,
        tp_count,
        dict(grads=grads, block=block, middle_grad=grad_middle_own),
        dict(
            vecs=vecs,
            second_sums=second_sums,
            hidden_vec_grads=hidden_vec_grads,
            head_vec_grads=head_vec_grads,
        ),
        (("grads", "w_pairs"),),
        8,
        tokens=tokens,
        loose=dict(w_query=w_query, w_key=w_key, w_value=w_value),
        owns=(
            ("sums", sums_shape),
            ("norm_own", shape_of((8, own_width))),
            ("norm_split", shape_of((8, split_width))),
        ),
        scratch=(
            ("w_pairs", pltpu.VMEM((model_width, 3 * head_width), BF16)),
            ("pair_sem", pltpu.SemaphoreType.DMA((3 * head_width // LANES,))),
            ("split", pltpu.VMEM((8, split_width), F32)),
            ("split_landed", pltpu.VMEM((seq_count, 8, split_width), F32)),
            ("full", pltpu.VMEM((8, model_width), F32)),
            ("full_landed", pltpu.VMEM((tp_count, 8, model_width), F32)),
            ("own_landed", pltpu.VMEM((seq_count, 8, own_width), F32)),
            ("split_send", seq_sem),
            ("split_recv", seq_sem),
            ("full_send", pair_sem),
            ("full_recv", pair_sem),
            ("own_send", seq_sem),
            ("own_recv", seq_sem),
        ),
        start=load_pairs,
        seq_count=seq_count,
    )

    def head_grad(index):
        columns = [
            head_grads[:, (3 * j + index) * LANES : (3 * j + index + 1) * LANES]
            for j in range(head_width // LANES)
        ]
        return jnp.concatenate(columns, axis=1).astype(F32)

    return (
        block_out.reshape(block_in.shape),
        input_grad.reshape(block_in.shape),
        norm_own[2],
        norm_own[3],
        head_grad(0),
        head_grad(1),
        head_grad(2),
        norm_split[0, hidden_size:],
        norm_split[1, hidden_size:],
        head_grads[:, 3 * head_width :].astype(F32),
        norm_own[0],
        norm_own[1],
        w_up_grad.astype(F32),
        norm_split[0, :hidden_size],
        norm_split[1, :hidden_size],
        w_down_grad.astype(F32),
    )


def solution(mesh):
    return jax.shard_map(
        functools.partial(body, mesh.shape["seq"], mesh.shape["tp"]),
        mesh=mesh,
        in_specs=(
            P(None, "seq", None),
            P(),
            P(),
            P(),
            P(None, "tp"),
            P(None, "tp"),
            P(None, "tp"),
            P("tp"),
            P("tp"),
            P(None, "tp"),
            P(),
            P(),
            P(None, "tp"),
            P("tp"),
            P("tp"),
            P(None, "tp"),
            P(None, "seq", None),
        ),
        out_specs=(
            P(None, "seq", None),
            P(None, "seq", None),
            P("seq"),
            P("seq"),
            P("seq", "tp"),
            P("seq", "tp"),
            P("seq", "tp"),
            P("tp"),
            P("tp"),
            P("seq", "tp"),
            P("seq"),
            P("seq"),
            P("seq", "tp"),
            P("tp"),
            P("tp"),
            P("seq", "tp"),
        ),
        check_vma=False,
    )
```

```python
import functools
import math

import jax
import jax.numpy as jnp
from jax import lax
from jax.experimental import pallas as pl
from jax.experimental.pallas import tpu as pltpu
from jax.sharding import PartitionSpec as P

HEAD = 64
LANES = 128
BLOCK = 256
EPSILON = 1e-05
MASKED = -1e30
MESH = pl.DeviceIdType.MESH
F32 = jnp.float32
BF16 = jnp.bfloat16
CHUNKS = 16
SLACK = 2
GROUP = 4
ROWS = 256
TILE = 512
VMEM_LIMIT = 60 * 1024 * 1024


def cost(micros):
    return pl.CostEstimate(flops=int(micros * 1.1e9), bytes_accessed=0, transcendentals=0)


def dot(left, right, left_dim, right_dim):
    return lax.dot_general(
        left, right, (((left_dim,), (right_dim,)), ((), ())), preferred_element_type=F32
    )


def seq_signal(count):
    me = lax.axis_index("seq")
    barrier = pltpu.get_barrier_semaphore()
    for k in range(1, count):
        pl.semaphore_signal(
            barrier, inc=1, device_id={"seq": lax.rem(me + k, count)}, device_id_type=MESH
        )


def seq_wait(count):
    pl.semaphore_wait(pltpu.get_barrier_semaphore(), count - 1)


def send(source, target, send_sem, recv_sem, device):
    return pltpu.make_async_remote_copy(
        src_ref=source,
        dst_ref=target,
        send_sem=send_sem,
        recv_sem=recv_sem,
        device_id={"seq": device},
        device_id_type=MESH,
    )


def spans(index, span):
    return pl.ds(pl.multiple_of(index * span, LANES), span)


def swap_halves(values):
    lane = lax.broadcasted_iota(jnp.int32, values.shape, 1)
    return jnp.where(
        lane % HEAD < HEAD // 2,
        pltpu.roll(values, LANES - HEAD // 2, 1),
        pltpu.roll(values, HEAD // 2, 1),
    )


def head_masks(values):
    lane = lax.broadcasted_iota(jnp.int32, values.shape, 1)
    zero = jnp.zeros_like(values)
    return jnp.where(lane < HEAD, values, zero), jnp.where(lane < HEAD, zero, values)


def block_rows(index):
    return slice(index * BLOCK, (index + 1) * BLOCK)


def rotated(values, tables, first, rows):
    values = values.astype(F32)
    return values * tables[first, rows, :] + swap_halves(values) * tables[first + 1, rows, :]


def rotated_back(values, tables, first, rows):
    return values * tables[first, rows, :] - swap_halves(values) * tables[first + 1, rows, :]


def norm_parts(values):
    center = jnp.mean(values, axis=-1, keepdims=True)
    shifted = values - center
    inverse = lax.rsqrt(jnp.mean(shifted * shifted, axis=-1, keepdims=True) + EPSILON)
    return shifted * inverse, inverse


def expand_tables(packed, tables):
    quarter = HEAD // 2
    for block in range(packed.shape[0] // BLOCK):
        rows = block_rows(block)
        lane = lax.broadcasted_iota(jnp.int32, (BLOCK, LANES), 1)
        group = lane // quarter
        turns = [packed[rows, :]]
        for k in range(1, 4):
            turns.append(pltpu.roll(turns[0], k * quarter, 1))

        def spread(index):
            values = turns[(0 - index) % 4]
            for g in range(1, 4):
                values = jnp.where(group == g, turns[(g - index) % 4], values)
            return values

        cos_part = spread(0)
        sin_part = spread(1)
        sin_part = jnp.where(lane % HEAD < quarter, -sin_part, sin_part)
        for k in range(2):
            factor = spread(2 + k)
            tables[2 * k, rows, :] = cos_part * factor
            tables[2 * k + 1, rows, :] = sin_part * factor


def front_kernel(
    count, groups, x_ref, wq_ref, wk_ref, wv_ref, vecs_ref, packed_ref, segc_ref, segr_ref,
    act_ref, qkv_ref, o_ref, lse_ref, mixed_ref,
    weights, staged, tab_ref, bias, qs, ks, load_sem, send_sem, recv_sem, back_send_sem, back_recv_sem,
):
    me = lax.axis_index("seq")
    pairs, length = qkv_ref.shape[:2]
    tokens, width = x_ref.shape
    span = length // count
    blocks = length // BLOCK
    mine, row = lax.rem(me, groups), me // groups
    seq_signal(count)
    loads = []
    for j in range(pairs * groups):
        for i, source in enumerate((wq_ref, wk_ref, wv_ref)):
            copy = pltpu.make_async_copy(
                source.at[:, j * LANES : (j + 1) * LANES],
                weights.at[j, :, i * LANES : (i + 1) * LANES],
                load_sem.at[3 * j + i],
            )
            copy.start()
            loads.append(copy)

    def norm_step(r, carry):
        rows = pl.ds(pl.multiple_of(r * LANES, LANES), LANES)
        normed, _ = norm_parts(x_ref[rows, :].astype(F32))
        act_ref[rows, :] = (normed * vecs_ref[:, :width] + vecs_ref[:, width : 2 * width]).astype(BF16)
        return carry

    lax.fori_loop(0, tokens // LANES, norm_step, 0)
    for copy in loads:
        copy.wait()

    def there(p, k):
        device = lax.rem(me + k, count)
        return send(
            staged.at[lax.rem(device, groups) * pairs + p, spans(device // groups, span), :],
            qkv_ref.at[p, spans(me, span), :],
            send_sem.at[p, k],
            recv_sem.at[p, k],
            device,
        )

    def back(p, k):
        device = lax.rem(me + k, count)
        return send(
            o_ref.at[p, spans(device, span), :],
            mixed_ref.at[spans(row, span), spans(mine * pairs + p, LANES)],
            back_send_sem.at[p, k],
            back_recv_sem.at[p, k],
            device,
        )

    def project(p, carry):
        for group in range(groups):

            def rows_step(r, inner):
                rows = pl.ds(pl.multiple_of(r * BLOCK, BLOCK), BLOCK)
                j = group * pairs + p
                staged[j, rows, :] = dot(act_ref[rows, :], weights[j], 1, 0).astype(BF16)
                return inner

            lax.fori_loop(0, tokens // BLOCK, rows_step, 0)

        @pl.when(p == 0)
        def _():
            seq_wait(count)

        for k in range(1, count):
            there(p, k).start()
        qkv_ref[p, spans(me, span), :] = staged[mine * pairs + p, spans(row, span), :]
        return carry

    lax.fori_loop(0, pairs, project, 0)
    expand_tables(packed_ref, tab_ref)
    for qb in range(blocks):
        rows = block_rows(qb)
        keys = (qb + 1) * BLOCK
        same = segc_ref[rows, :] == segr_ref[:, :keys]
        query = lax.broadcasted_iota(jnp.int32, (BLOCK, keys), 0) + qb * BLOCK
        key = lax.broadcasted_iota(jnp.int32, (BLOCK, keys), 1)
        bias[rows, :keys] = jnp.where(same & (key <= query), 0.0, MASKED)

    def attend(p, carry):
        for k in range(1, count):
            there(p, k).wait_recv()
        for qb in range(blocks):
            rows = block_rows(qb)
            q = rotated(qkv_ref[p, rows, :LANES], tab_ref, 0, rows) * (HEAD**-0.5)
            q0, q1 = head_masks(q)
            qs[0, rows, :] = q0.astype(BF16)
            qs[1, rows, :] = q1.astype(BF16)
            k = rotated(qkv_ref[p, rows, LANES : 2 * LANES], tab_ref, 2, rows)
            ks[rows, :] = k.astype(BF16)
        for qb in range(blocks):
            rows = block_rows(qb)
            keys = (qb + 1) * BLOCK
            outs = []
            logs = []
            for h in range(2):
                scores = dot(qs[h, rows, :], ks[:keys, :], 1, 1) + bias[rows, :keys]
                top = jnp.max(scores, axis=1, keepdims=True)
                expo = jnp.exp(scores - top)
                total = jnp.sum(expo, axis=1, keepdims=True)
                outs.append(dot(expo.astype(BF16), qkv_ref[p, :keys, 2 * LANES :], 1, 0) / total)
                logs.append(jnp.broadcast_to(top + jnp.log(total), (BLOCK, LANES)))
            lane = lax.broadcasted_iota(jnp.int32, (BLOCK, LANES), 1)
            o_ref[p, rows, :] = jnp.where(lane < HEAD, outs[0], outs[1]).astype(BF16)
            logs_t = jnp.transpose(jnp.where(lane < HEAD, logs[0], logs[1]))
            lse_ref[p, 0:1, rows] = logs_t[0:1]
            lse_ref[p, 1:2, rows] = logs_t[HEAD : HEAD + 1]
        for k in range(1, count):
            back(p, k).start()
        mixed_ref[spans(row, span), spans(mine * pairs + p, LANES)] = o_ref[p, spans(me, span), :]
        return carry

    lax.fori_loop(0, pairs, attend, 0)

    def drain(p, carry):
        for k in range(1, count):
            there(p, k).wait_send()
            back(p, k).wait()
        return carry

    lax.fori_loop(0, pairs, drain, 0)


def front(x, w_query, w_key, w_value, vecs, tables, seg_col, seg_row, count, groups, collective_id):
    tokens, model_width = x.shape
    head_width = w_query.shape[1]
    length = seg_col.shape[0]
    pairs = head_width // groups // LANES
    whole = pl.BlockSpec(memory_space=pltpu.VMEM)
    any_space = pl.BlockSpec(memory_space=pl.ANY)
    return pl.pallas_call(
        functools.partial(front_kernel, count, groups),
        out_shape=[
            jax.ShapeDtypeStruct((tokens, model_width), BF16),
            jax.ShapeDtypeStruct((pairs, length, 3 * LANES), BF16),
            jax.ShapeDtypeStruct((pairs, length, LANES), BF16),
            jax.ShapeDtypeStruct((pairs, 8, length), F32),
            jax.ShapeDtypeStruct((tokens, head_width), BF16),
        ],
        in_specs=[whole] + [any_space] * 3 + [whole] * 4,
        out_specs=[whole] * 5,
        scratch_shapes=[
            pltpu.VMEM((pairs * groups, model_width, 3 * LANES), BF16),
            pltpu.VMEM((pairs * groups, tokens, 3 * LANES), BF16),
            pltpu.VMEM((4, length, LANES), F32),
            pltpu.VMEM((length, length), F32),
            pltpu.VMEM((2, length, LANES), BF16),
            pltpu.VMEM((length, LANES), BF16),
            pltpu.SemaphoreType.DMA((3 * pairs * groups,)),
        ]
        + [pltpu.SemaphoreType.DMA((pairs, count))] * 4,
        compiler_params=pltpu.CompilerParams(
            collective_id=collective_id, has_side_effects=True, vmem_limit_bytes=VMEM_LIMIT
        ),
        cost_estimate=cost(60),
    )(x, w_query, w_key, w_value, vecs, tables, seg_col, seg_row)


def back_work(env, count, tp_count, groups):
    low_ref, wout_ref, mixed_ref = env["low"], env["w_out"], env["mixed"]
    sums_ref, qkv_ref, o_ref, lse_ref = env["head_sums"], env["qkv"], env["o"], env["lse"]
    segc_ref, segr_ref, tab_ref, bias = env["seg_col"], env["seg_row"], env["tables"], env["bias"]
    grads_ref, vec_grads_ref = env["grads"], env["head_vec_grads"]
    do_ref, scaled, part = env["do"], env["scaled"], env["head_part"]
    do_row, made, delta = env["do_row"], env["made"], env["delta"]
    qs, ks, kms, dos, dq, dk, dv = (env[name] for name in ("qs", "ks", "kms", "dos", "dq", "dk", "dv"))
    me = lax.axis_index("seq")
    pairs, length = qkv_ref.shape[:2]
    tokens, features = low_ref.shape
    head_width = mixed_ref.shape[1]
    span = length // count
    blocks = length // BLOCK
    mine, row = lax.rem(me, groups), me // groups
    gain = head_vec(env["vecs"], head_width, 0)

    def normed_rows(rows):
        first, second = to_columns(sums_ref[:, rows], 2)
        center = first / features
        inverse = lax.rsqrt(second / features - center * center + EPSILON)
        return (mixed_ref[rows, :].astype(F32) - center) * inverse, inverse

    def head_terms(r):
        wide = pl.ds(pl.multiple_of(r * BLOCK, BLOCK), BLOCK)
        scaled[wide, :] = dot(low_ref[wide, :], wout_ref[...], 1, 0)
        for k in range(BLOCK // LANES):
            rows = row_block(r * (BLOCK // LANES) + k)
            normed, _ = normed_rows(rows)
            grad = scaled[rows, :]
            vec_grads_ref[0] += fold(grad * normed)
            vec_grads_ref[1] += fold(grad)
            grad = grad * gain
            scaled[rows, :] = grad
            part[:, rows] = to_row(
                [
                    jnp.sum(grad, axis=-1, keepdims=True),
                    jnp.sum(grad * normed, axis=-1, keepdims=True),
                ]
            )

    def part_copies(start):
        return share("tp", tp_count, lambda d: part, env["head_landed"], *env_pair(env, "head"), start)

    def head_apply(r, carry):
        rows = row_block(r)
        normed, inverse = normed_rows(rows)
        first, second = to_columns(part[:, rows], 2)
        grad = scaled[rows, :] - first / features - normed * (second / features)
        do_ref[rows, :] = (inverse * grad).astype(BF16)
        return carry

    def there(p, k):
        device = lax.rem(me + k, count)
        return send(
            do_ref.at[spans(device // groups, span), spans(lax.rem(device, groups) * pairs + p, LANES)],
            do_row.at[p, spans(me, span), :],
            env["there_send"].at[p, k],
            env["there_recv"].at[p, k],
            device,
        )

    def back(p, k):
        device = lax.rem(me + k, count)
        return send(
            made.at[p, spans(device, span), :],
            grads_ref.at[spans(row, span), spans(mine * pairs + p, 3 * LANES)],
            env["back_send"].at[p, k],
            env["back_recv"].at[p, k],
            device,
        )

    def share_out(p, carry):
        for k in range(1, count):
            there(p, k).start()
        do_row[p, spans(me, span), :] = do_ref[spans(row, span), spans(mine * pairs + p, LANES)]
        return carry

    def prepare():
        expand_tables(env["packed"], tab_ref)
        for kb in range(blocks):
            rows = block_rows(kb)
            start = kb * BLOCK
            shape = (BLOCK, length - start)
            same = segc_ref[rows, :] == segr_ref[:, start:]
            key = lax.broadcasted_iota(jnp.int32, shape, 0)
            query = lax.broadcasted_iota(jnp.int32, shape, 1)
            bias[rows, start:] = jnp.where(same & (key <= query), 0.0, MASKED)

    def pair_start(p):
        for qb in range(blocks):
            rows = block_rows(qb)
            q = rotated(qkv_ref[p, rows, :LANES], tab_ref, 0, rows) * (HEAD**-0.5)
            q0, q1 = head_masks(q)
            qs[0, rows, :] = q0.astype(BF16)
            qs[1, rows, :] = q1.astype(BF16)
            k = rotated(qkv_ref[p, rows, LANES : 2 * LANES], tab_ref, 2, rows)
            ks[rows, :] = k.astype(BF16)
            k0, k1 = head_masks(k)
            kms[0, rows, :] = k0.astype(BF16)
            kms[1, rows, :] = k1.astype(BF16)
        dq[...] = jnp.zeros_like(dq)
        dk[...] = jnp.zeros_like(dk)
        dv[...] = jnp.zeros_like(dv)
        for k in range(1, count):
            there(p, k).wait_recv()
        for qb in range(blocks):
            rows = block_rows(qb)
            grad = do_row[p, rows, :].astype(F32)
            d0, d1 = head_masks(grad)
            dos[0, rows, :] = d0.astype(BF16)
            dos[1, rows, :] = d1.astype(BF16)
            prod = jnp.transpose(grad * o_ref[p, rows, :].astype(F32))
            delta[0:1, rows] = jnp.sum(prod[:HEAD], axis=0, keepdims=True)
            delta[1:2, rows] = jnp.sum(prod[HEAD:], axis=0, keepdims=True)

    def pair_block(p, qb):
        cols = block_rows(qb)
        for kb in range(qb + 1):
            rows = block_rows(kb)
            value = qkv_ref[p, rows, 2 * LANES :]
            for h in range(2):
                scores = dot(ks[rows, :], qs[h, cols, :], 1, 1) + bias[rows, cols]
                probs = jnp.exp(scores - lse_ref[p, h : h + 1, cols])
                grads = dot(value, dos[h, cols, :], 1, 1)
                dscores = (probs * (grads - delta[h : h + 1, cols])).astype(BF16)
                dv[rows, :] += dot(probs.astype(BF16), dos[h, cols, :], 1, 0)
                dk[rows, :] += dot(dscores, qs[h, cols, :], 1, 0)
                dq[cols, :] += dot(dscores, kms[h, rows, :], 0, 0)

    def pair_end(p):
        for qb in range(blocks):
            rows = block_rows(qb)
            grad = dq[rows, :] * (HEAD**-0.5)
            made[p, rows, :LANES] = rotated_back(grad, tab_ref, 0, rows).astype(BF16)
            made[p, rows, LANES : 2 * LANES] = rotated_back(dk[rows, :], tab_ref, 2, rows).astype(BF16)
            made[p, rows, 2 * LANES :] = dv[rows, :].astype(BF16)
        for k in range(1, count):
            back(p, k).start()
        grads_ref[spans(row, span), spans(mine * pairs + p, 3 * LANES)] = made[p, spans(me, span), :]

    head_steps = tokens // BLOCK
    vec_grads_ref[...] = jnp.zeros_like(vec_grads_ref)

    def step(now):
        t = now - 1
        pl.when((t >= 0) & (t < head_steps))(lambda: head_terms(t))

        @pl.when(t == head_steps - 1)
        def _():
            part_copies(True)
            env["head_landed"][lax.axis_index("tp")] = part[...]

        pl.when(t == head_steps)(prepare)

        @pl.when(t == head_steps + 1)
        def _():
            for copy in part_copies(False):
                copy.wait()
            part[...] = total_of(env["head_landed"], tp_count)
            lax.fori_loop(0, tokens // LANES, head_apply, 0)
            lax.fori_loop(0, pairs, share_out, 0)

        turn = t - (head_steps + 3)
        p = turn // blocks
        for qb in range(blocks):

            @pl.when((turn >= 0) & (turn < pairs * blocks) & (lax.rem(turn + 8 * blocks, blocks) == qb))
            def _():
                if qb == 0:
                    pair_start(p)
                pair_block(p, qb)
                if qb == blocks - 1:
                    pair_end(p)

    def end():
        def drain(p, carry):
            for k in range(1, count):
                there(p, k).wait_send()
                back(p, k).wait()
            return carry

        lax.fori_loop(0, pairs, drain, 0)

    return step, end, 1 + head_steps + 3 + pairs * blocks


def weight_kernel(act_ref, grads_ref, low_ref, head_ref, out_ref):
    wide = grads_ref.shape[1]
    out_ref[:, :wide] = dot(jnp.transpose(act_ref[...]), grads_ref[...], 1, 0).astype(BF16)
    out_ref[:, wide:] = dot(jnp.transpose(low_ref[...]), head_ref[...], 1, 0).astype(BF16)


def head_weights(act, grads, low, head_act):
    tokens, model_width = act.shape
    wide, narrow = grads.shape[1], head_act.shape[1]
    tile = pl.BlockSpec((tokens, ROWS), lambda i: (0, i))
    return pl.pallas_call(
        weight_kernel,
        grid=(model_width // ROWS,),
        out_shape=jax.ShapeDtypeStruct((model_width, wide + narrow), BF16),
        in_specs=[
            tile,
            pl.BlockSpec((tokens, wide), lambda i: (0, 0)),
            tile,
            pl.BlockSpec((tokens, narrow), lambda i: (0, 0)),
        ],
        out_specs=pl.BlockSpec((ROWS, wide + narrow), lambda i: (i, 0)),
        compiler_params=pltpu.CompilerParams(vmem_limit_bytes=VMEM_LIMIT),
        cost_estimate=cost(10),
    )(act, grads, low, head_act)


def fold(values):
    rows, width = values.shape
    return jnp.sum(values.reshape(rows // 8, 8, width), axis=0)


def model_vec(env, index):
    width = env["out"].shape[1]
    return env["vecs"][:, index * width : (index + 1) * width]


def hidden_vec(env, index, cols=slice(None)):
    width = env["hidden_act"].shape[1]
    first = 4 * env["out"].shape[1] + index * width
    return env["vecs"][:, first : first + width][:, cols]


def head_vec(vecs_ref, width, index):
    total = vecs_ref.shape[1]
    first = total - (2 - index) * width
    return vecs_ref[:, first : first + width]


def finish_middle(total, here, own, env):
    middle = env["block"][here, :].astype(F32) + total
    env["middle"][own, :] = middle
    normed, _ = norm_parts(middle)
    return normed * model_vec(env, 2) + model_vec(env, 3)


def norm_back(base, values, total, gain, sums):
    normed, inverse = norm_parts(values)
    scaled = total * gain
    grad = base + inverse * (
        scaled
        - jnp.mean(scaled, axis=-1, keepdims=True)
        - normed * jnp.mean(scaled * normed, axis=-1, keepdims=True)
    )
    sums[0] += fold(total * normed)
    sums[1] += fold(total)
    return grad


def finish_second(total, here, own, env):
    base = env["cotangent"][here, :].astype(F32)
    grad = norm_back(base, env["middle"][own, :], total, model_vec(env, 2), env["sums"])
    env["middle_grad"][own, :] = grad
    return grad


def finish_first(total, here, own, env):
    values = env["block"][here, :].astype(F32)
    return norm_back(env["middle_grad"][own, :], values, total, model_vec(env, 0), env["sums"])


def to_row(columns):
    lane = lax.broadcasted_iota(jnp.int32, (LANES, LANES), 1)
    packed = jnp.zeros((LANES, LANES), F32)
    for i, column in enumerate(columns):
        packed = jnp.where(lane == i, column, packed)
    return jnp.transpose(packed)[:8]


def to_columns(rows, number):
    packed = jnp.transpose(jnp.concatenate([rows] * (LANES // 8), axis=0))
    return [packed[:, i : i + 1] for i in range(number)]


def row_block(r):
    return pl.ds(pl.multiple_of(r * LANES, LANES), LANES)


def tp_total(part, landed, send_sem, recv_sem, count):
    copies = share("tp", count, lambda d: part, landed, send_sem, recv_sem)
    landed[lax.axis_index("tp")] = part[...]
    for copy in copies:
        copy.wait()
    part[...] = total_of(landed, count)


def norm_heads(env, count, features):
    mixed, act, part = env["mixed"], env["head_act"], env["head_sums"]
    blocks = mixed.shape[0] // LANES

    def sums(r, carry):
        values = mixed[row_block(r), :].astype(F32)
        part[:, row_block(r)] = to_row(
            [
                jnp.sum(values, axis=-1, keepdims=True),
                jnp.sum(values * values, axis=-1, keepdims=True),
            ]
        )
        return carry

    lax.fori_loop(0, blocks, sums, 0)
    tp_total(part, env["head_landed"], env["head_send"], env["head_recv"], count)

    def apply(r, carry):
        first, second = to_columns(part[:, row_block(r)], 2)
        center = first / features
        inverse = lax.rsqrt(second / features - center * center + EPSILON)
        values = (mixed[row_block(r), :].astype(F32) - center) * inverse
        act[row_block(r), :] = (
            values * head_vec(env["vecs"], act.shape[1], 0) + head_vec(env["vecs"], act.shape[1], 1)
        ).astype(BF16)
        return carry

    lax.fori_loop(0, blocks, apply, 0)


def normal_parts(values):
    size = jnp.abs(values) * (0.5**0.5)
    bell = jnp.exp(-0.5 * values * values)
    t = 1.0 / (1.0 + 0.3275911 * size)
    poly = 1.061405429
    for factor in (-1.453152027, 1.421413741, -0.284496736, 0.254829592):
        poly = poly * t + factor
    tail = 0.5 * poly * t * bell
    return jnp.where(values < 0.0, tail, 1.0 - tail), bell * (1.0 / math.sqrt(2.0 * math.pi))


def hidden_copies(env, count, block):
    me = lax.axis_index("tp")
    send_sem, recv_sem = env_pair(env, "hidden")
    return [
        pltpu.make_async_remote_copy(
            src_ref=env["hidden_sums"].at[:, row_block(block)],
            dst_ref=env["hidden_landed"].at[me, :, row_block(block)],
            send_sem=send_sem.at[block, k],
            recv_sem=recv_sem.at[block, k],
            device_id={"tp": lax.rem(me + k, count)},
            device_id_type=MESH,
        )
        for k in range(1, count)
    ]


def hidden_rows(env, count, block):
    rows = row_block(block)
    width = env["w_up"].shape[1]
    sums = [jnp.zeros((LANES, 1), F32)] * 4
    for n in range(width // TILE):
        cols = slice(n * TILE, (n + 1) * TILE)
        values = dot(env["out"][rows, :], env["w_up"][:, cols], 1, 0)
        below, density = normal_parts(values)
        active = values * below
        env["hidden_act"][rows, cols] = active.astype(BF16)
        env["grad_up"][rows, cols] = (below + values * density).astype(BF16)
        scaled = env["hidden_grad"][rows, cols].astype(F32) * hidden_vec(env, 0, cols)
        for i, term in enumerate((active, active * active, scaled, scaled * active)):
            sums[i] = sums[i] + jnp.sum(term, axis=-1, keepdims=True)
    packed = to_row(sums)
    env["hidden_sums"][:, rows] = packed
    env["hidden_landed"][lax.axis_index("tp"), :, rows] = packed
    for copy in hidden_copies(env, count, block):
        copy.start()


def norm_hidden(env, count, features, block):
    act, slope, landed = env["hidden_act"], env["grad_up"], env["hidden_landed"]
    rows = row_block(block)
    for copy in hidden_copies(env, count, block):
        copy.wait()
    total = landed[0, :, rows]
    for k in range(1, count):
        total = total + landed[k, :, rows]
    sums = [column / features for column in to_columns(total, 4)]
    center = sums[0]
    inverse = lax.rsqrt(sums[1] - center * center + EPSILON)
    cross = inverse * (sums[3] - center * sums[2])
    for n in range(act.shape[1] // TILE):
        cols = slice(n * TILE, (n + 1) * TILE)
        gain = hidden_vec(env, 0, cols)
        normed = (act[rows, cols].astype(F32) - center) * inverse
        grad = env["hidden_grad"][rows, cols].astype(F32)
        back = inverse * (grad * gain - sums[2] - normed * cross)
        slope[rows, cols] = (back * slope[rows, cols].astype(F32)).astype(BF16)
        act[rows, cols] = (normed * gain + hidden_vec(env, 1, cols)).astype(BF16)
        env["hidden_vec_grads"][0, :, cols] += fold(grad * normed)
        env["hidden_vec_grads"][1, :, cols] += fold(grad)
    for name in ("hidden_act", "grad_up"):
        row_store(env, name, block).start()


def row_store(env, name, block):
    rows = row_block(block)
    return pltpu.make_async_copy(
        env[name].at[rows, :], env["target " + name].at[rows, :], env["sem " + name].at[block]
    )


def whole_store(env, name):
    return pltpu.make_async_copy(env[name], env["target " + name], env["sem " + name].at[0])


def split_copies(env, seq_count):
    split = env["split"]
    return share("seq", seq_count, lambda d: split, env["split_landed"], *env_pair(env, "split"), False)


def env_pair(env, name):
    return env[name + "_send"], env[name + "_recv"]


def split_start(env, seq_count):
    hidden = env["hidden_vec_grads"].shape[2]
    split = env["split"]
    split[...] = jnp.zeros_like(split)
    for i in range(2):
        split[i : i + 1, :hidden] = jnp.sum(env["hidden_vec_grads"][i], axis=0, keepdims=True)
        split[i : i + 1, hidden:] = jnp.sum(env["head_vec_grads"][i], axis=0, keepdims=True)
    for copy in split_copies(env, seq_count):
        copy.start()
    env["split_landed"][lax.axis_index("seq")] = split[...]


def full_copies(env, count):
    full = env["full"]
    return share("tp", count, lambda d: full, env["full_landed"], *env_pair(env, "full"), False)


def full_start(env, count):
    full = env["full"]
    full[...] = jnp.zeros_like(full)
    for i in range(2):
        full[i : i + 1, :] = jnp.sum(env["second_sums"][i], axis=0, keepdims=True)
        full[2 + i : 3 + i, :] = jnp.sum(env["sums"][i], axis=0, keepdims=True)
    for copy in full_copies(env, count):
        copy.start()
    env["full_landed"][lax.axis_index("tp")] = full[...]


def norm_finish(env, seq_count, count):
    full, own = env["full"], env["norm_own"].shape[1]
    me = lax.axis_index("seq")
    for copy in full_copies(env, count):
        copy.wait()
    full[...] = total_of(env["full_landed"], count)

    def piece(device):
        return pl.ds(pl.multiple_of(device * own, LANES), own)

    copies = share(
        "seq", seq_count, lambda d: full.at[:, piece(d)], env["own_landed"], *env_pair(env, "own")
    )
    env["own_landed"][me] = full[:, piece(me)]
    for copy in split_copies(env, seq_count):
        copy.wait()
    env["norm_split"][...] = total_of(env["split_landed"], seq_count)
    for copy in copies:
        copy.wait()
    env["norm_own"][...] = total_of(env["own_landed"], seq_count)


def load_pairs(env):
    copies = []
    for i, name in enumerate(("w_query", "w_key", "w_value")):
        for j in range(env[name].shape[1] // LANES):
            copy = pltpu.make_async_copy(
                env[name].at[:, j * LANES : (j + 1) * LANES],
                env["w_pairs"].at[:, (3 * j + i) * LANES : (3 * j + i + 1) * LANES],
                env["pair_sem"].at[3 * j + i],
            )
            copy.start()
            copies.append(copy)
    return copies


def line_kernel(plan, count, chunks, slack, *refs):
    env = dict(zip(plan["order"], refs, strict=True))
    finish, parts, tasks = plan["finish"], plan["parts"], plan["tasks"]
    num_task = len(tasks)
    out_ref = env["out"]
    in_a, in_b = env["in_a"], env["in_b"]
    rsa_s, rsa_r, rsb_s, rsb_r = (env[name] for name in ("rsa_s", "rsa_r", "rsb_s", "rsb_r"))
    aga_s, aga_r, agb_s, agb_r = (env[name] for name in ("aga_s", "aga_r", "agb_s", "agb_r"))
    z = lax.axis_index("tp")
    tokens, width = out_ref.shape
    half = tokens // 2
    size = half // chunks
    ahead = slack * (count - 1)
    steps = chunks + 2 * ahead
    from_first, from_last = slack * z, slack * (count - 1 - z)
    first, last = z == 0, z == count - 1
    up = jnp.minimum(z + 1, count - 1)
    down = jnp.maximum(z - 1, 0)

    loads = {
        name: pltpu.make_async_copy(env["source " + name], env[name], env["load_sem"].at[i])
        for i, name in enumerate(plan["held"])
    }
    behind = plan["late"] + plan["later"]
    for name in plan["held"]:
        if name not in behind:
            loads[name].start()
    started = plan["start"](env) if plan["start"] else []
    seq_count = plan["seq_count"]
    axis_barrier([("tp", count)] + ([("seq", plan["seq_barrier"])] if plan["seq_barrier"] else []))
    if "sums" in env:
        env["sums"][...] = jnp.zeros_like(env["sums"])
    if seq_count:
        split_start(env, seq_count)

    def own_rows(c):
        return pl.ds(pl.multiple_of(c * size, size), size)

    def a_rows(c):
        return own_rows(c)

    def b_rows(c):
        return pl.ds(pl.multiple_of(half + c * size, size), size)

    def hop(source, target, send, recv, c, device):
        return pltpu.make_async_remote_copy(
            src_ref=source,
            dst_ref=target,
            send_sem=send.at[c],
            recv_sem=recv.at[c],
            device_id={"tp": device},
            device_id_type=MESH,
        )

    def gather_a(c):
        rows = out_ref.at[a_rows(c), :]
        return hop(rows, rows, aga_s, aga_r, c, up)

    def gather_b(c):
        rows = out_ref.at[b_rows(c), :]
        return hop(rows, rows, agb_s, agb_r, c, down)

    def reduce_a(c):
        rows = in_a.at[own_rows(c), :]
        return hop(rows, rows, rsa_s, rsa_r, c, down)

    def reduce_b(c):
        rows = in_b.at[own_rows(c), :]
        return hop(rows, rows, rsb_s, rsb_r, c, up)

    def block_start(t, offset):
        return jnp.clip((t - lax.rem(t, GROUP) - offset) * size, 0, half - GROUP * size)

    def reduce_step(t, c, offset, place, rows, landed, move, gather, starts, ends):
        here = rows(c)
        own = own_rows(c)

        def term():
            if not parts:
                return env["ready"][here, :].astype(F32)
            row = place * GROUP * size + c * size - block_start(t, offset)
            return env["part"][pl.ds(pl.multiple_of(row, size), size), :]

        @pl.when(starts)
        def _():
            landed[own, :] = term().astype(BF16)
            move(c).start()

        @pl.when(jnp.logical_not(starts))
        def _():
            move(c).wait_recv()

        @pl.when(jnp.logical_not(starts | ends))
        def _():
            landed[own, :] = (landed[own, :].astype(F32) + term()).astype(BF16)
            move(c).start()

        @pl.when(ends)
        def _():
            total = landed[own, :].astype(F32) + term()
            out_ref[here, :] = finish(total, here, own, env).astype(BF16)
            gather(c).start()

    def gather_step(c, gather, starts, ends):
        @pl.when(jnp.logical_not(starts))
        def _():
            gather(c).wait_recv()

        @pl.when(jnp.logical_not(starts | ends))
        def _():
            gather(c).start()

    def when_chunk(c, work):
        pl.when((c >= 0) & (c < chunks))(lambda: work(c))

    def make_parts(t):
        top = pl.ds(pl.multiple_of(block_start(t, from_last), size), GROUP * size)
        low = pl.ds(pl.multiple_of(half + block_start(t, from_first), size), GROUP * size)

        def columns(n, carry):
            cols = pl.ds(pl.multiple_of(n * TILE, TILE), TILE)
            total = 0.0
            for left, right in parts:
                rows = jnp.concatenate([env[left][top, :], env[left][low, :]], axis=0)
                total = total + dot(rows, env[right][cols, :], 1, 1)
            env["part"][:, cols] = total
            return carry

        lax.fori_loop(0, width // TILE, columns, 0)

    def run_task(index, tile, slot):
        kind, left, right, name = tasks[index]
        target = env[name]
        rows = pl.ds(pl.multiple_of(tile * ROWS, ROWS), ROWS)
        if kind == "weight":
            env["turned"][...] = jnp.transpose(env[left][:, rows])

        def columns(n, carry):
            cols = pl.ds(pl.multiple_of(n * TILE, TILE), TILE)
            if kind == "weight":
                value = dot(env["turned"][...], env[right][:, cols], 1, 0)
            elif kind == "keep":
                value = dot(env[left][rows, :], env[right][:, cols], 1, 0)
            else:
                value = dot(env[left][rows, :], env[right][cols, :], 1, 1)
                top = tile * ROWS < half
                mine = (first & top) | (last & jnp.logical_not(top))
                own = pl.multiple_of(lax.rem(tile * ROWS, half), ROWS)
                base = env["middle"][pl.ds(own, ROWS), cols]
                value = value + jnp.where(mine, base, 0.0)
            if kind == "keep":
                target[rows, cols] = value.astype(BF16)
            else:
                env["stage"][slot, :, cols] = value.astype(BF16)
            return carry

        lax.fori_loop(0, target.shape[1] // TILE, columns, 0)
        if kind != "keep":
            stage_copy(index, tile, slot).start()

    def stage_copy(index, tile, slot):
        target = env[tasks[index][3]]
        rows = pl.ds(pl.multiple_of(tile * ROWS, ROWS), ROWS)
        return pltpu.make_async_copy(
            env["stage"].at[slot, :, : target.shape[1]], target.at[rows, :], env["stage_sem"].at[slot]
        )

    starts_at = [0]
    for task in tasks:
        starts_at.append(starts_at[-1] + env[task[3]].shape[0] // ROWS)
    task_total = starts_at[-1]
    per_group = GROUP - 1
    staged = any(task[0] != "keep" for task in tasks)

    def step(t, carry):
        if parts:
            pl.when(lax.rem(t, GROUP) == 0)(lambda: make_parts(t))
        when_chunk(
            t - from_last,
            lambda c: reduce_step(t, c, from_last, 0, a_rows, in_a, reduce_a, gather_a, last, first),
        )
        when_chunk(
            t - from_first,
            lambda c: reduce_step(t, c, from_first, 1, b_rows, in_b, reduce_b, gather_b, first, last),
        )
        when_chunk(t - ahead - from_first, lambda c: gather_step(c, gather_a, first, last))
        when_chunk(t - ahead - from_last, lambda c: gather_step(c, gather_b, last, first))
        for moment, group in ((1, plan["late"]), (4, plan["later"])):

            @pl.when(t == moment)
            def _():
                for name in group:
                    loads[name].wait()

        if num_task:
            turn = (t // GROUP) * per_group + lax.rem(t, GROUP) - 1
            free = lax.rem(t, GROUP) != 0
            slot = lax.rem(turn + per_group + 1, 2)

            for index in range(num_task if staged else 0):
                low, high = starts_at[index] + 2, min(starts_at[index + 1] + 2, task_total)
                pl.when(free & (turn >= low) & (turn < high))(
                    lambda index=index, low=low: stage_copy(index, turn - low, slot).wait()
                )
            for index in range(num_task):
                low, high = starts_at[index], starts_at[index + 1]
                pl.when(free & (turn >= low) & (turn < high))(
                    lambda index=index, low=low: run_task(index, turn - low, slot)
                )
        if work_step:
            work_step(t)
        if seq_count:
            pl.when(t == chunks + ahead)(lambda: full_start(env, count))
        for name, moment in plan["stores"].items():
            if moment == "reduced":
                pl.when(t == chunks + ahead)(lambda name=name: whole_store(env, name).start())
        done_a = t - ahead - from_first - (GROUP - 1)
        done_b = t - ahead - from_last - (GROUP - 1)
        has_a = (done_a >= 0) & (done_a < chunks) & (lax.rem(done_a + 64, GROUP) == 0)
        has_b = (done_b >= 0) & (done_b < chunks) & (lax.rem(done_b + 64, GROUP) == 0)

        @pl.when(has_a | has_b)
        def _():
            block = jnp.where(has_a, done_a // GROUP, chunks // GROUP + done_b // GROUP)
            row_store(env, "out", block).start()
            if plan["rows_done"]:
                plan["rows_done"](env, block)

        if plan["rows_late"]:
            late_a = t - 2 * ahead - (GROUP - 1) - 2

            place = lax.rem(late_a + 64, GROUP)

            @pl.when((late_a >= 0) & (place < 2))
            def _():
                plan["rows_late"](env, place * (chunks // GROUP) + late_a // GROUP)

        return carry

    for name in plan["held"]:
        if name not in behind:
            loads[name].wait()
    for copy in started:
        copy.wait()
    for name in behind:
        loads[name].start()
    if plan["before"]:
        plan["before"](env)
    for name, moment in plan["stores"].items():
        if moment == "before":
            whole_store(env, name).start()
    work_step = None
    if plan["work"]:
        work_step, work_end, work_steps = plan["work"](env)
        assert work_steps <= steps
    lax.fori_loop(0, steps, step, 0)
    if num_task:
        assert (steps // GROUP) * per_group >= task_total
    if staged:
        assert task_total >= 2
        for turn in (task_total - 2, task_total - 1):
            index = max(i for i in range(num_task) if starts_at[i] <= turn)
            stage_copy(index, turn - starts_at[index], turn % 2).wait()
    if plan["rows_late"]:
        assert chunks + 2 * ahead == steps and GROUP == 4

        def rest(place, carry):
            plan["rows_late"](env, (place + 1) * (chunks // GROUP) - 1)
            return carry

        lax.fori_loop(0, 2, rest, 0)
    if work_step:
        work_end()
    if seq_count:
        norm_finish(env, seq_count, count)

    def drain(c, carry):
        @pl.when(jnp.logical_not(first))
        def _():
            reduce_a(c).wait_send()
            gather_b(c).wait_send()

        @pl.when(jnp.logical_not(last))
        def _():
            reduce_b(c).wait_send()
            gather_a(c).wait_send()

        return carry

    lax.fori_loop(0, chunks, drain, 0)
    for name, moment in plan["stores"].items():
        if moment == "rows":
            for block in range(tokens // LANES):
                row_store(env, name, block).wait()
        else:
            whole_store(env, name).wait()


def line_sum(
    finish, count, held, vecs, parts, collective_id, *, tokens, late=(), later=(), tasks=(), owns=(),
    sent=(), stores=(), scratch=(), loose=(), start=None, before=None, rows_done=None, rows_late=None, work=None,
    seq_count=0, seq_barrier=0, micros=110,
):
    names = dict(scratch)
    if parts:
        width = (held.get(parts[0][1]) if parts[0][1] in held else names[parts[0][1]]).shape[0]
    else:
        width = held["ready"].shape[1]
    half = tokens // 2
    depth = tokens if any(task[0] == "weight" for task in tasks) else LANES
    stage_width = max([shape.shape[1] for _, shape in sent] + [LANES])
    fixed = [
        ("in_a", pltpu.VMEM((half, width), BF16)),
        ("in_b", pltpu.VMEM((half, width), BF16)),
        ("part", pltpu.VMEM((2 * GROUP * half // CHUNKS if parts else 8, width), F32)),
        ("turned", pltpu.VMEM((ROWS, depth), BF16)),
        ("stage", pltpu.VMEM((2, ROWS if sent else 16, stage_width), BF16)),
        ("load_sem", pltpu.SemaphoreType.DMA((len(held),))),
        ("stage_sem", pltpu.SemaphoreType.DMA((2,))),
    ] + [
        (name, pltpu.SemaphoreType.DMA((CHUNKS,)))
        for name in ("rsa_s", "rsa_r", "rsb_s", "rsb_r", "aga_s", "aga_r", "agb_s", "agb_r")
    ]
    assert half // CHUNKS * GROUP == LANES
    loose = dict(loose)
    stores = dict(stores, out="rows")
    shapes = [("out", jax.ShapeDtypeStruct((tokens, width), BF16))] + list(owns)
    scratch = list(scratch) + fixed
    for name, shape in shapes:
        if name in stores:
            scratch.append((name, pltpu.VMEM(shape.shape, shape.dtype)))
            number = tokens // LANES if stores[name] == "rows" else 1
            scratch.append(("sem " + name, pltpu.SemaphoreType.DMA((number,))))
    order = (
        ["source " + name for name in held]
        + list(loose)
        + list(vecs)
        + ["target " + name if name in stores else name for name, _ in shapes]
        + [name for name, _ in sent]
        + list(held)
        + [name for name, _ in scratch]
    )
    plan = dict(
        finish=finish,
        order=order,
        held=list(held),
        parts=parts,
        late=tuple(late),
        later=tuple(later),
        stores=stores,
        tasks=tasks,
        start=start,
        work=work,
        seq_count=seq_count,
        seq_barrier=seq_barrier or seq_count,
        before=before,
        rows_done=rows_done,
        rows_late=rows_late,
    )
    whole = pl.BlockSpec(memory_space=pltpu.VMEM)
    any_space = pl.BlockSpec(memory_space=pl.ANY)
    return pl.pallas_call(
        functools.partial(line_kernel, plan, count, CHUNKS, SLACK),
        out_shape=[shape for _, shape in shapes] + [shape for _, shape in sent],
        in_specs=[any_space] * (len(held) + len(loose)) + [whole] * len(vecs),
        out_specs=[any_space if name in stores else whole for name, _ in shapes]
        + [any_space] * len(sent),
        scratch_shapes=[pltpu.VMEM(array.shape, array.dtype) for array in held.values()]
        + [shape for _, shape in scratch],
        compiler_params=pltpu.CompilerParams(
            collective_id=collective_id, has_side_effects=True, vmem_limit_bytes=VMEM_LIMIT
        ),
        cost_estimate=cost(micros),
    )(*held.values(), *loose.values(), *vecs.values())


def axis_barrier(counts):
    barrier = pltpu.get_barrier_semaphore()
    for axis, count in counts:
        me = lax.axis_index(axis)
        for k in range(1, count):
            pl.semaphore_signal(
                barrier, inc=1, device_id={axis: lax.rem(me + k, count)}, device_id_type=MESH
            )
    pl.semaphore_wait(barrier, sum(count - 1 for _, count in counts))


def share(axis, count, pick, landed, send_sem, recv_sem, start=True):
    me = lax.axis_index(axis)
    copies = []
    for k in range(1, count):
        device = lax.rem(me + k, count)
        copy = pltpu.make_async_remote_copy(
            src_ref=pick(device),
            dst_ref=landed.at[me],
            send_sem=send_sem.at[k],
            recv_sem=recv_sem.at[k],
            device_id={axis: device},
            device_id_type=MESH,
        )
        if start:
            copy.start()
        copies.append(copy)
    return copies


def total_of(landed, count):
    total = landed[0]
    for k in range(1, count):
        total = total + landed[k]
    return total


def matmul(left, right, left_dim, right_dim, kind=F32):
    return dot(left, right, left_dim, right_dim).astype(kind)


def rotation_tables(positions):
    half_size = HEAD // 2
    index_pairs = jnp.arange(half_size, dtype=F32)
    theta_rate = jnp.exp(-2.0 * index_pairs / HEAD * jnp.log(10000.0))
    zeta_base = (2.0 * index_pairs + 0.4 * HEAD) / (1.4 * HEAD)
    place_float = positions.astype(F32)[..., None]
    angles = place_float * theta_rate
    power = jnp.log(zeta_base) * place_float / 512.0
    return jnp.concatenate(
        [jnp.cos(angles), jnp.sin(angles), jnp.exp(power), jnp.exp(-power)], axis=-1
    )


def body(
    seq_count,
    tp_count,
    block_in,
    segment_ids,
    first_gain,
    first_bias,
    w_query,
    w_key,
    w_value,
    head_gain,
    head_bias,
    w_out,
    second_gain,
    second_bias,
    w_up,
    hidden_gain,
    hidden_bias,
    w_down,
    out_cotangent,
):
    seq_index = lax.axis_index("seq")
    row_count, span, model_width = block_in.shape
    length = span * seq_count
    tokens = row_count * span
    head_width = w_query.shape[1]
    hidden_width = w_up.shape[1] * tp_count
    groups = seq_count // row_count

    vecs = jnp.concatenate(
        [
            first_gain, first_bias, second_gain, second_bias,
            hidden_gain, hidden_bias, head_gain, head_bias,
        ]
    ).astype(F32)[None]

    seg_row = lax.dynamic_slice_in_dim(segment_ids, seq_index // groups, 1, 0)
    seg_col = seg_row.reshape(length, 1)
    earlier = jnp.sum((seg_row < seg_col).astype(jnp.int32), axis=-1)
    tables = rotation_tables(jnp.arange(length, dtype=jnp.int32) - earlier)

    block = block_in.reshape(tokens, model_width)
    cotangent = out_cotangent.reshape(tokens, model_width)

    first_act, qkv_row, o_row, lse, mixed = front(
        block,
        w_query,
        w_key,
        w_value,
        vecs,
        tables,
        seg_col,
        seg_row,
        seq_count,
        groups,
        1,
    )
    def shape_of(dims, kind=F32):
        return jax.ShapeDtypeStruct(dims, kind)

    hidden_size = hidden_gain.shape[0]
    own_shape = shape_of((tokens // 2, model_width))
    sums_shape = shape_of((2, 8, model_width))
    landed = pltpu.VMEM((tp_count, 8, tokens), F32)
    pair_sem = pltpu.SemaphoreType.DMA((tp_count,))
    block_sem = pltpu.SemaphoreType.DMA((tokens // LANES, tp_count))

    def before_middle(env):
        env["hidden_vec_grads"][...] = jnp.zeros_like(env["hidden_vec_grads"])
        norm_heads(env, tp_count, model_width)

    (
        second_act, middle_own, head_act, head_sums, hidden_act, grad_up, hidden_vec_grads
    ) = line_sum(
        finish_middle,
        tp_count,
        dict(mixed=mixed, w_out=w_out, block=block, cotangent=cotangent, w_down=w_down, w_up=w_up),
        dict(vecs=vecs),
        (("head_act", "w_out"),),
        3,
        tokens=tokens,
        late=("cotangent", "w_down"),
        later=("block", "w_up"),
        stores=dict(middle="reduced", head_act="before", hidden_act="rows", grad_up="rows"),
        tasks=(("keep", "cotangent", "w_down", "hidden_grad"),),
        owns=(
            ("middle", own_shape),
            ("head_act", shape_of((tokens, head_width), BF16)),
            ("head_sums", shape_of((8, tokens))),
            ("hidden_act", shape_of((tokens, hidden_size), BF16)),
            ("grad_up", shape_of((tokens, hidden_size), BF16)),
            ("hidden_vec_grads", shape_of((2, 8, hidden_size))),
        ),
        scratch=(
            ("hidden_grad", pltpu.VMEM((tokens, hidden_size), BF16)),
            ("hidden_sums", pltpu.VMEM((8, tokens), F32)),
            ("head_landed", landed),
            ("hidden_landed", landed),
            ("head_send", pair_sem),
            ("head_recv", pair_sem),
            ("hidden_send", block_sem),
            ("hidden_recv", block_sem),
        ),
        before=before_middle,
        rows_done=lambda env, block: hidden_rows(env, tp_count, block),
        rows_late=lambda env, block: norm_hidden(env, tp_count, hidden_width, block),
        micros=140,
    )

    weight_shape = shape_of((model_width, hidden_size), BF16)
    grad_middle_low, second_sums, grad_middle_own, down_part, w_down_terms, w_up_terms = line_sum(
        finish_second,
        tp_count,
        dict(
            grad_up=grad_up,
            w_up=w_up,
            cotangent=cotangent,
            middle=middle_own,
            hidden_act=hidden_act,
            w_down=w_down,
            second_act=second_act,
        ),
        dict(vecs=vecs),
        (("grad_up", "w_up"),),
        4,
        tokens=tokens,
        late=("hidden_act", "w_down", "middle"),
        later=("cotangent", "second_act"),
        stores=dict(middle_grad="reduced"),
        tasks=(
            ("down", "hidden_act", "w_down", "down_part"),
            ("weight", "cotangent", "hidden_act", "w_down_terms"),
            ("weight", "second_act", "grad_up", "w_up_terms"),
        ),
        owns=(("sums", sums_shape), ("middle_grad", own_shape)),
        sent=(
            ("down_part", shape_of((tokens, model_width), BF16)),
            ("w_down_terms", weight_shape),
            ("w_up_terms", weight_shape),
        ),
    )
    def scatter(grad):
        return lax.psum_scatter(grad, "seq", scatter_dimension=0, tiled=True)

    w_down_grad = scatter(w_down_terms)
    w_up_grad = scatter(w_up_terms)

    pairs = head_width // groups // LANES
    many = pltpu.SemaphoreType.DMA((pairs, seq_count))
    pair_rows = pltpu.VMEM((length, LANES), BF16)
    pair_sums = pltpu.VMEM((length, LANES), F32)
    pair_heads = pltpu.VMEM((2, length, LANES), BF16)
    block_out, grads, head_vec_grads = line_sum(
        lambda total, here, own, env: total,
        tp_count,
        dict(
            ready=down_part,
            low=grad_middle_low,
            w_out=w_out,
            mixed=mixed,
            head_sums=head_sums,
            qkv=qkv_row,
            o=o_row,
            lse=lse,
            packed=tables,
        ),
        dict(vecs=vecs, seg_col=seg_col, seg_row=seg_row),
        (),
        5,
        tokens=tokens,
        late=("low", "w_out", "mixed", "head_sums"),
        later=("qkv", "o", "lse", "packed"),
        owns=(
            ("grads", shape_of((tokens, 3 * head_width), BF16)),
            ("head_vec_grads", shape_of((2, 8, head_width))),
        ),
        scratch=(
            ("do", pltpu.VMEM((tokens, head_width), BF16)),
            ("scaled", pltpu.VMEM((tokens, head_width), F32)),
            ("head_part", pltpu.VMEM((8, tokens), F32)),
            ("head_landed", landed),
            ("tables", pltpu.VMEM((4, length, LANES), F32)),
            ("do_row", pltpu.VMEM((pairs, length, LANES), BF16)),
            ("made", pltpu.VMEM((pairs, length, 3 * LANES), BF16)),
            ("bias", pltpu.VMEM((length, length), F32)),
            ("qs", pair_heads),
            ("ks", pair_rows),
            ("kms", pair_heads),
            ("dos", pair_heads),
            ("delta", pltpu.VMEM((8, length), F32)),
            ("dq", pair_sums),
            ("dk", pair_sums),
            ("dv", pair_sums),
            ("head_send", pair_sem),
            ("head_recv", pair_sem),
            ("there_send", many),
            ("there_recv", many),
            ("back_send", many),
            ("back_recv", many),
        ),
        work=lambda env: back_work(env, seq_count, tp_count, groups),
        seq_barrier=seq_count,
    )
    head_terms = head_weights(first_act, grads, grad_middle_low, head_act)
    grads, head_terms, w_down_grad = lax.optimization_barrier((grads, head_terms, w_down_grad))
    head_grads = scatter(head_terms)
    own_width = model_width // seq_count
    split_width = hidden_size + head_width
    seq_sem = pltpu.SemaphoreType.DMA((seq_count,))
    input_grad, _, norm_own, norm_split = line_sum(
        finish_first,
        tp_count,
        dict(grads=grads, block=block, middle_grad=grad_middle_own),
        dict(
            vecs=vecs,
            second_sums=second_sums,
            hidden_vec_grads=hidden_vec_grads,
            head_vec_grads=head_vec_grads,
        ),
        (("grads", "w_pairs"),),
        8,
        tokens=tokens,
        later=("block", "middle_grad"),
        loose=dict(w_query=w_query, w_key=w_key, w_value=w_value),
        owns=(
            ("sums", sums_shape),
            ("norm_own", shape_of((8, own_width))),
            ("norm_split", shape_of((8, split_width))),
        ),
        scratch=(
            ("w_pairs", pltpu.VMEM((model_width, 3 * head_width), BF16)),
            ("pair_sem", pltpu.SemaphoreType.DMA((3 * head_width // LANES,))),
            ("split", pltpu.VMEM((8, split_width), F32)),
            ("split_landed", pltpu.VMEM((seq_count, 8, split_width), F32)),
            ("full", pltpu.VMEM((8, model_width), F32)),
            ("full_landed", pltpu.VMEM((tp_count, 8, model_width), F32)),
            ("own_landed", pltpu.VMEM((seq_count, 8, own_width), F32)),
            ("split_send", seq_sem),
            ("split_recv", seq_sem),
            ("full_send", pair_sem),
            ("full_recv", pair_sem),
            ("own_send", seq_sem),
            ("own_recv", seq_sem),
        ),
        start=load_pairs,
        seq_count=seq_count,
    )

    def head_grad(index):
        columns = [
            head_grads[:, (3 * j + index) * LANES : (3 * j + index + 1) * LANES]
            for j in range(head_width // LANES)
        ]
        return jnp.concatenate(columns, axis=1).astype(F32)

    return (
        block_out.reshape(block_in.shape),
        input_grad.reshape(block_in.shape),
        norm_own[2],
        norm_own[3],
        head_grad(0),
        head_grad(1),
        head_grad(2),
        norm_split[0, hidden_size:],
        norm_split[1, hidden_size:],
        head_grads[:, 3 * head_width :].astype(F32),
        norm_own[0],
        norm_own[1],
        w_up_grad.astype(F32),
        norm_split[0, :hidden_size],
        norm_split[1, :hidden_size],
        w_down_grad.astype(F32),
    )


def solution(mesh):
    return jax.shard_map(
        functools.partial(body, mesh.shape["seq"], mesh.shape["tp"]),
        mesh=mesh,
        in_specs=(
            P(None, "seq", None),
            P(),
            P(),
            P(),
            P(None, "tp"),
            P(None, "tp"),
            P(None, "tp"),
            P("tp"),
            P("tp"),
            P(None, "tp"),
            P(),
            P(),
            P(None, "tp"),
            P("tp"),
            P("tp"),
            P(None, "tp"),
            P(None, "seq", None),
        ),
        out_specs=(
            P(None, "seq", None),
            P(None, "seq", None),
            P("seq"),
            P("seq"),
            P("seq", "tp"),
            P("seq", "tp"),
            P("seq", "tp"),
            P("tp"),
            P("tp"),
            P("seq", "tp"),
            P("seq"),
            P("seq"),
            P("seq", "tp"),
            P("tp"),
            P("tp"),
            P("seq", "tp"),
        ),
        check_vma=False,
    )
```

```python
import functools
import math

import jax
import jax.numpy as jnp
from jax import lax
from jax.experimental import pallas as pl
from jax.experimental.pallas import tpu as pltpu
from jax.sharding import PartitionSpec as P

HEAD = 64
LANES = 128
BLOCK = 256
EPSILON = 1e-05
MASKED = -1e30
MESH = pl.DeviceIdType.MESH
F32 = jnp.float32
BF16 = jnp.bfloat16
CHUNKS = 16
SLACK = 2
GROUP = 4
ROWS = 256
TILE = 512
VMEM_LIMIT = 60 * 1024 * 1024


def cost(micros):
    return pl.CostEstimate(flops=int(micros * 1.1e9), bytes_accessed=0, transcendentals=0)


def dot(left, right, left_dim, right_dim):
    return lax.dot_general(
        left, right, (((left_dim,), (right_dim,)), ((), ())), preferred_element_type=F32
    )


def seq_signal(count):
    me = lax.axis_index("seq")
    barrier = pltpu.get_barrier_semaphore()
    for k in range(1, count):
        pl.semaphore_signal(
            barrier, inc=1, device_id={"seq": lax.rem(me + k, count)}, device_id_type=MESH
        )


def seq_wait(count):
    pl.semaphore_wait(pltpu.get_barrier_semaphore(), count - 1)


def send(source, target, send_sem, recv_sem, device):
    return pltpu.make_async_remote_copy(
        src_ref=source,
        dst_ref=target,
        send_sem=send_sem,
        recv_sem=recv_sem,
        device_id={"seq": device},
        device_id_type=MESH,
    )


def spans(index, span):
    return pl.ds(pl.multiple_of(index * span, LANES), span)


def swap_halves(values):
    lane = lax.broadcasted_iota(jnp.int32, values.shape, 1)
    return jnp.where(
        lane % HEAD < HEAD // 2,
        pltpu.roll(values, LANES - HEAD // 2, 1),
        pltpu.roll(values, HEAD // 2, 1),
    )


def head_masks(values):
    lane = lax.broadcasted_iota(jnp.int32, values.shape, 1)
    zero = jnp.zeros_like(values)
    return jnp.where(lane < HEAD, values, zero), jnp.where(lane < HEAD, zero, values)


def block_rows(index):
    return slice(index * BLOCK, (index + 1) * BLOCK)


def rotated(values, tables, first, rows):
    values = values.astype(F32)
    return values * tables[first, rows, :] + swap_halves(values) * tables[first + 1, rows, :]


def rotated_back(values, tables, first, rows):
    return values * tables[first, rows, :] - swap_halves(values) * tables[first + 1, rows, :]


def norm_parts(values):
    center = jnp.mean(values, axis=-1, keepdims=True)
    shifted = values - center
    inverse = lax.rsqrt(jnp.mean(shifted * shifted, axis=-1, keepdims=True) + EPSILON)
    return shifted * inverse, inverse


def expand_tables(packed, tables):
    quarter = HEAD // 2
    for block in range(packed.shape[0] // BLOCK):
        rows = block_rows(block)
        lane = lax.broadcasted_iota(jnp.int32, (BLOCK, LANES), 1)
        group = lane // quarter
        turns = [packed[rows, :]]
        for k in range(1, 4):
            turns.append(pltpu.roll(turns[0], k * quarter, 1))

        def spread(index):
            values = turns[(0 - index) % 4]
            for g in range(1, 4):
                values = jnp.where(group == g, turns[(g - index) % 4], values)
            return values

        cos_part = spread(0)
        sin_part = spread(1)
        sin_part = jnp.where(lane % HEAD < quarter, -sin_part, sin_part)
        for k in range(2):
            factor = spread(2 + k)
            tables[2 * k, rows, :] = cos_part * factor
            tables[2 * k + 1, rows, :] = sin_part * factor


def front_kernel(
    count, groups, num_vec, *refs
):
    (x_ref, wq_ref, wk_ref, wv_ref, packed_ref, segc_ref, segr_ref), refs = refs[:7], refs[7:]
    pieces, refs = refs[:num_vec], refs[num_vec:]
    (
        act_out, qkv_out, o_ref, lse_ref, mixed_ref, vecs_ref, act_ref, qkv_ref,
        weights, staged, tab_ref, bias, qs, ks, load_sem, act_sem, qkv_sem, send_sem, recv_sem, back_send_sem, back_recv_sem,
    ) = refs
    me = lax.axis_index("seq")
    pairs, length = qkv_ref.shape[:2]
    tokens, width = x_ref.shape
    span = length // count
    blocks = length // BLOCK
    mine, row = lax.rem(me, groups), me // groups
    seq_signal(count)
    loads = []
    for j in range(pairs * groups):
        for i, source in enumerate((wq_ref, wk_ref, wv_ref)):
            copy = pltpu.make_async_copy(
                source.at[:, j * LANES : (j + 1) * LANES],
                weights.at[j, :, i * LANES : (i + 1) * LANES],
                load_sem.at[3 * j + i],
            )
            copy.start()
            loads.append(copy)

    place = 0
    for piece in pieces:
        for i in range(piece.shape[0]):
            vecs_ref[:, place : place + LANES] = piece[i : i + 1, :].astype(F32)
            place += LANES

    def there_to(p, device):
        k = lax.rem(device - me + count, count)
        return send(
            staged.at[lax.rem(device, groups) * pairs + p, spans(device // groups, span), :],
            qkv_ref.at[p, spans(me, span), :],
            send_sem.at[p, k],
            recv_sem.at[p, k],
            device,
        )

    def there(p, k):
        return there_to(p, lax.rem(me + k, count))

    def project_rows(p, rows):
        for group in range(groups):
            j = group * pairs + p
            staged[j, rows, :] = dot(act_ref[rows, :], weights[j], 1, 0).astype(BF16)

    for copy in loads:
        copy.wait()
    seq_wait(count)
    steps = tokens // BLOCK
    rows_each = BLOCK // span

    def first_step(b, carry):
        block = lax.rem(row // rows_each + b, steps)
        for i in range(BLOCK // LANES):
            rows = pl.ds(pl.multiple_of(block * BLOCK + i * LANES, LANES), LANES)
            normed, _ = norm_parts(x_ref[rows, :].astype(F32))
            act = normed * vecs_ref[:, :width] + vecs_ref[:, width : 2 * width]
            act_ref[rows, :] = act.astype(BF16)
        project_rows(0, pl.ds(pl.multiple_of(block * BLOCK, BLOCK), BLOCK))
        for i in range(rows_each * groups):
            device = block * rows_each * groups + i
            pl.when(device != me)(lambda device=device: there_to(0, device).start())
        return carry

    lax.fori_loop(0, steps, first_step, 0)
    act_copy = pltpu.make_async_copy(act_ref, act_out, act_sem)
    act_copy.start()

    def qkv_copy(p):
        return pltpu.make_async_copy(qkv_ref.at[p], qkv_out.at[p], qkv_sem.at[p])

    def keep_own(p):
        qkv_ref[p, spans(me, span), :] = staged[mine * pairs + p, spans(row, span), :]

    keep_own(0)

    def back(p, k):
        device = lax.rem(me + k, count)
        return send(
            o_ref.at[p, spans(device, span), :],
            mixed_ref.at[spans(row, span), spans(mine * pairs + p, LANES)],
            back_send_sem.at[p, k],
            back_recv_sem.at[p, k],
            device,
        )

    def project(p, carry):
        def rows_step(r, inner):
            project_rows(p, pl.ds(pl.multiple_of(r * BLOCK, BLOCK), BLOCK))
            return inner

        lax.fori_loop(0, steps, rows_step, 0)
        for k in range(1, count):
            there(p, k).start()
        keep_own(p)
        return carry

    lax.fori_loop(1, pairs, project, 0)
    expand_tables(packed_ref, tab_ref)
    for qb in range(blocks):
        rows = block_rows(qb)
        keys = (qb + 1) * BLOCK
        same = segc_ref[rows, :] == segr_ref[:, :keys]
        query = lax.broadcasted_iota(jnp.int32, (BLOCK, keys), 0) + qb * BLOCK
        key = lax.broadcasted_iota(jnp.int32, (BLOCK, keys), 1)
        bias[rows, :keys] = jnp.where(same & (key <= query), 0.0, MASKED)

    def attend(p, carry):
        for k in range(1, count):
            there(p, k).wait_recv()
        qkv_copy(p).start()
        for qb in range(blocks):
            rows = block_rows(qb)
            q = rotated(qkv_ref[p, rows, :LANES], tab_ref, 0, rows) * (HEAD**-0.5)
            q0, q1 = head_masks(q)
            qs[0, rows, :] = q0.astype(BF16)
            qs[1, rows, :] = q1.astype(BF16)
            k = rotated(qkv_ref[p, rows, LANES : 2 * LANES], tab_ref, 2, rows)
            ks[rows, :] = k.astype(BF16)
        for qb in range(blocks):
            rows = block_rows(qb)
            keys = (qb + 1) * BLOCK
            outs = []
            logs = []
            for h in range(2):
                scores = dot(qs[h, rows, :], ks[:keys, :], 1, 1) + bias[rows, :keys]
                top = jnp.max(scores, axis=1, keepdims=True)
                expo = jnp.exp(scores - top)
                total = jnp.sum(expo, axis=1, keepdims=True)
                outs.append(dot(expo.astype(BF16), qkv_ref[p, :keys, 2 * LANES :], 1, 0) / total)
                logs.append(jnp.broadcast_to(top + jnp.log(total), (BLOCK, LANES)))
            lane = lax.broadcasted_iota(jnp.int32, (BLOCK, LANES), 1)
            o_ref[p, rows, :] = jnp.where(lane < HEAD, outs[0], outs[1]).astype(BF16)
            logs_t = jnp.transpose(jnp.where(lane < HEAD, logs[0], logs[1]))
            lse_ref[p, 0:1, rows] = logs_t[0:1]
            lse_ref[p, 1:2, rows] = logs_t[HEAD : HEAD + 1]
        for k in range(1, count):
            back(p, k).start()
        mixed_ref[spans(row, span), spans(mine * pairs + p, LANES)] = o_ref[p, spans(me, span), :]
        return carry

    lax.fori_loop(0, pairs, attend, 0)

    def drain(p, carry):
        for k in range(1, count):
            there(p, k).wait_send()
            back(p, k).wait()
        return carry

    lax.fori_loop(0, pairs, drain, 0)
    act_copy.wait()
    for p in range(pairs):
        qkv_copy(p).wait()


def front(
    x, w_query, w_key, w_value, tables, seg_col, seg_row, vectors, count, groups, collective_id
):
    tokens, model_width = x.shape
    pieces = [vector.reshape(vector.shape[0] // LANES, LANES) for vector in vectors]
    total = sum(vector.shape[0] for vector in vectors)
    head_width = w_query.shape[1]
    length = seg_col.shape[0]
    pairs = head_width // groups // LANES
    whole = pl.BlockSpec(memory_space=pltpu.VMEM)
    any_space = pl.BlockSpec(memory_space=pl.ANY)
    return pl.pallas_call(
        functools.partial(front_kernel, count, groups, len(pieces)),
        out_shape=[
            jax.ShapeDtypeStruct((tokens, model_width), BF16),
            jax.ShapeDtypeStruct((pairs, length, 3 * LANES), BF16),
            jax.ShapeDtypeStruct((pairs, length, LANES), BF16),
            jax.ShapeDtypeStruct((pairs, 8, length), F32),
            jax.ShapeDtypeStruct((tokens, head_width), BF16),
            jax.ShapeDtypeStruct((1, total), F32),
        ],
        in_specs=[whole] + [any_space] * 3 + [whole] * (3 + len(pieces)),
        out_specs=[any_space] * 2 + [whole] * 4,
        scratch_shapes=[
            pltpu.VMEM((tokens, model_width), BF16),
            pltpu.VMEM((pairs, length, 3 * LANES), BF16),
            pltpu.VMEM((pairs * groups, model_width, 3 * LANES), BF16),
            pltpu.VMEM((pairs * groups, tokens, 3 * LANES), BF16),
            pltpu.VMEM((4, length, LANES), F32),
            pltpu.VMEM((length, length), F32),
            pltpu.VMEM((2, length, LANES), BF16),
            pltpu.VMEM((length, LANES), BF16),
            pltpu.SemaphoreType.DMA((3 * pairs * groups,)),
            pltpu.SemaphoreType.DMA,
            pltpu.SemaphoreType.DMA((pairs,)),
        ]
        + [pltpu.SemaphoreType.DMA((pairs, count))] * 4,
        compiler_params=pltpu.CompilerParams(
            collective_id=collective_id, has_side_effects=True, vmem_limit_bytes=VMEM_LIMIT
        ),
        cost_estimate=cost(60),
    )(x, w_query, w_key, w_value, tables, seg_col, seg_row, *pieces)


def back_work(env, count, tp_count, groups):
    low_ref, wout_ref, mixed_ref = env["low"], env["w_out"], env["mixed"]
    sums_ref, qkv_ref, o_ref, lse_ref = env["head_sums"], env["qkv"], env["o"], env["lse"]
    segc_ref, segr_ref, tab_ref, bias = env["seg_col"], env["seg_row"], env["tables"], env["bias"]
    grads_ref, vec_grads_ref = env["grads"], env["head_vec_grads"]
    do_ref, scaled, part = env["do"], env["scaled"], env["head_part"]
    do_row, made, delta = env["do_row"], env["made"], env["delta"]
    qs, ks, kms, dos, dq, dk, dv = (env[name] for name in ("qs", "ks", "kms", "dos", "dq", "dk", "dv"))
    me = lax.axis_index("seq")
    pairs, length = qkv_ref.shape[:2]
    tokens, features = low_ref.shape
    head_width = mixed_ref.shape[1]
    span = length // count
    blocks = length // BLOCK
    mine, row = lax.rem(me, groups), me // groups
    gain = head_vec(env["vecs"], head_width, 0)

    def normed_rows(rows):
        first, second = to_columns(sums_ref[:, rows], 2)
        center = first / features
        inverse = lax.rsqrt(second / features - center * center + EPSILON)
        return (mixed_ref[rows, :].astype(F32) - center) * inverse, inverse

    def head_terms(r):
        wide = pl.ds(pl.multiple_of(r * BLOCK, BLOCK), BLOCK)
        scaled[wide, :] = dot(low_ref[wide, :], wout_ref[...], 1, 0)
        for k in range(BLOCK // LANES):
            rows = row_block(r * (BLOCK // LANES) + k)
            normed, _ = normed_rows(rows)
            grad = scaled[rows, :]
            vec_grads_ref[0] += fold(grad * normed)
            vec_grads_ref[1] += fold(grad)
            grad = grad * gain
            scaled[rows, :] = grad
            part[:, rows] = to_row(
                [
                    jnp.sum(grad, axis=-1, keepdims=True),
                    jnp.sum(grad * normed, axis=-1, keepdims=True),
                ]
            )

    def part_copies(start):
        return share("tp", tp_count, lambda d: part, env["head_landed"], *env_pair(env, "head"), start)

    def head_apply(r, carry):
        rows = row_block(r)
        normed, inverse = normed_rows(rows)
        first, second = to_columns(part[:, rows], 2)
        grad = scaled[rows, :] - first / features - normed * (second / features)
        do_ref[rows, :] = (inverse * grad).astype(BF16)
        return carry

    def there(p, k):
        device = lax.rem(me + k, count)
        return send(
            do_ref.at[spans(device // groups, span), spans(lax.rem(device, groups) * pairs + p, LANES)],
            do_row.at[p, spans(me, span), :],
            env["there_send"].at[p, k],
            env["there_recv"].at[p, k],
            device,
        )

    def back(p, k):
        device = lax.rem(me + k, count)
        return send(
            made.at[p, spans(device, span), :],
            grads_ref.at[spans(row, span), spans(mine * pairs + p, 3 * LANES)],
            env["back_send"].at[p, k],
            env["back_recv"].at[p, k],
            device,
        )

    def share_out(p, carry):
        for k in range(1, count):
            there(p, k).start()
        do_row[p, spans(me, span), :] = do_ref[spans(row, span), spans(mine * pairs + p, LANES)]
        return carry

    def prepare():
        expand_tables(env["packed"], tab_ref)
        for kb in range(blocks):
            rows = block_rows(kb)
            start = kb * BLOCK
            shape = (BLOCK, length - start)
            same = segc_ref[rows, :] == segr_ref[:, start:]
            key = lax.broadcasted_iota(jnp.int32, shape, 0)
            query = lax.broadcasted_iota(jnp.int32, shape, 1)
            bias[rows, start:] = jnp.where(same & (key <= query), 0.0, MASKED)

    def pair_start(p):
        for qb in range(blocks):
            rows = block_rows(qb)
            q = rotated(qkv_ref[p, rows, :LANES], tab_ref, 0, rows) * (HEAD**-0.5)
            q0, q1 = head_masks(q)
            qs[0, rows, :] = q0.astype(BF16)
            qs[1, rows, :] = q1.astype(BF16)
            k = rotated(qkv_ref[p, rows, LANES : 2 * LANES], tab_ref, 2, rows)
            ks[rows, :] = k.astype(BF16)
            k0, k1 = head_masks(k)
            kms[0, rows, :] = k0.astype(BF16)
            kms[1, rows, :] = k1.astype(BF16)
        dq[...] = jnp.zeros_like(dq)
        dk[...] = jnp.zeros_like(dk)
        dv[...] = jnp.zeros_like(dv)
        for k in range(1, count):
            there(p, k).wait_recv()
        for qb in range(blocks):
            rows = block_rows(qb)
            grad = do_row[p, rows, :].astype(F32)
            d0, d1 = head_masks(grad)
            dos[0, rows, :] = d0.astype(BF16)
            dos[1, rows, :] = d1.astype(BF16)
            prod = jnp.transpose(grad * o_ref[p, rows, :].astype(F32))
            delta[0:1, rows] = jnp.sum(prod[:HEAD], axis=0, keepdims=True)
            delta[1:2, rows] = jnp.sum(prod[HEAD:], axis=0, keepdims=True)

    def pair_block(p, qb):
        cols = block_rows(qb)
        for kb in range(qb + 1):
            rows = block_rows(kb)
            value = qkv_ref[p, rows, 2 * LANES :]
            for h in range(2):
                scores = dot(ks[rows, :], qs[h, cols, :], 1, 1) + bias[rows, cols]
                probs = jnp.exp(scores - lse_ref[p, h : h + 1, cols])
                grads = dot(value, dos[h, cols, :], 1, 1)
                dscores = (probs * (grads - delta[h : h + 1, cols])).astype(BF16)
                dv[rows, :] += dot(probs.astype(BF16), dos[h, cols, :], 1, 0)
                dk[rows, :] += dot(dscores, qs[h, cols, :], 1, 0)
                dq[cols, :] += dot(dscores, kms[h, rows, :], 0, 0)

    def pair_end(p):
        for qb in range(blocks):
            rows = block_rows(qb)
            grad = dq[rows, :] * (HEAD**-0.5)
            made[p, rows, :LANES] = rotated_back(grad, tab_ref, 0, rows).astype(BF16)
            made[p, rows, LANES : 2 * LANES] = rotated_back(dk[rows, :], tab_ref, 2, rows).astype(BF16)
            made[p, rows, 2 * LANES :] = dv[rows, :].astype(BF16)
        for k in range(1, count):
            back(p, k).start()
        grads_ref[spans(row, span), spans(mine * pairs + p, 3 * LANES)] = made[p, spans(me, span), :]

    head_steps = tokens // BLOCK
    vec_grads_ref[...] = jnp.zeros_like(vec_grads_ref)

    def step(now):
        t = now - 1
        pl.when((t >= 0) & (t < head_steps))(lambda: head_terms(t))

        @pl.when(t == head_steps - 1)
        def _():
            part_copies(True)
            env["head_landed"][lax.axis_index("tp")] = part[...]

        pl.when(t == head_steps)(prepare)

        @pl.when(t == head_steps + 1)
        def _():
            for copy in part_copies(False):
                copy.wait()
            part[...] = total_of(env["head_landed"], tp_count)
            lax.fori_loop(0, tokens // LANES, head_apply, 0)
            lax.fori_loop(0, pairs, share_out, 0)

        turn = t - (head_steps + 3)
        p = turn // blocks
        for qb in range(blocks):

            @pl.when((turn >= 0) & (turn < pairs * blocks) & (lax.rem(turn + 8 * blocks, blocks) == qb))
            def _():
                if qb == 0:
                    pair_start(p)
                pair_block(p, qb)
                if qb == blocks - 1:
                    pair_end(p)

    def end():
        def drain(p, carry):
            for k in range(1, count):
                there(p, k).wait_send()
                back(p, k).wait()
            return carry

        lax.fori_loop(0, pairs, drain, 0)

    return step, end, 1 + head_steps + 3 + pairs * blocks


def weight_kernel(
    act_ref, grads_ref, low_ref, head_ref, down_ref, block_ref, out_ref, down_out, block_out
):
    wide = grads_ref.shape[1]
    out_ref[:, :wide] = dot(jnp.transpose(act_ref[...]), grads_ref[...], 1, 0).astype(BF16)
    out_ref[:, wide:] = dot(jnp.transpose(low_ref[...]), head_ref[...], 1, 0).astype(BF16)
    down_out[...] = down_ref[...].astype(F32)
    block_out[...] = block_ref[...]


def head_weights(act, grads, low, head_act, down_grad, block_out):
    tokens, model_width = act.shape
    wide, narrow = grads.shape[1], head_act.shape[1]
    steps = model_width // ROWS
    tile = pl.BlockSpec((tokens, ROWS), lambda i: (0, i))
    part = pl.BlockSpec((tokens // steps, model_width), lambda i: (i, 0))
    own_rows, own_width = down_grad.shape
    own = pl.BlockSpec((own_rows // steps, own_width), lambda i: (i, 0))
    return pl.pallas_call(
        weight_kernel,
        grid=(steps,),
        out_shape=[
            jax.ShapeDtypeStruct((model_width, wide + narrow), BF16),
            jax.ShapeDtypeStruct(down_grad.shape, F32),
            jax.ShapeDtypeStruct(block_out.shape, BF16),
        ],
        in_specs=[
            tile,
            pl.BlockSpec((tokens, wide), lambda i: (0, 0)),
            tile,
            pl.BlockSpec((tokens, narrow), lambda i: (0, 0)),
            own,
            part,
        ],
        out_specs=[pl.BlockSpec((ROWS, wide + narrow), lambda i: (i, 0)), own, part],
        compiler_params=pltpu.CompilerParams(vmem_limit_bytes=VMEM_LIMIT),
        cost_estimate=cost(10),
    )(act, grads, low, head_act, down_grad, block_out)


def last_kernel(head_ref, up_ref, grad_ref, *refs):
    outs, up_out, grad_out = refs[:4], refs[4], refs[5]
    grad_out[...] = grad_ref[...]
    width = outs[0].shape[1]
    for j in range(width // LANES):
        for i in range(3):
            start = (3 * j + i) * LANES
            outs[i][:, j * LANES : (j + 1) * LANES] = head_ref[:, start : start + LANES].astype(F32)
    outs[3][...] = head_ref[:, 3 * width :].astype(F32)
    up_out[...] = up_ref[...].astype(F32)


def last_results(head_grads, up_grad, input_grad, head_width):
    rows = head_grads.shape[0]
    steps = rows // 32

    def block(width):
        return pl.BlockSpec((rows // steps, width), lambda i: (i, 0))

    tokens, width = input_grad.shape
    part = pl.BlockSpec((tokens // steps, width), lambda i: (i, 0))
    return pl.pallas_call(
        last_kernel,
        grid=(steps,),
        out_shape=[jax.ShapeDtypeStruct((rows, head_width), F32)] * 4
        + [
            jax.ShapeDtypeStruct(up_grad.shape, F32),
            jax.ShapeDtypeStruct(input_grad.shape, BF16),
        ],
        in_specs=[block(head_grads.shape[1]), block(up_grad.shape[1]), part],
        out_specs=[block(head_width)] * 4 + [block(up_grad.shape[1]), part],
        compiler_params=pltpu.CompilerParams(vmem_limit_bytes=VMEM_LIMIT),
        cost_estimate=cost(6),
    )(head_grads, up_grad, input_grad)


def fold(values):
    rows, width = values.shape
    return jnp.sum(values.reshape(rows // 8, 8, width), axis=0)


def model_vec(env, index):
    width = env["out"].shape[1]
    return env["vecs"][:, index * width : (index + 1) * width]


def hidden_vec(env, index, cols=slice(None)):
    width = env["hidden_act"].shape[1]
    first = 4 * env["out"].shape[1] + index * width
    return env["vecs"][:, first : first + width][:, cols]


def head_vec(vecs_ref, width, index):
    total = vecs_ref.shape[1]
    first = total - (2 - index) * width
    return vecs_ref[:, first : first + width]


def finish_middle(total, here, own, env):
    middle = env["block"][here, :].astype(F32) + total
    env["middle"][own, :] = middle
    normed, _ = norm_parts(middle)
    return normed * model_vec(env, 2) + model_vec(env, 3)


def norm_back(base, values, total, gain, sums):
    normed, inverse = norm_parts(values)
    scaled = total * gain
    grad = base + inverse * (
        scaled
        - jnp.mean(scaled, axis=-1, keepdims=True)
        - normed * jnp.mean(scaled * normed, axis=-1, keepdims=True)
    )
    sums[0] += fold(total * normed)
    sums[1] += fold(total)
    return grad


def finish_second(total, here, own, env):
    base = env["cotangent"][here, :].astype(F32)
    grad = norm_back(base, env["middle"][own, :], total, model_vec(env, 2), env["sums"])
    env["middle_grad"][own, :] = grad
    return grad


def finish_first(total, here, own, env):
    values = env["block"][here, :].astype(F32)
    return norm_back(env["middle_grad"][own, :], values, total, model_vec(env, 0), env["sums"])


def to_row(columns):
    lane = lax.broadcasted_iota(jnp.int32, (LANES, LANES), 1)
    packed = jnp.zeros((LANES, LANES), F32)
    for i, column in enumerate(columns):
        packed = jnp.where(lane == i, column, packed)
    return jnp.transpose(packed)[:8]


def to_columns(rows, number):
    packed = jnp.transpose(jnp.concatenate([rows] * (LANES // 8), axis=0))
    return [packed[:, i : i + 1] for i in range(number)]


def row_block(r):
    return pl.ds(pl.multiple_of(r * LANES, LANES), LANES)


def tp_total(part, landed, send_sem, recv_sem, count):
    copies = share("tp", count, lambda d: part, landed, send_sem, recv_sem)
    landed[lax.axis_index("tp")] = part[...]
    for copy in copies:
        copy.wait()
    part[...] = total_of(landed, count)


def norm_heads(env, count, features):
    mixed, act, part = env["mixed"], env["head_act"], env["head_sums"]
    blocks = mixed.shape[0] // LANES

    def sums(r, carry):
        values = mixed[row_block(r), :].astype(F32)
        part[:, row_block(r)] = to_row(
            [
                jnp.sum(values, axis=-1, keepdims=True),
                jnp.sum(values * values, axis=-1, keepdims=True),
            ]
        )
        return carry

    lax.fori_loop(0, blocks, sums, 0)
    tp_total(part, env["head_landed"], env["head_send"], env["head_recv"], count)

    def apply(r, carry):
        first, second = to_columns(part[:, row_block(r)], 2)
        center = first / features
        inverse = lax.rsqrt(second / features - center * center + EPSILON)
        values = (mixed[row_block(r), :].astype(F32) - center) * inverse
        act[row_block(r), :] = (
            values * head_vec(env["vecs"], act.shape[1], 0) + head_vec(env["vecs"], act.shape[1], 1)
        ).astype(BF16)
        return carry

    lax.fori_loop(0, blocks, apply, 0)


def normal_parts(values):
    size = jnp.abs(values) * (0.5**0.5)
    bell = jnp.exp(-0.5 * values * values)
    t = 1.0 / (1.0 + 0.3275911 * size)
    poly = 1.061405429
    for factor in (-1.453152027, 1.421413741, -0.284496736, 0.254829592):
        poly = poly * t + factor
    tail = 0.5 * poly * t * bell
    return jnp.where(values < 0.0, tail, 1.0 - tail), bell * (1.0 / math.sqrt(2.0 * math.pi))


def hidden_copies(env, count, block):
    me = lax.axis_index("tp")
    send_sem, recv_sem = env_pair(env, "hidden")
    return [
        pltpu.make_async_remote_copy(
            src_ref=env["hidden_sums"].at[:, row_block(block)],
            dst_ref=env["hidden_landed"].at[me, :, row_block(block)],
            send_sem=send_sem.at[block, k],
            recv_sem=recv_sem.at[block, k],
            device_id={"tp": lax.rem(me + k, count)},
            device_id_type=MESH,
        )
        for k in range(1, count)
    ]


def hidden_rows(env, count, block):
    rows = row_block(block)
    width = env["w_up"].shape[1]
    sums = [jnp.zeros((LANES, 1), F32)] * 4
    for n in range(width // TILE):
        cols = slice(n * TILE, (n + 1) * TILE)
        values = dot(env["out"][rows, :], env["w_up"][:, cols], 1, 0)
        below, density = normal_parts(values)
        active = values * below
        env["hidden_act"][rows, cols] = active.astype(BF16)
        env["grad_up"][rows, cols] = (below + values * density).astype(BF16)
        scaled = env["hidden_grad"][rows, cols].astype(F32) * hidden_vec(env, 0, cols)
        for i, term in enumerate((active, active * active, scaled, scaled * active)):
            sums[i] = sums[i] + jnp.sum(term, axis=-1, keepdims=True)
    packed = to_row(sums)
    env["hidden_sums"][:, rows] = packed
    env["hidden_landed"][lax.axis_index("tp"), :, rows] = packed
    for copy in hidden_copies(env, count, block):
        copy.start()


def norm_hidden(env, count, features, block):
    act, slope, landed = env["hidden_act"], env["grad_up"], env["hidden_landed"]
    rows = row_block(block)
    for copy in hidden_copies(env, count, block):
        copy.wait()
    total = landed[0, :, rows]
    for k in range(1, count):
        total = total + landed[k, :, rows]
    sums = [column / features for column in to_columns(total, 4)]
    center = sums[0]
    inverse = lax.rsqrt(sums[1] - center * center + EPSILON)
    cross = inverse * (sums[3] - center * sums[2])
    for n in range(act.shape[1] // TILE):
        cols = slice(n * TILE, (n + 1) * TILE)
        gain = hidden_vec(env, 0, cols)
        normed = (act[rows, cols].astype(F32) - center) * inverse
        grad = env["hidden_grad"][rows, cols].astype(F32)
        back = inverse * (grad * gain - sums[2] - normed * cross)
        slope[rows, cols] = (back * slope[rows, cols].astype(F32)).astype(BF16)
        act[rows, cols] = (normed * gain + hidden_vec(env, 1, cols)).astype(BF16)
        env["hidden_vec_grads"][0, :, cols] += fold(grad * normed)
        env["hidden_vec_grads"][1, :, cols] += fold(grad)
    for name in ("hidden_act", "grad_up"):
        row_store(env, name, block).start()


def row_store(env, name, block):
    rows = row_block(block)
    return pltpu.make_async_copy(
        env[name].at[rows, :], env["target " + name].at[rows, :], env["sem " + name].at[block]
    )


def whole_store(env, name):
    return pltpu.make_async_copy(env[name], env["target " + name], env["sem " + name].at[0])


def split_copies(env, seq_count):
    split = env["split"]
    return share("seq", seq_count, lambda d: split, env["split_landed"], *env_pair(env, "split"), False)


def env_pair(env, name):
    return env[name + "_send"], env[name + "_recv"]


def split_start(env, seq_count):
    hidden = env["hidden_vec_grads"].shape[2]
    split = env["split"]
    split[...] = jnp.zeros_like(split)
    for i in range(2):
        split[i : i + 1, :hidden] = jnp.sum(env["hidden_vec_grads"][i], axis=0, keepdims=True)
        split[i : i + 1, hidden:] = jnp.sum(env["head_vec_grads"][i], axis=0, keepdims=True)
    for copy in split_copies(env, seq_count):
        copy.start()
    env["split_landed"][lax.axis_index("seq")] = split[...]


def full_copies(env, count):
    full = env["full"]
    return share("tp", count, lambda d: full, env["full_landed"], *env_pair(env, "full"), False)


def full_start(env, count):
    full = env["full"]
    full[...] = jnp.zeros_like(full)
    for i in range(2):
        full[i : i + 1, :] = jnp.sum(env["second_sums"][i], axis=0, keepdims=True)
        full[2 + i : 3 + i, :] = jnp.sum(env["sums"][i], axis=0, keepdims=True)
    for copy in full_copies(env, count):
        copy.start()
    env["full_landed"][lax.axis_index("tp")] = full[...]


def norm_finish(env, seq_count, count):
    full, own = env["full"], env["norm_own"].shape[1]
    me = lax.axis_index("seq")
    for copy in full_copies(env, count):
        copy.wait()
    full[...] = total_of(env["full_landed"], count)

    def piece(device):
        return pl.ds(pl.multiple_of(device * own, LANES), own)

    copies = share(
        "seq", seq_count, lambda d: full.at[:, piece(d)], env["own_landed"], *env_pair(env, "own")
    )
    env["own_landed"][me] = full[:, piece(me)]
    for copy in split_copies(env, seq_count):
        copy.wait()
    env["norm_split"][...] = total_of(env["split_landed"], seq_count)
    for copy in copies:
        copy.wait()
    env["norm_own"][...] = total_of(env["own_landed"], seq_count)


def load_pairs(env):
    copies = []
    for i, name in enumerate(("w_query", "w_key", "w_value")):
        for j in range(env[name].shape[1] // LANES):
            copy = pltpu.make_async_copy(
                env[name].at[:, j * LANES : (j + 1) * LANES],
                env["w_pairs"].at[:, (3 * j + i) * LANES : (3 * j + i + 1) * LANES],
                env["pair_sem"].at[3 * j + i],
            )
            copy.start()
            copies.append(copy)
    return copies


def line_kernel(plan, count, chunks, slack, *refs):
    env = dict(zip(plan["order"], refs, strict=True))
    finish, parts, tasks = plan["finish"], plan["parts"], plan["tasks"]
    num_task = len(tasks)
    out_ref = env["out"]
    in_a, in_b = env["in_a"], env["in_b"]
    rsa_s, rsa_r, rsb_s, rsb_r = (env[name] for name in ("rsa_s", "rsa_r", "rsb_s", "rsb_r"))
    aga_s, aga_r, agb_s, agb_r = (env[name] for name in ("aga_s", "aga_r", "agb_s", "agb_r"))
    z = lax.axis_index("tp")
    tokens, width = out_ref.shape
    half = tokens // 2
    size = half // chunks
    ahead = slack * (count - 1)
    steps = chunks + 2 * ahead
    from_first, from_last = slack * z, slack * (count - 1 - z)
    first, last = z == 0, z == count - 1
    up = jnp.minimum(z + 1, count - 1)
    down = jnp.maximum(z - 1, 0)

    loads = {
        name: pltpu.make_async_copy(env["source " + name], env[name], env["load_sem"].at[i])
        for i, name in enumerate(plan["held"])
    }
    behind = plan["late"] + plan["later"]
    for name in plan["held"]:
        if name not in behind:
            loads[name].start()
    started = plan["start"](env) if plan["start"] else []
    seq_count = plan["seq_count"]
    axis_barrier([("tp", count)] + ([("seq", plan["seq_barrier"])] if plan["seq_barrier"] else []))
    if "sums" in env:
        env["sums"][...] = jnp.zeros_like(env["sums"])
    if seq_count:
        split_start(env, seq_count)

    def own_rows(c):
        return pl.ds(pl.multiple_of(c * size, size), size)

    def a_rows(c):
        return own_rows(c)

    def b_rows(c):
        return pl.ds(pl.multiple_of(half + c * size, size), size)

    def hop(source, target, send, recv, c, device):
        return pltpu.make_async_remote_copy(
            src_ref=source,
            dst_ref=target,
            send_sem=send.at[c],
            recv_sem=recv.at[c],
            device_id={"tp": device},
            device_id_type=MESH,
        )

    def gather_a(c):
        rows = out_ref.at[a_rows(c), :]
        return hop(rows, rows, aga_s, aga_r, c, up)

    def gather_b(c):
        rows = out_ref.at[b_rows(c), :]
        return hop(rows, rows, agb_s, agb_r, c, down)

    def reduce_a(c):
        rows = in_a.at[own_rows(c), :]
        return hop(rows, rows, rsa_s, rsa_r, c, down)

    def reduce_b(c):
        rows = in_b.at[own_rows(c), :]
        return hop(rows, rows, rsb_s, rsb_r, c, up)

    def block_start(t, offset):
        return jnp.clip((t - lax.rem(t, GROUP) - offset) * size, 0, half - GROUP * size)

    def reduce_step(t, c, offset, place, rows, landed, move, gather, starts, ends):
        here = rows(c)
        own = own_rows(c)

        def term():
            if not parts:
                return env["ready"][here, :].astype(F32)
            row = place * GROUP * size + c * size - block_start(t, offset)
            return env["part"][pl.ds(pl.multiple_of(row, size), size), :]

        @pl.when(starts)
        def _():
            landed[own, :] = term().astype(BF16)
            move(c).start()

        @pl.when(jnp.logical_not(starts))
        def _():
            move(c).wait_recv()

        @pl.when(jnp.logical_not(starts | ends))
        def _():
            landed[own, :] = (landed[own, :].astype(F32) + term()).astype(BF16)
            move(c).start()

        @pl.when(ends)
        def _():
            total = landed[own, :].astype(F32) + term()
            out_ref[here, :] = finish(total, here, own, env).astype(BF16)
            gather(c).start()

    def gather_step(c, gather, starts, ends):
        @pl.when(jnp.logical_not(starts))
        def _():
            gather(c).wait_recv()

        @pl.when(jnp.logical_not(starts | ends))
        def _():
            gather(c).start()

    def when_chunk(c, work):
        pl.when((c >= 0) & (c < chunks))(lambda: work(c))

    def make_parts(t):
        top = pl.ds(pl.multiple_of(block_start(t, from_last), size), GROUP * size)
        low = pl.ds(pl.multiple_of(half + block_start(t, from_first), size), GROUP * size)

        def columns(n, carry):
            cols = pl.ds(pl.multiple_of(n * TILE, TILE), TILE)
            total = 0.0
            for left, right in parts:
                rows = jnp.concatenate([env[left][top, :], env[left][low, :]], axis=0)
                total = total + dot(rows, env[right][cols, :], 1, 1)
            env["part"][:, cols] = total
            return carry

        lax.fori_loop(0, width // TILE, columns, 0)

    def run_task(index, tile, slot):
        kind, left, right, name = tasks[index]
        target = env[name]
        rows = pl.ds(pl.multiple_of(tile * ROWS, ROWS), ROWS)
        if kind == "weight":
            env["turned"][...] = jnp.transpose(env[left][:, rows])

        def columns(n, carry):
            cols = pl.ds(pl.multiple_of(n * TILE, TILE), TILE)
            if kind == "weight":
                value = dot(env["turned"][...], env[right][:, cols], 1, 0)
            elif kind == "keep":
                value = dot(env[left][rows, :], env[right][:, cols], 1, 0)
            else:
                value = dot(env[left][rows, :], env[right][cols, :], 1, 1)
                top = tile * ROWS < half
                mine = (first & top) | (last & jnp.logical_not(top))
                own = pl.multiple_of(lax.rem(tile * ROWS, half), ROWS)
                base = env["middle"][pl.ds(own, ROWS), cols]
                value = value + jnp.where(mine, base, 0.0)
            if kind == "keep":
                target[rows, cols] = value.astype(BF16)
            else:
                env["stage"][slot, :, cols] = value.astype(BF16)
            return carry

        lax.fori_loop(0, target.shape[1] // TILE, columns, 0)
        if kind != "keep":
            stage_copy(index, tile, slot).start()

    def stage_copy(index, tile, slot):
        target = env[tasks[index][3]]
        rows = pl.ds(pl.multiple_of(tile * ROWS, ROWS), ROWS)
        return pltpu.make_async_copy(
            env["stage"].at[slot, :, : target.shape[1]], target.at[rows, :], env["stage_sem"].at[slot]
        )

    starts_at = [0]
    for task in tasks:
        starts_at.append(starts_at[-1] + env[task[3]].shape[0] // ROWS)
    task_total = starts_at[-1]
    per_group = GROUP - 1
    staged = any(task[0] != "keep" for task in tasks)

    def step(t, carry):
        if parts:
            pl.when(lax.rem(t, GROUP) == 0)(lambda: make_parts(t))
        when_chunk(
            t - from_last,
            lambda c: reduce_step(t, c, from_last, 0, a_rows, in_a, reduce_a, gather_a, last, first),
        )
        when_chunk(
            t - from_first,
            lambda c: reduce_step(t, c, from_first, 1, b_rows, in_b, reduce_b, gather_b, first, last),
        )
        when_chunk(t - ahead - from_first, lambda c: gather_step(c, gather_a, first, last))
        when_chunk(t - ahead - from_last, lambda c: gather_step(c, gather_b, last, first))
        for moment, group in ((1, plan["late"]), (4, plan["later"])):

            @pl.when(t == moment)
            def _():
                for name in group:
                    loads[name].wait()

        if num_task:
            turn = (t // GROUP) * per_group + lax.rem(t, GROUP) - 1
            free = lax.rem(t, GROUP) != 0
            slot = lax.rem(turn + per_group + 1, 2)

            for index in range(num_task if staged else 0):
                low, high = starts_at[index] + 2, min(starts_at[index + 1] + 2, task_total)
                pl.when(free & (turn >= low) & (turn < high))(
                    lambda index=index, low=low: stage_copy(index, turn - low, slot).wait()
                )
            for index in range(num_task):
                low, high = starts_at[index], starts_at[index + 1]
                pl.when(free & (turn >= low) & (turn < high))(
                    lambda index=index, low=low: run_task(index, turn - low, slot)
                )
        if work_step:
            work_step(t)
        if seq_count:
            pl.when(t == chunks + ahead)(lambda: full_start(env, count))
        for name, moment in plan["stores"].items():
            if moment == "reduced":
                pl.when(t == chunks + ahead)(lambda name=name: whole_store(env, name).start())
        done_a = t - ahead - from_first - (GROUP - 1)
        done_b = t - ahead - from_last - (GROUP - 1)
        has_a = (done_a >= 0) & (done_a < chunks) & (lax.rem(done_a + 64, GROUP) == 0)
        has_b = (done_b >= 0) & (done_b < chunks) & (lax.rem(done_b + 64, GROUP) == 0)

        @pl.when(has_a | has_b)
        def _():
            block = jnp.where(has_a, done_a // GROUP, chunks // GROUP + done_b // GROUP)
            row_store(env, "out", block).start()
            if plan["rows_done"]:
                plan["rows_done"](env, block)

        if plan["rows_late"]:
            late_a = t - 2 * ahead - (GROUP - 1) - 2

            place = lax.rem(late_a + 64, GROUP)

            @pl.when((late_a >= 0) & (place < 2))
            def _():
                plan["rows_late"](env, place * (chunks // GROUP) + late_a // GROUP)

        return carry

    for name in plan["held"]:
        if name not in behind:
            loads[name].wait()
    for copy in started:
        copy.wait()
    for name in behind:
        loads[name].start()
    if plan["before"]:
        plan["before"](env)
    for name, moment in plan["stores"].items():
        if moment == "before":
            whole_store(env, name).start()
    work_step = None
    if plan["work"]:
        work_step, work_end, work_steps = plan["work"](env)
        assert work_steps <= steps
    lax.fori_loop(0, steps, step, 0)
    if num_task:
        assert (steps // GROUP) * per_group >= task_total
    if staged:
        assert task_total >= 2
        for turn in (task_total - 2, task_total - 1):
            index = max(i for i in range(num_task) if starts_at[i] <= turn)
            stage_copy(index, turn - starts_at[index], turn % 2).wait()
    if plan["rows_late"]:
        assert chunks + 2 * ahead == steps and GROUP == 4

        def rest(place, carry):
            plan["rows_late"](env, (place + 1) * (chunks // GROUP) - 1)
            return carry

        lax.fori_loop(0, 2, rest, 0)
    if work_step:
        work_end()
    if seq_count:
        norm_finish(env, seq_count, count)

    def drain(c, carry):
        @pl.when(jnp.logical_not(first))
        def _():
            reduce_a(c).wait_send()
            gather_b(c).wait_send()

        @pl.when(jnp.logical_not(last))
        def _():
            reduce_b(c).wait_send()
            gather_a(c).wait_send()

        return carry

    lax.fori_loop(0, chunks, drain, 0)
    for name, moment in plan["stores"].items():
        if moment == "rows":
            for block in range(tokens // LANES):
                row_store(env, name, block).wait()
        else:
            whole_store(env, name).wait()


def line_sum(
    finish, count, held, vecs, parts, collective_id, *, tokens, late=(), later=(), tasks=(), owns=(),
    sent=(), stores=(), scratch=(), loose=(), start=None, before=None, rows_done=None, rows_late=None, work=None,
    seq_count=0, seq_barrier=0, micros=110,
):
    names = dict(scratch)
    if parts:
        width = (held.get(parts[0][1]) if parts[0][1] in held else names[parts[0][1]]).shape[0]
    else:
        width = held["ready"].shape[1]
    half = tokens // 2
    depth = tokens if any(task[0] == "weight" for task in tasks) else LANES
    stage_width = max([shape.shape[1] for _, shape in sent] + [LANES])
    fixed = [
        ("in_a", pltpu.VMEM((half, width), BF16)),
        ("in_b", pltpu.VMEM((half, width), BF16)),
        ("part", pltpu.VMEM((2 * GROUP * half // CHUNKS if parts else 8, width), F32)),
        ("turned", pltpu.VMEM((ROWS, depth), BF16)),
        ("stage", pltpu.VMEM((2, ROWS if sent else 16, stage_width), BF16)),
        ("load_sem", pltpu.SemaphoreType.DMA((len(held),))),
        ("stage_sem", pltpu.SemaphoreType.DMA((2,))),
    ] + [
        (name, pltpu.SemaphoreType.DMA((CHUNKS,)))
        for name in ("rsa_s", "rsa_r", "rsb_s", "rsb_r", "aga_s", "aga_r", "agb_s", "agb_r")
    ]
    assert half // CHUNKS * GROUP == LANES
    loose = dict(loose)
    stores = dict(stores, out="rows")
    shapes = [("out", jax.ShapeDtypeStruct((tokens, width), BF16))] + list(owns)
    scratch = list(scratch) + fixed
    for name, shape in shapes:
        if name in stores:
            scratch.append((name, pltpu.VMEM(shape.shape, shape.dtype)))
            number = tokens // LANES if stores[name] == "rows" else 1
            scratch.append(("sem " + name, pltpu.SemaphoreType.DMA((number,))))
    order = (
        ["source " + name for name in held]
        + list(loose)
        + list(vecs)
        + ["target " + name if name in stores else name for name, _ in shapes]
        + [name for name, _ in sent]
        + list(held)
        + [name for name, _ in scratch]
    )
    plan = dict(
        finish=finish,
        order=order,
        held=list(held),
        parts=parts,
        late=tuple(late),
        later=tuple(later),
        stores=stores,
        tasks=tasks,
        start=start,
        work=work,
        seq_count=seq_count,
        seq_barrier=seq_barrier or seq_count,
        before=before,
        rows_done=rows_done,
        rows_late=rows_late,
    )
    whole = pl.BlockSpec(memory_space=pltpu.VMEM)
    any_space = pl.BlockSpec(memory_space=pl.ANY)
    return pl.pallas_call(
        functools.partial(line_kernel, plan, count, CHUNKS, SLACK),
        out_shape=[shape for _, shape in shapes] + [shape for _, shape in sent],
        in_specs=[any_space] * (len(held) + len(loose)) + [whole] * len(vecs),
        out_specs=[any_space if name in stores else whole for name, _ in shapes]
        + [any_space] * len(sent),
        scratch_shapes=[pltpu.VMEM(array.shape, array.dtype) for array in held.values()]
        + [shape for _, shape in scratch],
        compiler_params=pltpu.CompilerParams(
            collective_id=collective_id, has_side_effects=True, vmem_limit_bytes=VMEM_LIMIT
        ),
        cost_estimate=cost(micros),
    )(*held.values(), *loose.values(), *vecs.values())


def axis_barrier(counts):
    barrier = pltpu.get_barrier_semaphore()
    for axis, count in counts:
        me = lax.axis_index(axis)
        for k in range(1, count):
            pl.semaphore_signal(
                barrier, inc=1, device_id={axis: lax.rem(me + k, count)}, device_id_type=MESH
            )
    pl.semaphore_wait(barrier, sum(count - 1 for _, count in counts))


def share(axis, count, pick, landed, send_sem, recv_sem, start=True):
    me = lax.axis_index(axis)
    copies = []
    for k in range(1, count):
        device = lax.rem(me + k, count)
        copy = pltpu.make_async_remote_copy(
            src_ref=pick(device),
            dst_ref=landed.at[me],
            send_sem=send_sem.at[k],
            recv_sem=recv_sem.at[k],
            device_id={axis: device},
            device_id_type=MESH,
        )
        if start:
            copy.start()
        copies.append(copy)
    return copies


def total_of(landed, count):
    total = landed[0]
    for k in range(1, count):
        total = total + landed[k]
    return total


def matmul(left, right, left_dim, right_dim, kind=F32):
    return dot(left, right, left_dim, right_dim).astype(kind)


def rotation_tables(positions):
    half_size = HEAD // 2
    index_pairs = jnp.arange(half_size, dtype=F32)
    theta_rate = jnp.exp(-2.0 * index_pairs / HEAD * jnp.log(10000.0))
    zeta_base = (2.0 * index_pairs + 0.4 * HEAD) / (1.4 * HEAD)
    place_float = positions.astype(F32)[..., None]
    angles = place_float * theta_rate
    power = jnp.log(zeta_base) * place_float / 512.0
    return jnp.concatenate(
        [jnp.cos(angles), jnp.sin(angles), jnp.exp(power), jnp.exp(-power)], axis=-1
    )


def body(
    seq_count,
    tp_count,
    block_in,
    segment_ids,
    first_gain,
    first_bias,
    w_query,
    w_key,
    w_value,
    head_gain,
    head_bias,
    w_out,
    second_gain,
    second_bias,
    w_up,
    hidden_gain,
    hidden_bias,
    w_down,
    out_cotangent,
):
    seq_index = lax.axis_index("seq")
    row_count, span, model_width = block_in.shape
    length = span * seq_count
    tokens = row_count * span
    head_width = w_query.shape[1]
    hidden_width = w_up.shape[1] * tp_count
    groups = seq_count // row_count

    seg_row = lax.dynamic_slice_in_dim(segment_ids, seq_index // groups, 1, 0)
    seg_col = seg_row.reshape(length, 1)
    earlier = jnp.sum((seg_row < seg_col).astype(jnp.int32), axis=-1)
    tables = rotation_tables(jnp.arange(length, dtype=jnp.int32) - earlier)

    block = block_in.reshape(tokens, model_width)
    cotangent = out_cotangent.reshape(tokens, model_width)

    first_act, qkv_row, o_row, lse, mixed, vecs = front(
        block,
        w_query,
        w_key,
        w_value,
        tables,
        seg_col,
        seg_row,
        (
            first_gain, first_bias, second_gain, second_bias,
            hidden_gain, hidden_bias, head_gain, head_bias,
        ),
        seq_count,
        groups,
        1,
    )
    def shape_of(dims, kind=F32):
        return jax.ShapeDtypeStruct(dims, kind)

    hidden_size = hidden_gain.shape[0]
    own_shape = shape_of((tokens // 2, model_width))
    sums_shape = shape_of((2, 8, model_width))
    landed = pltpu.VMEM((tp_count, 8, tokens), F32)
    pair_sem = pltpu.SemaphoreType.DMA((tp_count,))
    block_sem = pltpu.SemaphoreType.DMA((tokens // LANES, tp_count))

    def before_middle(env):
        env["hidden_vec_grads"][...] = jnp.zeros_like(env["hidden_vec_grads"])
        norm_heads(env, tp_count, model_width)

    (
        second_act, middle_own, head_act, head_sums, hidden_act, grad_up, hidden_vec_grads
    ) = line_sum(
        finish_middle,
        tp_count,
        dict(mixed=mixed, w_out=w_out, block=block, cotangent=cotangent, w_down=w_down, w_up=w_up),
        dict(vecs=vecs),
        (("head_act", "w_out"),),
        3,
        tokens=tokens,
        late=("cotangent", "w_down"),
        later=("block", "w_up"),
        stores=dict(middle="reduced", head_act="before", hidden_act="rows", grad_up="rows"),
        tasks=(("keep", "cotangent", "w_down", "hidden_grad"),),
        owns=(
            ("middle", own_shape),
            ("head_act", shape_of((tokens, head_width), BF16)),
            ("head_sums", shape_of((8, tokens))),
            ("hidden_act", shape_of((tokens, hidden_size), BF16)),
            ("grad_up", shape_of((tokens, hidden_size), BF16)),
            ("hidden_vec_grads", shape_of((2, 8, hidden_size))),
        ),
        scratch=(
            ("hidden_grad", pltpu.VMEM((tokens, hidden_size), BF16)),
            ("hidden_sums", pltpu.VMEM((8, tokens), F32)),
            ("head_landed", landed),
            ("hidden_landed", landed),
            ("head_send", pair_sem),
            ("head_recv", pair_sem),
            ("hidden_send", block_sem),
            ("hidden_recv", block_sem),
        ),
        before=before_middle,
        rows_done=lambda env, block: hidden_rows(env, tp_count, block),
        rows_late=lambda env, block: norm_hidden(env, tp_count, hidden_width, block),
        micros=140,
    )

    weight_shape = shape_of((model_width, hidden_size), BF16)
    grad_middle_low, second_sums, grad_middle_own, down_part, w_down_terms, w_up_terms = line_sum(
        finish_second,
        tp_count,
        dict(
            grad_up=grad_up,
            w_up=w_up,
            cotangent=cotangent,
            middle=middle_own,
            hidden_act=hidden_act,
            w_down=w_down,
            second_act=second_act,
        ),
        dict(vecs=vecs),
        (("grad_up", "w_up"),),
        4,
        tokens=tokens,
        late=("hidden_act", "w_down", "middle"),
        later=("cotangent", "second_act"),
        stores=dict(middle_grad="reduced"),
        tasks=(
            ("down", "hidden_act", "w_down", "down_part"),
            ("weight", "cotangent", "hidden_act", "w_down_terms"),
            ("weight", "second_act", "grad_up", "w_up_terms"),
        ),
        owns=(("sums", sums_shape), ("middle_grad", own_shape)),
        sent=(
            ("down_part", shape_of((tokens, model_width), BF16)),
            ("w_down_terms", weight_shape),
            ("w_up_terms", weight_shape),
        ),
    )
    def scatter(grad):
        return lax.psum_scatter(grad, "seq", scatter_dimension=0, tiled=True)

    w_down_grad = scatter(w_down_terms)
    w_up_grad = scatter(w_up_terms)

    pairs = head_width // groups // LANES
    many = pltpu.SemaphoreType.DMA((pairs, seq_count))
    pair_rows = pltpu.VMEM((length, LANES), BF16)
    pair_sums = pltpu.VMEM((length, LANES), F32)
    pair_heads = pltpu.VMEM((2, length, LANES), BF16)
    block_out, grads, head_vec_grads = line_sum(
        lambda total, here, own, env: total,
        tp_count,
        dict(
            ready=down_part,
            low=grad_middle_low,
            w_out=w_out,
            mixed=mixed,
            head_sums=head_sums,
            qkv=qkv_row,
            o=o_row,
            lse=lse,
            packed=tables,
        ),
        dict(vecs=vecs, seg_col=seg_col, seg_row=seg_row),
        (),
        5,
        tokens=tokens,
        late=("low", "w_out", "mixed", "head_sums"),
        later=("qkv", "o", "lse", "packed"),
        owns=(
            ("grads", shape_of((tokens, 3 * head_width), BF16)),
            ("head_vec_grads", shape_of((2, 8, head_width))),
        ),
        scratch=(
            ("do", pltpu.VMEM((tokens, head_width), BF16)),
            ("scaled", pltpu.VMEM((tokens, head_width), F32)),
            ("head_part", pltpu.VMEM((8, tokens), F32)),
            ("head_landed", landed),
            ("tables", pltpu.VMEM((4, length, LANES), F32)),
            ("do_row", pltpu.VMEM((pairs, length, LANES), BF16)),
            ("made", pltpu.VMEM((pairs, length, 3 * LANES), BF16)),
            ("bias", pltpu.VMEM((length, length), F32)),
            ("qs", pair_heads),
            ("ks", pair_rows),
            ("kms", pair_heads),
            ("dos", pair_heads),
            ("delta", pltpu.VMEM((8, length), F32)),
            ("dq", pair_sums),
            ("dk", pair_sums),
            ("dv", pair_sums),
            ("head_send", pair_sem),
            ("head_recv", pair_sem),
            ("there_send", many),
            ("there_recv", many),
            ("back_send", many),
            ("back_recv", many),
        ),
        work=lambda env: back_work(env, seq_count, tp_count, groups),
        seq_barrier=seq_count,
    )
    head_terms, w_down_grad, block_out = head_weights(
        first_act, grads, grad_middle_low, head_act, w_down_grad, block_out
    )
    grads, head_terms = lax.optimization_barrier((grads, head_terms))
    head_grads = scatter(head_terms)
    own_width = model_width // seq_count
    split_width = hidden_size + head_width
    seq_sem = pltpu.SemaphoreType.DMA((seq_count,))
    input_grad, _, norm_own, norm_split = line_sum(
        finish_first,
        tp_count,
        dict(grads=grads, block=block, middle_grad=grad_middle_own),
        dict(
            vecs=vecs,
            second_sums=second_sums,
            hidden_vec_grads=hidden_vec_grads,
            head_vec_grads=head_vec_grads,
        ),
        (("grads", "w_pairs"),),
        8,
        tokens=tokens,
        later=("block", "middle_grad"),
        loose=dict(w_query=w_query, w_key=w_key, w_value=w_value),
        owns=(
            ("sums", sums_shape),
            ("norm_own", shape_of((8, own_width))),
            ("norm_split", shape_of((8, split_width))),
        ),
        scratch=(
            ("w_pairs", pltpu.VMEM((model_width, 3 * head_width), BF16)),
            ("pair_sem", pltpu.SemaphoreType.DMA((3 * head_width // LANES,))),
            ("split", pltpu.VMEM((8, split_width), F32)),
            ("split_landed", pltpu.VMEM((seq_count, 8, split_width), F32)),
            ("full", pltpu.VMEM((8, model_width), F32)),
            ("full_landed", pltpu.VMEM((tp_count, 8, model_width), F32)),
            ("own_landed", pltpu.VMEM((seq_count, 8, own_width), F32)),
            ("split_send", seq_sem),
            ("split_recv", seq_sem),
            ("full_send", pair_sem),
            ("full_recv", pair_sem),
            ("own_send", seq_sem),
            ("own_recv", seq_sem),
        ),
        start=load_pairs,
        seq_count=seq_count,
    )

    w_query_grad, w_key_grad, w_value_grad, w_out_grad, w_up_grad, input_grad = last_results(
        head_grads, w_up_grad, input_grad, head_width
    )
    return (
        block_out.reshape(block_in.shape),
        input_grad.reshape(block_in.shape),
        norm_own[2],
        norm_own[3],
        w_query_grad,
        w_key_grad,
        w_value_grad,
        norm_split[0, hidden_size:],
        norm_split[1, hidden_size:],
        w_out_grad,
        norm_own[0],
        norm_own[1],
        w_up_grad,
        norm_split[0, :hidden_size],
        norm_split[1, :hidden_size],
        w_down_grad,
    )


def solution(mesh):
    return jax.shard_map(
        functools.partial(body, mesh.shape["seq"], mesh.shape["tp"]),
        mesh=mesh,
        in_specs=(
            P(None, "seq", None),
            P(),
            P(),
            P(),
            P(None, "tp"),
            P(None, "tp"),
            P(None, "tp"),
            P("tp"),
            P("tp"),
            P(None, "tp"),
            P(),
            P(),
            P(None, "tp"),
            P("tp"),
            P("tp"),
            P(None, "tp"),
            P(None, "seq", None),
        ),
        out_specs=(
            P(None, "seq", None),
            P(None, "seq", None),
            P("seq"),
            P("seq"),
            P("seq", "tp"),
            P("seq", "tp"),
            P("seq", "tp"),
            P("tp"),
            P("tp"),
            P("seq", "tp"),
            P("seq"),
            P("seq"),
            P("seq", "tp"),
            P("tp"),
            P("tp"),
            P("seq", "tp"),
        ),
        check_vma=False,
    )
```

```python
import functools
import math

import jax
import jax.numpy as jnp
from jax import lax
from jax.experimental import pallas as pl
from jax.experimental.pallas import tpu as pltpu
from jax.sharding import PartitionSpec as P

HEAD = 64
LANES = 128
BLOCK = 256
EPSILON = 1e-05
MASKED = -1e30
MESH = pl.DeviceIdType.MESH
F32 = jnp.float32
BF16 = jnp.bfloat16
SLACK = 2
ROWS = 256
TILE = 512
VMEM_LIMIT = 60 * 1024 * 1024


def cost(micros):
    return pl.CostEstimate(flops=int(micros * 1.1e9), bytes_accessed=0, transcendentals=0)


def dot(left, right, left_dim, right_dim):
    return lax.dot_general(
        left, right, (((left_dim,), (right_dim,)), ((), ())), preferred_element_type=F32
    )


def seq_signal(count):
    me = lax.axis_index("seq")
    barrier = pltpu.get_barrier_semaphore()
    for k in range(1, count):
        pl.semaphore_signal(
            barrier, inc=1, device_id={"seq": lax.rem(me + k, count)}, device_id_type=MESH
        )


def seq_wait(count):
    pl.semaphore_wait(pltpu.get_barrier_semaphore(), count - 1)


def send(source, target, send_sem, recv_sem, device):
    return pltpu.make_async_remote_copy(
        src_ref=source,
        dst_ref=target,
        send_sem=send_sem,
        recv_sem=recv_sem,
        device_id={"seq": device},
        device_id_type=MESH,
    )


def spans(index, span):
    return pl.ds(pl.multiple_of(index * span, LANES), span)


def swap_halves(values):
    lane = lax.broadcasted_iota(jnp.int32, values.shape, 1)
    return jnp.where(
        lane % HEAD < HEAD // 2,
        pltpu.roll(values, LANES - HEAD // 2, 1),
        pltpu.roll(values, HEAD // 2, 1),
    )


def head_masks(values):
    lane = lax.broadcasted_iota(jnp.int32, values.shape, 1)
    zero = jnp.zeros_like(values)
    return jnp.where(lane < HEAD, values, zero), jnp.where(lane < HEAD, zero, values)


def block_rows(index):
    return slice(index * BLOCK, (index + 1) * BLOCK)


def rotated(values, tables, first, rows):
    values = values.astype(F32)
    return values * tables[first, rows, :] + swap_halves(values) * tables[first + 1, rows, :]


def rotated_back(values, tables, first, rows):
    return values * tables[first, rows, :] - swap_halves(values) * tables[first + 1, rows, :]


def norm_parts(values):
    center = jnp.mean(values, axis=-1, keepdims=True)
    shifted = values - center
    inverse = lax.rsqrt(jnp.mean(shifted * shifted, axis=-1, keepdims=True) + EPSILON)
    return shifted * inverse, inverse


def expand_tables(packed, tables):
    quarter = HEAD // 2
    for block in range(packed.shape[0] // BLOCK):
        rows = block_rows(block)
        lane = lax.broadcasted_iota(jnp.int32, (BLOCK, LANES), 1)
        group = lane // quarter
        turns = [packed[rows, :]]
        for k in range(1, 4):
            turns.append(pltpu.roll(turns[0], k * quarter, 1))

        def spread(index):
            values = turns[(0 - index) % 4]
            for g in range(1, 4):
                values = jnp.where(group == g, turns[(g - index) % 4], values)
            return values

        cos_part = spread(0)
        sin_part = spread(1)
        sin_part = jnp.where(lane % HEAD < quarter, -sin_part, sin_part)
        for k in range(2):
            factor = spread(2 + k)
            tables[2 * k, rows, :] = cos_part * factor
            tables[2 * k + 1, rows, :] = sin_part * factor


def front_kernel(
    count, groups, num_vec, *refs
):
    (x_ref, wq_ref, wk_ref, wv_ref, packed_ref, segc_ref, segr_ref), refs = refs[:7], refs[7:]
    pieces, refs = refs[:num_vec], refs[num_vec:]
    (
        act_out, qkv_out, o_ref, lse_ref, mixed_ref, vecs_ref, act_ref, qkv_ref,
        weights, staged, tab_ref, bias, qs, ks, load_sem, act_sem, qkv_sem, send_sem, recv_sem, back_send_sem, back_recv_sem,
    ) = refs
    me = lax.axis_index("seq")
    pairs, length = qkv_ref.shape[:2]
    tokens, width = x_ref.shape
    span = length // count
    blocks = length // BLOCK
    mine, row = lax.rem(me, groups), me // groups
    seq_signal(count)
    loads = []
    for j in range(pairs * groups):
        for i, source in enumerate((wq_ref, wk_ref, wv_ref)):
            copy = pltpu.make_async_copy(
                source.at[:, j * LANES : (j + 1) * LANES],
                weights.at[j, :, i * LANES : (i + 1) * LANES],
                load_sem.at[3 * j + i],
            )
            copy.start()
            loads.append(copy)

    place = 0
    for piece in pieces:
        for i in range(piece.shape[0]):
            vecs_ref[:, place : place + LANES] = piece[i : i + 1, :].astype(F32)
            place += LANES

    def there_to(p, device):
        k = lax.rem(device - me + count, count)
        return send(
            staged.at[lax.rem(device, groups) * pairs + p, spans(device // groups, span), :],
            qkv_ref.at[p, spans(me, span), :],
            send_sem.at[p, k],
            recv_sem.at[p, k],
            device,
        )

    def there(p, k):
        return there_to(p, lax.rem(me + k, count))

    def project_rows(p, rows):
        for group in range(groups):
            j = group * pairs + p
            staged[j, rows, :] = dot(act_ref[rows, :], weights[j], 1, 0).astype(BF16)

    for copy in loads:
        copy.wait()
    seq_wait(count)
    steps = tokens // BLOCK
    rows_each = BLOCK // span

    def first_step(b, carry):
        block = lax.rem(row // rows_each + b, steps)
        for i in range(BLOCK // LANES):
            rows = pl.ds(pl.multiple_of(block * BLOCK + i * LANES, LANES), LANES)
            normed, _ = norm_parts(x_ref[rows, :].astype(F32))
            act = normed * vecs_ref[:, :width] + vecs_ref[:, width : 2 * width]
            act_ref[rows, :] = act.astype(BF16)
        project_rows(0, pl.ds(pl.multiple_of(block * BLOCK, BLOCK), BLOCK))
        for i in range(rows_each * groups):
            device = block * rows_each * groups + i
            pl.when(device != me)(lambda device=device: there_to(0, device).start())
        return carry

    lax.fori_loop(0, steps, first_step, 0)
    act_copy = pltpu.make_async_copy(act_ref, act_out, act_sem)
    act_copy.start()

    def qkv_copy(p):
        return pltpu.make_async_copy(qkv_ref.at[p], qkv_out.at[p], qkv_sem.at[p])

    def keep_own(p):
        qkv_ref[p, spans(me, span), :] = staged[mine * pairs + p, spans(row, span), :]

    keep_own(0)

    def back(p, k):
        device = lax.rem(me + k, count)
        return send(
            o_ref.at[p, spans(device, span), :],
            mixed_ref.at[spans(row, span), spans(mine * pairs + p, LANES)],
            back_send_sem.at[p, k],
            back_recv_sem.at[p, k],
            device,
        )

    def project(p, carry):
        def rows_step(r, inner):
            project_rows(p, pl.ds(pl.multiple_of(r * BLOCK, BLOCK), BLOCK))
            return inner

        lax.fori_loop(0, steps, rows_step, 0)
        for k in range(1, count):
            there(p, k).start()
        keep_own(p)
        return carry

    lax.fori_loop(1, pairs, project, 0)
    expand_tables(packed_ref, tab_ref)
    for qb in range(blocks):
        rows = block_rows(qb)
        keys = (qb + 1) * BLOCK
        same = segc_ref[rows, :] == segr_ref[:, :keys]
        query = lax.broadcasted_iota(jnp.int32, (BLOCK, keys), 0) + qb * BLOCK
        key = lax.broadcasted_iota(jnp.int32, (BLOCK, keys), 1)
        bias[rows, :keys] = jnp.where(same & (key <= query), 0.0, MASKED)

    def attend(p, carry):
        for k in range(1, count):
            there(p, k).wait_recv()
        qkv_copy(p).start()
        for qb in range(blocks):
            rows = block_rows(qb)
            q = rotated(qkv_ref[p, rows, :LANES], tab_ref, 0, rows) * (HEAD**-0.5)
            q0, q1 = head_masks(q)
            qs[0, rows, :] = q0.astype(BF16)
            qs[1, rows, :] = q1.astype(BF16)
            k = rotated(qkv_ref[p, rows, LANES : 2 * LANES], tab_ref, 2, rows)
            ks[rows, :] = k.astype(BF16)
        for qb in range(blocks):
            rows = block_rows(qb)
            keys = (qb + 1) * BLOCK
            outs = []
            logs = []
            for h in range(2):
                scores = dot(qs[h, rows, :], ks[:keys, :], 1, 1) + bias[rows, :keys]
                top = jnp.max(scores, axis=1, keepdims=True)
                expo = jnp.exp(scores - top)
                total = jnp.sum(expo, axis=1, keepdims=True)
                outs.append(dot(expo.astype(BF16), qkv_ref[p, :keys, 2 * LANES :], 1, 0) / total)
                logs.append(jnp.broadcast_to(top + jnp.log(total), (BLOCK, LANES)))
            lane = lax.broadcasted_iota(jnp.int32, (BLOCK, LANES), 1)
            o_ref[p, rows, :] = jnp.where(lane < HEAD, outs[0], outs[1]).astype(BF16)
            logs_t = jnp.transpose(jnp.where(lane < HEAD, logs[0], logs[1]))
            lse_ref[p, 0:1, rows] = logs_t[0:1]
            lse_ref[p, 1:2, rows] = logs_t[HEAD : HEAD + 1]
        for k in range(1, count):
            back(p, k).start()
        mixed_ref[spans(row, span), spans(mine * pairs + p, LANES)] = o_ref[p, spans(me, span), :]
        return carry

    lax.fori_loop(0, pairs, attend, 0)

    def drain(p, carry):
        for k in range(1, count):
            there(p, k).wait_send()
            back(p, k).wait()
        return carry

    lax.fori_loop(0, pairs, drain, 0)
    act_copy.wait()
    for p in range(pairs):
        qkv_copy(p).wait()


def front(
    x, w_query, w_key, w_value, tables, seg_col, seg_row, vectors, count, groups, collective_id
):
    tokens, model_width = x.shape
    pieces = [vector.reshape(vector.shape[0] // LANES, LANES) for vector in vectors]
    total = sum(vector.shape[0] for vector in vectors)
    head_width = w_query.shape[1]
    length = seg_col.shape[0]
    pairs = head_width // groups // LANES
    whole = pl.BlockSpec(memory_space=pltpu.VMEM)
    any_space = pl.BlockSpec(memory_space=pl.ANY)
    return pl.pallas_call(
        functools.partial(front_kernel, count, groups, len(pieces)),
        out_shape=[
            jax.ShapeDtypeStruct((tokens, model_width), BF16),
            jax.ShapeDtypeStruct((pairs, length, 3 * LANES), BF16),
            jax.ShapeDtypeStruct((pairs, length, LANES), BF16),
            jax.ShapeDtypeStruct((pairs, 8, length), F32),
            jax.ShapeDtypeStruct((tokens, head_width), BF16),
            jax.ShapeDtypeStruct((1, total), F32),
        ],
        in_specs=[whole] + [any_space] * 3 + [whole] * (3 + len(pieces)),
        out_specs=[any_space] * 2 + [whole] * 4,
        scratch_shapes=[
            pltpu.VMEM((tokens, model_width), BF16),
            pltpu.VMEM((pairs, length, 3 * LANES), BF16),
            pltpu.VMEM((pairs * groups, model_width, 3 * LANES), BF16),
            pltpu.VMEM((pairs * groups, tokens, 3 * LANES), BF16),
            pltpu.VMEM((4, length, LANES), F32),
            pltpu.VMEM((length, length), F32),
            pltpu.VMEM((2, length, LANES), BF16),
            pltpu.VMEM((length, LANES), BF16),
            pltpu.SemaphoreType.DMA((3 * pairs * groups,)),
            pltpu.SemaphoreType.DMA,
            pltpu.SemaphoreType.DMA((pairs,)),
        ]
        + [pltpu.SemaphoreType.DMA((pairs, count))] * 4,
        compiler_params=pltpu.CompilerParams(
            collective_id=collective_id, has_side_effects=True, vmem_limit_bytes=VMEM_LIMIT
        ),
        cost_estimate=cost(60),
    )(x, w_query, w_key, w_value, tables, seg_col, seg_row, *pieces)


def back_work(env, count, tp_count, groups):
    low_ref, wout_ref, mixed_ref = env["low"], env["w_out"], env["mixed"]
    sums_ref, qkv_ref, o_ref, lse_ref = env["head_sums"], env["qkv"], env["o"], env["lse"]
    segc_ref, segr_ref, tab_ref, bias = env["seg_col"], env["seg_row"], env["tables"], env["bias"]
    grads_ref, vec_grads_ref = env["grads"], env["head_vec_grads"]
    do_ref, scaled, part = env["do"], env["scaled"], env["head_part"]
    do_row, made, delta = env["do_row"], env["made"], env["delta"]
    qs, ks, kms, dos, dq, dk, dv = (env[name] for name in ("qs", "ks", "kms", "dos", "dq", "dk", "dv"))
    me = lax.axis_index("seq")
    pairs, length = qkv_ref.shape[:2]
    tokens, features = low_ref.shape
    head_width = mixed_ref.shape[1]
    span = length // count
    blocks = length // BLOCK
    mine, row = lax.rem(me, groups), me // groups
    gain = head_vec(env["vecs"], head_width, 0)

    def normed_rows(rows):
        first, second = to_columns(sums_ref[:, rows], 2)
        center = first / features
        inverse = lax.rsqrt(second / features - center * center + EPSILON)
        return (mixed_ref[rows, :].astype(F32) - center) * inverse, inverse

    def head_terms(r):
        wide = pl.ds(pl.multiple_of(r * BLOCK, BLOCK), BLOCK)
        scaled[wide, :] = dot(low_ref[wide, :], wout_ref[...], 1, 0)
        for k in range(BLOCK // LANES):
            rows = row_block(r * (BLOCK // LANES) + k)
            normed, _ = normed_rows(rows)
            grad = scaled[rows, :]
            vec_grads_ref[0] += fold(grad * normed)
            vec_grads_ref[1] += fold(grad)
            grad = grad * gain
            scaled[rows, :] = grad
            part[:, rows] = to_row(
                [
                    jnp.sum(grad, axis=-1, keepdims=True),
                    jnp.sum(grad * normed, axis=-1, keepdims=True),
                ]
            )

    def part_copies(start):
        return share("tp", tp_count, lambda d: part, env["head_landed"], *env_pair(env, "head"), start)

    def head_apply(r, carry):
        rows = row_block(r)
        normed, inverse = normed_rows(rows)
        first, second = to_columns(part[:, rows], 2)
        grad = scaled[rows, :] - first / features - normed * (second / features)
        do_ref[rows, :] = (inverse * grad).astype(BF16)
        return carry

    def there(p, k):
        device = lax.rem(me + k, count)
        return send(
            do_ref.at[spans(device // groups, span), spans(lax.rem(device, groups) * pairs + p, LANES)],
            do_row.at[p, spans(me, span), :],
            env["there_send"].at[p, k],
            env["there_recv"].at[p, k],
            device,
        )

    def back(p, k):
        device = lax.rem(me + k, count)
        return send(
            made.at[p, spans(device, span), :],
            grads_ref.at[spans(row, span), spans(mine * pairs + p, 3 * LANES)],
            env["back_send"].at[p, k],
            env["back_recv"].at[p, k],
            device,
        )

    def share_out(p, carry):
        for k in range(1, count):
            there(p, k).start()
        do_row[p, spans(me, span), :] = do_ref[spans(row, span), spans(mine * pairs + p, LANES)]
        return carry

    def prepare():
        expand_tables(env["packed"], tab_ref)
        for kb in range(blocks):
            rows = block_rows(kb)
            start = kb * BLOCK
            shape = (BLOCK, length - start)
            same = segc_ref[rows, :] == segr_ref[:, start:]
            key = lax.broadcasted_iota(jnp.int32, shape, 0)
            query = lax.broadcasted_iota(jnp.int32, shape, 1)
            bias[rows, start:] = jnp.where(same & (key <= query), 0.0, MASKED)

    def pair_start(p):
        for qb in range(blocks):
            rows = block_rows(qb)
            q = rotated(qkv_ref[p, rows, :LANES], tab_ref, 0, rows) * (HEAD**-0.5)
            q0, q1 = head_masks(q)
            qs[0, rows, :] = q0.astype(BF16)
            qs[1, rows, :] = q1.astype(BF16)
            k = rotated(qkv_ref[p, rows, LANES : 2 * LANES], tab_ref, 2, rows)
            ks[rows, :] = k.astype(BF16)
            k0, k1 = head_masks(k)
            kms[0, rows, :] = k0.astype(BF16)
            kms[1, rows, :] = k1.astype(BF16)
        dq[...] = jnp.zeros_like(dq)
        dk[...] = jnp.zeros_like(dk)
        dv[...] = jnp.zeros_like(dv)
        for k in range(1, count):
            there(p, k).wait_recv()
        for qb in range(blocks):
            rows = block_rows(qb)
            grad = do_row[p, rows, :].astype(F32)
            d0, d1 = head_masks(grad)
            dos[0, rows, :] = d0.astype(BF16)
            dos[1, rows, :] = d1.astype(BF16)
            prod = jnp.transpose(grad * o_ref[p, rows, :].astype(F32))
            delta[0:1, rows] = jnp.sum(prod[:HEAD], axis=0, keepdims=True)
            delta[1:2, rows] = jnp.sum(prod[HEAD:], axis=0, keepdims=True)

    def pair_block(p, qb):
        cols = block_rows(qb)
        for kb in range(qb + 1):
            rows = block_rows(kb)
            value = qkv_ref[p, rows, 2 * LANES :]
            for h in range(2):
                scores = dot(ks[rows, :], qs[h, cols, :], 1, 1) + bias[rows, cols]
                probs = jnp.exp(scores - lse_ref[p, h : h + 1, cols])
                grads = dot(value, dos[h, cols, :], 1, 1)
                dscores = (probs * (grads - delta[h : h + 1, cols])).astype(BF16)
                dv[rows, :] += dot(probs.astype(BF16), dos[h, cols, :], 1, 0)
                dk[rows, :] += dot(dscores, qs[h, cols, :], 1, 0)
                dq[cols, :] += dot(dscores, kms[h, rows, :], 0, 0)

    def pair_end(p):
        for qb in range(blocks):
            rows = block_rows(qb)
            grad = dq[rows, :] * (HEAD**-0.5)
            made[p, rows, :LANES] = rotated_back(grad, tab_ref, 0, rows).astype(BF16)
            made[p, rows, LANES : 2 * LANES] = rotated_back(dk[rows, :], tab_ref, 2, rows).astype(BF16)
            made[p, rows, 2 * LANES :] = dv[rows, :].astype(BF16)
        for k in range(1, count):
            back(p, k).start()
        grads_ref[spans(row, span), spans(mine * pairs + p, 3 * LANES)] = made[p, spans(me, span), :]

    head_steps = tokens // BLOCK
    attend_at = head_steps + 3
    weights_at = attend_at + pairs * (blocks // 2) + 3
    tiles = features // ROWS

    def weight_copy(tile):
        rows = pl.ds(pl.multiple_of(tile * ROWS, ROWS), ROWS)
        slot = lax.rem(tile, 2)
        return pltpu.make_async_copy(
            env["weight_stage"].at[slot], env["head_terms"].at[rows, :], env["weight_sem"].at[slot]
        )

    def head_weights(tile):
        cols = pl.ds(pl.multiple_of(tile * ROWS, ROWS), ROWS)
        slot = lax.rem(tile, 2)
        wide = 3 * head_width
        for left, right, first in (
            (env["first_act"], grads_ref, 0), (low_ref, env["head_act"], wide)
        ):
            env["turned"][...] = jnp.transpose(left[:, cols])
            for n in range(right.shape[1] // head_width):
                part_cols = slice(n * head_width, (n + 1) * head_width)
                target = slice(first + n * head_width, first + (n + 1) * head_width)
                value = dot(env["turned"][...], right[:, part_cols], 1, 0)
                env["weight_stage"][slot, :, target] = value.astype(BF16)
        weight_copy(tile).start()

    vec_grads_ref[...] = jnp.zeros_like(vec_grads_ref)

    def step(now):
        t = now - 1
        pl.when((t >= 0) & (t < head_steps))(lambda: head_terms(t))

        @pl.when(t == head_steps - 1)
        def _():
            part_copies(True)
            env["head_landed"][lax.axis_index("tp")] = part[...]

        pl.when(t == head_steps)(prepare)

        @pl.when(t == head_steps + 1)
        def _():
            for copy in part_copies(False):
                copy.wait()
            part[...] = total_of(env["head_landed"], tp_count)
            lax.fori_loop(0, tokens // LANES, head_apply, 0)
            lax.fori_loop(0, pairs, share_out, 0)

        each = blocks // 2
        turn = t - attend_at
        p = turn // each
        for i in range(each):

            @pl.when((turn >= 0) & (turn < pairs * each) & (lax.rem(turn + 32 * each, each) == i))
            def _():
                if i == 0:
                    pair_start(p)
                pair_block(p, 2 * i)
                pair_block(p, 2 * i + 1)
                if i == each - 1:
                    pair_end(p)

        tile = t - weights_at

        @pl.when(tile == 0)
        def _():
            def arrive(p, carry):
                for k in range(1, count):
                    back(p, k).wait_recv()
                return carry

            lax.fori_loop(0, pairs, arrive, 0)

        pl.when((tile >= 2) & (tile < tiles))(lambda: weight_copy(tile - 2).wait())
        pl.when((tile >= 0) & (tile < tiles))(lambda: head_weights(tile))

    def end():
        def drain(p, carry):
            for k in range(1, count):
                there(p, k).wait_send()
                back(p, k).wait_send()
            return carry

        lax.fori_loop(0, pairs, drain, 0)
        for tile in (tiles - 2, tiles - 1):
            weight_copy(tile).wait()

    return step, end, 1 + weights_at + tiles


def last_kernel(
    head_ref, up_ref, down_ref, grad_ref, block_ref, own_ref, split_ref,
    query_out, key_out, value_out, out_out, up_out, down_out, grad_out, block_out, *vectors
):
    grad_out[...] = grad_ref[...]
    block_out[...] = block_ref[...]
    up_out[...] = up_ref[...].astype(F32)
    down = down_ref[0].astype(F32)
    for k in range(1, down_ref.shape[0]):
        down = down + down_ref[k].astype(F32)
    down_out[...] = down
    width = out_out.shape[1]
    for j in range(width // LANES):
        for i, target in enumerate((query_out, key_out, value_out)):
            start = (3 * j + i) * LANES
            target[:, j * LANES : (j + 1) * LANES] = head_ref[:, start : start + LANES].astype(F32)
    out_out[...] = head_ref[:, 3 * width :].astype(F32)

    @pl.when(pl.program_id(0) == 0)
    def _():
        places = [(own_ref, i, 0) for i in range(4)]
        hidden = vectors[4].shape[0] * LANES
        places += [(split_ref, i, 0) for i in range(2)] + [(split_ref, i, hidden) for i in range(2)]
        for target, (source, row, first) in zip(vectors, places):
            for i in range(target.shape[0]):
                start = first + i * LANES
                target[i : i + 1, :] = source[row : row + 1, start : start + LANES]


def last_results(
    head_grads, up_grad, down_terms, input_grad, block_out, norm_own, norm_split, head_width
):
    rows = head_grads.shape[0]
    steps = rows // 32
    tokens, width = input_grad.shape

    def block(columns):
        return pl.BlockSpec((rows // steps, columns), lambda i: (i, 0))

    def whole(shape):
        return pl.BlockSpec(shape, lambda i: (0, 0))

    part = pl.BlockSpec((tokens // steps, width), lambda i: (i, 0))
    own = norm_own.shape[1]
    hidden = norm_split.shape[1] - head_width
    vectors = [(size // LANES, LANES) for size in (own,) * 4 + (hidden,) * 2 + (head_width,) * 2]
    sizes = [head_width] * 4 + [up_grad.shape[1]] * 2
    return pl.pallas_call(
        last_kernel,
        grid=(steps,),
        out_shape=[jax.ShapeDtypeStruct((rows, size), F32) for size in sizes]
        + [jax.ShapeDtypeStruct((tokens, width), BF16)] * 2
        + [jax.ShapeDtypeStruct(shape, F32) for shape in vectors],
        in_specs=[
            block(head_grads.shape[1]),
            block(up_grad.shape[1]),
            pl.BlockSpec((down_terms.shape[0], rows // steps, down_terms.shape[2]), lambda i: (0, i, 0)),
        ]
        + [part] * 2
        + [whole(norm_own.shape), whole(norm_split.shape)],
        out_specs=[block(size) for size in sizes] + [part] * 2 + [whole(shape) for shape in vectors],
        compiler_params=pltpu.CompilerParams(vmem_limit_bytes=VMEM_LIMIT),
        cost_estimate=cost(10),
    )(head_grads, up_grad, down_terms, input_grad, block_out, norm_own, norm_split)


def fold(values):
    rows, width = values.shape
    return jnp.sum(values.reshape(rows // 8, 8, width), axis=0)


def model_vec(env, index):
    width = env["out"].shape[1]
    return env["vecs"][:, index * width : (index + 1) * width]


def hidden_vec(env, index, cols=slice(None)):
    width = env["hidden_act"].shape[1]
    first = 4 * env["out"].shape[1] + index * width
    return env["vecs"][:, first : first + width][:, cols]


def head_vec(vecs_ref, width, index):
    total = vecs_ref.shape[1]
    first = total - (2 - index) * width
    return vecs_ref[:, first : first + width]


def finish_middle(total, here, own, env):
    middle = env["block"][here, :].astype(F32) + total
    env["middle"][own, :] = middle
    normed, _ = norm_parts(middle)
    return normed * model_vec(env, 2) + model_vec(env, 3)


def norm_back(base, values, total, gain, sums):
    normed, inverse = norm_parts(values)
    scaled = total * gain
    grad = base + inverse * (
        scaled
        - jnp.mean(scaled, axis=-1, keepdims=True)
        - normed * jnp.mean(scaled * normed, axis=-1, keepdims=True)
    )
    sums[0] += fold(total * normed)
    sums[1] += fold(total)
    return grad


def finish_second(total, here, own, env):
    base = env["cotangent"][here, :].astype(F32)
    grad = norm_back(base, env["middle"][own, :], total, model_vec(env, 2), env["sums"])
    env["middle_grad"][own, :] = grad
    return grad


def finish_first(total, here, own, env):
    values = env["block"][here, :].astype(F32)
    return norm_back(env["middle_grad"][own, :], values, total, model_vec(env, 0), env["sums"])


def to_row(columns):
    lane = lax.broadcasted_iota(jnp.int32, (LANES, LANES), 1)
    packed = jnp.zeros((LANES, LANES), F32)
    for i, column in enumerate(columns):
        packed = jnp.where(lane == i, column, packed)
    return jnp.transpose(packed)[:8]


def to_columns(rows, number):
    packed = jnp.transpose(jnp.concatenate([rows] * (LANES // 8), axis=0))
    return [packed[:, i : i + 1] for i in range(number)]


def row_block(r):
    return pl.ds(pl.multiple_of(r * LANES, LANES), LANES)


def tp_total(part, landed, send_sem, recv_sem, count):
    copies = share("tp", count, lambda d: part, landed, send_sem, recv_sem)
    landed[lax.axis_index("tp")] = part[...]
    for copy in copies:
        copy.wait()
    part[...] = total_of(landed, count)


def norm_heads(env, count, features):
    mixed, act, part = env["mixed"], env["head_act"], env["head_sums"]
    blocks = mixed.shape[0] // LANES

    def sums(r, carry):
        values = mixed[row_block(r), :].astype(F32)
        part[:, row_block(r)] = to_row(
            [
                jnp.sum(values, axis=-1, keepdims=True),
                jnp.sum(values * values, axis=-1, keepdims=True),
            ]
        )
        return carry

    lax.fori_loop(0, blocks, sums, 0)
    tp_total(part, env["head_landed"], env["head_send"], env["head_recv"], count)

    def apply(r, carry):
        first, second = to_columns(part[:, row_block(r)], 2)
        center = first / features
        inverse = lax.rsqrt(second / features - center * center + EPSILON)
        values = (mixed[row_block(r), :].astype(F32) - center) * inverse
        act[row_block(r), :] = (
            values * head_vec(env["vecs"], act.shape[1], 0) + head_vec(env["vecs"], act.shape[1], 1)
        ).astype(BF16)
        return carry

    lax.fori_loop(0, blocks, apply, 0)


def normal_parts(values):
    size = jnp.abs(values) * (0.5**0.5)
    bell = jnp.exp(-0.5 * values * values)
    t = 1.0 / (1.0 + 0.3275911 * size)
    poly = 1.061405429
    for factor in (-1.453152027, 1.421413741, -0.284496736, 0.254829592):
        poly = poly * t + factor
    tail = 0.5 * poly * t * bell
    return jnp.where(values < 0.0, tail, 1.0 - tail), bell * (1.0 / math.sqrt(2.0 * math.pi))


def hidden_copies(env, count, block):
    me = lax.axis_index("tp")
    send_sem, recv_sem = env_pair(env, "hidden")
    return [
        pltpu.make_async_remote_copy(
            src_ref=env["hidden_sums"].at[:, row_block(block)],
            dst_ref=env["hidden_landed"].at[me, :, row_block(block)],
            send_sem=send_sem.at[block, k],
            recv_sem=recv_sem.at[block, k],
            device_id={"tp": lax.rem(me + k, count)},
            device_id_type=MESH,
        )
        for k in range(1, count)
    ]


def hidden_rows(env, count, block):
    rows = row_block(block)
    width = env["w_up"].shape[1]
    sums = [jnp.zeros((LANES, 1), F32)] * 4
    for n in range(width // TILE):
        cols = slice(n * TILE, (n + 1) * TILE)
        values = dot(env["out"][rows, :], env["w_up"][:, cols], 1, 0)
        below, density = normal_parts(values)
        active = values * below
        env["hidden_act"][rows, cols] = active.astype(BF16)
        env["grad_up"][rows, cols] = (below + values * density).astype(BF16)
        scaled = env["hidden_grad"][rows, cols].astype(F32) * hidden_vec(env, 0, cols)
        for i, term in enumerate((active, active * active, scaled, scaled * active)):
            sums[i] = sums[i] + jnp.sum(term, axis=-1, keepdims=True)
    packed = to_row(sums)
    env["hidden_sums"][:, rows] = packed
    env["hidden_landed"][lax.axis_index("tp"), :, rows] = packed
    for copy in hidden_copies(env, count, block):
        copy.start()


def norm_hidden(env, count, features, block):
    act, slope, landed = env["hidden_act"], env["grad_up"], env["hidden_landed"]
    rows = row_block(block)
    for copy in hidden_copies(env, count, block):
        copy.wait()
    total = landed[0, :, rows]
    for k in range(1, count):
        total = total + landed[k, :, rows]
    sums = [column / features for column in to_columns(total, 4)]
    center = sums[0]
    inverse = lax.rsqrt(sums[1] - center * center + EPSILON)
    cross = inverse * (sums[3] - center * sums[2])
    for n in range(act.shape[1] // TILE):
        cols = slice(n * TILE, (n + 1) * TILE)
        gain = hidden_vec(env, 0, cols)
        normed = (act[rows, cols].astype(F32) - center) * inverse
        grad = env["hidden_grad"][rows, cols].astype(F32)
        back = inverse * (grad * gain - sums[2] - normed * cross)
        slope[rows, cols] = (back * slope[rows, cols].astype(F32)).astype(BF16)
        act[rows, cols] = (normed * gain + hidden_vec(env, 1, cols)).astype(BF16)
        env["hidden_vec_grads"][0, :, cols] += fold(grad * normed)
        env["hidden_vec_grads"][1, :, cols] += fold(grad)
    for name in ("hidden_act", "grad_up"):
        row_store(env, name, block).start()


def row_store(env, name, block):
    rows = row_block(block)
    return pltpu.make_async_copy(
        env[name].at[rows, :], env["target " + name].at[rows, :], env["sem " + name].at[block]
    )


def whole_store(env, name):
    return pltpu.make_async_copy(env[name], env["target " + name], env["sem " + name].at[0])


def spread_copy(env, device):
    landed, terms = env["spread"], env["w_down_terms"]
    count, own = landed.shape[:2]
    me = lax.axis_index("seq")
    k = lax.rem(device - me + count, count)
    rows = pl.ds(pl.multiple_of(device * own, own), own)
    return pltpu.make_async_remote_copy(
        src_ref=terms.at[rows, :],
        dst_ref=landed.at[me],
        send_sem=env["spread_send"].at[k],
        recv_sem=env["spread_recv"].at[k],
        device_id={"seq": device},
        device_id_type=MESH,
    )


def spread_own(env):
    landed, terms = env["spread"], env["w_down_terms"]
    own = landed.shape[1]
    me = lax.axis_index("seq")
    rows = pl.ds(pl.multiple_of(me * own, own), own)
    return pltpu.make_async_copy(terms.at[rows, :], landed.at[me], env["spread_own"].at[0])


def spread_rows(env, rows):
    own = env["spread"].shape[1]
    me = lax.axis_index("seq")
    for i in range(ROWS // own):
        device = rows.start // own + i
        pl.when(device != me)(lambda device=device: spread_copy(env, device).start())
        pl.when(device == me)(lambda: spread_own(env).start())


def spread_wait(env):
    count = env["spread"].shape[0]
    me = lax.axis_index("seq")
    for k in range(1, count):
        spread_copy(env, lax.rem(me + k, count)).wait()
    spread_own(env).wait()


def split_copies(env, seq_count):
    split = env["split"]
    return share("seq", seq_count, lambda d: split, env["split_landed"], *env_pair(env, "split"), False)


def env_pair(env, name):
    return env[name + "_send"], env[name + "_recv"]


def split_start(env, seq_count):
    hidden = env["hidden_vec_grads"].shape[2]
    split = env["split"]
    split[...] = jnp.zeros_like(split)
    for i in range(2):
        split[i : i + 1, :hidden] = jnp.sum(env["hidden_vec_grads"][i], axis=0, keepdims=True)
        split[i : i + 1, hidden:] = jnp.sum(env["head_vec_grads"][i], axis=0, keepdims=True)
    for copy in split_copies(env, seq_count):
        copy.start()
    env["split_landed"][lax.axis_index("seq")] = split[...]


def full_copies(env, count):
    full = env["full"]
    return share("tp", count, lambda d: full, env["full_landed"], *env_pair(env, "full"), False)


def full_start(env, count):
    full = env["full"]
    full[...] = jnp.zeros_like(full)
    for i in range(2):
        full[i : i + 1, :] = jnp.sum(env["second_sums"][i], axis=0, keepdims=True)
        full[2 + i : 3 + i, :] = jnp.sum(env["sums"][i], axis=0, keepdims=True)
    for copy in full_copies(env, count):
        copy.start()
    env["full_landed"][lax.axis_index("tp")] = full[...]


def norm_finish(env, seq_count, count):
    full, own = env["full"], env["norm_own"].shape[1]
    me = lax.axis_index("seq")
    for copy in full_copies(env, count):
        copy.wait()
    full[...] = total_of(env["full_landed"], count)

    def piece(device):
        return pl.ds(pl.multiple_of(device * own, LANES), own)

    copies = share(
        "seq", seq_count, lambda d: full.at[:, piece(d)], env["own_landed"], *env_pair(env, "own")
    )
    env["own_landed"][me] = full[:, piece(me)]
    for copy in split_copies(env, seq_count):
        copy.wait()
    env["norm_split"][...] = total_of(env["split_landed"], seq_count)
    for copy in copies:
        copy.wait()
    env["norm_own"][...] = total_of(env["own_landed"], seq_count)


def load_pairs(env):
    copies = []
    for i, name in enumerate(("w_query", "w_key", "w_value")):
        for j in range(env[name].shape[1] // LANES):
            copy = pltpu.make_async_copy(
                env[name].at[:, j * LANES : (j + 1) * LANES],
                env["w_pairs"].at[:, (3 * j + i) * LANES : (3 * j + i + 1) * LANES],
                env["pair_sem"].at[3 * j + i],
            )
            copy.start()
            copies.append(copy)
    return copies


def line_kernel(plan, count, chunks, group, slack, *refs):
    env = dict(zip(plan["order"], refs, strict=True))
    finish, parts, tasks = plan["finish"], plan["parts"], plan["tasks"]
    num_task = len(tasks)
    out_ref = env["out"]
    in_a, in_b = env["in_a"], env["in_b"]
    rsa_s, rsa_r, rsb_s, rsb_r = (env[name] for name in ("rsa_s", "rsa_r", "rsb_s", "rsb_r"))
    aga_s, aga_r, agb_s, agb_r = (env[name] for name in ("aga_s", "aga_r", "agb_s", "agb_r"))
    z = lax.axis_index("tp")
    tokens, width = out_ref.shape
    half = tokens // 2
    size = half // chunks
    ahead = slack * (count - 1)
    steps = chunks + 2 * ahead
    from_first, from_last = slack * z, slack * (count - 1 - z)
    first, last = z == 0, z == count - 1
    up = jnp.minimum(z + 1, count - 1)
    down = jnp.maximum(z - 1, 0)

    loads = {
        name: pltpu.make_async_copy(env["source " + name], env[name], env["load_sem"].at[i])
        for i, name in enumerate(plan["held"])
    }
    behind = plan["late"] + plan["later"]
    for name in plan["held"]:
        if name not in behind:
            loads[name].start()
    started = plan["start"](env) if plan["start"] else []
    seq_count = plan["seq_count"]
    axis_barrier([("tp", count)] + ([("seq", plan["seq_barrier"])] if plan["seq_barrier"] else []))
    if "sums" in env:
        env["sums"][...] = jnp.zeros_like(env["sums"])
    if seq_count:
        split_start(env, seq_count)

    def own_rows(c):
        return pl.ds(pl.multiple_of(c * size, size), size)

    def a_rows(c):
        return own_rows(c)

    def b_rows(c):
        return pl.ds(pl.multiple_of(half + c * size, size), size)

    def hop(source, target, send, recv, c, device):
        return pltpu.make_async_remote_copy(
            src_ref=source,
            dst_ref=target,
            send_sem=send.at[c],
            recv_sem=recv.at[c],
            device_id={"tp": device},
            device_id_type=MESH,
        )

    def gather_a(c):
        rows = out_ref.at[a_rows(c), :]
        return hop(rows, rows, aga_s, aga_r, c, up)

    def gather_b(c):
        rows = out_ref.at[b_rows(c), :]
        return hop(rows, rows, agb_s, agb_r, c, down)

    def reduce_a(c):
        rows = in_a.at[own_rows(c), :]
        return hop(rows, rows, rsa_s, rsa_r, c, down)

    def reduce_b(c):
        rows = in_b.at[own_rows(c), :]
        return hop(rows, rows, rsb_s, rsb_r, c, up)

    def block_start(t, offset):
        return jnp.clip((t - lax.rem(t, group) - offset) * size, 0, half - group * size)

    def reduce_step(t, c, offset, place, rows, landed, move, gather, starts, ends):
        here = rows(c)
        own = own_rows(c)

        def term():
            if not parts:
                return env["ready"][here, :].astype(F32)
            row = place * group * size + c * size - block_start(t, offset)
            return env["part"][pl.ds(pl.multiple_of(row, size), size), :]

        @pl.when(starts)
        def _():
            landed[own, :] = term().astype(BF16)
            move(c).start()

        @pl.when(jnp.logical_not(starts))
        def _():
            move(c).wait_recv()

        @pl.when(jnp.logical_not(starts | ends))
        def _():
            landed[own, :] = (landed[own, :].astype(F32) + term()).astype(BF16)
            move(c).start()

        @pl.when(ends)
        def _():
            total = landed[own, :].astype(F32) + term()
            out_ref[here, :] = finish(total, here, own, env).astype(BF16)
            gather(c).start()

    def gather_step(c, gather, starts, ends):
        @pl.when(jnp.logical_not(starts))
        def _():
            gather(c).wait_recv()

        @pl.when(jnp.logical_not(starts | ends))
        def _():
            gather(c).start()

    def when_chunk(c, work):
        pl.when((c >= 0) & (c < chunks))(lambda: work(c))

    def make_parts(t):
        top = pl.ds(pl.multiple_of(block_start(t, from_last), size), group * size)
        low = pl.ds(pl.multiple_of(half + block_start(t, from_first), size), group * size)

        def columns(n, carry):
            cols = pl.ds(pl.multiple_of(n * TILE, TILE), TILE)
            total = 0.0
            for left, right in parts:
                rows = jnp.concatenate([env[left][top, :], env[left][low, :]], axis=0)
                total = total + dot(rows, env[right][cols, :], 1, 1)
            env["part"][:, cols] = total
            return carry

        lax.fori_loop(0, width // TILE, columns, 0)

    def task_rows(index, tile):
        if tasks[index][0] == "spread":
            tiles = env[tasks[index][3]].shape[0] // ROWS
            own = ROWS // env["spread"].shape[1]
            tile = lax.rem(lax.axis_index("seq") // own + 1 + tile, tiles)
        return pl.ds(pl.multiple_of(tile * ROWS, ROWS), ROWS)

    def run_task(index, tile, slot):
        kind, left, right, name = tasks[index]
        target = env[name]
        rows = task_rows(index, tile)
        if kind in ("weight", "spread"):
            env["turned"][...] = jnp.transpose(env[left][:, rows])

        def columns(n, carry):
            cols = pl.ds(pl.multiple_of(n * TILE, TILE), TILE)
            if kind in ("weight", "spread"):
                value = dot(env["turned"][...], env[right][:, cols], 1, 0)
            elif kind == "keep":
                value = dot(env[left][rows, :], env[right][:, cols], 1, 0)
            else:
                value = dot(env[left][rows, :], env[right][cols, :], 1, 1)
                top = tile * ROWS < half
                mine = (first & top) | (last & jnp.logical_not(top))
                own = pl.multiple_of(lax.rem(tile * ROWS, half), ROWS)
                base = env["middle"][pl.ds(own, ROWS), cols]
                value = value + jnp.where(mine, base, 0.0)
            if kind == "keep":
                target[rows, cols] = value.astype(BF16)
            else:
                env["stage"][slot, :, cols] = value.astype(BF16)
            return carry

        lax.fori_loop(0, target.shape[1] // TILE, columns, 0)
        if kind != "keep":
            stage_copy(index, tile, slot).start()

    def stage_copy(index, tile, slot):
        target = env[tasks[index][3]]
        rows = task_rows(index, tile)
        return pltpu.make_async_copy(
            env["stage"].at[slot, :, : target.shape[1]], target.at[rows, :], env["stage_sem"].at[slot]
        )

    starts_at = [0]
    for task in tasks:
        starts_at.append(starts_at[-1] + env[task[3]].shape[0] // ROWS)
    task_total = starts_at[-1]
    per_group = group - 1
    staged = any(task[0] != "keep" for task in tasks)

    def step(t, carry):
        if parts:
            pl.when(lax.rem(t, group) == 0)(lambda: make_parts(t))
        when_chunk(
            t - from_last,
            lambda c: reduce_step(t, c, from_last, 0, a_rows, in_a, reduce_a, gather_a, last, first),
        )
        when_chunk(
            t - from_first,
            lambda c: reduce_step(t, c, from_first, 1, b_rows, in_b, reduce_b, gather_b, first, last),
        )
        when_chunk(t - ahead - from_first, lambda c: gather_step(c, gather_a, first, last))
        when_chunk(t - ahead - from_last, lambda c: gather_step(c, gather_b, last, first))
        for moment, waited in ((1, plan["late"]), (4, plan["later"])):

            @pl.when(t == moment)
            def _():
                for name in waited:
                    loads[name].wait()

        if num_task:
            turn = (t // group) * per_group + lax.rem(t, group) - 1
            free = lax.rem(t, group) != 0
            slot = lax.rem(turn + per_group + 1, 2)

            for index in range(num_task if staged else 0):
                low, high = starts_at[index] + 2, min(starts_at[index + 1] + 2, task_total)

                def staged_done(index=index, low=low):
                    stage_copy(index, turn - low, slot).wait()
                    if tasks[index][0] == "spread":
                        spread_rows(env, task_rows(index, turn - low))

                pl.when(free & (turn >= low) & (turn < high))(staged_done)
            for index in range(num_task):
                low, high = starts_at[index], starts_at[index + 1]
                pl.when(free & (turn >= low) & (turn < high))(
                    lambda index=index, low=low: run_task(index, turn - low, slot)
                )
        if work_step:
            work_step(t)
        if seq_count:
            pl.when(t == chunks + ahead)(lambda: full_start(env, count))
        for name, moment in plan["stores"].items():
            if moment == "reduced":
                pl.when(t == chunks + ahead)(lambda name=name: whole_store(env, name).start())
        done_a = t - ahead - from_first - (group - 1)
        done_b = t - ahead - from_last - (group - 1)
        has_a = (done_a >= 0) & (done_a < chunks) & (lax.rem(done_a + 64, group) == 0)
        has_b = (done_b >= 0) & (done_b < chunks) & (lax.rem(done_b + 64, group) == 0)

        @pl.when(has_a | has_b)
        def _():
            block = jnp.where(has_a, done_a // group, chunks // group + done_b // group)
            row_store(env, "out", block).start()
            if plan["rows_done"]:
                plan["rows_done"](env, block)

        if plan["rows_late"]:
            late_a = t - 2 * ahead - (group - 1) - 2

            place = lax.rem(late_a + 64, group)

            @pl.when((late_a >= 0) & (place < 2))
            def _():
                plan["rows_late"](env, place * (chunks // group) + late_a // group)

        return carry

    for name in plan["held"]:
        if name not in behind:
            loads[name].wait()
    for copy in started:
        copy.wait()
    for name in behind:
        loads[name].start()
    if plan["before"]:
        plan["before"](env)
    for name, moment in plan["stores"].items():
        if moment == "before":
            whole_store(env, name).start()
    work_step = None
    if plan["work"]:
        work_step, work_end, work_steps = plan["work"](env)
        assert work_steps <= steps
    lax.fori_loop(0, steps, step, 0)
    if num_task:
        assert (steps // group) * per_group >= task_total
    if staged:
        assert task_total >= 2
        for turn in (task_total - 2, task_total - 1):
            index = max(i for i in range(num_task) if starts_at[i] <= turn)
            stage_copy(index, turn - starts_at[index], turn % 2).wait()
    if "spread" in env:
        spread_wait(env)
    if plan["rows_late"]:
        assert chunks + 2 * ahead == steps and group == 4

        def rest(place, carry):
            plan["rows_late"](env, (place + 1) * (chunks // group) - 1)
            return carry

        lax.fori_loop(0, 2, rest, 0)
    if work_step:
        work_end()
    if seq_count:
        norm_finish(env, seq_count, count)

    def drain(c, carry):
        @pl.when(jnp.logical_not(first))
        def _():
            reduce_a(c).wait_send()
            gather_b(c).wait_send()

        @pl.when(jnp.logical_not(last))
        def _():
            reduce_b(c).wait_send()
            gather_a(c).wait_send()

        return carry

    lax.fori_loop(0, chunks, drain, 0)
    for name, moment in plan["stores"].items():
        if moment == "rows":
            for block in range(tokens // LANES):
                row_store(env, name, block).wait()
        else:
            whole_store(env, name).wait()


def line_sum(
    finish, count, held, vecs, parts, collective_id, *, tokens, late=(), later=(), tasks=(), owns=(),
    sent=(), stores=(), scratch=(), loose=(), chunks=16, group=4, turned=False, start=None, before=None, rows_done=None, rows_late=None, work=None,
    seq_count=0, seq_barrier=0, micros=110,
):
    names = dict(scratch)
    if parts:
        width = (held.get(parts[0][1]) if parts[0][1] in held else names[parts[0][1]]).shape[0]
    else:
        width = held["ready"].shape[1]
    half = tokens // 2
    depth = tokens if turned or any(task[0] == "weight" for task in tasks) else LANES
    staged = [shape.shape[-1] for _, shape in sent] if tasks else []
    stage_width = max(staged + [LANES])
    fixed = [
        ("in_a", pltpu.VMEM((half, width), BF16)),
        ("in_b", pltpu.VMEM((half, width), BF16)),
        ("part", pltpu.VMEM((2 * group * half // chunks if parts else 8, width), F32)),
        ("turned", pltpu.VMEM((ROWS, depth), BF16)),
        ("stage", pltpu.VMEM((2, ROWS if staged else 16, stage_width), BF16)),
        ("load_sem", pltpu.SemaphoreType.DMA((len(held),))),
        ("stage_sem", pltpu.SemaphoreType.DMA((2,))),
    ] + [
        (name, pltpu.SemaphoreType.DMA((chunks,)))
        for name in ("rsa_s", "rsa_r", "rsb_s", "rsb_r", "aga_s", "aga_r", "agb_s", "agb_r")
    ]
    assert half // chunks * group == LANES
    loose = dict(loose)
    stores = dict(stores, out="rows")
    shapes = [("out", jax.ShapeDtypeStruct((tokens, width), BF16))] + list(owns)
    scratch = list(scratch) + fixed
    for name, shape in shapes:
        if name in stores:
            scratch.append((name, pltpu.VMEM(shape.shape, shape.dtype)))
            number = tokens // LANES if stores[name] == "rows" else 1
            scratch.append(("sem " + name, pltpu.SemaphoreType.DMA((number,))))
    order = (
        ["source " + name for name in held]
        + list(loose)
        + list(vecs)
        + ["target " + name if name in stores else name for name, _ in shapes]
        + [name for name, _ in sent]
        + list(held)
        + [name for name, _ in scratch]
    )
    plan = dict(
        finish=finish,
        order=order,
        held=list(held),
        parts=parts,
        late=tuple(late),
        later=tuple(later),
        stores=stores,
        tasks=tasks,
        start=start,
        work=work,
        seq_count=seq_count,
        seq_barrier=seq_barrier or seq_count,
        before=before,
        rows_done=rows_done,
        rows_late=rows_late,
    )
    whole = pl.BlockSpec(memory_space=pltpu.VMEM)
    any_space = pl.BlockSpec(memory_space=pl.ANY)
    return pl.pallas_call(
        functools.partial(line_kernel, plan, count, chunks, group, SLACK),
        out_shape=[shape for _, shape in shapes] + [shape for _, shape in sent],
        in_specs=[any_space] * (len(held) + len(loose)) + [whole] * len(vecs),
        out_specs=[any_space if name in stores else whole for name, _ in shapes]
        + [any_space] * len(sent),
        scratch_shapes=[pltpu.VMEM(array.shape, array.dtype) for array in held.values()]
        + [shape for _, shape in scratch],
        compiler_params=pltpu.CompilerParams(
            collective_id=collective_id, has_side_effects=True, vmem_limit_bytes=VMEM_LIMIT
        ),
        cost_estimate=cost(micros),
    )(*held.values(), *loose.values(), *vecs.values())


def axis_barrier(counts):
    barrier = pltpu.get_barrier_semaphore()
    for axis, count in counts:
        me = lax.axis_index(axis)
        for k in range(1, count):
            pl.semaphore_signal(
                barrier, inc=1, device_id={axis: lax.rem(me + k, count)}, device_id_type=MESH
            )
    pl.semaphore_wait(barrier, sum(count - 1 for _, count in counts))


def share(axis, count, pick, landed, send_sem, recv_sem, start=True):
    me = lax.axis_index(axis)
    copies = []
    for k in range(1, count):
        device = lax.rem(me + k, count)
        copy = pltpu.make_async_remote_copy(
            src_ref=pick(device),
            dst_ref=landed.at[me],
            send_sem=send_sem.at[k],
            recv_sem=recv_sem.at[k],
            device_id={axis: device},
            device_id_type=MESH,
        )
        if start:
            copy.start()
        copies.append(copy)
    return copies


def total_of(landed, count):
    total = landed[0]
    for k in range(1, count):
        total = total + landed[k]
    return total


def matmul(left, right, left_dim, right_dim, kind=F32):
    return dot(left, right, left_dim, right_dim).astype(kind)


def rotation_tables(positions):
    half_size = HEAD // 2
    index_pairs = jnp.arange(half_size, dtype=F32)
    theta_rate = jnp.exp(-2.0 * index_pairs / HEAD * jnp.log(10000.0))
    zeta_base = (2.0 * index_pairs + 0.4 * HEAD) / (1.4 * HEAD)
    place_float = positions.astype(F32)[..., None]
    angles = place_float * theta_rate
    power = jnp.log(zeta_base) * place_float / 512.0
    return jnp.concatenate(
        [jnp.cos(angles), jnp.sin(angles), jnp.exp(power), jnp.exp(-power)], axis=-1
    )


def body(
    seq_count,
    tp_count,
    block_in,
    segment_ids,
    first_gain,
    first_bias,
    w_query,
    w_key,
    w_value,
    head_gain,
    head_bias,
    w_out,
    second_gain,
    second_bias,
    w_up,
    hidden_gain,
    hidden_bias,
    w_down,
    out_cotangent,
):
    seq_index = lax.axis_index("seq")
    row_count, span, model_width = block_in.shape
    length = span * seq_count
    tokens = row_count * span
    head_width = w_query.shape[1]
    hidden_width = w_up.shape[1] * tp_count
    groups = seq_count // row_count

    seg_row = lax.dynamic_slice_in_dim(segment_ids, seq_index // groups, 1, 0)
    seg_col = seg_row.reshape(length, 1)
    earlier = jnp.sum((seg_row < seg_col).astype(jnp.int32), axis=-1)
    tables = rotation_tables(jnp.arange(length, dtype=jnp.int32) - earlier)

    block = block_in.reshape(tokens, model_width)
    cotangent = out_cotangent.reshape(tokens, model_width)

    first_act, qkv_row, o_row, lse, mixed, vecs = front(
        block,
        w_query,
        w_key,
        w_value,
        tables,
        seg_col,
        seg_row,
        (
            first_gain, first_bias, second_gain, second_bias,
            hidden_gain, hidden_bias, head_gain, head_bias,
        ),
        seq_count,
        groups,
        1,
    )
    def shape_of(dims, kind=F32):
        return jax.ShapeDtypeStruct(dims, kind)

    hidden_size = hidden_gain.shape[0]
    own_shape = shape_of((tokens // 2, model_width))
    sums_shape = shape_of((2, 8, model_width))
    landed = pltpu.VMEM((tp_count, 8, tokens), F32)
    pair_sem = pltpu.SemaphoreType.DMA((tp_count,))
    block_sem = pltpu.SemaphoreType.DMA((tokens // LANES, tp_count))

    def before_middle(env):
        env["hidden_vec_grads"][...] = jnp.zeros_like(env["hidden_vec_grads"])
        norm_heads(env, tp_count, model_width)

    (
        second_act, middle_own, head_act, head_sums, hidden_act, grad_up, hidden_vec_grads
    ) = line_sum(
        finish_middle,
        tp_count,
        dict(mixed=mixed, w_out=w_out, block=block, cotangent=cotangent, w_down=w_down, w_up=w_up),
        dict(vecs=vecs),
        (("head_act", "w_out"),),
        3,
        tokens=tokens,
        late=("cotangent", "w_down"),
        later=("block", "w_up"),
        stores=dict(middle="reduced", head_act="before", hidden_act="rows", grad_up="rows"),
        tasks=(("keep", "cotangent", "w_down", "hidden_grad"),),
        owns=(
            ("middle", own_shape),
            ("head_act", shape_of((tokens, head_width), BF16)),
            ("head_sums", shape_of((8, tokens))),
            ("hidden_act", shape_of((tokens, hidden_size), BF16)),
            ("grad_up", shape_of((tokens, hidden_size), BF16)),
            ("hidden_vec_grads", shape_of((2, 8, hidden_size))),
        ),
        scratch=(
            ("hidden_grad", pltpu.VMEM((tokens, hidden_size), BF16)),
            ("hidden_sums", pltpu.VMEM((8, tokens), F32)),
            ("head_landed", landed),
            ("hidden_landed", landed),
            ("head_send", pair_sem),
            ("head_recv", pair_sem),
            ("hidden_send", block_sem),
            ("hidden_recv", block_sem),
        ),
        before=before_middle,
        rows_done=lambda env, block: hidden_rows(env, tp_count, block),
        rows_late=lambda env, block: norm_hidden(env, tp_count, hidden_width, block),
        micros=140,
    )

    weight_shape = shape_of((model_width, hidden_size), BF16)
    grad_middle_low, second_sums, grad_middle_own, down_part, _, w_up_terms, down_terms = line_sum(
        finish_second,
        tp_count,
        dict(
            grad_up=grad_up,
            w_up=w_up,
            cotangent=cotangent,
            middle=middle_own,
            hidden_act=hidden_act,
            w_down=w_down,
            second_act=second_act,
        ),
        dict(vecs=vecs),
        (("grad_up", "w_up"),),
        4,
        tokens=tokens,
        late=("hidden_act", "cotangent"),
        later=("w_down", "middle", "second_act"),
        stores=dict(middle_grad="reduced"),
        tasks=(
            ("spread", "cotangent", "hidden_act", "w_down_terms"),
            ("down", "hidden_act", "w_down", "down_part"),
            ("weight", "second_act", "grad_up", "w_up_terms"),
        ),
        owns=(("sums", sums_shape), ("middle_grad", own_shape)),
        sent=(
            ("down_part", shape_of((tokens, model_width), BF16)),
            ("w_down_terms", weight_shape),
            ("w_up_terms", weight_shape),
            ("spread", shape_of((seq_count, model_width // seq_count, hidden_size), BF16)),
        ),
        scratch=(
            ("spread_send", pltpu.SemaphoreType.DMA((seq_count,))),
            ("spread_recv", pltpu.SemaphoreType.DMA((seq_count,))),
            ("spread_own", pltpu.SemaphoreType.DMA((1,))),
        ),
        seq_barrier=seq_count,
    )
    def scatter(grad):
        return lax.psum_scatter(grad, "seq", scatter_dimension=0, tiled=True)

    w_up_grad = scatter(w_up_terms)

    pairs = head_width // groups // LANES
    many = pltpu.SemaphoreType.DMA((pairs, seq_count))
    pair_rows = pltpu.VMEM((length, LANES), BF16)
    pair_sums = pltpu.VMEM((length, LANES), F32)
    pair_heads = pltpu.VMEM((2, length, LANES), BF16)
    block_out, grads, head_vec_grads, head_terms = line_sum(
        lambda total, here, own, env: total,
        tp_count,
        dict(
            ready=down_part,
            low=grad_middle_low,
            w_out=w_out,
            mixed=mixed,
            head_sums=head_sums,
            qkv=qkv_row,
            o=o_row,
            lse=lse,
            packed=tables,
            first_act=first_act,
            head_act=head_act,
        ),
        dict(vecs=vecs, seg_col=seg_col, seg_row=seg_row),
        (),
        5,
        tokens=tokens,
        late=("low", "w_out", "mixed", "head_sums"),
        later=("qkv", "o", "lse", "packed", "first_act", "head_act"),
        owns=(
            ("grads", shape_of((tokens, 3 * head_width), BF16)),
            ("head_vec_grads", shape_of((2, 8, head_width))),
        ),
        sent=(("head_terms", shape_of((model_width, 4 * head_width), BF16)),),
        turned=True,
        scratch=(
            ("weight_stage", pltpu.VMEM((2, ROWS, 4 * head_width), BF16)),
            ("weight_sem", pltpu.SemaphoreType.DMA((2,))),
            ("do", pltpu.VMEM((tokens, head_width), BF16)),
            ("scaled", pltpu.VMEM((tokens, head_width), F32)),
            ("head_part", pltpu.VMEM((8, tokens), F32)),
            ("head_landed", landed),
            ("tables", pltpu.VMEM((4, length, LANES), F32)),
            ("do_row", pltpu.VMEM((pairs, length, LANES), BF16)),
            ("made", pltpu.VMEM((pairs, length, 3 * LANES), BF16)),
            ("bias", pltpu.VMEM((length, length), F32)),
            ("qs", pair_heads),
            ("ks", pair_rows),
            ("kms", pair_heads),
            ("dos", pair_heads),
            ("delta", pltpu.VMEM((8, length), F32)),
            ("dq", pair_sums),
            ("dk", pair_sums),
            ("dv", pair_sums),
            ("head_send", pair_sem),
            ("head_recv", pair_sem),
            ("there_send", many),
            ("there_recv", many),
            ("back_send", many),
            ("back_recv", many),
        ),
        work=lambda env: back_work(env, seq_count, tp_count, groups),
        seq_barrier=seq_count,
    )
    grads, head_terms, w_up_grad = lax.optimization_barrier((grads, head_terms, w_up_grad))
    head_grads = scatter(head_terms)
    own_width = model_width // seq_count
    split_width = hidden_size + head_width
    seq_sem = pltpu.SemaphoreType.DMA((seq_count,))
    input_grad, _, norm_own, norm_split = line_sum(
        finish_first,
        tp_count,
        dict(grads=grads, block=block, middle_grad=grad_middle_own),
        dict(
            vecs=vecs,
            second_sums=second_sums,
            hidden_vec_grads=hidden_vec_grads,
            head_vec_grads=head_vec_grads,
        ),
        (("grads", "w_pairs"),),
        8,
        tokens=tokens,
        chunks=32,
        group=8,
        later=("block", "middle_grad"),
        loose=dict(w_query=w_query, w_key=w_key, w_value=w_value),
        owns=(
            ("sums", sums_shape),
            ("norm_own", shape_of((8, own_width))),
            ("norm_split", shape_of((8, split_width))),
        ),
        scratch=(
            ("w_pairs", pltpu.VMEM((model_width, 3 * head_width), BF16)),
            ("pair_sem", pltpu.SemaphoreType.DMA((3 * head_width // LANES,))),
            ("split", pltpu.VMEM((8, split_width), F32)),
            ("split_landed", pltpu.VMEM((seq_count, 8, split_width), F32)),
            ("full", pltpu.VMEM((8, model_width), F32)),
            ("full_landed", pltpu.VMEM((tp_count, 8, model_width), F32)),
            ("own_landed", pltpu.VMEM((seq_count, 8, own_width), F32)),
            ("split_send", seq_sem),
            ("split_recv", seq_sem),
            ("full_send", pair_sem),
            ("full_recv", pair_sem),
            ("own_send", seq_sem),
            ("own_recv", seq_sem),
        ),
        start=load_pairs,
        seq_count=seq_count,
    )

    (
        w_query_grad, w_key_grad, w_value_grad, w_out_grad, w_up_grad, w_down_grad, input_grad,
        block_out, *vectors,
    ) = last_results(
        head_grads, w_up_grad, down_terms, input_grad, block_out, norm_own, norm_split, head_width
    )
    vectors = [vector.reshape(-1) for vector in vectors]
    return (
        block_out.reshape(block_in.shape),
        input_grad.reshape(block_in.shape),
        vectors[2],
        vectors[3],
        w_query_grad,
        w_key_grad,
        w_value_grad,
        vectors[6],
        vectors[7],
        w_out_grad,
        vectors[0],
        vectors[1],
        w_up_grad,
        vectors[4],
        vectors[5],
        w_down_grad,
    )


def solution(mesh):
    return jax.shard_map(
        functools.partial(body, mesh.shape["seq"], mesh.shape["tp"]),
        mesh=mesh,
        in_specs=(
            P(None, "seq", None),
            P(),
            P(),
            P(),
            P(None, "tp"),
            P(None, "tp"),
            P(None, "tp"),
            P("tp"),
            P("tp"),
            P(None, "tp"),
            P(),
            P(),
            P(None, "tp"),
            P("tp"),
            P("tp"),
            P(None, "tp"),
            P(None, "seq", None),
        ),
        out_specs=(
            P(None, "seq", None),
            P(None, "seq", None),
            P("seq"),
            P("seq"),
            P("seq", "tp"),
            P("seq", "tp"),
            P("seq", "tp"),
            P("tp"),
            P("tp"),
            P("seq", "tp"),
            P("seq"),
            P("seq"),
            P("seq", "tp"),
            P("tp"),
            P("tp"),
            P("seq", "tp"),
        ),
        check_vma=False,
    )
```

```python
import functools
import math

import jax
import jax.numpy as jnp
from jax import lax
from jax.experimental import pallas as pl
from jax.experimental.pallas import tpu as pltpu
from jax.sharding import PartitionSpec as P

HEAD = 64
LANES = 128
BLOCK = 256
EPSILON = 1e-05
MASKED = -1e30
MESH = pl.DeviceIdType.MESH
F32 = jnp.float32
BF16 = jnp.bfloat16
SLACK = 2
SLACK_OUT = 2
ROWS = 256
TILE = 512
VMEM_LIMIT = 60 * 1024 * 1024


def cost(micros):
    return pl.CostEstimate(flops=int(micros * 1.1e9), bytes_accessed=0, transcendentals=0)


def dot(left, right, left_dim, right_dim):
    return lax.dot_general(
        left, right, (((left_dim,), (right_dim,)), ((), ())), preferred_element_type=F32
    )


def seq_signal(count):
    me = lax.axis_index("seq")
    barrier = pltpu.get_barrier_semaphore()
    for k in range(1, count):
        pl.semaphore_signal(
            barrier, inc=1, device_id={"seq": lax.rem(me + k, count)}, device_id_type=MESH
        )


def seq_wait(count):
    pl.semaphore_wait(pltpu.get_barrier_semaphore(), count - 1)


def send(source, target, send_sem, recv_sem, device):
    return pltpu.make_async_remote_copy(
        src_ref=source,
        dst_ref=target,
        send_sem=send_sem,
        recv_sem=recv_sem,
        device_id={"seq": device},
        device_id_type=MESH,
    )


def spans(index, span):
    return pl.ds(pl.multiple_of(index * span, LANES), span)


def swap_halves(values):
    lane = lax.broadcasted_iota(jnp.int32, values.shape, 1)
    return jnp.where(
        lane % HEAD < HEAD // 2,
        pltpu.roll(values, LANES - HEAD // 2, 1),
        pltpu.roll(values, HEAD // 2, 1),
    )


def head_masks(values):
    lane = lax.broadcasted_iota(jnp.int32, values.shape, 1)
    zero = jnp.zeros_like(values)
    return jnp.where(lane < HEAD, values, zero), jnp.where(lane < HEAD, zero, values)


def block_rows(index):
    return slice(index * BLOCK, (index + 1) * BLOCK)


def rotated(values, tables, first, rows):
    values = values.astype(F32)
    return values * tables[first, rows, :] + swap_halves(values) * tables[first + 1, rows, :]


def rotated_back(values, tables, first, rows):
    return values * tables[first, rows, :] - swap_halves(values) * tables[first + 1, rows, :]


def norm_parts(values):
    center = jnp.mean(values, axis=-1, keepdims=True)
    shifted = values - center
    inverse = lax.rsqrt(jnp.mean(shifted * shifted, axis=-1, keepdims=True) + EPSILON)
    return shifted * inverse, inverse


def seg_column(seg_row, index, size):
    columns = []
    for i in range(size // LANES):
        start = index * size + i * LANES
        square = jnp.broadcast_to(seg_row[:, start : start + LANES], (LANES, LANES))
        columns.append(jnp.transpose(square)[:, :1])
    return jnp.concatenate(columns, axis=0)


def make_tables(seg_row, tables):
    lane = lax.broadcasted_iota(jnp.int32, (1, LANES), 1)
    index = (lane % (HEAD // 2)).astype(F32)
    theta_rate = jnp.exp(-2.0 * index / HEAD * math.log(10000.0))
    zeta_base = (2.0 * index + 0.4 * HEAD) / (1.4 * HEAD)
    rate = jnp.log(zeta_base) / 512.0
    for block in range(seg_row.shape[1] // LANES):
        rows = slice(block * LANES, (block + 1) * LANES)
        before = (seg_row[...] < seg_column(seg_row, block, LANES)).astype(F32)
        place = lax.broadcasted_iota(jnp.int32, (LANES, 1), 0) + block * LANES
        place = place.astype(F32) - jnp.sum(before, axis=1, keepdims=True)
        cos_part = jnp.cos(place * theta_rate)
        sin_part = jnp.sin(place * theta_rate)
        sin_part = jnp.where(lane % HEAD < HEAD // 2, -sin_part, sin_part)
        for k, factor in enumerate((jnp.exp(place * rate), jnp.exp(-place * rate))):
            tables[2 * k, rows, :] = cos_part * factor
            tables[2 * k + 1, rows, :] = sin_part * factor


def front_kernel(
    count, groups, num_vec, *refs
):
    (x_ref, wq_ref, wk_ref, wv_ref, segr_ref), refs = refs[:5], refs[5:]
    pieces, refs = refs[:num_vec], refs[num_vec:]
    (
        act_out, qkv_out, tab_out, o_ref, lse_ref, mixed_ref, vecs_ref, act_ref, qkv_ref,
        weights, staged, tab_ref, bias, qs, ks, load_sem, act_sem, tab_sem, qkv_sem, send_sem, recv_sem, back_send_sem, back_recv_sem,
    ) = refs
    me = lax.axis_index("seq")
    pairs, length = qkv_ref.shape[:2]
    tokens, width = x_ref.shape
    span = length // count
    blocks = length // BLOCK
    mine, row = lax.rem(me, groups), me // groups
    seq_signal(count)
    loads = []
    for j in range(pairs * groups):
        for i, source in enumerate((wq_ref, wk_ref, wv_ref)):
            copy = pltpu.make_async_copy(
                source.at[:, j * LANES : (j + 1) * LANES],
                weights.at[j, :, i * LANES : (i + 1) * LANES],
                load_sem.at[3 * j + i],
            )
            copy.start()
            loads.append(copy)

    place = 0
    for piece in pieces:
        for i in range(piece.shape[0]):
            vecs_ref[:, place : place + LANES] = piece[i : i + 1, :].astype(F32)
            place += LANES

    def there_to(p, device):
        k = lax.rem(device - me + count, count)
        return send(
            staged.at[lax.rem(device, groups) * pairs + p, spans(device // groups, span), :],
            qkv_ref.at[p, spans(me, span), :],
            send_sem.at[p, k],
            recv_sem.at[p, k],
            device,
        )

    def there(p, k):
        return there_to(p, lax.rem(me + k, count))

    def project_rows(p, rows):
        for group in range(groups):
            j = group * pairs + p
            staged[j, rows, :] = dot(act_ref[rows, :], weights[j], 1, 0).astype(BF16)

    for copy in loads:
        copy.wait()
    seq_wait(count)
    steps = tokens // BLOCK
    rows_each = BLOCK // span

    def first_step(b, carry):
        block = lax.rem(row // rows_each + b, steps)
        for i in range(BLOCK // LANES):
            rows = pl.ds(pl.multiple_of(block * BLOCK + i * LANES, LANES), LANES)
            normed, _ = norm_parts(x_ref[rows, :].astype(F32))
            act = normed * vecs_ref[:, :width] + vecs_ref[:, width : 2 * width]
            act_ref[rows, :] = act.astype(BF16)
        project_rows(0, pl.ds(pl.multiple_of(block * BLOCK, BLOCK), BLOCK))
        for i in range(rows_each * groups):
            device = block * rows_each * groups + i
            pl.when(device != me)(lambda device=device: there_to(0, device).start())
        return carry

    lax.fori_loop(0, steps, first_step, 0)
    act_copy = pltpu.make_async_copy(act_ref, act_out, act_sem)
    act_copy.start()

    def qkv_copy(p):
        return pltpu.make_async_copy(qkv_ref.at[p], qkv_out.at[p], qkv_sem.at[p])

    def keep_own(p):
        qkv_ref[p, spans(me, span), :] = staged[mine * pairs + p, spans(row, span), :]

    keep_own(0)

    def back(p, k):
        device = lax.rem(me + k, count)
        return send(
            o_ref.at[p, spans(device, span), :],
            mixed_ref.at[spans(row, span), spans(mine * pairs + p, LANES)],
            back_send_sem.at[p, k],
            back_recv_sem.at[p, k],
            device,
        )

    def project(p, carry):
        def rows_step(r, inner):
            project_rows(p, pl.ds(pl.multiple_of(r * BLOCK, BLOCK), BLOCK))
            return inner

        lax.fori_loop(0, steps, rows_step, 0)
        for k in range(1, count):
            there(p, k).start()
        keep_own(p)
        return carry

    lax.fori_loop(1, pairs, project, 0)
    make_tables(segr_ref, tab_ref)
    tab_copy = pltpu.make_async_copy(tab_ref, tab_out, tab_sem)
    tab_copy.start()
    for qb in range(blocks):
        rows = block_rows(qb)
        keys = (qb + 1) * BLOCK
        same = seg_column(segr_ref, qb, BLOCK) == segr_ref[:, :keys]
        query = lax.broadcasted_iota(jnp.int32, (BLOCK, keys), 0) + qb * BLOCK
        key = lax.broadcasted_iota(jnp.int32, (BLOCK, keys), 1)
        bias[rows, :keys] = jnp.where(same & (key <= query), 0.0, MASKED)

    def attend(p, carry):
        for k in range(1, count):
            there(p, k).wait_recv()
        qkv_copy(p).start()
        for qb in range(blocks):
            rows = block_rows(qb)
            q = rotated(qkv_ref[p, rows, :LANES], tab_ref, 0, rows) * (HEAD**-0.5)
            q0, q1 = head_masks(q)
            qs[0, rows, :] = q0.astype(BF16)
            qs[1, rows, :] = q1.astype(BF16)
            k = rotated(qkv_ref[p, rows, LANES : 2 * LANES], tab_ref, 2, rows)
            ks[rows, :] = k.astype(BF16)
        for qb in range(blocks):
            rows = block_rows(qb)
            keys = (qb + 1) * BLOCK
            outs = []
            logs = []
            for h in range(2):
                scores = dot(qs[h, rows, :], ks[:keys, :], 1, 1) + bias[rows, :keys]
                top = jnp.max(scores, axis=1, keepdims=True)
                expo = jnp.exp(scores - top)
                total = jnp.sum(expo, axis=1, keepdims=True)
                outs.append(dot(expo.astype(BF16), qkv_ref[p, :keys, 2 * LANES :], 1, 0) / total)
                logs.append(jnp.broadcast_to(top + jnp.log(total), (BLOCK, LANES)))
            lane = lax.broadcasted_iota(jnp.int32, (BLOCK, LANES), 1)
            o_ref[p, rows, :] = jnp.where(lane < HEAD, outs[0], outs[1]).astype(BF16)
            logs_t = jnp.transpose(jnp.where(lane < HEAD, logs[0], logs[1]))
            lse_ref[p, 0:1, rows] = logs_t[0:1]
            lse_ref[p, 1:2, rows] = logs_t[HEAD : HEAD + 1]
        for k in range(1, count):
            back(p, k).start()
        mixed_ref[spans(row, span), spans(mine * pairs + p, LANES)] = o_ref[p, spans(me, span), :]
        return carry

    lax.fori_loop(0, pairs, attend, 0)

    def drain(p, carry):
        for k in range(1, count):
            there(p, k).wait_send()
            back(p, k).wait()
        return carry

    lax.fori_loop(0, pairs, drain, 0)
    act_copy.wait()
    tab_copy.wait()
    for p in range(pairs):
        qkv_copy(p).wait()


def front(
    x, w_query, w_key, w_value, seg_row, vectors, count, groups, collective_id
):
    tokens, model_width = x.shape
    pieces = [vector.reshape(vector.shape[0] // LANES, LANES) for vector in vectors]
    total = sum(vector.shape[0] for vector in vectors)
    head_width = w_query.shape[1]
    length = seg_row.shape[1]
    pairs = head_width // groups // LANES
    whole = pl.BlockSpec(memory_space=pltpu.VMEM)
    any_space = pl.BlockSpec(memory_space=pl.ANY)
    return pl.pallas_call(
        functools.partial(front_kernel, count, groups, len(pieces)),
        out_shape=[
            jax.ShapeDtypeStruct((tokens, model_width), BF16),
            jax.ShapeDtypeStruct((pairs, length, 3 * LANES), BF16),
            jax.ShapeDtypeStruct((4, length, LANES), F32),
            jax.ShapeDtypeStruct((pairs, length, LANES), BF16),
            jax.ShapeDtypeStruct((pairs, 8, length), F32),
            jax.ShapeDtypeStruct((tokens, head_width), BF16),
            jax.ShapeDtypeStruct((1, total), F32),
        ],
        in_specs=[whole] + [any_space] * 3 + [whole] * (1 + len(pieces)),
        out_specs=[any_space] * 3 + [whole] * 4,
        scratch_shapes=[
            pltpu.VMEM((tokens, model_width), BF16),
            pltpu.VMEM((pairs, length, 3 * LANES), BF16),
            pltpu.VMEM((pairs * groups, model_width, 3 * LANES), BF16),
            pltpu.VMEM((pairs * groups, tokens, 3 * LANES), BF16),
            pltpu.VMEM((4, length, LANES), F32),
            pltpu.VMEM((length, length), F32),
            pltpu.VMEM((2, length, LANES), BF16),
            pltpu.VMEM((length, LANES), BF16),
            pltpu.SemaphoreType.DMA((3 * pairs * groups,)),
            pltpu.SemaphoreType.DMA,
            pltpu.SemaphoreType.DMA,
            pltpu.SemaphoreType.DMA((pairs,)),
        ]
        + [pltpu.SemaphoreType.DMA((pairs, count))] * 4,
        compiler_params=pltpu.CompilerParams(
            collective_id=collective_id, has_side_effects=True, vmem_limit_bytes=VMEM_LIMIT
        ),
        cost_estimate=cost(60),
    )(x, w_query, w_key, w_value, seg_row, *pieces)


def back_work(env, count, tp_count, groups):
    low_ref, wout_ref, mixed_ref = env["low"], env["w_out"], env["mixed"]
    sums_ref, qkv_ref, o_ref, lse_ref = env["head_sums"], env["qkv"], env["o"], env["lse"]
    segr_ref, tab_ref, bias = env["seg_row"], env["tables"], env["bias"]
    grads_ref, vec_grads_ref = env["grads"], env["head_vec_grads"]
    do_ref, scaled, part = env["do"], env["scaled"], env["head_part"]
    do_row, made, delta = env["do_row"], env["made"], env["delta"]
    qs, ks, kms, dos, dq, dk, dv = (env[name] for name in ("qs", "ks", "kms", "dos", "dq", "dk", "dv"))
    me = lax.axis_index("seq")
    pairs, length = qkv_ref.shape[:2]
    tokens, features = low_ref.shape
    head_width = mixed_ref.shape[1]
    span = length // count
    blocks = length // BLOCK
    mine, row = lax.rem(me, groups), me // groups
    gain = head_vec(env["vecs"], head_width, 0)

    def normed_rows(rows):
        first, second = to_columns(sums_ref[:, rows], 2)
        center = first / features
        inverse = lax.rsqrt(second / features - center * center + EPSILON)
        return (mixed_ref[rows, :].astype(F32) - center) * inverse, inverse

    def head_terms(r):
        wide = pl.ds(pl.multiple_of(r * BLOCK, BLOCK), BLOCK)
        scaled[wide, :] = dot(low_ref[wide, :], wout_ref[...], 1, 0)
        for k in range(BLOCK // LANES):
            rows = row_block(r * (BLOCK // LANES) + k)
            normed, _ = normed_rows(rows)
            grad = scaled[rows, :]
            vec_grads_ref[0] += fold(grad * normed)
            vec_grads_ref[1] += fold(grad)
            grad = grad * gain
            scaled[rows, :] = grad
            part[:, rows] = to_row(
                [
                    jnp.sum(grad, axis=-1, keepdims=True),
                    jnp.sum(grad * normed, axis=-1, keepdims=True),
                ]
            )

    def part_copies(start):
        return share("tp", tp_count, lambda d: part, env["head_landed"], *env_pair(env, "head"), start)

    def head_apply(r, carry):
        rows = row_block(r)
        normed, inverse = normed_rows(rows)
        first, second = to_columns(part[:, rows], 2)
        grad = scaled[rows, :] - first / features - normed * (second / features)
        do_ref[rows, :] = (inverse * grad).astype(BF16)
        return carry

    def there(p, k):
        device = lax.rem(me + k, count)
        return send(
            do_ref.at[spans(device // groups, span), spans(lax.rem(device, groups) * pairs + p, LANES)],
            do_row.at[p, spans(me, span), :],
            env["there_send"].at[p, k],
            env["there_recv"].at[p, k],
            device,
        )

    def back(p, k):
        device = lax.rem(me + k, count)
        return send(
            made.at[p, spans(device, span), :],
            grads_ref.at[spans(row, span), spans(mine * pairs + p, 3 * LANES)],
            env["back_send"].at[p, k],
            env["back_recv"].at[p, k],
            device,
        )

    def share_out(p, carry):
        for k in range(1, count):
            there(p, k).start()
        do_row[p, spans(me, span), :] = do_ref[spans(row, span), spans(mine * pairs + p, LANES)]
        return carry

    def prepare():
        for kb in range(blocks):
            rows = block_rows(kb)
            start = kb * BLOCK
            shape = (BLOCK, length - start)
            same = seg_column(segr_ref, kb, BLOCK) == segr_ref[:, start:]
            key = lax.broadcasted_iota(jnp.int32, shape, 0)
            query = lax.broadcasted_iota(jnp.int32, shape, 1)
            bias[rows, start:] = jnp.where(same & (key <= query), 0.0, MASKED)

    def pair_start(p):
        for qb in range(blocks):
            rows = block_rows(qb)
            q = rotated(qkv_ref[p, rows, :LANES], tab_ref, 0, rows) * (HEAD**-0.5)
            q0, q1 = head_masks(q)
            qs[0, rows, :] = q0.astype(BF16)
            qs[1, rows, :] = q1.astype(BF16)
            k = rotated(qkv_ref[p, rows, LANES : 2 * LANES], tab_ref, 2, rows)
            ks[rows, :] = k.astype(BF16)
            k0, k1 = head_masks(k)
            kms[0, rows, :] = k0.astype(BF16)
            kms[1, rows, :] = k1.astype(BF16)
        dq[...] = jnp.zeros_like(dq)
        dk[...] = jnp.zeros_like(dk)
        dv[...] = jnp.zeros_like(dv)
        for k in range(1, count):
            there(p, k).wait_recv()
        for qb in range(blocks):
            rows = block_rows(qb)
            grad = do_row[p, rows, :].astype(F32)
            d0, d1 = head_masks(grad)
            dos[0, rows, :] = d0.astype(BF16)
            dos[1, rows, :] = d1.astype(BF16)
            prod = jnp.transpose(grad * o_ref[p, rows, :].astype(F32))
            delta[0:1, rows] = jnp.sum(prod[:HEAD], axis=0, keepdims=True)
            delta[1:2, rows] = jnp.sum(prod[HEAD:], axis=0, keepdims=True)

    def pair_block(p, qb):
        cols = block_rows(qb)
        for kb in range(qb + 1):
            rows = block_rows(kb)
            value = qkv_ref[p, rows, 2 * LANES :]
            for h in range(2):
                scores = dot(ks[rows, :], qs[h, cols, :], 1, 1) + bias[rows, cols]
                probs = jnp.exp(scores - lse_ref[p, h : h + 1, cols])
                grads = dot(value, dos[h, cols, :], 1, 1)
                dscores = (probs * (grads - delta[h : h + 1, cols])).astype(BF16)
                dv[rows, :] += dot(probs.astype(BF16), dos[h, cols, :], 1, 0)
                dk[rows, :] += dot(dscores, qs[h, cols, :], 1, 0)
                dq[cols, :] += dot(dscores, kms[h, rows, :], 0, 0)

    def pair_end(p):
        for qb in range(blocks):
            rows = block_rows(qb)
            grad = dq[rows, :] * (HEAD**-0.5)
            made[p, rows, :LANES] = rotated_back(grad, tab_ref, 0, rows).astype(BF16)
            made[p, rows, LANES : 2 * LANES] = rotated_back(dk[rows, :], tab_ref, 2, rows).astype(BF16)
            made[p, rows, 2 * LANES :] = dv[rows, :].astype(BF16)
        for k in range(1, count):
            back(p, k).start()
        grads_ref[spans(row, span), spans(mine * pairs + p, 3 * LANES)] = made[p, spans(me, span), :]

    head_steps = tokens // BLOCK
    attend_at = head_steps + 3
    weights_at = attend_at + pairs * (blocks // 2) + 3
    tiles = features // ROWS

    def weight_copy(tile):
        rows = pl.ds(pl.multiple_of(tile * ROWS, ROWS), ROWS)
        slot = lax.rem(tile, 2)
        return pltpu.make_async_copy(
            env["weight_stage"].at[slot], env["head_terms"].at[rows, :], env["weight_sem"].at[slot]
        )

    def head_weights(tile):
        cols = pl.ds(pl.multiple_of(tile * ROWS, ROWS), ROWS)
        slot = lax.rem(tile, 2)
        wide = 3 * head_width
        for left, right, first in (
            (env["first_act"], grads_ref, 0), (low_ref, env["head_act"], wide)
        ):
            env["turned"][...] = jnp.transpose(left[:, cols])
            for n in range(right.shape[1] // head_width):
                part_cols = slice(n * head_width, (n + 1) * head_width)
                target = slice(first + n * head_width, first + (n + 1) * head_width)
                value = dot(env["turned"][...], right[:, part_cols], 1, 0)
                env["weight_stage"][slot, :, target] = value.astype(BF16)
        weight_copy(tile).start()

    vec_grads_ref[...] = jnp.zeros_like(vec_grads_ref)

    def step(now):
        t = now - 1
        pl.when((t >= 0) & (t < head_steps))(lambda: head_terms(t))

        @pl.when(t == head_steps - 1)
        def _():
            part_copies(True)
            env["head_landed"][lax.axis_index("tp")] = part[...]

        pl.when(t == head_steps)(prepare)

        @pl.when(t == head_steps + 1)
        def _():
            for copy in part_copies(False):
                copy.wait()
            part[...] = total_of(env["head_landed"], tp_count)
            lax.fori_loop(0, tokens // LANES, head_apply, 0)
            lax.fori_loop(0, pairs, share_out, 0)

        each = blocks // 2
        turn = t - attend_at
        p = turn // each
        for i in range(each):

            @pl.when((turn >= 0) & (turn < pairs * each) & (lax.rem(turn + 32 * each, each) == i))
            def _():
                if i == 0:
                    pair_start(p)
                pair_block(p, 2 * i)
                pair_block(p, 2 * i + 1)
                if i == each - 1:
                    pair_end(p)

        tile = t - weights_at

        @pl.when(tile == 0)
        def _():
            def arrive(p, carry):
                for k in range(1, count):
                    back(p, k).wait_recv()
                return carry

            lax.fori_loop(0, pairs, arrive, 0)

        pl.when((tile >= 2) & (tile < tiles))(lambda: weight_copy(tile - 2).wait())
        pl.when((tile >= 0) & (tile < tiles))(lambda: head_weights(tile))

    def end():
        def drain(p, carry):
            for k in range(1, count):
                there(p, k).wait_send()
                back(p, k).wait_send()
            return carry

        lax.fori_loop(0, pairs, drain, 0)
        for tile in (tiles - 2, tiles - 1):
            weight_copy(tile).wait()

    return step, end, 1 + weights_at + tiles


def last_kernel(
    head_ref, up_ref, down_ref, grad_ref, block_ref, own_ref, split_ref,
    query_out, key_out, value_out, out_out, up_out, down_out, grad_out, block_out, *vectors
):
    grad_out[...] = grad_ref[...]
    block_out[...] = block_ref[...]
    up_out[...] = up_ref[...].astype(F32)
    down = down_ref[0].astype(F32)
    for k in range(1, down_ref.shape[0]):
        down = down + down_ref[k].astype(F32)
    down_out[...] = down
    width = out_out.shape[1]
    for j in range(width // LANES):
        for i, target in enumerate((query_out, key_out, value_out)):
            start = (3 * j + i) * LANES
            target[:, j * LANES : (j + 1) * LANES] = head_ref[:, start : start + LANES].astype(F32)
    out_out[...] = head_ref[:, 3 * width :].astype(F32)

    @pl.when(pl.program_id(0) == 0)
    def _():
        places = [(own_ref, i, 0) for i in range(4)]
        hidden = vectors[4].shape[0] * LANES
        places += [(split_ref, i, 0) for i in range(2)] + [(split_ref, i, hidden) for i in range(2)]
        for target, (source, row, first) in zip(vectors, places):
            for i in range(target.shape[0]):
                start = first + i * LANES
                target[i : i + 1, :] = source[row : row + 1, start : start + LANES]


def last_results(
    head_grads, up_grad, down_terms, input_grad, block_out, norm_own, norm_split, head_width
):
    rows = head_grads.shape[0]
    steps = rows // 32
    tokens, width = input_grad.shape

    def block(columns):
        return pl.BlockSpec((rows // steps, columns), lambda i: (i, 0))

    def whole(shape):
        return pl.BlockSpec(shape, lambda i: (0, 0))

    part = pl.BlockSpec((tokens // steps, width), lambda i: (i, 0))
    own = norm_own.shape[1]
    hidden = norm_split.shape[1] - head_width
    vectors = [(size // LANES, LANES) for size in (own,) * 4 + (hidden,) * 2 + (head_width,) * 2]
    sizes = [head_width] * 4 + [up_grad.shape[1]] * 2
    return pl.pallas_call(
        last_kernel,
        grid=(steps,),
        out_shape=[jax.ShapeDtypeStruct((rows, size), F32) for size in sizes]
        + [jax.ShapeDtypeStruct((tokens, width), BF16)] * 2
        + [jax.ShapeDtypeStruct(shape, F32) for shape in vectors],
        in_specs=[
            block(head_grads.shape[1]),
            block(up_grad.shape[1]),
            pl.BlockSpec((down_terms.shape[0], rows // steps, down_terms.shape[2]), lambda i: (0, i, 0)),
        ]
        + [part] * 2
        + [whole(norm_own.shape), whole(norm_split.shape)],
        out_specs=[block(size) for size in sizes] + [part] * 2 + [whole(shape) for shape in vectors],
        compiler_params=pltpu.CompilerParams(vmem_limit_bytes=VMEM_LIMIT),
        cost_estimate=cost(10),
    )(head_grads, up_grad, down_terms, input_grad, block_out, norm_own, norm_split)


def fold(values):
    rows, width = values.shape
    return jnp.sum(values.reshape(rows // 8, 8, width), axis=0)


def model_vec(env, index):
    width = env["out"].shape[1]
    return env["vecs"][:, index * width : (index + 1) * width]


def hidden_vec(env, index, cols=slice(None)):
    width = env["hidden_act"].shape[1]
    first = 4 * env["out"].shape[1] + index * width
    return env["vecs"][:, first : first + width][:, cols]


def head_vec(vecs_ref, width, index):
    total = vecs_ref.shape[1]
    first = total - (2 - index) * width
    return vecs_ref[:, first : first + width]


def finish_middle(total, here, own, env):
    middle = env["block"][here, :].astype(F32) + total
    env["middle"][own, :] = middle
    normed, _ = norm_parts(middle)
    return normed * model_vec(env, 2) + model_vec(env, 3)


def norm_back(base, values, total, gain, sums):
    normed, inverse = norm_parts(values)
    scaled = total * gain
    grad = base + inverse * (
        scaled
        - jnp.mean(scaled, axis=-1, keepdims=True)
        - normed * jnp.mean(scaled * normed, axis=-1, keepdims=True)
    )
    sums[0] += fold(total * normed)
    sums[1] += fold(total)
    return grad


def finish_second(total, here, own, env):
    base = env["cotangent"][here, :].astype(F32)
    grad = norm_back(base, env["middle"][own, :], total, model_vec(env, 2), env["sums"])
    env["middle_grad"][own, :] = grad
    return grad


def finish_first(total, here, own, env):
    values = env["block"][here, :].astype(F32)
    return norm_back(env["middle_grad"][own, :], values, total, model_vec(env, 0), env["sums"])


def to_row(columns):
    lane = lax.broadcasted_iota(jnp.int32, (LANES, LANES), 1)
    packed = jnp.zeros((LANES, LANES), F32)
    for i, column in enumerate(columns):
        packed = jnp.where(lane == i, column, packed)
    return jnp.transpose(packed)[:8]


def to_columns(rows, number):
    packed = jnp.transpose(jnp.concatenate([rows] * (LANES // 8), axis=0))
    return [packed[:, i : i + 1] for i in range(number)]


def row_block(r):
    return pl.ds(pl.multiple_of(r * LANES, LANES), LANES)


def tp_total(part, landed, send_sem, recv_sem, count):
    copies = share("tp", count, lambda d: part, landed, send_sem, recv_sem)
    landed[lax.axis_index("tp")] = part[...]
    for copy in copies:
        copy.wait()
    part[...] = total_of(landed, count)


def norm_heads(env, count, features):
    mixed, act, part = env["mixed"], env["head_act"], env["head_sums"]
    blocks = mixed.shape[0] // LANES

    def sums(r, carry):
        values = mixed[row_block(r), :].astype(F32)
        part[:, row_block(r)] = to_row(
            [
                jnp.sum(values, axis=-1, keepdims=True),
                jnp.sum(values * values, axis=-1, keepdims=True),
            ]
        )
        return carry

    lax.fori_loop(0, blocks, sums, 0)
    tp_total(part, env["head_landed"], env["head_send"], env["head_recv"], count)

    def apply(r, carry):
        first, second = to_columns(part[:, row_block(r)], 2)
        center = first / features
        inverse = lax.rsqrt(second / features - center * center + EPSILON)
        values = (mixed[row_block(r), :].astype(F32) - center) * inverse
        act[row_block(r), :] = (
            values * head_vec(env["vecs"], act.shape[1], 0) + head_vec(env["vecs"], act.shape[1], 1)
        ).astype(BF16)
        return carry

    lax.fori_loop(0, blocks, apply, 0)


def normal_parts(values):
    size = jnp.abs(values) * (0.5**0.5)
    bell = jnp.exp(-0.5 * values * values)
    t = 1.0 / (1.0 + 0.3275911 * size)
    poly = 1.061405429
    for factor in (-1.453152027, 1.421413741, -0.284496736, 0.254829592):
        poly = poly * t + factor
    tail = 0.5 * poly * t * bell
    return jnp.where(values < 0.0, tail, 1.0 - tail), bell * (1.0 / math.sqrt(2.0 * math.pi))


def hidden_copies(env, count, block):
    me = lax.axis_index("tp")
    send_sem, recv_sem = env_pair(env, "hidden")
    return [
        pltpu.make_async_remote_copy(
            src_ref=env["hidden_sums"].at[:, row_block(block)],
            dst_ref=env["hidden_landed"].at[me, :, row_block(block)],
            send_sem=send_sem.at[block, k],
            recv_sem=recv_sem.at[block, k],
            device_id={"tp": lax.rem(me + k, count)},
            device_id_type=MESH,
        )
        for k in range(1, count)
    ]


def hidden_rows(env, count, block):
    rows = row_block(block)
    width = env["w_up"].shape[1]
    sums = [jnp.zeros((LANES, 1), F32)] * 4
    for n in range(width // TILE):
        cols = slice(n * TILE, (n + 1) * TILE)
        values = dot(env["out"][rows, :], env["w_up"][:, cols], 1, 0)
        below, density = normal_parts(values)
        active = values * below
        env["hidden_act"][rows, cols] = active.astype(BF16)
        env["grad_up"][rows, cols] = (below + values * density).astype(BF16)
        scaled = env["hidden_grad"][rows, cols].astype(F32) * hidden_vec(env, 0, cols)
        for i, term in enumerate((active, active * active, scaled, scaled * active)):
            sums[i] = sums[i] + jnp.sum(term, axis=-1, keepdims=True)
    packed = to_row(sums)
    env["hidden_sums"][:, rows] = packed
    env["hidden_landed"][lax.axis_index("tp"), :, rows] = packed
    for copy in hidden_copies(env, count, block):
        copy.start()


def norm_hidden(env, count, features, block):
    act, slope, landed = env["hidden_act"], env["grad_up"], env["hidden_landed"]
    rows = row_block(block)
    for copy in hidden_copies(env, count, block):
        copy.wait()
    total = landed[0, :, rows]
    for k in range(1, count):
        total = total + landed[k, :, rows]
    sums = [column / features for column in to_columns(total, 4)]
    center = sums[0]
    inverse = lax.rsqrt(sums[1] - center * center + EPSILON)
    cross = inverse * (sums[3] - center * sums[2])
    for n in range(act.shape[1] // TILE):
        cols = slice(n * TILE, (n + 1) * TILE)
        gain = hidden_vec(env, 0, cols)
        normed = (act[rows, cols].astype(F32) - center) * inverse
        grad = env["hidden_grad"][rows, cols].astype(F32)
        back = inverse * (grad * gain - sums[2] - normed * cross)
        slope[rows, cols] = (back * slope[rows, cols].astype(F32)).astype(BF16)
        act[rows, cols] = (normed * gain + hidden_vec(env, 1, cols)).astype(BF16)
        env["hidden_vec_grads"][0, :, cols] += fold(grad * normed)
        env["hidden_vec_grads"][1, :, cols] += fold(grad)
    for name in ("hidden_act", "grad_up"):
        row_store(env, name, block).start()


def row_store(env, name, block):
    rows = row_block(block)
    return pltpu.make_async_copy(
        env[name].at[rows, :], env["target " + name].at[rows, :], env["sem " + name].at[block]
    )


def whole_store(env, name):
    return pltpu.make_async_copy(env[name], env["target " + name], env["sem " + name].at[0])


def spread_copy(env, device):
    landed, terms = env["spread"], env["w_down_terms"]
    count, own = landed.shape[:2]
    me = lax.axis_index("seq")
    k = lax.rem(device - me + count, count)
    rows = pl.ds(pl.multiple_of(device * own, own), own)
    return pltpu.make_async_remote_copy(
        src_ref=terms.at[rows, :],
        dst_ref=landed.at[me],
        send_sem=env["spread_send"].at[k],
        recv_sem=env["spread_recv"].at[k],
        device_id={"seq": device},
        device_id_type=MESH,
    )


def spread_own(env):
    landed, terms = env["spread"], env["w_down_terms"]
    own = landed.shape[1]
    me = lax.axis_index("seq")
    rows = pl.ds(pl.multiple_of(me * own, own), own)
    return pltpu.make_async_copy(terms.at[rows, :], landed.at[me], env["spread_own"].at[0])


def spread_rows(env, rows):
    own = env["spread"].shape[1]
    me = lax.axis_index("seq")
    for i in range(ROWS // own):
        device = rows.start // own + i
        pl.when(device != me)(lambda device=device: spread_copy(env, device).start())
        pl.when(device == me)(lambda: spread_own(env).start())


def spread_wait(env):
    count = env["spread"].shape[0]
    me = lax.axis_index("seq")
    for k in range(1, count):
        spread_copy(env, lax.rem(me + k, count)).wait()
    spread_own(env).wait()


def split_copies(env, seq_count):
    split = env["split"]
    return share("seq", seq_count, lambda d: split, env["split_landed"], *env_pair(env, "split"), False)


def env_pair(env, name):
    return env[name + "_send"], env[name + "_recv"]


def split_start(env, seq_count):
    hidden = env["hidden_vec_grads"].shape[2]
    split = env["split"]
    split[...] = jnp.zeros_like(split)
    for i in range(2):
        split[i : i + 1, :hidden] = jnp.sum(env["hidden_vec_grads"][i], axis=0, keepdims=True)
        split[i : i + 1, hidden:] = jnp.sum(env["head_vec_grads"][i], axis=0, keepdims=True)
    for copy in split_copies(env, seq_count):
        copy.start()
    env["split_landed"][lax.axis_index("seq")] = split[...]


def full_copies(env, count):
    full = env["full"]
    return share("tp", count, lambda d: full, env["full_landed"], *env_pair(env, "full"), False)


def full_start(env, count):
    full = env["full"]
    full[...] = jnp.zeros_like(full)
    for i in range(2):
        full[i : i + 1, :] = jnp.sum(env["second_sums"][i], axis=0, keepdims=True)
        full[2 + i : 3 + i, :] = jnp.sum(env["sums"][i], axis=0, keepdims=True)
    for copy in full_copies(env, count):
        copy.start()
    env["full_landed"][lax.axis_index("tp")] = full[...]


def norm_finish(env, seq_count, count):
    full, own = env["full"], env["norm_own"].shape[1]
    me = lax.axis_index("seq")
    for copy in full_copies(env, count):
        copy.wait()
    full[...] = total_of(env["full_landed"], count)

    def piece(device):
        return pl.ds(pl.multiple_of(device * own, LANES), own)

    copies = share(
        "seq", seq_count, lambda d: full.at[:, piece(d)], env["own_landed"], *env_pair(env, "own")
    )
    env["own_landed"][me] = full[:, piece(me)]
    for copy in split_copies(env, seq_count):
        copy.wait()
    env["norm_split"][...] = total_of(env["split_landed"], seq_count)
    for copy in copies:
        copy.wait()
    env["norm_own"][...] = total_of(env["own_landed"], seq_count)


def load_pairs(env):
    copies = []
    for i, name in enumerate(("w_query", "w_key", "w_value")):
        for j in range(env[name].shape[1] // LANES):
            copy = pltpu.make_async_copy(
                env[name].at[:, j * LANES : (j + 1) * LANES],
                env["w_pairs"].at[:, (3 * j + i) * LANES : (3 * j + i + 1) * LANES],
                env["pair_sem"].at[3 * j + i],
            )
            copy.start()
            copies.append(copy)
    return copies


def line_kernel(plan, count, chunks, group, slack, *refs):
    env = dict(zip(plan["order"], refs, strict=True))
    finish, parts, tasks = plan["finish"], plan["parts"], plan["tasks"]
    num_task = len(tasks)
    out_ref = env["out"]
    in_a, in_b = env["in_a"], env["in_b"]
    rsa_s, rsa_r, rsb_s, rsb_r = (env[name] for name in ("rsa_s", "rsa_r", "rsb_s", "rsb_r"))
    aga_s, aga_r, agb_s, agb_r = (env[name] for name in ("aga_s", "aga_r", "agb_s", "agb_r"))
    z = lax.axis_index("tp")
    tokens, width = out_ref.shape
    half = tokens // 2
    size = half // chunks
    ahead = slack * (count - 1)
    spread_out = SLACK_OUT * (count - 1)
    steps = chunks + ahead + spread_out
    from_first, from_last = slack * z, slack * (count - 1 - z)
    out_first, out_last = SLACK_OUT * z, SLACK_OUT * (count - 1 - z)
    first, last = z == 0, z == count - 1
    up = jnp.minimum(z + 1, count - 1)
    down = jnp.maximum(z - 1, 0)

    loads = {
        name: pltpu.make_async_copy(env["source " + name], env[name], env["load_sem"].at[i])
        for i, name in enumerate(plan["held"])
    }
    behind = plan["late"] + plan["later"]
    for name in plan["held"]:
        if name not in behind:
            loads[name].start()
    started = plan["start"](env) if plan["start"] else []
    seq_count = plan["seq_count"]
    axis_barrier([("tp", count)] + ([("seq", plan["seq_barrier"])] if plan["seq_barrier"] else []))
    if "sums" in env:
        env["sums"][...] = jnp.zeros_like(env["sums"])
    if seq_count:
        split_start(env, seq_count)

    def own_rows(c):
        return pl.ds(pl.multiple_of(c * size, size), size)

    def a_rows(c):
        return own_rows(c)

    def b_rows(c):
        return pl.ds(pl.multiple_of(half + c * size, size), size)

    def hop(source, target, send, recv, c, device):
        return pltpu.make_async_remote_copy(
            src_ref=source,
            dst_ref=target,
            send_sem=send.at[c],
            recv_sem=recv.at[c],
            device_id={"tp": device},
            device_id_type=MESH,
        )

    def gather_a(c):
        rows = out_ref.at[a_rows(c), :]
        return hop(rows, rows, aga_s, aga_r, c, up)

    def gather_b(c):
        rows = out_ref.at[b_rows(c), :]
        return hop(rows, rows, agb_s, agb_r, c, down)

    def reduce_a(c):
        rows = in_a.at[own_rows(c), :]
        return hop(rows, rows, rsa_s, rsa_r, c, down)

    def reduce_b(c):
        rows = in_b.at[own_rows(c), :]
        return hop(rows, rows, rsb_s, rsb_r, c, up)

    def block_start(t, offset):
        return jnp.clip((t - lax.rem(t, group) - offset) * size, 0, half - group * size)

    def reduce_step(t, c, offset, place, rows, landed, move, gather, starts, ends):
        here = rows(c)
        own = own_rows(c)

        def term():
            if not parts:
                return env["ready"][here, :].astype(F32)
            row = place * group * size + c * size - block_start(t, offset)
            return env["part"][pl.ds(pl.multiple_of(row, size), size), :]

        @pl.when(starts)
        def _():
            landed[own, :] = term().astype(BF16)
            move(c).start()

        @pl.when(jnp.logical_not(starts))
        def _():
            move(c).wait_recv()

        @pl.when(jnp.logical_not(starts | ends))
        def _():
            landed[own, :] = (landed[own, :].astype(F32) + term()).astype(BF16)
            move(c).start()

        @pl.when(ends)
        def _():
            total = landed[own, :].astype(F32) + term()
            out_ref[here, :] = finish(total, here, own, env).astype(BF16)
            gather(c).start()

    def gather_step(c, gather, starts, ends):
        @pl.when(jnp.logical_not(starts))
        def _():
            gather(c).wait_recv()

        @pl.when(jnp.logical_not(starts | ends))
        def _():
            gather(c).start()

    def when_chunk(c, work):
        pl.when((c >= 0) & (c < chunks))(lambda: work(c))

    def make_parts(t):
        top = pl.ds(pl.multiple_of(block_start(t, from_last), size), group * size)
        low = pl.ds(pl.multiple_of(half + block_start(t, from_first), size), group * size)

        def columns(n, carry):
            cols = pl.ds(pl.multiple_of(n * TILE, TILE), TILE)
            total = 0.0
            for left, right in parts:
                rows = jnp.concatenate([env[left][top, :], env[left][low, :]], axis=0)
                total = total + dot(rows, env[right][cols, :], 1, 1)
            env["part"][:, cols] = total
            return carry

        lax.fori_loop(0, width // TILE, columns, 0)

    def task_rows(index, tile):
        if tasks[index][0] == "spread":
            tiles = env[tasks[index][3]].shape[0] // ROWS
            own = ROWS // env["spread"].shape[1]
            tile = lax.rem(lax.axis_index("seq") // own + 1 + tile, tiles)
        return pl.ds(pl.multiple_of(tile * ROWS, ROWS), ROWS)

    def run_task(index, tile, slot):
        kind, left, right, name = tasks[index]
        target = env[name]
        rows = task_rows(index, tile)
        if kind in ("weight", "spread"):
            env["turned"][...] = jnp.transpose(env[left][:, rows])

        def columns(n, carry):
            cols = pl.ds(pl.multiple_of(n * TILE, TILE), TILE)
            if kind in ("weight", "spread"):
                value = dot(env["turned"][...], env[right][:, cols], 1, 0)
            elif kind == "keep":
                value = dot(env[left][rows, :], env[right][:, cols], 1, 0)
            else:
                value = dot(env[left][rows, :], env[right][cols, :], 1, 1)
                top = tile * ROWS < half
                mine = (first & top) | (last & jnp.logical_not(top))
                own = pl.multiple_of(lax.rem(tile * ROWS, half), ROWS)
                base = env["middle"][pl.ds(own, ROWS), cols]
                value = value + jnp.where(mine, base, 0.0)
            if kind == "keep":
                target[rows, cols] = value.astype(BF16)
            else:
                env["stage"][slot, :, cols] = value.astype(BF16)
            return carry

        lax.fori_loop(0, target.shape[1] // TILE, columns, 0)
        if kind != "keep":
            stage_copy(index, tile, slot).start()

    def stage_copy(index, tile, slot):
        target = env[tasks[index][3]]
        rows = task_rows(index, tile)
        return pltpu.make_async_copy(
            env["stage"].at[slot, :, : target.shape[1]], target.at[rows, :], env["stage_sem"].at[slot]
        )

    starts_at = [0]
    for task in tasks:
        starts_at.append(starts_at[-1] + env[task[3]].shape[0] // ROWS)
    task_total = starts_at[-1]
    staged = any(task[0] != "keep" for task in tasks)

    def step(t, carry):
        if parts:
            pl.when(lax.rem(t, group) == 0)(lambda: make_parts(t))
        when_chunk(
            t - from_last,
            lambda c: reduce_step(t, c, from_last, 0, a_rows, in_a, reduce_a, gather_a, last, first),
        )
        when_chunk(
            t - from_first,
            lambda c: reduce_step(t, c, from_first, 1, b_rows, in_b, reduce_b, gather_b, first, last),
        )
        when_chunk(t - ahead - out_first, lambda c: gather_step(c, gather_a, first, last))
        when_chunk(t - ahead - out_last, lambda c: gather_step(c, gather_b, last, first))
        for moment, waited in ((1, plan["late"]), (4, plan["later"])):

            @pl.when(t == moment)
            def _():
                for name in waited:
                    loads[name].wait()

        if num_task:
            turn = t - 1
            slot = lax.rem(turn + 2, 2)

            for index in range(num_task if staged else 0):
                low, high = starts_at[index] + 2, min(starts_at[index + 1] + 2, task_total)

                def staged_done(index=index, low=low):
                    stage_copy(index, turn - low, slot).wait()
                    if tasks[index][0] == "spread":
                        spread_rows(env, task_rows(index, turn - low))

                pl.when((turn >= low) & (turn < high))(staged_done)
            for index in range(num_task):
                low, high = starts_at[index], starts_at[index + 1]
                pl.when((turn >= low) & (turn < high))(
                    lambda index=index, low=low: run_task(index, turn - low, slot)
                )
        if work_step:
            work_step(t)
        if seq_count:
            pl.when(t == chunks + ahead)(lambda: full_start(env, count))
        for name, moment in plan["stores"].items():
            if moment == "reduced":
                pl.when(t == chunks + ahead)(lambda name=name: whole_store(env, name).start())
        done_a = t - ahead - out_first - (group - 1)
        done_b = t - ahead - out_last - (group - 1)
        has_a = (done_a >= 0) & (done_a < chunks) & (lax.rem(done_a + 64, group) == 0)
        has_b = (done_b >= 0) & (done_b < chunks) & (lax.rem(done_b + 64, group) == 0)

        @pl.when(has_a | has_b)
        def _():
            block = jnp.where(has_a, done_a // group, chunks // group + done_b // group)
            row_store(env, "out", block).start()
            if plan["rows_done"]:
                plan["rows_done"](env, block)

        if plan["rows_late"]:
            late_a = t - ahead - spread_out - (group - 1) - 2

            place = lax.rem(late_a + 64, group)

            @pl.when((late_a >= 0) & (place < 2))
            def _():
                plan["rows_late"](env, place * (chunks // group) + late_a // group)

        return carry

    for name in plan["held"]:
        if name not in behind:
            loads[name].wait()
    for copy in started:
        copy.wait()
    for name in behind:
        loads[name].start()
    if plan["before"]:
        plan["before"](env)
    for name, moment in plan["stores"].items():
        if moment == "before":
            whole_store(env, name).start()
    work_step = None
    if plan["work"]:
        work_step, work_end, work_steps = plan["work"](env)
        assert work_steps <= steps
    lax.fori_loop(0, steps, step, 0)
    if num_task:
        assert steps - 1 >= task_total
    if staged:
        assert task_total >= 2
        for turn in (task_total - 2, task_total - 1):
            index = max(i for i in range(num_task) if starts_at[i] <= turn)
            stage_copy(index, turn - starts_at[index], turn % 2).wait()
    if "spread" in env:
        spread_wait(env)
    if plan["rows_late"]:
        assert group > 2

        def rest(place, carry):
            plan["rows_late"](env, (place + 1) * (chunks // group) - 1)
            return carry

        lax.fori_loop(0, 2, rest, 0)
    if work_step:
        work_end()
    if seq_count:
        norm_finish(env, seq_count, count)

    def drain(c, carry):
        @pl.when(jnp.logical_not(first))
        def _():
            reduce_a(c).wait_send()
            gather_b(c).wait_send()

        @pl.when(jnp.logical_not(last))
        def _():
            reduce_b(c).wait_send()
            gather_a(c).wait_send()

        return carry

    lax.fori_loop(0, chunks, drain, 0)
    for name, moment in plan["stores"].items():
        if moment == "rows":
            for block in range(tokens // LANES):
                row_store(env, name, block).wait()
        else:
            whole_store(env, name).wait()


def line_sum(
    finish, count, held, vecs, parts, collective_id, *, tokens, late=(), later=(), tasks=(), owns=(),
    sent=(), stores=(), scratch=(), loose=(), chunks=16, group=4, turned=False, start=None, before=None, rows_done=None, rows_late=None, work=None,
    seq_count=0, seq_barrier=0, micros=110,
):
    names = dict(scratch)
    if parts:
        width = (held.get(parts[0][1]) if parts[0][1] in held else names[parts[0][1]]).shape[0]
    else:
        width = held["ready"].shape[1]
    half = tokens // 2
    depth = tokens if turned or any(task[0] == "weight" for task in tasks) else LANES
    staged = [shape.shape[-1] for _, shape in sent] if tasks else []
    stage_width = max(staged + [LANES])
    fixed = [
        ("in_a", pltpu.VMEM((half, width), BF16)),
        ("in_b", pltpu.VMEM((half, width), BF16)),
        ("part", pltpu.VMEM((2 * group * half // chunks if parts else 8, width), F32)),
        ("turned", pltpu.VMEM((ROWS, depth), BF16)),
        ("stage", pltpu.VMEM((2, ROWS if staged else 16, stage_width), BF16)),
        ("load_sem", pltpu.SemaphoreType.DMA((len(held),))),
        ("stage_sem", pltpu.SemaphoreType.DMA((2,))),
    ] + [
        (name, pltpu.SemaphoreType.DMA((chunks,)))
        for name in ("rsa_s", "rsa_r", "rsb_s", "rsb_r", "aga_s", "aga_r", "agb_s", "agb_r")
    ]
    assert half // chunks * group == LANES
    loose = dict(loose)
    stores = dict(stores, out="rows")
    shapes = [("out", jax.ShapeDtypeStruct((tokens, width), BF16))] + list(owns)
    scratch = list(scratch) + fixed
    for name, shape in shapes:
        if name in stores:
            scratch.append((name, pltpu.VMEM(shape.shape, shape.dtype)))
            number = tokens // LANES if stores[name] == "rows" else 1
            scratch.append(("sem " + name, pltpu.SemaphoreType.DMA((number,))))
    order = (
        ["source " + name for name in held]
        + list(loose)
        + list(vecs)
        + ["target " + name if name in stores else name for name, _ in shapes]
        + [name for name, _ in sent]
        + list(held)
        + [name for name, _ in scratch]
    )
    plan = dict(
        finish=finish,
        order=order,
        held=list(held),
        parts=parts,
        late=tuple(late),
        later=tuple(later),
        stores=stores,
        tasks=tasks,
        start=start,
        work=work,
        seq_count=seq_count,
        seq_barrier=seq_barrier or seq_count,
        before=before,
        rows_done=rows_done,
        rows_late=rows_late,
    )
    whole = pl.BlockSpec(memory_space=pltpu.VMEM)
    any_space = pl.BlockSpec(memory_space=pl.ANY)
    return pl.pallas_call(
        functools.partial(line_kernel, plan, count, chunks, group, SLACK),
        out_shape=[shape for _, shape in shapes] + [shape for _, shape in sent],
        in_specs=[any_space] * (len(held) + len(loose)) + [whole] * len(vecs),
        out_specs=[any_space if name in stores else whole for name, _ in shapes]
        + [any_space] * len(sent),
        scratch_shapes=[pltpu.VMEM(array.shape, array.dtype) for array in held.values()]
        + [shape for _, shape in scratch],
        compiler_params=pltpu.CompilerParams(
            collective_id=collective_id, has_side_effects=True, vmem_limit_bytes=VMEM_LIMIT
        ),
        cost_estimate=cost(micros),
    )(*held.values(), *loose.values(), *vecs.values())


def axis_barrier(counts):
    barrier = pltpu.get_barrier_semaphore()
    for axis, count in counts:
        me = lax.axis_index(axis)
        for k in range(1, count):
            pl.semaphore_signal(
                barrier, inc=1, device_id={axis: lax.rem(me + k, count)}, device_id_type=MESH
            )
    pl.semaphore_wait(barrier, sum(count - 1 for _, count in counts))


def share(axis, count, pick, landed, send_sem, recv_sem, start=True):
    me = lax.axis_index(axis)
    copies = []
    for k in range(1, count):
        device = lax.rem(me + k, count)
        copy = pltpu.make_async_remote_copy(
            src_ref=pick(device),
            dst_ref=landed.at[me],
            send_sem=send_sem.at[k],
            recv_sem=recv_sem.at[k],
            device_id={axis: device},
            device_id_type=MESH,
        )
        if start:
            copy.start()
        copies.append(copy)
    return copies


def total_of(landed, count):
    total = landed[0]
    for k in range(1, count):
        total = total + landed[k]
    return total


def matmul(left, right, left_dim, right_dim, kind=F32):
    return dot(left, right, left_dim, right_dim).astype(kind)


def body(
    seq_count,
    tp_count,
    block_in,
    segment_ids,
    first_gain,
    first_bias,
    w_query,
    w_key,
    w_value,
    head_gain,
    head_bias,
    w_out,
    second_gain,
    second_bias,
    w_up,
    hidden_gain,
    hidden_bias,
    w_down,
    out_cotangent,
):
    seq_index = lax.axis_index("seq")
    row_count, span, model_width = block_in.shape
    length = span * seq_count
    tokens = row_count * span
    head_width = w_query.shape[1]
    hidden_width = w_up.shape[1] * tp_count
    groups = seq_count // row_count

    seg_row = lax.dynamic_slice_in_dim(segment_ids, seq_index // groups, 1, 0)
    block = block_in.reshape(tokens, model_width)
    cotangent = out_cotangent.reshape(tokens, model_width)

    first_act, qkv_row, tables, o_row, lse, mixed, vecs = front(
        block,
        w_query,
        w_key,
        w_value,
        seg_row,
        (
            first_gain, first_bias, second_gain, second_bias,
            hidden_gain, hidden_bias, head_gain, head_bias,
        ),
        seq_count,
        groups,
        1,
    )
    def shape_of(dims, kind=F32):
        return jax.ShapeDtypeStruct(dims, kind)

    hidden_size = hidden_gain.shape[0]
    own_shape = shape_of((tokens // 2, model_width))
    sums_shape = shape_of((2, 8, model_width))
    landed = pltpu.VMEM((tp_count, 8, tokens), F32)
    pair_sem = pltpu.SemaphoreType.DMA((tp_count,))
    block_sem = pltpu.SemaphoreType.DMA((tokens // LANES, tp_count))

    def before_middle(env):
        env["hidden_vec_grads"][...] = jnp.zeros_like(env["hidden_vec_grads"])
        norm_heads(env, tp_count, model_width)

    (
        second_act, middle_own, head_act, head_sums, hidden_act, grad_up, hidden_vec_grads
    ) = line_sum(
        finish_middle,
        tp_count,
        dict(mixed=mixed, w_out=w_out, block=block, cotangent=cotangent, w_down=w_down, w_up=w_up),
        dict(vecs=vecs),
        (("head_act", "w_out"),),
        3,
        tokens=tokens,
        late=("cotangent", "w_down"),
        later=("block", "w_up"),
        stores=dict(middle="reduced", head_act="before", hidden_act="rows", grad_up="rows"),
        tasks=(("keep", "cotangent", "w_down", "hidden_grad"),),
        owns=(
            ("middle", own_shape),
            ("head_act", shape_of((tokens, head_width), BF16)),
            ("head_sums", shape_of((8, tokens))),
            ("hidden_act", shape_of((tokens, hidden_size), BF16)),
            ("grad_up", shape_of((tokens, hidden_size), BF16)),
            ("hidden_vec_grads", shape_of((2, 8, hidden_size))),
        ),
        scratch=(
            ("hidden_grad", pltpu.VMEM((tokens, hidden_size), BF16)),
            ("hidden_sums", pltpu.VMEM((8, tokens), F32)),
            ("head_landed", landed),
            ("hidden_landed", landed),
            ("head_send", pair_sem),
            ("head_recv", pair_sem),
            ("hidden_send", block_sem),
            ("hidden_recv", block_sem),
        ),
        before=before_middle,
        rows_done=lambda env, block: hidden_rows(env, tp_count, block),
        rows_late=lambda env, block: norm_hidden(env, tp_count, hidden_width, block),
        micros=140,
    )

    weight_shape = shape_of((model_width, hidden_size), BF16)
    grad_middle_low, second_sums, grad_middle_own, down_part, _, w_up_terms, down_terms = line_sum(
        finish_second,
        tp_count,
        dict(
            grad_up=grad_up,
            w_up=w_up,
            cotangent=cotangent,
            middle=middle_own,
            hidden_act=hidden_act,
            w_down=w_down,
            second_act=second_act,
        ),
        dict(vecs=vecs),
        (("grad_up", "w_up"),),
        4,
        tokens=tokens,
        late=("hidden_act", "cotangent"),
        later=("w_down", "middle", "second_act"),
        stores=dict(middle_grad="reduced"),
        tasks=(
            ("spread", "cotangent", "hidden_act", "w_down_terms"),
            ("down", "hidden_act", "w_down", "down_part"),
            ("weight", "second_act", "grad_up", "w_up_terms"),
        ),
        owns=(("sums", sums_shape), ("middle_grad", own_shape)),
        sent=(
            ("down_part", shape_of((tokens, model_width), BF16)),
            ("w_down_terms", weight_shape),
            ("w_up_terms", weight_shape),
            ("spread", shape_of((seq_count, model_width // seq_count, hidden_size), BF16)),
        ),
        scratch=(
            ("spread_send", pltpu.SemaphoreType.DMA((seq_count,))),
            ("spread_recv", pltpu.SemaphoreType.DMA((seq_count,))),
            ("spread_own", pltpu.SemaphoreType.DMA((1,))),
        ),
        seq_barrier=seq_count,
    )
    def scatter(grad):
        return lax.psum_scatter(grad, "seq", scatter_dimension=0, tiled=True)

    w_up_grad = scatter(w_up_terms)

    pairs = head_width // groups // LANES
    many = pltpu.SemaphoreType.DMA((pairs, seq_count))
    pair_rows = pltpu.VMEM((length, LANES), BF16)
    pair_sums = pltpu.VMEM((length, LANES), F32)
    pair_heads = pltpu.VMEM((2, length, LANES), BF16)
    block_out, grads, head_vec_grads, head_terms = line_sum(
        lambda total, here, own, env: total,
        tp_count,
        dict(
            ready=down_part,
            low=grad_middle_low,
            w_out=w_out,
            mixed=mixed,
            head_sums=head_sums,
            qkv=qkv_row,
            o=o_row,
            lse=lse,
            tables=tables,
            first_act=first_act,
            head_act=head_act,
        ),
        dict(vecs=vecs, seg_row=seg_row),
        (),
        5,
        tokens=tokens,
        late=("low", "w_out", "mixed", "head_sums"),
        later=("qkv", "o", "lse", "tables", "first_act", "head_act"),
        owns=(
            ("grads", shape_of((tokens, 3 * head_width), BF16)),
            ("head_vec_grads", shape_of((2, 8, head_width))),
        ),
        sent=(("head_terms", shape_of((model_width, 4 * head_width), BF16)),),
        turned=True,
        scratch=(
            ("weight_stage", pltpu.VMEM((2, ROWS, 4 * head_width), BF16)),
            ("weight_sem", pltpu.SemaphoreType.DMA((2,))),
            ("do", pltpu.VMEM((tokens, head_width), BF16)),
            ("scaled", pltpu.VMEM((tokens, head_width), F32)),
            ("head_part", pltpu.VMEM((8, tokens), F32)),
            ("head_landed", landed),
            ("do_row", pltpu.VMEM((pairs, length, LANES), BF16)),
            ("made", pltpu.VMEM((pairs, length, 3 * LANES), BF16)),
            ("bias", pltpu.VMEM((length, length), F32)),
            ("qs", pair_heads),
            ("ks", pair_rows),
            ("kms", pair_heads),
            ("dos", pair_heads),
            ("delta", pltpu.VMEM((8, length), F32)),
            ("dq", pair_sums),
            ("dk", pair_sums),
            ("dv", pair_sums),
            ("head_send", pair_sem),
            ("head_recv", pair_sem),
            ("there_send", many),
            ("there_recv", many),
            ("back_send", many),
            ("back_recv", many),
        ),
        work=lambda env: back_work(env, seq_count, tp_count, groups),
        seq_barrier=seq_count,
    )
    grads, head_terms, w_up_grad = lax.optimization_barrier((grads, head_terms, w_up_grad))
    head_grads = scatter(head_terms)
    own_width = model_width // seq_count
    split_width = hidden_size + head_width
    seq_sem = pltpu.SemaphoreType.DMA((seq_count,))
    input_grad, _, norm_own, norm_split = line_sum(
        finish_first,
        tp_count,
        dict(grads=grads, block=block, middle_grad=grad_middle_own),
        dict(
            vecs=vecs,
            second_sums=second_sums,
            hidden_vec_grads=hidden_vec_grads,
            head_vec_grads=head_vec_grads,
        ),
        (("grads", "w_pairs"),),
        8,
        tokens=tokens,
        chunks=32,
        group=8,
        later=("block", "middle_grad"),
        loose=dict(w_query=w_query, w_key=w_key, w_value=w_value),
        owns=(
            ("sums", sums_shape),
            ("norm_own", shape_of((8, own_width))),
            ("norm_split", shape_of((8, split_width))),
        ),
        scratch=(
            ("w_pairs", pltpu.VMEM((model_width, 3 * head_width), BF16)),
            ("pair_sem", pltpu.SemaphoreType.DMA((3 * head_width // LANES,))),
            ("split", pltpu.VMEM((8, split_width), F32)),
            ("split_landed", pltpu.VMEM((seq_count, 8, split_width), F32)),
            ("full", pltpu.VMEM((8, model_width), F32)),
            ("full_landed", pltpu.VMEM((tp_count, 8, model_width), F32)),
            ("own_landed", pltpu.VMEM((seq_count, 8, own_width), F32)),
            ("split_send", seq_sem),
            ("split_recv", seq_sem),
            ("full_send", pair_sem),
            ("full_recv", pair_sem),
            ("own_send", seq_sem),
            ("own_recv", seq_sem),
        ),
        start=load_pairs,
        seq_count=seq_count,
    )

    (
        w_query_grad, w_key_grad, w_value_grad, w_out_grad, w_up_grad, w_down_grad, input_grad,
        block_out, *vectors,
    ) = last_results(
        head_grads, w_up_grad, down_terms, input_grad, block_out, norm_own, norm_split, head_width
    )
    vectors = [vector.reshape(-1) for vector in vectors]
    return (
        block_out.reshape(block_in.shape),
        input_grad.reshape(block_in.shape),
        vectors[2],
        vectors[3],
        w_query_grad,
        w_key_grad,
        w_value_grad,
        vectors[6],
        vectors[7],
        w_out_grad,
        vectors[0],
        vectors[1],
        w_up_grad,
        vectors[4],
        vectors[5],
        w_down_grad,
    )


def solution(mesh):
    return jax.shard_map(
        functools.partial(body, mesh.shape["seq"], mesh.shape["tp"]),
        mesh=mesh,
        in_specs=(
            P(None, "seq", None),
            P(),
            P(),
            P(),
            P(None, "tp"),
            P(None, "tp"),
            P(None, "tp"),
            P("tp"),
            P("tp"),
            P(None, "tp"),
            P(),
            P(),
            P(None, "tp"),
            P("tp"),
            P("tp"),
            P(None, "tp"),
            P(None, "seq", None),
        ),
        out_specs=(
            P(None, "seq", None),
            P(None, "seq", None),
            P("seq"),
            P("seq"),
            P("seq", "tp"),
            P("seq", "tp"),
            P("seq", "tp"),
            P("tp"),
            P("tp"),
            P("seq", "tp"),
            P("seq"),
            P("seq"),
            P("seq", "tp"),
            P("tp"),
            P("tp"),
            P("seq", "tp"),
        ),
        check_vma=False,
    )
```

```python
import functools
import math

import jax
import jax.numpy as jnp
from jax import lax
from jax.experimental import pallas as pl
from jax.experimental.pallas import tpu as pltpu
from jax.sharding import PartitionSpec as P

HEAD = 64
LANES = 128
BLOCK = 256
EPSILON = 1e-05
MASKED = -1e30
MESH = pl.DeviceIdType.MESH
F32 = jnp.float32
BF16 = jnp.bfloat16
SLACK = 2
SLACK_OUT = 2
ROWS = 256
TILE = 1024
VMEM_LIMIT = 60 * 1024 * 1024


def cost(micros):
    return pl.CostEstimate(flops=int(micros * 1.1e9), bytes_accessed=0, transcendentals=0)


def dot(left, right, left_dim, right_dim):
    return lax.dot_general(
        left, right, (((left_dim,), (right_dim,)), ((), ())), preferred_element_type=F32
    )


def seq_signal(count):
    me = lax.axis_index("seq")
    barrier = pltpu.get_barrier_semaphore()
    for k in range(1, count):
        pl.semaphore_signal(
            barrier, inc=1, device_id={"seq": lax.rem(me + k, count)}, device_id_type=MESH
        )


def seq_wait(count):
    pl.semaphore_wait(pltpu.get_barrier_semaphore(), count - 1)


def send(source, target, send_sem, recv_sem, device):
    return pltpu.make_async_remote_copy(
        src_ref=source,
        dst_ref=target,
        send_sem=send_sem,
        recv_sem=recv_sem,
        device_id={"seq": device},
        device_id_type=MESH,
    )


def spans(index, span):
    return pl.ds(pl.multiple_of(index * span, LANES), span)


def swap_halves(values):
    lane = lax.broadcasted_iota(jnp.int32, values.shape, 1)
    return jnp.where(
        lane % HEAD < HEAD // 2,
        pltpu.roll(values, LANES - HEAD // 2, 1),
        pltpu.roll(values, HEAD // 2, 1),
    )


def head_masks(values):
    lane = lax.broadcasted_iota(jnp.int32, values.shape, 1)
    zero = jnp.zeros_like(values)
    return jnp.where(lane < HEAD, values, zero), jnp.where(lane < HEAD, zero, values)


def block_rows(index):
    return slice(index * BLOCK, (index + 1) * BLOCK)


def rotated(values, tables, first, rows):
    values = values.astype(F32)
    return values * tables[first, rows, :] + swap_halves(values) * tables[first + 1, rows, :]


def rotated_back(values, tables, first, rows):
    return values * tables[first, rows, :] - swap_halves(values) * tables[first + 1, rows, :]


def norm_parts(values):
    center = jnp.mean(values, axis=-1, keepdims=True)
    shifted = values - center
    inverse = lax.rsqrt(jnp.mean(shifted * shifted, axis=-1, keepdims=True) + EPSILON)
    return shifted * inverse, inverse


def seg_column(seg_row, index, size):
    columns = []
    for i in range(size // LANES):
        start = index * size + i * LANES
        square = jnp.broadcast_to(seg_row[:, start : start + LANES], (LANES, LANES))
        columns.append(jnp.transpose(square)[:, :1])
    return jnp.concatenate(columns, axis=0)


def make_tables(seg_row, tables):
    lane = lax.broadcasted_iota(jnp.int32, (1, LANES), 1)
    index = (lane % (HEAD // 2)).astype(F32)
    theta_rate = jnp.exp(-2.0 * index / HEAD * math.log(10000.0))
    zeta_base = (2.0 * index + 0.4 * HEAD) / (1.4 * HEAD)
    rate = jnp.log(zeta_base) / 512.0
    for block in range(seg_row.shape[1] // LANES):
        rows = slice(block * LANES, (block + 1) * LANES)
        before = (seg_row[...] < seg_column(seg_row, block, LANES)).astype(F32)
        place = lax.broadcasted_iota(jnp.int32, (LANES, 1), 0) + block * LANES
        place = place.astype(F32) - jnp.sum(before, axis=1, keepdims=True)
        cos_part = jnp.cos(place * theta_rate)
        sin_part = jnp.sin(place * theta_rate)
        sin_part = jnp.where(lane % HEAD < HEAD // 2, -sin_part, sin_part)
        for k, factor in enumerate((jnp.exp(place * rate), jnp.exp(-place * rate))):
            tables[2 * k, rows, :] = cos_part * factor
            tables[2 * k + 1, rows, :] = sin_part * factor


def front_kernel(
    count, groups, num_vec, *refs
):
    (x_ref, wq_ref, wk_ref, wv_ref, segr_ref), refs = refs[:5], refs[5:]
    pieces, refs = refs[:num_vec], refs[num_vec:]
    (
        act_out, qkv_out, tab_out, o_ref, lse_ref, mixed_ref, vecs_ref, act_ref, qkv_ref,
        weights, staged, tab_ref, bias, qs, ks, load_sem, act_sem, tab_sem, qkv_sem, send_sem, recv_sem, back_send_sem, back_recv_sem,
    ) = refs
    me = lax.axis_index("seq")
    pairs, length = qkv_ref.shape[:2]
    tokens, width = x_ref.shape
    span = length // count
    blocks = length // BLOCK
    mine, row = lax.rem(me, groups), me // groups
    seq_signal(count)
    loads = []
    for j in range(pairs * groups):
        for i, source in enumerate((wq_ref, wk_ref, wv_ref)):
            copy = pltpu.make_async_copy(
                source.at[:, j * LANES : (j + 1) * LANES],
                weights.at[j, :, i * LANES : (i + 1) * LANES],
                load_sem.at[3 * j + i],
            )
            copy.start()
            loads.append(copy)

    place = 0
    for piece in pieces:
        for i in range(piece.shape[0]):
            vecs_ref[:, place : place + LANES] = piece[i : i + 1, :].astype(F32)
            place += LANES

    def there_to(p, device):
        k = lax.rem(device - me + count, count)
        return send(
            staged.at[lax.rem(device, groups) * pairs + p, spans(device // groups, span), :],
            qkv_ref.at[p, spans(me, span), :],
            send_sem.at[p, k],
            recv_sem.at[p, k],
            device,
        )

    def there(p, k):
        return there_to(p, lax.rem(me + k, count))

    def project_rows(p, rows):
        for group in range(groups):
            j = group * pairs + p
            staged[j, rows, :] = dot(act_ref[rows, :], weights[j], 1, 0).astype(BF16)

    for copy in loads:
        copy.wait()
    seq_wait(count)
    steps = tokens // BLOCK
    rows_each = BLOCK // span

    def first_step(b, carry):
        block = lax.rem(row // rows_each + b, steps)
        for i in range(BLOCK // LANES):
            rows = pl.ds(pl.multiple_of(block * BLOCK + i * LANES, LANES), LANES)
            normed, _ = norm_parts(x_ref[rows, :].astype(F32))
            act = normed * vecs_ref[:, :width] + vecs_ref[:, width : 2 * width]
            act_ref[rows, :] = act.astype(BF16)
        project_rows(0, pl.ds(pl.multiple_of(block * BLOCK, BLOCK), BLOCK))
        for i in range(rows_each * groups):
            device = block * rows_each * groups + i
            pl.when(device != me)(lambda device=device: there_to(0, device).start())
        return carry

    lax.fori_loop(0, steps, first_step, 0)
    act_copy = pltpu.make_async_copy(act_ref, act_out, act_sem)
    act_copy.start()

    def qkv_copy(p):
        return pltpu.make_async_copy(qkv_ref.at[p], qkv_out.at[p], qkv_sem.at[p])

    def keep_own(p):
        qkv_ref[p, spans(me, span), :] = staged[mine * pairs + p, spans(row, span), :]

    keep_own(0)

    def back(p, k):
        device = lax.rem(me + k, count)
        return send(
            o_ref.at[p, spans(device, span), :],
            mixed_ref.at[spans(row, span), spans(mine * pairs + p, LANES)],
            back_send_sem.at[p, k],
            back_recv_sem.at[p, k],
            device,
        )

    def project(p, carry):
        def rows_step(r, inner):
            project_rows(p, pl.ds(pl.multiple_of(r * BLOCK, BLOCK), BLOCK))
            return inner

        lax.fori_loop(0, steps, rows_step, 0)
        for k in range(1, count):
            there(p, k).start()
        keep_own(p)
        return carry

    lax.fori_loop(1, pairs, project, 0)
    make_tables(segr_ref, tab_ref)
    tab_copy = pltpu.make_async_copy(tab_ref, tab_out, tab_sem)
    tab_copy.start()
    for qb in range(blocks):
        rows = block_rows(qb)
        keys = (qb + 1) * BLOCK
        same = seg_column(segr_ref, qb, BLOCK) == segr_ref[:, :keys]
        query = lax.broadcasted_iota(jnp.int32, (BLOCK, keys), 0) + qb * BLOCK
        key = lax.broadcasted_iota(jnp.int32, (BLOCK, keys), 1)
        bias[rows, :keys] = jnp.where(same & (key <= query), 0.0, MASKED)

    def attend(p, carry):
        for k in range(1, count):
            there(p, k).wait_recv()
        qkv_copy(p).start()
        for qb in range(blocks):
            rows = block_rows(qb)
            q = rotated(qkv_ref[p, rows, :LANES], tab_ref, 0, rows) * (HEAD**-0.5)
            q0, q1 = head_masks(q)
            qs[0, rows, :] = q0.astype(BF16)
            qs[1, rows, :] = q1.astype(BF16)
            k = rotated(qkv_ref[p, rows, LANES : 2 * LANES], tab_ref, 2, rows)
            ks[rows, :] = k.astype(BF16)
        for qb in range(blocks):
            rows = block_rows(qb)
            keys = (qb + 1) * BLOCK
            outs = []
            logs = []
            for h in range(2):
                scores = dot(qs[h, rows, :], ks[:keys, :], 1, 1) + bias[rows, :keys]
                top = jnp.max(scores, axis=1, keepdims=True)
                expo = jnp.exp(scores - top)
                total = jnp.sum(expo, axis=1, keepdims=True)
                outs.append(dot(expo.astype(BF16), qkv_ref[p, :keys, 2 * LANES :], 1, 0) / total)
                logs.append(jnp.broadcast_to(top + jnp.log(total), (BLOCK, LANES)))
            lane = lax.broadcasted_iota(jnp.int32, (BLOCK, LANES), 1)
            o_ref[p, rows, :] = jnp.where(lane < HEAD, outs[0], outs[1]).astype(BF16)
            logs_t = jnp.transpose(jnp.where(lane < HEAD, logs[0], logs[1]))
            lse_ref[p, 0:1, rows] = logs_t[0:1]
            lse_ref[p, 1:2, rows] = logs_t[HEAD : HEAD + 1]
        for k in range(1, count):
            back(p, k).start()
        mixed_ref[spans(row, span), spans(mine * pairs + p, LANES)] = o_ref[p, spans(me, span), :]
        return carry

    lax.fori_loop(0, pairs, attend, 0)

    def drain(p, carry):
        for k in range(1, count):
            there(p, k).wait_send()
            back(p, k).wait()
        return carry

    lax.fori_loop(0, pairs, drain, 0)
    act_copy.wait()
    tab_copy.wait()
    for p in range(pairs):
        qkv_copy(p).wait()


def front(
    x, w_query, w_key, w_value, seg_row, vectors, count, groups, collective_id
):
    tokens, model_width = x.shape
    pieces = [vector.reshape(vector.shape[0] // LANES, LANES) for vector in vectors]
    total = sum(vector.shape[0] for vector in vectors)
    head_width = w_query.shape[1]
    length = seg_row.shape[1]
    pairs = head_width // groups // LANES
    whole = pl.BlockSpec(memory_space=pltpu.VMEM)
    any_space = pl.BlockSpec(memory_space=pl.ANY)
    return pl.pallas_call(
        functools.partial(front_kernel, count, groups, len(pieces)),
        out_shape=[
            jax.ShapeDtypeStruct((tokens, model_width), BF16),
            jax.ShapeDtypeStruct((pairs, length, 3 * LANES), BF16),
            jax.ShapeDtypeStruct((4, length, LANES), F32),
            jax.ShapeDtypeStruct((pairs, length, LANES), BF16),
            jax.ShapeDtypeStruct((pairs, 8, length), F32),
            jax.ShapeDtypeStruct((tokens, head_width), BF16),
            jax.ShapeDtypeStruct((1, total), F32),
        ],
        in_specs=[whole] + [any_space] * 3 + [whole] * (1 + len(pieces)),
        out_specs=[any_space] * 3 + [whole] * 4,
        scratch_shapes=[
            pltpu.VMEM((tokens, model_width), BF16),
            pltpu.VMEM((pairs, length, 3 * LANES), BF16),
            pltpu.VMEM((pairs * groups, model_width, 3 * LANES), BF16),
            pltpu.VMEM((pairs * groups, tokens, 3 * LANES), BF16),
            pltpu.VMEM((4, length, LANES), F32),
            pltpu.VMEM((length, length), F32),
            pltpu.VMEM((2, length, LANES), BF16),
            pltpu.VMEM((length, LANES), BF16),
            pltpu.SemaphoreType.DMA((3 * pairs * groups,)),
            pltpu.SemaphoreType.DMA,
            pltpu.SemaphoreType.DMA,
            pltpu.SemaphoreType.DMA((pairs,)),
        ]
        + [pltpu.SemaphoreType.DMA((pairs, count))] * 4,
        compiler_params=pltpu.CompilerParams(
            collective_id=collective_id, has_side_effects=True, vmem_limit_bytes=VMEM_LIMIT
        ),
        cost_estimate=cost(60),
    )(x, w_query, w_key, w_value, seg_row, *pieces)


def back_work(env, count, tp_count, groups):
    low_ref, wout_ref, mixed_ref = env["low"], env["w_out"], env["mixed"]
    sums_ref, qkv_ref, o_ref, lse_ref = env["head_sums"], env["qkv"], env["o"], env["lse"]
    segr_ref, tab_ref, bias = env["seg_row"], env["tables"], env["bias"]
    grads_ref, vec_grads_ref = env["grads"], env["head_vec_grads"]
    do_ref, scaled, part = env["do"], env["scaled"], env["head_part"]
    do_row, made, delta = env["do_row"], env["made"], env["delta"]
    qs, ks, kms, dos, dq, dk, dv = (env[name] for name in ("qs", "ks", "kms", "dos", "dq", "dk", "dv"))
    me = lax.axis_index("seq")
    pairs, length = qkv_ref.shape[:2]
    tokens, features = low_ref.shape
    head_width = mixed_ref.shape[1]
    span = length // count
    blocks = length // BLOCK
    mine, row = lax.rem(me, groups), me // groups
    gain = head_vec(env["vecs"], head_width, 0)

    def normed_rows(rows):
        first, second = to_columns(sums_ref[:, rows], 2)
        center = first / features
        inverse = lax.rsqrt(second / features - center * center + EPSILON)
        return (mixed_ref[rows, :].astype(F32) - center) * inverse, inverse

    def head_terms(r):
        wide = pl.ds(pl.multiple_of(r * BLOCK, BLOCK), BLOCK)
        scaled[wide, :] = dot(low_ref[wide, :], wout_ref[...], 1, 0)
        for k in range(BLOCK // LANES):
            rows = row_block(r * (BLOCK // LANES) + k)
            normed, _ = normed_rows(rows)
            grad = scaled[rows, :]
            vec_grads_ref[0] += fold(grad * normed)
            vec_grads_ref[1] += fold(grad)
            grad = grad * gain
            scaled[rows, :] = grad
            part[:, rows] = to_row(
                [
                    jnp.sum(grad, axis=-1, keepdims=True),
                    jnp.sum(grad * normed, axis=-1, keepdims=True),
                ]
            )

    def part_copies(start):
        return share("tp", tp_count, lambda d: part, env["head_landed"], *env_pair(env, "head"), start)

    def head_apply(r, carry):
        rows = row_block(r)
        normed, inverse = normed_rows(rows)
        first, second = to_columns(part[:, rows], 2)
        grad = scaled[rows, :] - first / features - normed * (second / features)
        do_ref[rows, :] = (inverse * grad).astype(BF16)
        return carry

    def there(p, k):
        device = lax.rem(me + k, count)
        return send(
            do_ref.at[spans(device // groups, span), spans(lax.rem(device, groups) * pairs + p, LANES)],
            do_row.at[p, spans(me, span), :],
            env["there_send"].at[p, k],
            env["there_recv"].at[p, k],
            device,
        )

    def back(p, k):
        device = lax.rem(me + k, count)
        return send(
            made.at[p, spans(device, span), :],
            grads_ref.at[spans(row, span), spans(mine * pairs + p, 3 * LANES)],
            env["back_send"].at[p, k],
            env["back_recv"].at[p, k],
            device,
        )

    def share_out(p, carry):
        for k in range(1, count):
            there(p, k).start()
        do_row[p, spans(me, span), :] = do_ref[spans(row, span), spans(mine * pairs + p, LANES)]
        return carry

    def prepare():
        for kb in range(blocks):
            rows = block_rows(kb)
            start = kb * BLOCK
            shape = (BLOCK, length - start)
            same = seg_column(segr_ref, kb, BLOCK) == segr_ref[:, start:]
            key = lax.broadcasted_iota(jnp.int32, shape, 0)
            query = lax.broadcasted_iota(jnp.int32, shape, 1)
            bias[rows, start:] = jnp.where(same & (key <= query), 0.0, MASKED)

    def pair_start(p):
        for qb in range(blocks):
            rows = block_rows(qb)
            q = rotated(qkv_ref[p, rows, :LANES], tab_ref, 0, rows) * (HEAD**-0.5)
            q0, q1 = head_masks(q)
            qs[0, rows, :] = q0.astype(BF16)
            qs[1, rows, :] = q1.astype(BF16)
            k = rotated(qkv_ref[p, rows, LANES : 2 * LANES], tab_ref, 2, rows)
            ks[rows, :] = k.astype(BF16)
            k0, k1 = head_masks(k)
            kms[0, rows, :] = k0.astype(BF16)
            kms[1, rows, :] = k1.astype(BF16)
        dq[...] = jnp.zeros_like(dq)
        dk[...] = jnp.zeros_like(dk)
        dv[...] = jnp.zeros_like(dv)
        for k in range(1, count):
            there(p, k).wait_recv()
        for qb in range(blocks):
            rows = block_rows(qb)
            grad = do_row[p, rows, :].astype(F32)
            d0, d1 = head_masks(grad)
            dos[0, rows, :] = d0.astype(BF16)
            dos[1, rows, :] = d1.astype(BF16)
            prod = jnp.transpose(grad * o_ref[p, rows, :].astype(F32))
            delta[0:1, rows] = jnp.sum(prod[:HEAD], axis=0, keepdims=True)
            delta[1:2, rows] = jnp.sum(prod[HEAD:], axis=0, keepdims=True)

    def pair_block(p, qb):
        cols = block_rows(qb)
        for kb in range(qb + 1):
            rows = block_rows(kb)
            value = qkv_ref[p, rows, 2 * LANES :]
            for h in range(2):
                scores = dot(ks[rows, :], qs[h, cols, :], 1, 1) + bias[rows, cols]
                probs = jnp.exp(scores - lse_ref[p, h : h + 1, cols])
                grads = dot(value, dos[h, cols, :], 1, 1)
                dscores = (probs * (grads - delta[h : h + 1, cols])).astype(BF16)
                dv[rows, :] += dot(probs.astype(BF16), dos[h, cols, :], 1, 0)
                dk[rows, :] += dot(dscores, qs[h, cols, :], 1, 0)
                dq[cols, :] += dot(dscores, kms[h, rows, :], 0, 0)

    def pair_end(p):
        for qb in range(blocks):
            rows = block_rows(qb)
            grad = dq[rows, :] * (HEAD**-0.5)
            made[p, rows, :LANES] = rotated_back(grad, tab_ref, 0, rows).astype(BF16)
            made[p, rows, LANES : 2 * LANES] = rotated_back(dk[rows, :], tab_ref, 2, rows).astype(BF16)
            made[p, rows, 2 * LANES :] = dv[rows, :].astype(BF16)
        for k in range(1, count):
            back(p, k).start()
        grads_ref[spans(row, span), spans(mine * pairs + p, 3 * LANES)] = made[p, spans(me, span), :]

    head_steps = tokens // BLOCK
    attend_at = head_steps + 3
    weights_at = attend_at + pairs * (blocks // 2) + 3
    tiles = features // ROWS

    def weight_copy(tile):
        rows = pl.ds(pl.multiple_of(tile * ROWS, ROWS), ROWS)
        slot = lax.rem(tile, 2)
        return pltpu.make_async_copy(
            env["weight_stage"].at[slot], env["head_terms"].at[rows, :], env["weight_sem"].at[slot]
        )

    def head_weights(tile):
        cols = pl.ds(pl.multiple_of(tile * ROWS, ROWS), ROWS)
        slot = lax.rem(tile, 2)
        wide = 3 * head_width
        for left, right, first in (
            (env["first_act"], grads_ref, 0), (low_ref, env["head_act"], wide)
        ):
            env["turned"][...] = jnp.transpose(left[:, cols])
            for n in range(right.shape[1] // head_width):
                part_cols = slice(n * head_width, (n + 1) * head_width)
                target = slice(first + n * head_width, first + (n + 1) * head_width)
                value = dot(env["turned"][...], right[:, part_cols], 1, 0)
                env["weight_stage"][slot, :, target] = value.astype(BF16)
        weight_copy(tile).start()

    vec_grads_ref[...] = jnp.zeros_like(vec_grads_ref)

    def step(now):
        t = now - 1
        pl.when((t >= 0) & (t < head_steps))(lambda: head_terms(t))

        @pl.when(t == head_steps - 1)
        def _():
            part_copies(True)
            env["head_landed"][lax.axis_index("tp")] = part[...]

        pl.when(t == head_steps)(prepare)

        @pl.when(t == head_steps + 1)
        def _():
            for copy in part_copies(False):
                copy.wait()
            part[...] = total_of(env["head_landed"], tp_count)
            lax.fori_loop(0, tokens // LANES, head_apply, 0)
            lax.fori_loop(0, pairs, share_out, 0)

        each = blocks // 2
        turn = t - attend_at
        p = turn // each
        for i in range(each):

            @pl.when((turn >= 0) & (turn < pairs * each) & (lax.rem(turn + 32 * each, each) == i))
            def _():
                if i == 0:
                    pair_start(p)
                pair_block(p, 2 * i)
                pair_block(p, 2 * i + 1)
                if i == each - 1:
                    pair_end(p)

        tile = t - weights_at

        @pl.when(tile == 0)
        def _():
            def arrive(p, carry):
                for k in range(1, count):
                    back(p, k).wait_recv()
                return carry

            lax.fori_loop(0, pairs, arrive, 0)

        pl.when((tile >= 2) & (tile < tiles))(lambda: weight_copy(tile - 2).wait())
        pl.when((tile >= 0) & (tile < tiles))(lambda: head_weights(tile))

    def end():
        def drain(p, carry):
            for k in range(1, count):
                there(p, k).wait_send()
                back(p, k).wait_send()
            return carry

        lax.fori_loop(0, pairs, drain, 0)
        for tile in (tiles - 2, tiles - 1):
            weight_copy(tile).wait()

    return step, end, 1 + weights_at + tiles


def last_kernel(
    head_ref, up_ref, down_ref, grad_ref, block_ref, own_ref, split_ref,
    query_out, key_out, value_out, out_out, up_out, down_out, grad_out, block_out, *vectors
):
    grad_out[...] = grad_ref[...]
    block_out[...] = block_ref[...]
    up_out[...] = up_ref[...].astype(F32)
    down = down_ref[0].astype(F32)
    for k in range(1, down_ref.shape[0]):
        down = down + down_ref[k].astype(F32)
    down_out[...] = down
    width = out_out.shape[1]
    for j in range(width // LANES):
        for i, target in enumerate((query_out, key_out, value_out)):
            start = (3 * j + i) * LANES
            target[:, j * LANES : (j + 1) * LANES] = head_ref[:, start : start + LANES].astype(F32)
    out_out[...] = head_ref[:, 3 * width :].astype(F32)

    @pl.when(pl.program_id(0) == 0)
    def _():
        places = [(own_ref, i, 0) for i in range(4)]
        hidden = vectors[4].shape[0] * LANES
        places += [(split_ref, i, 0) for i in range(2)] + [(split_ref, i, hidden) for i in range(2)]
        for target, (source, row, first) in zip(vectors, places):
            for i in range(target.shape[0]):
                start = first + i * LANES
                target[i : i + 1, :] = source[row : row + 1, start : start + LANES]


def last_results(
    head_grads, up_grad, down_terms, input_grad, block_out, norm_own, norm_split, head_width
):
    rows = head_grads.shape[0]
    steps = rows // 32
    tokens, width = input_grad.shape

    def block(columns):
        return pl.BlockSpec((rows // steps, columns), lambda i: (i, 0))

    def whole(shape):
        return pl.BlockSpec(shape, lambda i: (0, 0))

    part = pl.BlockSpec((tokens // steps, width), lambda i: (i, 0))
    own = norm_own.shape[1]
    hidden = norm_split.shape[1] - head_width
    vectors = [(size // LANES, LANES) for size in (own,) * 4 + (hidden,) * 2 + (head_width,) * 2]
    sizes = [head_width] * 4 + [up_grad.shape[1]] * 2
    return pl.pallas_call(
        last_kernel,
        grid=(steps,),
        out_shape=[jax.ShapeDtypeStruct((rows, size), F32) for size in sizes]
        + [jax.ShapeDtypeStruct((tokens, width), BF16)] * 2
        + [jax.ShapeDtypeStruct(shape, F32) for shape in vectors],
        in_specs=[
            block(head_grads.shape[1]),
            block(up_grad.shape[1]),
            pl.BlockSpec((down_terms.shape[0], rows // steps, down_terms.shape[2]), lambda i: (0, i, 0)),
        ]
        + [part] * 2
        + [whole(norm_own.shape), whole(norm_split.shape)],
        out_specs=[block(size) for size in sizes] + [part] * 2 + [whole(shape) for shape in vectors],
        compiler_params=pltpu.CompilerParams(vmem_limit_bytes=VMEM_LIMIT),
        cost_estimate=cost(10),
    )(head_grads, up_grad, down_terms, input_grad, block_out, norm_own, norm_split)


def fold(values):
    rows, width = values.shape
    return jnp.sum(values.reshape(rows // 8, 8, width), axis=0)


def model_vec(env, index):
    width = env["out"].shape[1]
    return env["vecs"][:, index * width : (index + 1) * width]


def hidden_vec(env, index, cols=slice(None)):
    width = env["hidden_act"].shape[1]
    first = 4 * env["out"].shape[1] + index * width
    return env["vecs"][:, first : first + width][:, cols]


def head_vec(vecs_ref, width, index):
    total = vecs_ref.shape[1]
    first = total - (2 - index) * width
    return vecs_ref[:, first : first + width]


def finish_middle(total, here, own, env):
    middle = env["block"][here, :].astype(F32) + total
    env["middle"][own, :] = middle
    normed, _ = norm_parts(middle)
    return normed * model_vec(env, 2) + model_vec(env, 3)


def norm_back(base, values, total, gain, sums):
    normed, inverse = norm_parts(values)
    scaled = total * gain
    grad = base + inverse * (
        scaled
        - jnp.mean(scaled, axis=-1, keepdims=True)
        - normed * jnp.mean(scaled * normed, axis=-1, keepdims=True)
    )
    sums[0] += fold(total * normed)
    sums[1] += fold(total)
    return grad


def finish_second(total, here, own, env):
    base = env["cotangent"][here, :].astype(F32)
    grad = norm_back(base, env["middle"][own, :], total, model_vec(env, 2), env["sums"])
    env["middle_grad"][own, :] = grad
    return grad


def finish_first(total, here, own, env):
    values = env["block"][here, :].astype(F32)
    return norm_back(env["middle_grad"][own, :], values, total, model_vec(env, 0), env["sums"])


def to_row(columns):
    lane = lax.broadcasted_iota(jnp.int32, (LANES, LANES), 1)
    packed = jnp.zeros((LANES, LANES), F32)
    for i, column in enumerate(columns):
        packed = jnp.where(lane == i, column, packed)
    return jnp.transpose(packed)[:8]


def to_columns(rows, number):
    packed = jnp.transpose(jnp.concatenate([rows] * (LANES // 8), axis=0))
    return [packed[:, i : i + 1] for i in range(number)]


def row_block(r):
    return pl.ds(pl.multiple_of(r * LANES, LANES), LANES)


def tp_total(part, landed, send_sem, recv_sem, count):
    copies = share("tp", count, lambda d: part, landed, send_sem, recv_sem)
    landed[lax.axis_index("tp")] = part[...]
    for copy in copies:
        copy.wait()
    part[...] = total_of(landed, count)


def norm_heads(env, count, features):
    mixed, act, part = env["mixed"], env["head_act"], env["head_sums"]
    blocks = mixed.shape[0] // LANES

    def sums(r, carry):
        values = mixed[row_block(r), :].astype(F32)
        part[:, row_block(r)] = to_row(
            [
                jnp.sum(values, axis=-1, keepdims=True),
                jnp.sum(values * values, axis=-1, keepdims=True),
            ]
        )
        return carry

    lax.fori_loop(0, blocks, sums, 0)
    tp_total(part, env["head_landed"], env["head_send"], env["head_recv"], count)

    def apply(r, carry):
        first, second = to_columns(part[:, row_block(r)], 2)
        center = first / features
        inverse = lax.rsqrt(second / features - center * center + EPSILON)
        values = (mixed[row_block(r), :].astype(F32) - center) * inverse
        act[row_block(r), :] = (
            values * head_vec(env["vecs"], act.shape[1], 0) + head_vec(env["vecs"], act.shape[1], 1)
        ).astype(BF16)
        return carry

    lax.fori_loop(0, blocks, apply, 0)


def normal_parts(values):
    size = jnp.abs(values) * (0.5**0.5)
    bell = jnp.exp(-0.5 * values * values)
    t = 1.0 / (1.0 + 0.3275911 * size)
    poly = 1.061405429
    for factor in (-1.453152027, 1.421413741, -0.284496736, 0.254829592):
        poly = poly * t + factor
    tail = 0.5 * poly * t * bell
    return jnp.where(values < 0.0, tail, 1.0 - tail), bell * (1.0 / math.sqrt(2.0 * math.pi))


def hidden_copies(env, count, block):
    me = lax.axis_index("tp")
    send_sem, recv_sem = env_pair(env, "hidden")
    return [
        pltpu.make_async_remote_copy(
            src_ref=env["hidden_sums"].at[:, row_block(block)],
            dst_ref=env["hidden_landed"].at[me, :, row_block(block)],
            send_sem=send_sem.at[block, k],
            recv_sem=recv_sem.at[block, k],
            device_id={"tp": lax.rem(me + k, count)},
            device_id_type=MESH,
        )
        for k in range(1, count)
    ]


def hidden_rows(env, count, block):
    rows = row_block(block)
    width = env["w_up"].shape[1]
    sums = [jnp.zeros((LANES, 1), F32)] * 4
    for n in range(width // TILE):
        cols = slice(n * TILE, (n + 1) * TILE)
        values = dot(env["out"][rows, :], env["w_up"][:, cols], 1, 0)
        below, density = normal_parts(values)
        active = values * below
        env["hidden_act"][rows, cols] = active.astype(BF16)
        env["grad_up"][rows, cols] = (below + values * density).astype(BF16)
        scaled = env["hidden_grad"][rows, cols].astype(F32) * hidden_vec(env, 0, cols)
        for i, term in enumerate((active, active * active, scaled, scaled * active)):
            sums[i] = sums[i] + jnp.sum(term, axis=-1, keepdims=True)
    packed = to_row(sums)
    env["hidden_sums"][:, rows] = packed
    env["hidden_landed"][lax.axis_index("tp"), :, rows] = packed
    for copy in hidden_copies(env, count, block):
        copy.start()


def norm_hidden(env, count, features, block):
    act, slope, landed = env["hidden_act"], env["grad_up"], env["hidden_landed"]
    rows = row_block(block)
    for copy in hidden_copies(env, count, block):
        copy.wait()
    total = landed[0, :, rows]
    for k in range(1, count):
        total = total + landed[k, :, rows]
    sums = [column / features for column in to_columns(total, 4)]
    center = sums[0]
    inverse = lax.rsqrt(sums[1] - center * center + EPSILON)
    cross = inverse * (sums[3] - center * sums[2])
    for n in range(act.shape[1] // TILE):
        cols = slice(n * TILE, (n + 1) * TILE)
        gain = hidden_vec(env, 0, cols)
        normed = (act[rows, cols].astype(F32) - center) * inverse
        grad = env["hidden_grad"][rows, cols].astype(F32)
        back = inverse * (grad * gain - sums[2] - normed * cross)
        slope[rows, cols] = (back * slope[rows, cols].astype(F32)).astype(BF16)
        act[rows, cols] = (normed * gain + hidden_vec(env, 1, cols)).astype(BF16)
        env["hidden_vec_grads"][0, :, cols] += fold(grad * normed)
        env["hidden_vec_grads"][1, :, cols] += fold(grad)
    for name in ("hidden_act", "grad_up"):
        row_store(env, name, block).start()


def row_store(env, name, block):
    rows = row_block(block)
    return pltpu.make_async_copy(
        env[name].at[rows, :], env["target " + name].at[rows, :], env["sem " + name].at[block]
    )


def whole_store(env, name):
    return pltpu.make_async_copy(env[name], env["target " + name], env["sem " + name].at[0])


def spread_copy(env, device):
    landed, terms = env["spread"], env["w_down_terms"]
    count, own = landed.shape[:2]
    me = lax.axis_index("seq")
    k = lax.rem(device - me + count, count)
    rows = pl.ds(pl.multiple_of(device * own, own), own)
    return pltpu.make_async_remote_copy(
        src_ref=terms.at[rows, :],
        dst_ref=landed.at[me],
        send_sem=env["spread_send"].at[k],
        recv_sem=env["spread_recv"].at[k],
        device_id={"seq": device},
        device_id_type=MESH,
    )


def spread_own(env):
    landed, terms = env["spread"], env["w_down_terms"]
    own = landed.shape[1]
    me = lax.axis_index("seq")
    rows = pl.ds(pl.multiple_of(me * own, own), own)
    return pltpu.make_async_copy(terms.at[rows, :], landed.at[me], env["spread_own"].at[0])


def spread_rows(env, rows):
    own = env["spread"].shape[1]
    me = lax.axis_index("seq")
    for i in range(ROWS // own):
        device = rows.start // own + i
        pl.when(device != me)(lambda device=device: spread_copy(env, device).start())
        pl.when(device == me)(lambda: spread_own(env).start())


def spread_wait(env):
    count = env["spread"].shape[0]
    me = lax.axis_index("seq")
    for k in range(1, count):
        spread_copy(env, lax.rem(me + k, count)).wait()
    spread_own(env).wait()


def split_copies(env, seq_count):
    split = env["split"]
    return share("seq", seq_count, lambda d: split, env["split_landed"], *env_pair(env, "split"), False)


def env_pair(env, name):
    return env[name + "_send"], env[name + "_recv"]


def split_start(env, seq_count):
    hidden = env["hidden_vec_grads"].shape[2]
    split = env["split"]
    split[...] = jnp.zeros_like(split)
    for i in range(2):
        split[i : i + 1, :hidden] = jnp.sum(env["hidden_vec_grads"][i], axis=0, keepdims=True)
        split[i : i + 1, hidden:] = jnp.sum(env["head_vec_grads"][i], axis=0, keepdims=True)
    for copy in split_copies(env, seq_count):
        copy.start()
    env["split_landed"][lax.axis_index("seq")] = split[...]


def full_copies(env, count):
    full = env["full"]
    return share("tp", count, lambda d: full, env["full_landed"], *env_pair(env, "full"), False)


def full_start(env, count):
    full = env["full"]
    full[...] = jnp.zeros_like(full)
    for i in range(2):
        full[i : i + 1, :] = jnp.sum(env["second_sums"][i], axis=0, keepdims=True)
        full[2 + i : 3 + i, :] = jnp.sum(env["sums"][i], axis=0, keepdims=True)
    for copy in full_copies(env, count):
        copy.start()
    env["full_landed"][lax.axis_index("tp")] = full[...]


def norm_finish(env, seq_count, count):
    full, own = env["full"], env["norm_own"].shape[1]
    me = lax.axis_index("seq")
    for copy in full_copies(env, count):
        copy.wait()
    full[...] = total_of(env["full_landed"], count)

    def piece(device):
        return pl.ds(pl.multiple_of(device * own, LANES), own)

    copies = share(
        "seq", seq_count, lambda d: full.at[:, piece(d)], env["own_landed"], *env_pair(env, "own")
    )
    env["own_landed"][me] = full[:, piece(me)]
    for copy in split_copies(env, seq_count):
        copy.wait()
    env["norm_split"][...] = total_of(env["split_landed"], seq_count)
    for copy in copies:
        copy.wait()
    env["norm_own"][...] = total_of(env["own_landed"], seq_count)


def load_pairs(env):
    copies = []
    for i, name in enumerate(("w_query", "w_key", "w_value")):
        for j in range(env[name].shape[1] // LANES):
            copy = pltpu.make_async_copy(
                env[name].at[:, j * LANES : (j + 1) * LANES],
                env["w_pairs"].at[:, (3 * j + i) * LANES : (3 * j + i + 1) * LANES],
                env["pair_sem"].at[3 * j + i],
            )
            copy.start()
            copies.append(copy)
    return copies


def line_kernel(plan, count, chunks, group, slack, *refs):
    env = dict(zip(plan["order"], refs, strict=True))
    finish, parts, tasks = plan["finish"], plan["parts"], plan["tasks"]
    num_task = len(tasks)
    out_ref = env["out"]
    in_a, in_b = env["in_a"], env["in_b"]
    rsa_s, rsa_r, rsb_s, rsb_r = (env[name] for name in ("rsa_s", "rsa_r", "rsb_s", "rsb_r"))
    aga_s, aga_r, agb_s, agb_r = (env[name] for name in ("aga_s", "aga_r", "agb_s", "agb_r"))
    z = lax.axis_index("tp")
    tokens, width = out_ref.shape
    half = tokens // 2
    size = half // chunks
    ahead = slack * (count - 1)
    spread_out = SLACK_OUT * (count - 1)
    steps = chunks + ahead + spread_out
    from_first, from_last = slack * z, slack * (count - 1 - z)
    out_first, out_last = SLACK_OUT * z, SLACK_OUT * (count - 1 - z)
    first, last = z == 0, z == count - 1
    up = jnp.minimum(z + 1, count - 1)
    down = jnp.maximum(z - 1, 0)

    loads = {
        name: pltpu.make_async_copy(env["source " + name], env[name], env["load_sem"].at[i])
        for i, name in enumerate(plan["held"])
    }
    behind = plan["late"] + plan["later"]
    for name in plan["held"]:
        if name not in behind:
            loads[name].start()
    started = plan["start"](env) if plan["start"] else []
    seq_count = plan["seq_count"]
    axis_barrier([("tp", count)] + ([("seq", plan["seq_barrier"])] if plan["seq_barrier"] else []))
    if "sums" in env:
        env["sums"][...] = jnp.zeros_like(env["sums"])
    if seq_count:
        split_start(env, seq_count)

    def own_rows(c):
        return pl.ds(pl.multiple_of(c * size, size), size)

    def a_rows(c):
        return own_rows(c)

    def b_rows(c):
        return pl.ds(pl.multiple_of(half + c * size, size), size)

    def hop(source, target, send, recv, c, device):
        return pltpu.make_async_remote_copy(
            src_ref=source,
            dst_ref=target,
            send_sem=send.at[c],
            recv_sem=recv.at[c],
            device_id={"tp": device},
            device_id_type=MESH,
        )

    def gather_a(c):
        rows = out_ref.at[a_rows(c), :]
        return hop(rows, rows, aga_s, aga_r, c, up)

    def gather_b(c):
        rows = out_ref.at[b_rows(c), :]
        return hop(rows, rows, agb_s, agb_r, c, down)

    def reduce_a(c):
        rows = in_a.at[own_rows(c), :]
        return hop(rows, rows, rsa_s, rsa_r, c, down)

    def reduce_b(c):
        rows = in_b.at[own_rows(c), :]
        return hop(rows, rows, rsb_s, rsb_r, c, up)

    def block_start(t, offset):
        return jnp.clip((t - lax.rem(t, group) - offset) * size, 0, half - group * size)

    def reduce_step(t, c, offset, place, rows, landed, move, gather, starts, ends):
        here = rows(c)
        own = own_rows(c)

        def term():
            if not parts:
                return env["ready"][here, :].astype(F32)
            row = place * group * size + c * size - block_start(t, offset)
            return env["part"][pl.ds(pl.multiple_of(row, size), size), :]

        @pl.when(starts)
        def _():
            landed[own, :] = term().astype(BF16)
            move(c).start()

        @pl.when(jnp.logical_not(starts))
        def _():
            move(c).wait_recv()

        @pl.when(jnp.logical_not(starts | ends))
        def _():
            landed[own, :] = (landed[own, :].astype(F32) + term()).astype(BF16)
            move(c).start()

        @pl.when(ends)
        def _():
            total = landed[own, :].astype(F32) + term()
            out_ref[here, :] = finish(total, here, own, env).astype(BF16)
            gather(c).start()

    def gather_step(c, gather, starts, ends):
        @pl.when(jnp.logical_not(starts))
        def _():
            gather(c).wait_recv()

        @pl.when(jnp.logical_not(starts | ends))
        def _():
            gather(c).start()

    def when_chunk(c, work):
        pl.when((c >= 0) & (c < chunks))(lambda: work(c))

    def make_parts(t):
        top = pl.ds(pl.multiple_of(block_start(t, from_last), size), group * size)
        low = pl.ds(pl.multiple_of(half + block_start(t, from_first), size), group * size)

        def columns(n, carry):
            cols = pl.ds(pl.multiple_of(n * TILE, TILE), TILE)
            total = 0.0
            for left, right in parts:
                rows = jnp.concatenate([env[left][top, :], env[left][low, :]], axis=0)
                total = total + dot(rows, env[right][cols, :], 1, 1)
            env["part"][:, cols] = total
            return carry

        lax.fori_loop(0, width // TILE, columns, 0)

    def task_rows(index, tile):
        if tasks[index][0] == "spread":
            tiles = env[tasks[index][3]].shape[0] // ROWS
            own = ROWS // env["spread"].shape[1]
            tile = lax.rem(lax.axis_index("seq") // own + 1 + tile, tiles)
        return pl.ds(pl.multiple_of(tile * ROWS, ROWS), ROWS)

    def run_task(index, tile, slot):
        kind, left, right, name = tasks[index]
        target = env[name]
        rows = task_rows(index, tile)
        if kind in ("weight", "spread"):
            env["turned"][...] = jnp.transpose(env[left][:, rows])

        def columns(n, carry):
            cols = pl.ds(pl.multiple_of(n * TILE, TILE), TILE)
            if kind in ("weight", "spread"):
                value = dot(env["turned"][...], env[right][:, cols], 1, 0)
            elif kind == "keep":
                value = dot(env[left][rows, :], env[right][:, cols], 1, 0)
            else:
                value = dot(env[left][rows, :], env[right][cols, :], 1, 1)
                top = tile * ROWS < half
                mine = (first & top) | (last & jnp.logical_not(top))
                own = pl.multiple_of(lax.rem(tile * ROWS, half), ROWS)
                base = env["middle"][pl.ds(own, ROWS), cols]
                value = value + jnp.where(mine, base, 0.0)
            if kind == "keep":
                target[rows, cols] = value.astype(BF16)
            else:
                env["stage"][slot, :, cols] = value.astype(BF16)
            return carry

        lax.fori_loop(0, target.shape[1] // TILE, columns, 0)
        if kind != "keep":
            stage_copy(index, tile, slot).start()

    def stage_copy(index, tile, slot):
        target = env[tasks[index][3]]
        rows = task_rows(index, tile)
        return pltpu.make_async_copy(
            env["stage"].at[slot, :, : target.shape[1]], target.at[rows, :], env["stage_sem"].at[slot]
        )

    starts_at = [0]
    for task in tasks:
        starts_at.append(starts_at[-1] + env[task[3]].shape[0] // ROWS)
    task_total = starts_at[-1]
    staged = any(task[0] != "keep" for task in tasks)

    def step(t, carry):
        if parts:
            pl.when(lax.rem(t, group) == 0)(lambda: make_parts(t))
        when_chunk(
            t - from_last,
            lambda c: reduce_step(t, c, from_last, 0, a_rows, in_a, reduce_a, gather_a, last, first),
        )
        when_chunk(
            t - from_first,
            lambda c: reduce_step(t, c, from_first, 1, b_rows, in_b, reduce_b, gather_b, first, last),
        )
        when_chunk(t - ahead - out_first, lambda c: gather_step(c, gather_a, first, last))
        when_chunk(t - ahead - out_last, lambda c: gather_step(c, gather_b, last, first))
        for moment, waited in ((1, plan["late"]), (4, plan["later"])):

            @pl.when(t == moment)
            def _():
                for name in waited:
                    loads[name].wait()

        if num_task:
            turn = t - 1
            slot = lax.rem(turn + 2, 2)

            for index in range(num_task if staged else 0):
                low, high = starts_at[index] + 2, min(starts_at[index + 1] + 2, task_total)

                def staged_done(index=index, low=low):
                    stage_copy(index, turn - low, slot).wait()
                    if tasks[index][0] == "spread":
                        spread_rows(env, task_rows(index, turn - low))

                pl.when((turn >= low) & (turn < high))(staged_done)
            for index in range(num_task):
                low, high = starts_at[index], starts_at[index + 1]
                pl.when((turn >= low) & (turn < high))(
                    lambda index=index, low=low: run_task(index, turn - low, slot)
                )
        if work_step:
            work_step(t)
        if seq_count:
            pl.when(t == chunks + ahead)(lambda: full_start(env, count))
        for name, moment in plan["stores"].items():
            if moment == "reduced":
                pl.when(t == chunks + ahead)(lambda name=name: whole_store(env, name).start())
        done_a = t - ahead - out_first - (group - 1)
        done_b = t - ahead - out_last - (group - 1)
        has_a = (done_a >= 0) & (done_a < chunks) & (lax.rem(done_a + 64, group) == 0)
        has_b = (done_b >= 0) & (done_b < chunks) & (lax.rem(done_b + 64, group) == 0)

        @pl.when(has_a | has_b)
        def _():
            block = jnp.where(has_a, done_a // group, chunks // group + done_b // group)
            row_store(env, "out", block).start()
            if plan["rows_done"]:
                plan["rows_done"](env, block)

        if plan["rows_late"]:
            late_a = t - ahead - spread_out - (group - 1) - 2

            place = lax.rem(late_a + 64, group)

            @pl.when((late_a >= 0) & (place < 2))
            def _():
                plan["rows_late"](env, place * (chunks // group) + late_a // group)

        return carry

    for name in plan["held"]:
        if name not in behind:
            loads[name].wait()
    for copy in started:
        copy.wait()
    for name in behind:
        loads[name].start()
    if plan["before"]:
        plan["before"](env)
    for name, moment in plan["stores"].items():
        if moment == "before":
            whole_store(env, name).start()
    work_step = None
    if plan["work"]:
        work_step, work_end, work_steps = plan["work"](env)
        assert work_steps <= steps
    lax.fori_loop(0, steps, step, 0)
    if num_task:
        assert steps - 1 >= task_total
    if staged:
        assert task_total >= 2
        for turn in (task_total - 2, task_total - 1):
            index = max(i for i in range(num_task) if starts_at[i] <= turn)
            stage_copy(index, turn - starts_at[index], turn % 2).wait()
    if "spread" in env:
        spread_wait(env)
    if plan["rows_late"]:
        assert group > 2

        def rest(place, carry):
            plan["rows_late"](env, (place + 1) * (chunks // group) - 1)
            return carry

        lax.fori_loop(0, 2, rest, 0)
    if work_step:
        work_end()
    if seq_count:
        norm_finish(env, seq_count, count)

    def drain(c, carry):
        @pl.when(jnp.logical_not(first))
        def _():
            reduce_a(c).wait_send()
            gather_b(c).wait_send()

        @pl.when(jnp.logical_not(last))
        def _():
            reduce_b(c).wait_send()
            gather_a(c).wait_send()

        return carry

    lax.fori_loop(0, chunks, drain, 0)
    for name, moment in plan["stores"].items():
        if moment == "rows":
            for block in range(tokens // LANES):
                row_store(env, name, block).wait()
        else:
            whole_store(env, name).wait()


def line_sum(
    finish, count, held, vecs, parts, collective_id, *, tokens, late=(), later=(), tasks=(), owns=(),
    sent=(), stores=(), scratch=(), loose=(), chunks=16, group=4, turned=False, start=None, before=None, rows_done=None, rows_late=None, work=None,
    seq_count=0, seq_barrier=0, micros=110,
):
    names = dict(scratch)
    if parts:
        width = (held.get(parts[0][1]) if parts[0][1] in held else names[parts[0][1]]).shape[0]
    else:
        width = held["ready"].shape[1]
    half = tokens // 2
    depth = tokens if turned or any(task[0] == "weight" for task in tasks) else LANES
    staged = [shape.shape[-1] for _, shape in sent] if tasks else []
    stage_width = max(staged + [LANES])
    fixed = [
        ("in_a", pltpu.VMEM((half, width), BF16)),
        ("in_b", pltpu.VMEM((half, width), BF16)),
        ("part", pltpu.VMEM((2 * group * half // chunks if parts else 8, width), F32)),
        ("turned", pltpu.VMEM((ROWS, depth), BF16)),
        ("stage", pltpu.VMEM((2, ROWS if staged else 16, stage_width), BF16)),
        ("load_sem", pltpu.SemaphoreType.DMA((len(held),))),
        ("stage_sem", pltpu.SemaphoreType.DMA((2,))),
    ] + [
        (name, pltpu.SemaphoreType.DMA((chunks,)))
        for name in ("rsa_s", "rsa_r", "rsb_s", "rsb_r", "aga_s", "aga_r", "agb_s", "agb_r")
    ]
    assert half // chunks * group == LANES
    loose = dict(loose)
    stores = dict(stores, out="rows")
    shapes = [("out", jax.ShapeDtypeStruct((tokens, width), BF16))] + list(owns)
    scratch = list(scratch) + fixed
    for name, shape in shapes:
        if name in stores:
            scratch.append((name, pltpu.VMEM(shape.shape, shape.dtype)))
            number = tokens // LANES if stores[name] == "rows" else 1
            scratch.append(("sem " + name, pltpu.SemaphoreType.DMA((number,))))
    order = (
        ["source " + name for name in held]
        + list(loose)
        + list(vecs)
        + ["target " + name if name in stores else name for name, _ in shapes]
        + [name for name, _ in sent]
        + list(held)
        + [name for name, _ in scratch]
    )
    plan = dict(
        finish=finish,
        order=order,
        held=list(held),
        parts=parts,
        late=tuple(late),
        later=tuple(later),
        stores=stores,
        tasks=tasks,
        start=start,
        work=work,
        seq_count=seq_count,
        seq_barrier=seq_barrier or seq_count,
        before=before,
        rows_done=rows_done,
        rows_late=rows_late,
    )
    whole = pl.BlockSpec(memory_space=pltpu.VMEM)
    any_space = pl.BlockSpec(memory_space=pl.ANY)
    return pl.pallas_call(
        functools.partial(line_kernel, plan, count, chunks, group, SLACK),
        out_shape=[shape for _, shape in shapes] + [shape for _, shape in sent],
        in_specs=[any_space] * (len(held) + len(loose)) + [whole] * len(vecs),
        out_specs=[any_space if name in stores else whole for name, _ in shapes]
        + [any_space] * len(sent),
        scratch_shapes=[pltpu.VMEM(array.shape, array.dtype) for array in held.values()]
        + [shape for _, shape in scratch],
        compiler_params=pltpu.CompilerParams(
            collective_id=collective_id, has_side_effects=True, vmem_limit_bytes=VMEM_LIMIT
        ),
        cost_estimate=cost(micros),
    )(*held.values(), *loose.values(), *vecs.values())


def axis_barrier(counts):
    barrier = pltpu.get_barrier_semaphore()
    for axis, count in counts:
        me = lax.axis_index(axis)
        for k in range(1, count):
            pl.semaphore_signal(
                barrier, inc=1, device_id={axis: lax.rem(me + k, count)}, device_id_type=MESH
            )
    pl.semaphore_wait(barrier, sum(count - 1 for _, count in counts))


def share(axis, count, pick, landed, send_sem, recv_sem, start=True):
    me = lax.axis_index(axis)
    copies = []
    for k in range(1, count):
        device = lax.rem(me + k, count)
        copy = pltpu.make_async_remote_copy(
            src_ref=pick(device),
            dst_ref=landed.at[me],
            send_sem=send_sem.at[k],
            recv_sem=recv_sem.at[k],
            device_id={axis: device},
            device_id_type=MESH,
        )
        if start:
            copy.start()
        copies.append(copy)
    return copies


def total_of(landed, count):
    total = landed[0]
    for k in range(1, count):
        total = total + landed[k]
    return total


def matmul(left, right, left_dim, right_dim, kind=F32):
    return dot(left, right, left_dim, right_dim).astype(kind)


def body(
    seq_count,
    tp_count,
    block_in,
    segment_ids,
    first_gain,
    first_bias,
    w_query,
    w_key,
    w_value,
    head_gain,
    head_bias,
    w_out,
    second_gain,
    second_bias,
    w_up,
    hidden_gain,
    hidden_bias,
    w_down,
    out_cotangent,
):
    seq_index = lax.axis_index("seq")
    row_count, span, model_width = block_in.shape
    length = span * seq_count
    tokens = row_count * span
    head_width = w_query.shape[1]
    hidden_width = w_up.shape[1] * tp_count
    groups = seq_count // row_count

    seg_row = lax.dynamic_slice_in_dim(segment_ids, seq_index // groups, 1, 0)
    block = block_in.reshape(tokens, model_width)
    cotangent = out_cotangent.reshape(tokens, model_width)

    first_act, qkv_row, tables, o_row, lse, mixed, vecs = front(
        block,
        w_query,
        w_key,
        w_value,
        seg_row,
        (
            first_gain, first_bias, second_gain, second_bias,
            hidden_gain, hidden_bias, head_gain, head_bias,
        ),
        seq_count,
        groups,
        1,
    )
    def shape_of(dims, kind=F32):
        return jax.ShapeDtypeStruct(dims, kind)

    hidden_size = hidden_gain.shape[0]
    own_shape = shape_of((tokens // 2, model_width))
    sums_shape = shape_of((2, 8, model_width))
    landed = pltpu.VMEM((tp_count, 8, tokens), F32)
    pair_sem = pltpu.SemaphoreType.DMA((tp_count,))
    block_sem = pltpu.SemaphoreType.DMA((tokens // LANES, tp_count))

    def before_middle(env):
        env["hidden_vec_grads"][...] = jnp.zeros_like(env["hidden_vec_grads"])
        norm_heads(env, tp_count, model_width)

    (
        second_act, middle_own, head_act, head_sums, hidden_act, grad_up, hidden_vec_grads
    ) = line_sum(
        finish_middle,
        tp_count,
        dict(mixed=mixed, w_out=w_out, block=block, cotangent=cotangent, w_down=w_down, w_up=w_up),
        dict(vecs=vecs),
        (("head_act", "w_out"),),
        3,
        tokens=tokens,
        late=("cotangent", "w_down"),
        later=("block", "w_up"),
        stores=dict(middle="reduced", head_act="before", hidden_act="rows", grad_up="rows"),
        tasks=(("keep", "cotangent", "w_down", "hidden_grad"),),
        owns=(
            ("middle", own_shape),
            ("head_act", shape_of((tokens, head_width), BF16)),
            ("head_sums", shape_of((8, tokens))),
            ("hidden_act", shape_of((tokens, hidden_size), BF16)),
            ("grad_up", shape_of((tokens, hidden_size), BF16)),
            ("hidden_vec_grads", shape_of((2, 8, hidden_size))),
        ),
        scratch=(
            ("hidden_grad", pltpu.VMEM((tokens, hidden_size), BF16)),
            ("hidden_sums", pltpu.VMEM((8, tokens), F32)),
            ("head_landed", landed),
            ("hidden_landed", landed),
            ("head_send", pair_sem),
            ("head_recv", pair_sem),
            ("hidden_send", block_sem),
            ("hidden_recv", block_sem),
        ),
        before=before_middle,
        rows_done=lambda env, block: hidden_rows(env, tp_count, block),
        rows_late=lambda env, block: norm_hidden(env, tp_count, hidden_width, block),
        micros=140,
    )

    weight_shape = shape_of((model_width, hidden_size), BF16)
    grad_middle_low, second_sums, grad_middle_own, down_part, _, w_up_terms, down_terms = line_sum(
        finish_second,
        tp_count,
        dict(
            grad_up=grad_up,
            w_up=w_up,
            cotangent=cotangent,
            middle=middle_own,
            hidden_act=hidden_act,
            w_down=w_down,
            second_act=second_act,
        ),
        dict(vecs=vecs),
        (("grad_up", "w_up"),),
        4,
        tokens=tokens,
        late=("hidden_act", "cotangent"),
        later=("w_down", "middle", "second_act"),
        stores=dict(middle_grad="reduced"),
        tasks=(
            ("spread", "cotangent", "hidden_act", "w_down_terms"),
            ("down", "hidden_act", "w_down", "down_part"),
            ("weight", "second_act", "grad_up", "w_up_terms"),
        ),
        owns=(("sums", sums_shape), ("middle_grad", own_shape)),
        sent=(
            ("down_part", shape_of((tokens, model_width), BF16)),
            ("w_down_terms", weight_shape),
            ("w_up_terms", weight_shape),
            ("spread", shape_of((seq_count, model_width // seq_count, hidden_size), BF16)),
        ),
        scratch=(
            ("spread_send", pltpu.SemaphoreType.DMA((seq_count,))),
            ("spread_recv", pltpu.SemaphoreType.DMA((seq_count,))),
            ("spread_own", pltpu.SemaphoreType.DMA((1,))),
        ),
        seq_barrier=seq_count,
    )
    def scatter(grad):
        return lax.psum_scatter(grad, "seq", scatter_dimension=0, tiled=True)

    w_up_grad = scatter(w_up_terms)

    pairs = head_width // groups // LANES
    many = pltpu.SemaphoreType.DMA((pairs, seq_count))
    pair_rows = pltpu.VMEM((length, LANES), BF16)
    pair_sums = pltpu.VMEM((length, LANES), F32)
    pair_heads = pltpu.VMEM((2, length, LANES), BF16)
    block_out, grads, head_vec_grads, head_terms = line_sum(
        lambda total, here, own, env: total,
        tp_count,
        dict(
            ready=down_part,
            low=grad_middle_low,
            w_out=w_out,
            mixed=mixed,
            head_sums=head_sums,
            qkv=qkv_row,
            o=o_row,
            lse=lse,
            tables=tables,
            first_act=first_act,
            head_act=head_act,
        ),
        dict(vecs=vecs, seg_row=seg_row),
        (),
        5,
        tokens=tokens,
        late=("low", "w_out", "mixed", "head_sums"),
        later=("qkv", "o", "lse", "tables", "first_act", "head_act"),
        owns=(
            ("grads", shape_of((tokens, 3 * head_width), BF16)),
            ("head_vec_grads", shape_of((2, 8, head_width))),
        ),
        sent=(("head_terms", shape_of((model_width, 4 * head_width), BF16)),),
        turned=True,
        scratch=(
            ("weight_stage", pltpu.VMEM((2, ROWS, 4 * head_width), BF16)),
            ("weight_sem", pltpu.SemaphoreType.DMA((2,))),
            ("do", pltpu.VMEM((tokens, head_width), BF16)),
            ("scaled", pltpu.VMEM((tokens, head_width), F32)),
            ("head_part", pltpu.VMEM((8, tokens), F32)),
            ("head_landed", landed),
            ("do_row", pltpu.VMEM((pairs, length, LANES), BF16)),
            ("made", pltpu.VMEM((pairs, length, 3 * LANES), BF16)),
            ("bias", pltpu.VMEM((length, length), F32)),
            ("qs", pair_heads),
            ("ks", pair_rows),
            ("kms", pair_heads),
            ("dos", pair_heads),
            ("delta", pltpu.VMEM((8, length), F32)),
            ("dq", pair_sums),
            ("dk", pair_sums),
            ("dv", pair_sums),
            ("head_send", pair_sem),
            ("head_recv", pair_sem),
            ("there_send", many),
            ("there_recv", many),
            ("back_send", many),
            ("back_recv", many),
        ),
        work=lambda env: back_work(env, seq_count, tp_count, groups),
        seq_barrier=seq_count,
    )
    grads, head_terms, w_up_grad = lax.optimization_barrier((grads, head_terms, w_up_grad))
    head_grads = scatter(head_terms)
    own_width = model_width // seq_count
    split_width = hidden_size + head_width
    seq_sem = pltpu.SemaphoreType.DMA((seq_count,))
    input_grad, _, norm_own, norm_split = line_sum(
        finish_first,
        tp_count,
        dict(grads=grads, block=block, middle_grad=grad_middle_own),
        dict(
            vecs=vecs,
            second_sums=second_sums,
            hidden_vec_grads=hidden_vec_grads,
            head_vec_grads=head_vec_grads,
        ),
        (("grads", "w_pairs"),),
        8,
        tokens=tokens,
        chunks=32,
        group=8,
        later=("block", "middle_grad"),
        loose=dict(w_query=w_query, w_key=w_key, w_value=w_value),
        owns=(
            ("sums", sums_shape),
            ("norm_own", shape_of((8, own_width))),
            ("norm_split", shape_of((8, split_width))),
        ),
        scratch=(
            ("w_pairs", pltpu.VMEM((model_width, 3 * head_width), BF16)),
            ("pair_sem", pltpu.SemaphoreType.DMA((3 * head_width // LANES,))),
            ("split", pltpu.VMEM((8, split_width), F32)),
            ("split_landed", pltpu.VMEM((seq_count, 8, split_width), F32)),
            ("full", pltpu.VMEM((8, model_width), F32)),
            ("full_landed", pltpu.VMEM((tp_count, 8, model_width), F32)),
            ("own_landed", pltpu.VMEM((seq_count, 8, own_width), F32)),
            ("split_send", seq_sem),
            ("split_recv", seq_sem),
            ("full_send", pair_sem),
            ("full_recv", pair_sem),
            ("own_send", seq_sem),
            ("own_recv", seq_sem),
        ),
        start=load_pairs,
        seq_count=seq_count,
    )

    (
        w_query_grad, w_key_grad, w_value_grad, w_out_grad, w_up_grad, w_down_grad, input_grad,
        block_out, *vectors,
    ) = last_results(
        head_grads, w_up_grad, down_terms, input_grad, block_out, norm_own, norm_split, head_width
    )
    vectors = [vector.reshape(-1) for vector in vectors]
    return (
        block_out.reshape(block_in.shape),
        input_grad.reshape(block_in.shape),
        vectors[2],
        vectors[3],
        w_query_grad,
        w_key_grad,
        w_value_grad,
        vectors[6],
        vectors[7],
        w_out_grad,
        vectors[0],
        vectors[1],
        w_up_grad,
        vectors[4],
        vectors[5],
        w_down_grad,
    )


def solution(mesh):
    return jax.shard_map(
        functools.partial(body, mesh.shape["seq"], mesh.shape["tp"]),
        mesh=mesh,
        in_specs=(
            P(None, "seq", None),
            P(),
            P(),
            P(),
            P(None, "tp"),
            P(None, "tp"),
            P(None, "tp"),
            P("tp"),
            P("tp"),
            P(None, "tp"),
            P(),
            P(),
            P(None, "tp"),
            P("tp"),
            P("tp"),
            P(None, "tp"),
            P(None, "seq", None),
        ),
        out_specs=(
            P(None, "seq", None),
            P(None, "seq", None),
            P("seq"),
            P("seq"),
            P("seq", "tp"),
            P("seq", "tp"),
            P("seq", "tp"),
            P("tp"),
            P("tp"),
            P("seq", "tp"),
            P("seq"),
            P("seq"),
            P("seq", "tp"),
            P("tp"),
            P("tp"),
            P("seq", "tp"),
        ),
        check_vma=False,
    )
```
